32 devices in a mesh: groups: 2 (over y), date: 4 (over z), rng: 2 (over x), az: 2 (over core).
Axes of the slice: x: 2, y: 2, z: 4, core: 2. Of those that a mesh axis runs over, the one named last changes fastest.
Arguments:
- slc: bfloat16 [2, 8, 64, 5120], P(None, ('groups', 'date'), 'az', 'rng'), parts along dimension 1, may hold values from -24 to 24
- offsets: int32 [8, 2], P(('groups', 'date')), parts along dimension 0, may hold values from -24 to 24, as said below
- kernel_index: int32 [8, 2], P(('groups', 'date')), parts along dimension 0, may hold values from 0 to 15
- range_shift: float32 [8], P('groups'), parts along dimension 0, may hold values from -0.15 to 0.15
Outputs:
- ifg: float32 [2, 8, 8, 16, 256], P(None, ('groups', 'date'), None, 'az', 'rng'), parts along dimension 1
The draws below stay inside these ranges and needn't reach their ends.
There are 2 independent parts, one for each index of `groups`. The reference program is written for one: setup_inputs(seed, part) draws one part's arguments, and reference() takes and returns one part's arrays. A program takes and returns all parts, laid end to end along the dimension named above; each array names one. Nothing has to cross between parts.
Inputs may be any that keep to these rules, and one draw needn't show every extreme that they name: `offsets`: column 0 is the azimuth offset, within -8 to 8; column 1 is the range offset. Both ends of both ranges are taken by some date.
All inputs are finite; a program needn't handle non-finite values.
Results may differ from the reference program's by a relative error of at most 0.0039.
Values may be sent and summed in bfloat16 or wider, within the bound.
No kernel may reach another device: no remote copies, remote signals or barrier semaphores. Data moves between devices by JAX's collectives and lax.ppermute only.
A program may use at most 64 MiB of HBM per device.

```python
import jax
import jax.numpy as jnp
from jax import lax

LAGS = 8
MAX_AZ = 8
MAX_RG = 24
KERNELS = 16
FILTER_HALF = 8
LOOK_AZ = 4
LOOK_RG = 20
HALO_AZ = 12
HALO_RG = 36
DATES = 4
AZ = 64
RG = 5120


def draw_offsets(key, part):
    line_key, column_key, ranking_key = jax.random.split(key, 3)
    line_shift = jax.random.randint(line_key, (DATES,), -MAX_AZ, MAX_AZ + 1)
    column_shift = jax.random.randint(column_key, (DATES,), -MAX_RG, MAX_RG + 1)
    ranking = jax.random.permutation(ranking_key, DATES)
    line_shift = line_shift.at[ranking[0]].set(MAX_AZ).at[ranking[1]].set(-MAX_AZ)
    column_shift = column_shift.at[ranking[2]].set(MAX_RG).at[ranking[3]].set(-MAX_RG)
    return jnp.stack([line_shift, column_shift], axis=1).astype(jnp.int32)


def touch_ends(result, stream_key, least, largest):
    index_at = [jax.random.randint(jax.random.fold_in(stream_key, axis), (), 0, length) for axis, length in enumerate(result.shape)]
    longest = result.shape.index(max(result.shape))
    next_to = index_at[:longest] + [(index_at[longest] + 1) % result.shape[longest]] + index_at[longest + 1:]
    return result.at[tuple(index_at)].set(least).at[tuple(next_to)].set(largest)


def steps_of(stream_key, dims, pieces, smallest, high):
    level, own = 1.0, jax.random.fold_in(stream_key, 6)
    for dim, blocks in pieces:
        heights = jnp.exp(jax.random.uniform(jax.random.fold_in(own, dim), (blocks,), jnp.float32, smallest / len(pieces), high / len(pieces)))
        level = level * jnp.repeat(heights, dims[dim] // blocks).reshape([-1 if axis == dim else 1 for axis in range(len(dims))])
    return level


def scatter_about(key, shape, deviation, limit, cuts=(), held_as=jnp.bfloat16):
    loudness = steps_of(key, shape, cuts, -0.22, 0.18) if cuts else 1.0
    drawn = jax.random.normal(key, shape, jnp.float32) * deviation * loudness
    return jnp.minimum(jnp.maximum(drawn, -limit), limit).astype(held_as)


def setup_inputs(seed: int = 0, part: int = 0) -> dict:
    streams_of = jax.random.split(jax.random.key(seed), 5)
    part_keys = jax.random.split(jax.random.fold_in(streams_of[4], part), 5)
    slc = scatter_about(part_keys[0], (2, DATES, AZ, RG), 4.0, 24.0, ((1, 4), (2, 2), (3, 2)))
    offsets = draw_offsets(jax.random.fold_in(jax.random.fold_in(streams_of[4], part), 71), part)
    kernel_index = touch_ends(jax.random.randint(part_keys[2], (DATES, 2), 0, KERNELS), jax.random.fold_in(part_keys[2], 1), 0, KERNELS - 1).astype(jnp.int32)
    range_shift = jnp.clip(jax.random.uniform(part_keys[3], (DATES,), jnp.float32, -0.15, 0.15), -0.15, 0.15)
    return {"slc": slc, "offsets": offsets, "kernel_index": kernel_index, "range_shift": range_shift}


def kernel_taps(index):
    fraction = index.astype(jnp.float32) / KERNELS
    position = jnp.arange(8, dtype=jnp.float32) - 3.0 - fraction
    shaped = jnp.sinc(position) * (0.5 + 0.5 * jnp.cos(jnp.pi * position / 5.0))
    return shaped / jnp.sum(shaped)


def lowpass_taps(band_gap):
    spacing = jnp.arange(2 * FILTER_HALF + 1, dtype=jnp.float32) - FILTER_HALF
    window = 0.4 * jnp.sinc(0.4 * spacing) * (0.54 + 0.46 * jnp.cos(jnp.pi * spacing / (FILTER_HALF + 1)))
    phase_angle = jnp.pi * band_gap * spacing
    return window * jnp.cos(phase_angle), window * jnp.sin(phase_angle)


def resample(source, shift_pair, kernel_pair, line_count, column_count):
    span_width = column_count + 2 * FILTER_HALF
    line_start = (HALO_AZ + shift_pair[0] - 3).astype(jnp.int32)
    column_start = (HALO_RG - FILTER_HALF + shift_pair[1] - 3).astype(jnp.int32)
    window = lax.dynamic_slice(source, (jnp.int32(0), line_start, column_start), (2, line_count + 7, span_width + 7)).astype(jnp.float32)
    column_taps = kernel_taps(kernel_pair[1])
    line_taps = kernel_taps(kernel_pair[0])
    across = sum(column_taps[q] * window[:, :, q:q + span_width] for q in range(8))
    return sum(line_taps[p] * across[:, p:p + line_count, :] for p in range(8)).astype(jnp.bfloat16)


def spectral_gap(range_shift, own_date, other_date):
    own_value = lax.dynamic_index_in_dim(range_shift, own_date, 0, keepdims=False)
    other_value = lax.dynamic_index_in_dim(range_shift, other_date, 0, keepdims=False)
    return own_value - other_value


def pair_looks(master, partner, band_gap):
    cos_taps, sin_taps = lowpass_taps(band_gap)
    column_count = master.shape[-1] - 2 * FILTER_HALF
    line_count = master.shape[1]
    master_re = jnp.zeros((line_count, column_count), jnp.float32)
    master_im = master_re
    partner_re = master_re
    partner_im = master_re
    for t in range(2 * FILTER_HALF + 1):
        first_part = master[:, :, t:t + column_count].astype(jnp.float32)
        second_part = partner[:, :, t:t + column_count].astype(jnp.float32)
        master_re = master_re + cos_taps[t] * first_part[0] + sin_taps[t] * first_part[1]
        master_im = master_im + cos_taps[t] * first_part[1] - sin_taps[t] * first_part[0]
        partner_re = partner_re + cos_taps[t] * second_part[0] - sin_taps[t] * second_part[1]
        partner_im = partner_im + cos_taps[t] * second_part[1] + sin_taps[t] * second_part[0]
    product = jnp.stack([master_re * partner_re + master_im * partner_im, master_im * partner_re - master_re * partner_im])
    blocks = product.reshape(2, line_count // LOOK_AZ, LOOK_AZ, column_count // LOOK_RG, LOOK_RG)
    return jnp.mean(blocks, axis=(2, 4))


def reference(slc, offsets, kernel_index, range_shift):
    padded = jnp.pad(slc, ((0, 0), (0, 0), (HALO_AZ, HALO_AZ), (HALO_RG, HALO_RG)))

    def one_resample(inputs):
        source, shift_pair, kernel_pair = inputs
        return resample(source, shift_pair, kernel_pair, AZ, RG)

    resampled = lax.map(one_resample, (jnp.moveaxis(padded, 1, 0), offsets, kernel_index))

    def one_date(date_index):
        master = lax.dynamic_index_in_dim(resampled, date_index, 0, keepdims=False)
        lag_looks = []
        for step_ahead in range(1, LAGS + 1):
            target = date_index + step_ahead
            chosen = jnp.minimum(target, DATES - 1)
            partner = lax.dynamic_index_in_dim(resampled, chosen, 0, keepdims=False)
            usable = (target < DATES).astype(jnp.float32)
            lag_looks.append(pair_looks(master, partner, spectral_gap(range_shift, date_index, chosen)) * usable)
        return jnp.stack(lag_looks, axis=1)

    stacked = lax.map(one_date, jnp.arange(DATES, dtype=jnp.int32))
    return jnp.moveaxis(stacked, 0, 1)
```

```python
import functools

import jax
import jax.numpy as jnp
import numpy as np
from jax import lax
from jax.experimental import pallas as pl
from jax.experimental.pallas import tpu as pltpu
from jax.sharding import PartitionSpec as P

LAGS = 8
KERNELS = 16
TAPS = 8
FILTER_HALF = 8
FILTER_TAPS = 2 * FILTER_HALF + 1
LOOK_AZ = 4
LOOK_RG = 20
LANES = 128
META = 3
UNROLLED_PAIRS = 12


def up(value, unit):
    return -(-value // unit) * unit


def kernel_table():
    position = np.arange(TAPS) - 3.0 - np.arange(KERNELS)[:, None] / KERNELS
    shaped = np.sinc(position) * (0.5 + 0.5 * np.cos(np.pi * position / 5.0))
    table = np.zeros((KERNELS, LANES), np.float32)
    table[:, :TAPS] = shaped / shaped.sum(1, keepdims=True)
    return table


def lowpass_row(width):
    t = np.arange(FILTER_TAPS) - FILTER_HALF
    row = np.zeros((1, width), np.float32)
    row[0, :FILTER_TAPS] = 0.4 * np.sinc(0.4 * t) * (0.54 + 0.46 * np.cos(np.pi * t / (FILTER_HALF + 1)))
    return row


def halves(value):
    high = value.astype(jnp.bfloat16)
    return high, (value - high.astype(jnp.float32)).astype(jnp.bfloat16)


def dot(a, b):
    return jnp.dot(a, b, preferred_element_type=jnp.float32)


def dot_nt(a, b):
    return lax.dot_general(a, b, (((1,), (1,)), ((), ())), preferred_element_type=jnp.float32)


def pack_kernel(chunk, place_ref, offsets_ref, index_ref, slc_ref, before_ref, after_ref, out_ref, wide_ref):
    columns = slc_ref.shape[1]
    wide = out_ref.shape[2]
    first = place_ref[0] == 0
    last = place_ref[0] == place_ref[1] - 1
    zero = jnp.zeros_like(before_ref[...])
    wide_ref[:, :LANES] = jnp.where(first, zero, before_ref[...])
    wide_ref[:, LANES : LANES + columns] = slc_ref[...]
    wide_ref[:, LANES + columns :] = jnp.where(last, zero, after_ref[...])
    lane = lax.broadcasted_iota(jnp.int32, (slc_ref.shape[0], wide), 1)
    numbers = [offsets_ref[0, 0], index_ref[0, 0], index_ref[0, 1]]
    for j in range(out_ref.shape[0]):
        start = LANES + chunk * j - FILTER_HALF - 3 + offsets_ref[0, 1]
        tile = lax.shift_right_logical(start, 7)
        within = lax.bitwise_and(start, LANES - 1)
        window = wide_ref[:, pl.ds(pl.multiple_of(tile * LANES, LANES), wide + LANES)].astype(jnp.float32)
        moved = pltpu.roll(window, wide + LANES - within, 1)[:, :wide]
        for slot, number in enumerate(numbers):
            moved = jnp.where(lane == wide - META + slot, number.astype(jnp.float32), moved)
        out_ref[j] = moved.astype(jnp.bfloat16)


def picked_taps(table, index):
    row = lax.broadcasted_iota(jnp.int32, table.shape, 0).astype(jnp.float32)
    return jnp.sum(jnp.where(row == index, table, 0.0), axis=0, keepdims=True)


def banded(taps, distance):
    out = jnp.zeros(distance.shape, jnp.float32)
    for q in range(TAPS):
        out = jnp.where(distance == q, taps[:, q : q + 1], out)
    return out


def pairs_kernel(chunk, pairs, *refs):
    if isinstance(pairs, int):
        table_of_pairs, refs = refs[0], refs[1:]
    shift_ref, table_ref, lowpass_ref, recv_ref, out_ref, resampled_ref, weight_ref, product_ref = refs
    sources, rows, wide = recv_ref.shape
    dates = shift_ref.shape[0]
    az_count = sources // dates
    own_lines = rows // 2
    lines = own_lines * az_count
    groups = lines // LOOK_AZ
    looks = chunk // LOOK_RG
    table = table_ref[...]
    held = resampled_ref.shape[2]

    out_row = lax.broadcasted_iota(jnp.int32, (lines, lines), 0)
    in_row = lax.broadcasted_iota(jnp.int32, (lines, lines), 1)
    line = LOOK_AZ * (out_row % groups) + out_row // groups
    line_distance = (in_row - line + 3).astype(jnp.float32)
    span = min(2 * LANES, wide)
    column_distance = (
        lax.broadcasted_iota(jnp.int32, (span, LANES), 0) - lax.broadcasted_iota(jnp.int32, (span, LANES), 1)
    ).astype(jnp.float32)
    for date in range(dates):
        numbers = recv_ref[date * az_count, 0:16, wide - LANES :].astype(jnp.float32)[0:1, LANES - META :]
        line_offset, line_index, column_index = (numbers[:, s : s + 1] for s in range(META))
        line_taps = banded(picked_taps(table, line_index), line_distance - line_offset)
        line_taps = jnp.concatenate(halves(line_taps), axis=0)
        column_high, column_low = halves(banded(picked_taps(table, column_index), column_distance))
        moved = []
        for plane in range(2):
            rows_of = slice(plane * own_lines, (plane + 1) * own_lines)
            source = jnp.concatenate([recv_ref[date * az_count + a, rows_of, :] for a in range(az_count)], axis=0)
            both = dot(line_taps, source)
            moved.append(both[:lines] + both[lines:])
        moved_high, moved_low = halves(jnp.concatenate(moved, axis=0))
        for begin in range(0, held, LANES):
            end = min(begin + span, wide)
            taken = end - begin
            total = dot(moved_high[:, begin:end], column_high[:taken])
            total += dot(moved_low[:, begin:end], column_high[:taken])
            total += dot(moved_high[:, begin:end], column_low[:taken])
            resampled_ref[date, :, begin : begin + LANES] = total.astype(jnp.bfloat16)

    window = lowpass_ref[...]
    spacing = lax.broadcasted_iota(jnp.int32, window.shape, 1).astype(jnp.float32) - FILTER_HALF
    span = min(2 * LANES, held)

    def one_pair(place, own, other):
        gap = shift_ref[own] - shift_ref[other]
        angle = jnp.where(jnp.abs(spacing) <= FILTER_HALF, jnp.pi * gap * spacing, 0.0)
        for part, taps in enumerate((window * jnp.cos(angle), window * jnp.sin(angle))):
            spread = jnp.broadcast_to(taps, (LANES, 2 * LANES))
            spread = pltpu.roll(spread, 0, 1, stride=1, stride_axis=0)
            high, low = halves(spread)
            weight_ref[0, part * LANES : (part + 1) * LANES, :] = high
            weight_ref[1, part * LANES : (part + 1) * LANES, :] = low
        both = jnp.concatenate([resampled_ref[own], resampled_ref[other]], axis=0)
        for begin in range(0, up(chunk, LANES), LANES):
            end = min(begin + span, held)
            taken = end - begin
            total = dot_nt(both[:, begin:end], weight_ref[0, :, :taken])
            total += dot_nt(both[:, begin:end], weight_ref[1, :, :taken])
            cos, sin = total[:, :LANES], total[:, LANES:]
            re, im = slice(0, lines), slice(lines, 2 * lines)
            master_re = cos[re] + sin[im]
            master_im = cos[im] - sin[re]
            re, im = slice(2 * lines, 3 * lines), slice(3 * lines, 4 * lines)
            partner_re = cos[re] - sin[im]
            partner_im = cos[im] + sin[re]
            for part, product in enumerate(
                (
                    master_re * partner_re + master_im * partner_im,
                    master_im * partner_re - master_re * partner_im,
                )
            ):
                summed = sum(product[k * groups : (k + 1) * groups] for k in range(LOOK_AZ))
                product_ref[place, part, :, begin : begin + LANES] = summed

    if isinstance(pairs, int):
        count = pairs

        def step(place, carry):
            one_pair(place, table_of_pairs[place, 0], table_of_pairs[place, 1])
            return carry

        lax.fori_loop(0, count, step, 0)
    else:
        count = len(pairs)
        for place, (own, other) in enumerate(pairs):
            one_pair(place, own, other)

    out_width = out_ref.shape[2]
    column = lax.broadcasted_iota(jnp.int32, (product_ref.shape[3], out_width), 0)
    lane = lax.broadcasted_iota(jnp.int32, (product_ref.shape[3], out_width), 1)
    collect = jnp.where(column // LOOK_RG == lane % looks, 1.0, 0.0).astype(jnp.bfloat16)
    high, low = halves(product_ref[...].reshape(count * 2 * groups, product_ref.shape[3]))
    total = (dot(high, collect) + dot(low, collect)) * (1.0 / (LOOK_AZ * LOOK_RG))
    total = total.reshape(count, 2, groups, out_width)
    own_lane = lax.broadcasted_iota(jnp.int32, (groups, out_width), 1) // looks
    place = 0
    for own in range(dates):
        value = jnp.zeros((groups, out_width), jnp.float32)
        for lag in range(min(LAGS, dates - 1 - own)):
            for part in range(2):
                value = jnp.where(own_lane == lag * 2 + part, total[place, part], value)
            place += 1
        out_ref[own * az_count : (own + 1) * az_count] = value.reshape(az_count, groups // az_count, out_width)


def unpack_kernel(used_lags, looks, recv_ref, out_ref):
    sources, groups, width = recv_ref.shape
    columns = out_ref.shape[-1]
    lane = lax.broadcasted_iota(jnp.int32, (groups, columns), 1) // looks
    out_ref[...] = jnp.zeros_like(out_ref)
    for lag in range(used_lags):
        for part in range(2):
            value = jnp.zeros((groups, columns), jnp.float32)
            for source in range(sources):
                block = recv_ref[source]
                if width != columns:
                    block = block[:, :columns]
                shift = looks * (source - lag * 2 - part) % columns
                if shift:
                    block = pltpu.roll(block, shift, 1)
                value = jnp.where(lane == source, block, value)
            out_ref[part, lag] = value


def body(slc, offsets, kernel_index, range_shift):
    axes = ("date", "az")
    date_count, az_count, rng_count = (lax.axis_size(a) for a in ("date", "az", "rng"))
    peers = date_count * az_count
    lines, columns = slc.shape[2], slc.shape[3]
    dates = range_shift.shape[0]
    chunk = columns // peers
    looks = chunk // LOOK_RG
    groups = lines * az_count // LOOK_AZ
    wide = up(chunk + 2 * FILTER_HALF + TAPS - 1 + META, LANES)
    held = up(chunk + 2 * FILTER_HALF, LANES)
    used_lags = min(LAGS, dates - 1)
    out_width = up(used_lags * 2 * looks, LANES)
    vmem = pl.BlockSpec(memory_space=pltpu.VMEM)
    smem = pl.BlockSpec(memory_space=pltpu.SMEM)
    limit = pltpu.CompilerParams(vmem_limit_bytes=32 * 1024 * 1024)

    cells = slc.reshape(2 * lines, columns)
    place = lax.axis_index("rng")
    if rng_count == 2:
        edge = jnp.where(place == 0, cells[:, columns - LANES :], cells[:, :LANES])
        before = after = lax.ppermute(edge, "rng", [(0, 1), (1, 0)])
    else:
        forth = [(i, i + 1) for i in range(rng_count - 1)]
        before = lax.ppermute(cells[:, columns - LANES :], "rng", forth)
        after = lax.ppermute(cells[:, :LANES], "rng", [(b, a) for a, b in forth])

    packed = pl.pallas_call(
        functools.partial(pack_kernel, chunk),
        out_shape=jax.ShapeDtypeStruct((peers, 2 * lines, wide), jnp.bfloat16),
        in_specs=[smem] * 3 + [vmem] * 3,
        out_specs=vmem,
        scratch_shapes=[pltpu.VMEM((2 * lines, columns + 2 * LANES), jnp.bfloat16)],
        compiler_params=limit,
    )(jnp.stack([place, rng_count]).astype(jnp.int32), offsets, kernel_index, cells, before, after)
    arrived = lax.all_to_all(packed, axes, 0, 0, tiled=True)

    pairs = [(own, own + lag) for own in range(dates) for lag in range(1, LAGS + 1) if own + lag < dates]
    count = len(pairs)
    first = [jnp.asarray(np.array(pairs, np.int32))] if count > UNROLLED_PAIRS else []
    looked = pl.pallas_call(
        functools.partial(pairs_kernel, chunk, count if first else pairs),
        out_shape=jax.ShapeDtypeStruct((peers, groups // az_count, out_width), jnp.float32),
        in_specs=[smem] * len(first) + [smem] + [vmem] * 3,
        out_specs=vmem,
        scratch_shapes=[
            pltpu.VMEM((dates, 4 * (groups * LOOK_AZ) // 2, held), jnp.bfloat16),
            pltpu.VMEM((2, 2 * LANES, 2 * LANES), jnp.bfloat16),
            pltpu.VMEM((count, 2, groups, up(chunk, LANES)), jnp.float32),
        ],
        compiler_params=limit,
    )(*first, range_shift, jnp.asarray(kernel_table()), jnp.asarray(lowpass_row(2 * LANES)), arrived)
    returned = lax.all_to_all(looked, axes, 0, 0, tiled=True)

    out = pl.pallas_call(
        functools.partial(unpack_kernel, used_lags, looks),
        out_shape=jax.ShapeDtypeStruct((2, LAGS, groups // az_count, looks * peers), jnp.float32),
        in_specs=[vmem],
        out_specs=vmem,
        compiler_params=limit,
    )(returned)
    return out[:, None]


def solution(mesh):
    return jax.shard_map(
        body,
        mesh=mesh,
        in_specs=(
            P(None, ("groups", "date"), "az", "rng"),
            P(("groups", "date"), None),
            P(("groups", "date"), None),
            P("groups"),
        ),
        out_specs=P(None, ("groups", "date"), None, "az", "rng"),
        check_vma=False,
    )
```

```python
import functools

import jax
import jax.numpy as jnp
import numpy as np
from jax import lax
from jax.experimental import pallas as pl
from jax.experimental.pallas import tpu as pltpu
from jax.sharding import PartitionSpec as P

LAGS = 8
KERNELS = 16
TAPS = 8
FILTER_HALF = 8
FILTER_TAPS = 2 * FILTER_HALF + 1
LOOK_AZ = 4
LOOK_RG = 20
LANES = 128
META = 3
UNROLLED_PAIRS = 12


def up(value, unit):
    return -(-value // unit) * unit


def kernel_table():
    position = np.arange(TAPS) - 3.0 - np.arange(KERNELS)[:, None] / KERNELS
    shaped = np.sinc(position) * (0.5 + 0.5 * np.cos(np.pi * position / 5.0))
    table = np.zeros((KERNELS, LANES), np.float32)
    table[:, :TAPS] = shaped / shaped.sum(1, keepdims=True)
    return table


def lowpass_row(width):
    t = np.arange(FILTER_TAPS) - FILTER_HALF
    row = np.zeros((1, width), np.float32)
    row[0, :FILTER_TAPS] = 0.4 * np.sinc(0.4 * t) * (0.54 + 0.46 * np.cos(np.pi * t / (FILTER_HALF + 1)))
    return row


def halves(value):
    high = value.astype(jnp.bfloat16)
    return high, (value - high.astype(jnp.float32)).astype(jnp.bfloat16)


def dot(a, b):
    return jnp.dot(a, b, preferred_element_type=jnp.float32)


def dot_nt(a, b):
    return lax.dot_general(a, b, (((1,), (1,)), ((), ())), preferred_element_type=jnp.float32)


def pack_kernel(chunk, place_ref, offsets_ref, index_ref, slc_ref, before_ref, after_ref, out_ref, wide_ref):
    columns = slc_ref.shape[1]
    wide = out_ref.shape[2]
    first = place_ref[0] == 0
    last = place_ref[0] == place_ref[1] - 1
    zero = jnp.zeros_like(before_ref[...])
    wide_ref[:, :LANES] = jnp.where(first, zero, before_ref[...])
    wide_ref[:, LANES : LANES + columns] = slc_ref[...]
    wide_ref[:, LANES + columns :] = jnp.where(last, zero, after_ref[...])
    lane = lax.broadcasted_iota(jnp.int32, (slc_ref.shape[0], wide), 1)
    numbers = [offsets_ref[0, 0], index_ref[0, 0], index_ref[0, 1]]
    for j in range(out_ref.shape[0]):
        start = LANES + chunk * j - FILTER_HALF - 3 + offsets_ref[0, 1]
        tile = lax.shift_right_logical(start, 7)
        within = lax.bitwise_and(start, LANES - 1)
        window = wide_ref[:, pl.ds(pl.multiple_of(tile * LANES, LANES), wide + LANES)].astype(jnp.float32)
        moved = pltpu.roll(window, wide + LANES - within, 1)[:, :wide]
        for slot, number in enumerate(numbers):
            moved = jnp.where(lane == wide - META + slot, number.astype(jnp.float32), moved)
        out_ref[j] = moved.astype(jnp.bfloat16)


def picked_taps(table, index):
    row = lax.broadcasted_iota(jnp.int32, table.shape, 0).astype(jnp.float32)
    return jnp.sum(jnp.where(row == index, table, 0.0), axis=0, keepdims=True)


def banded(taps, distance):
    out = jnp.zeros(distance.shape, jnp.float32)
    for q in range(TAPS):
        out = jnp.where(distance == q, taps[:, q : q + 1], out)
    return out


def pairs_kernel(chunk, pairs, *refs):
    if isinstance(pairs, int):
        table_of_pairs, refs = refs[0], refs[1:]
    shift_ref, table_ref, lowpass_ref, recv_ref, out_ref, resampled_ref, weight_ref, product_ref = refs
    sources, rows, wide = recv_ref.shape
    dates = shift_ref.shape[0]
    az_count = sources // dates
    own_lines = rows // 2
    lines = own_lines * az_count
    groups = lines // LOOK_AZ
    looks = chunk // LOOK_RG
    table = table_ref[...]
    held = resampled_ref.shape[2]

    out_row = lax.broadcasted_iota(jnp.int32, (lines, lines), 0)
    in_row = lax.broadcasted_iota(jnp.int32, (lines, lines), 1)
    line = LOOK_AZ * (out_row % groups) + out_row // groups
    line_distance = (in_row - line + 3).astype(jnp.float32)
    span = min(2 * LANES, wide)
    column_distance = (
        lax.broadcasted_iota(jnp.int32, (span, LANES), 0) - lax.broadcasted_iota(jnp.int32, (span, LANES), 1)
    ).astype(jnp.float32)
    for date in range(dates):
        numbers = recv_ref[date * az_count, 0:16, wide - LANES :].astype(jnp.float32)[0:1, LANES - META :]
        line_offset, line_index, column_index = (numbers[:, s : s + 1] for s in range(META))
        line_taps = banded(picked_taps(table, line_index), line_distance - line_offset)
        line_taps = jnp.concatenate(halves(line_taps), axis=0)
        column_high, column_low = halves(banded(picked_taps(table, column_index), column_distance))
        moved = []
        for plane in range(2):
            rows_of = slice(plane * own_lines, (plane + 1) * own_lines)
            source = jnp.concatenate([recv_ref[date * az_count + a, rows_of, :] for a in range(az_count)], axis=0)
            both = dot(line_taps, source)
            moved.append(both[:lines] + both[lines:])
        moved_high, moved_low = halves(jnp.concatenate(moved, axis=0))
        for begin in range(0, held, LANES):
            end = min(begin + span, wide)
            taken = end - begin
            total = dot(moved_high[:, begin:end], column_high[:taken])
            total += dot(moved_low[:, begin:end], column_high[:taken])
            total += dot(moved_high[:, begin:end], column_low[:taken])
            resampled_ref[date, :, begin : begin + LANES] = total.astype(jnp.bfloat16)

    window = lowpass_ref[...]
    spacing = lax.broadcasted_iota(jnp.int32, window.shape, 1).astype(jnp.float32) - FILTER_HALF
    span = min(2 * LANES, held)

    def one_pair(place, own, other):
        gap = shift_ref[own] - shift_ref[other]
        angle = jnp.where(jnp.abs(spacing) <= FILTER_HALF, jnp.pi * gap * spacing, 0.0)
        for part, taps in enumerate((window * jnp.cos(angle), window * jnp.sin(angle))):
            spread = jnp.broadcast_to(taps, (LANES, 2 * LANES))
            spread = pltpu.roll(spread, 0, 1, stride=1, stride_axis=0)
            high, low = halves(spread)
            weight_ref[0, part * LANES : (part + 1) * LANES, :] = high
            weight_ref[1, part * LANES : (part + 1) * LANES, :] = low
        both = jnp.concatenate([resampled_ref[own], resampled_ref[other]], axis=0)
        for begin in range(0, up(chunk, LANES), LANES):
            end = min(begin + span, held)
            taken = end - begin
            total = dot_nt(both[:, begin:end], weight_ref[0, :, :taken])
            total += dot_nt(both[:, begin:end], weight_ref[1, :, :taken])
            cos, sin = total[:, :LANES], total[:, LANES:]
            re, im = slice(0, lines), slice(lines, 2 * lines)
            master_re = cos[re] + sin[im]
            master_im = cos[im] - sin[re]
            re, im = slice(2 * lines, 3 * lines), slice(3 * lines, 4 * lines)
            partner_re = cos[re] - sin[im]
            partner_im = cos[im] + sin[re]
            for part, product in enumerate(
                (
                    master_re * partner_re + master_im * partner_im,
                    master_im * partner_re - master_re * partner_im,
                )
            ):
                summed = sum(product[k * groups : (k + 1) * groups] for k in range(LOOK_AZ))
                product_ref[place, part, :, begin : begin + LANES] = summed

    if isinstance(pairs, int):
        count = pairs

        def step(place, carry):
            one_pair(place, table_of_pairs[place, 0], table_of_pairs[place, 1])
            return carry

        lax.fori_loop(0, count, step, 0)
    else:
        count = len(pairs)
        for place, (own, other) in enumerate(pairs):
            one_pair(place, own, other)

    out_width = out_ref.shape[2]
    column = lax.broadcasted_iota(jnp.int32, (product_ref.shape[3], out_width), 0)
    lane = lax.broadcasted_iota(jnp.int32, (product_ref.shape[3], out_width), 1)
    collect = jnp.where(column // LOOK_RG == lane % looks, 1.0, 0.0).astype(jnp.bfloat16)
    high, low = halves(product_ref[...].reshape(count * 2 * groups, product_ref.shape[3]))
    total = (dot(high, collect) + dot(low, collect)) * (1.0 / (LOOK_AZ * LOOK_RG))
    total = total.reshape(count, 2, groups, out_width)
    own_lane = lax.broadcasted_iota(jnp.int32, (groups, out_width), 1) // looks
    place = 0
    for own in range(dates):
        value = jnp.zeros((groups, out_width), jnp.float32)
        for lag in range(min(LAGS, dates - 1 - own)):
            for part in range(2):
                value = jnp.where(own_lane == lag * 2 + part, total[place, part], value)
            place += 1
        out_ref[own * az_count : (own + 1) * az_count] = value.reshape(az_count, groups // az_count, out_width)


def unpack_kernel(used_lags, looks, recv_ref, out_ref):
    sources, groups, width = recv_ref.shape
    columns = out_ref.shape[-1]
    lane = lax.broadcasted_iota(jnp.int32, (groups, columns), 1) // looks
    out_ref[...] = jnp.zeros_like(out_ref)
    for lag in range(used_lags):
        for part in range(2):
            value = jnp.zeros((groups, columns), jnp.float32)
            for source in range(sources):
                block = recv_ref[source]
                if width != columns:
                    block = block[:, :columns]
                shift = looks * (source - lag * 2 - part) % columns
                if shift:
                    block = pltpu.roll(block, shift, 1)
                value = jnp.where(lane == source, block, value)
            out_ref[part, lag] = value


def chunked_body(slc, offsets, kernel_index, range_shift):
    axes = ("date", "az")
    date_count, az_count, rng_count = (lax.axis_size(a) for a in ("date", "az", "rng"))
    peers = date_count * az_count
    lines, columns = slc.shape[2], slc.shape[3]
    dates = range_shift.shape[0]
    chunk = columns // peers
    looks = chunk // LOOK_RG
    groups = lines * az_count // LOOK_AZ
    wide = up(chunk + 2 * FILTER_HALF + TAPS - 1 + META, LANES)
    held = up(chunk + 2 * FILTER_HALF, LANES)
    used_lags = min(LAGS, dates - 1)
    out_width = up(used_lags * 2 * looks, LANES)
    vmem = pl.BlockSpec(memory_space=pltpu.VMEM)
    smem = pl.BlockSpec(memory_space=pltpu.SMEM)
    limit = pltpu.CompilerParams(vmem_limit_bytes=32 * 1024 * 1024)

    cells = slc.reshape(2 * lines, columns)
    place = lax.axis_index("rng")
    if rng_count == 2:
        edge = jnp.where(place == 0, cells[:, columns - LANES :], cells[:, :LANES])
        before = after = lax.ppermute(edge, "rng", [(0, 1), (1, 0)])
    else:
        forth = [(i, i + 1) for i in range(rng_count - 1)]
        before = lax.ppermute(cells[:, columns - LANES :], "rng", forth)
        after = lax.ppermute(cells[:, :LANES], "rng", [(b, a) for a, b in forth])

    packed = pl.pallas_call(
        functools.partial(pack_kernel, chunk),
        out_shape=jax.ShapeDtypeStruct((peers, 2 * lines, wide), jnp.bfloat16),
        in_specs=[smem] * 3 + [vmem] * 3,
        out_specs=vmem,
        scratch_shapes=[pltpu.VMEM((2 * lines, columns + 2 * LANES), jnp.bfloat16)],
        compiler_params=limit,
    )(jnp.stack([place, rng_count]).astype(jnp.int32), offsets, kernel_index, cells, before, after)
    arrived = lax.all_to_all(packed, axes, 0, 0, tiled=True)

    pairs = [(own, own + lag) for own in range(dates) for lag in range(1, LAGS + 1) if own + lag < dates]
    count = len(pairs)
    first = [jnp.asarray(np.array(pairs, np.int32))] if count > UNROLLED_PAIRS else []
    looked = pl.pallas_call(
        functools.partial(pairs_kernel, chunk, count if first else pairs),
        out_shape=jax.ShapeDtypeStruct((peers, groups // az_count, out_width), jnp.float32),
        in_specs=[smem] * len(first) + [smem] + [vmem] * 3,
        out_specs=vmem,
        scratch_shapes=[
            pltpu.VMEM((dates, 4 * (groups * LOOK_AZ) // 2, held), jnp.bfloat16),
            pltpu.VMEM((2, 2 * LANES, 2 * LANES), jnp.bfloat16),
            pltpu.VMEM((count, 2, groups, up(chunk, LANES)), jnp.float32),
        ],
        compiler_params=limit,
    )(*first, range_shift, jnp.asarray(kernel_table()), jnp.asarray(lowpass_row(2 * LANES)), arrived)
    returned = lax.all_to_all(looked, axes, 0, 0, tiled=True)

    out = pl.pallas_call(
        functools.partial(unpack_kernel, used_lags, looks),
        out_shape=jax.ShapeDtypeStruct((2, LAGS, groups // az_count, looks * peers), jnp.float32),
        in_specs=[vmem],
        out_specs=vmem,
        compiler_params=limit,
    )(returned)
    return out[:, None]


HALO_LINES = 16
LEAD = 32


def slots(count):
    if count == 2:
        return [[(0, 1), (1, 0)]]
    return [[(i, i + 1) for i in range(count - 1)], [(i + 1, i) for i in range(count - 1)]]


def edge_kernel(slc_ref, *refs):
    outs, semaphores = refs[:-1], refs[-1]
    lines, columns = slc_ref.shape[1:]
    row = pl.multiple_of((1 - lax.axis_index("az")) * (lines - HALO_LINES), HALO_LINES)
    if len(outs) == 3:
        starts = [pl.multiple_of((1 - lax.axis_index("rng")) * (columns - LANES), LANES)]
    else:
        starts = [columns - LANES, 0]
    wanted = [slc_ref.at[:, pl.ds(row, HALO_LINES), :]]
    wanted += [slc_ref.at[:, :, pl.ds(start, LANES)] for start in starts]
    wanted += [slc_ref.at[:, pl.ds(row, HALO_LINES), pl.ds(start, LANES)] for start in starts]
    copies = [pltpu.make_async_copy(w, o, semaphores.at[i]) for i, (w, o) in enumerate(zip(wanted, outs))]
    for copy in copies:
        copy.start()
    for copy in copies:
        copy.wait()


def taps_kernel(offsets_ref, index_ref, table_ref, slc_ref, line_ref, column_ref, held_ref, semaphore):
    copy = pltpu.make_async_copy(slc_ref, held_ref, semaphore)
    copy.start()
    lines = slc_ref.shape[1]
    groups = lines // LOOK_AZ
    table = table_ref[...]
    shape = (lines, lines + HALO_LINES)
    row = lax.broadcasted_iota(jnp.int32, shape, 0)
    place = lax.broadcasted_iota(jnp.int32, shape, 1)
    beyond = jnp.where(lax.axis_index("az") == 0, 0, -lines - HALO_LINES)
    source = jnp.where(place < lines, place, place + beyond)
    line = LOOK_AZ * (row % groups) + row // groups
    taps = banded(picked_taps(table, index_ref[0, 0].astype(jnp.float32)), source - line - offsets_ref[0, 0] + 3)
    line_ref[...] = jnp.concatenate(halves(taps), axis=0)
    shape = (2 * LANES, LANES)
    distance = lax.broadcasted_iota(jnp.int32, shape, 0) - lax.broadcasted_iota(jnp.int32, shape, 1)
    distance = distance - (LANES - LEAD - 3) - offsets_ref[0, 1]
    taps = banded(picked_taps(table, index_ref[0, 1].astype(jnp.float32)), distance)
    column_ref[...] = jnp.concatenate(halves(taps), axis=1)
    copy.wait()


def resample_kernel(last_block, slc_ref, lines_ref, left_ref, right_ref, left_corner, right_corner, line_ref, column_ref, *outs):
    outs, tiles_ref = outs[:-1], outs[-1]
    lines = slc_ref.shape[1]
    block = lax.axis_index("rng")
    moved = []
    for plane in range(2):
        own = jnp.concatenate([left_ref[plane], slc_ref[plane], right_ref[plane]], axis=1)
        halo = jnp.concatenate([left_corner[plane], lines_ref[plane], right_corner[plane]], axis=1)
        both = dot(line_ref[...], jnp.concatenate([own, halo], axis=0))
        moved.append(both[:lines] + both[lines:])
    moved = jnp.concatenate(moved, axis=0)
    width = moved.shape[1]
    left = jnp.where(block > 0, moved[:, :LANES], 0.0)
    right = jnp.where(block < last_block, moved[:, width - LANES :], 0.0)
    moved = jnp.concatenate([left, moved[:, LANES : width - LANES], right], axis=1)
    high, low = halves(moved)
    starts = range(0, width - LANES, LANES)
    high = jnp.concatenate([high[:, s : s + 2 * LANES] for s in starts], axis=0)
    low = jnp.concatenate([low[:, s : s + 2 * LANES] for s in starts], axis=0)
    total = dot(high, column_ref[...])
    total = total[:, :LANES] + total[:, LANES:] + dot(low, column_ref[:, :LANES])
    tiles_ref[...] = total.astype(jnp.bfloat16).reshape(tiles_ref.shape)
    date = lax.axis_index("date")
    each = outs[0].shape[0]
    for step, out_ref in enumerate(outs):
        out_ref[...] = tiles_ref[pl.ds((date ^ step) * (each - 1), each)]


def filter_kernel(pairs, shift_ref, lowpass_ref, out_ref):
    date = lax.axis_index("date")
    window = lowpass_ref[...]
    spacing = lax.broadcasted_iota(jnp.int32, window.shape, 1).astype(jnp.float32) - FILTER_HALF
    for place, (first, second) in enumerate(pairs):
        gap = shift_ref[date ^ first] - shift_ref[date ^ second]
        angle = jnp.where(jnp.abs(spacing) <= FILTER_HALF, jnp.pi * gap * spacing, 0.0)
        for part, taps in enumerate((window * jnp.cos(angle), window * jnp.sin(angle))):
            spread = jnp.broadcast_to(taps, (LANES, 2 * LANES))
            spread = pltpu.roll(spread, LEAD - FILTER_HALF, 1, stride=1, stride_axis=0)
            high, low = halves(spread)
            out_ref[place, 0, part * LANES : (part + 1) * LANES, :] = high
            out_ref[place, 1, part * LANES : (part + 1) * LANES, :] = low


def looks_kernel(pairs, dates, weight_ref, *refs):
    chunks, outs, window_ref, product_ref = refs[:dates], refs[dates : 2 * dates], refs[-2], refs[-1]
    blocks, rows = chunks[0].shape[0] - 1, chunks[0].shape[1]
    lines = rows // 2
    groups = lines // LOOK_AZ
    looks = blocks * LANES // LOOK_RG
    date = lax.axis_index("date")
    for step, chunk_ref in enumerate(chunks):
        for k in range(blocks):
            at = pl.ds(k * rows, rows)
            window_ref[step, at, :LANES] = chunk_ref[k]
            window_ref[step, at, LANES:] = chunk_ref[k + 1]
    for place, (first, second) in enumerate(pairs):
        def filtered(step):
            total = dot_nt(window_ref[step], weight_ref[place, 0]) + dot_nt(window_ref[step], weight_ref[place, 1])
            total = total.reshape(blocks, 2, lines, 2 * LANES)
            return total[:, 0, :, :LANES], total[:, 1, :, :LANES], total[:, 0, :, LANES:], total[:, 1, :, LANES:]

        cos_re, cos_im, sin_re, sin_im = filtered(first)
        master_re, master_im = cos_re + sin_im, cos_im - sin_re
        cos_re, cos_im, sin_re, sin_im = filtered(second)
        partner_re, partner_im = cos_re - sin_im, cos_im + sin_re
        for part, product in enumerate(
            (
                master_re * partner_re + master_im * partner_im,
                master_im * partner_re - master_re * partner_im,
            )
        ):
            summed = sum(product[:, k * groups : (k + 1) * groups] for k in range(LOOK_AZ))
            at = pl.ds((place * 2 + part) * groups, groups)
            for k in range(blocks):
                product_ref[at, k * LANES : (k + 1) * LANES] = summed[k]

    out_width = outs[0].shape[1]
    column = lax.broadcasted_iota(jnp.int32, (product_ref.shape[1], out_width), 0)
    lane = lax.broadcasted_iota(jnp.int32, (product_ref.shape[1], out_width), 1)
    collect = jnp.where(column // LOOK_RG == lane % looks, 1.0, 0.0).astype(jnp.bfloat16)
    high, low = halves(product_ref[...])
    total = (dot(high, collect) + dot(low, collect)) * (1.0 / (LOOK_AZ * LOOK_RG))
    total = total.reshape(len(pairs), 2, groups, out_width)
    own_lane = lax.broadcasted_iota(jnp.int32, (groups, out_width), 1) // looks
    for step, out_ref in enumerate(outs):
        value = jnp.zeros((groups, out_width), jnp.float32)
        for place, pair in enumerate(pairs):
            if step in pair:
                other = pair[1] if pair[0] == step else pair[0]
                lag = (date ^ other) - (date ^ step)
                for part in range(2):
                    signed = -total[place, part] if part == 1 and pair[1] == step else total[place, part]
                    value = jnp.where(own_lane == (lag - 1) * 2 + part, signed, value)
        out_ref[...] = value


def place_kernel(used_lags, looks, *refs):
    out_ref = refs[-1]
    groups, columns = out_ref.shape[2:]
    date = lax.axis_index("date")
    lane = lax.broadcasted_iota(jnp.int32, (groups, LANES), 1) // looks
    out_ref[...] = jnp.zeros_like(out_ref)
    each = LANES // looks
    for step, recv_ref in enumerate(refs[:-1]):
        chunk = date ^ step
        for lag in range(used_lags):
            for part in range(2):
                tile, group = divmod(lag * 2 + part, each)
                block = recv_ref[:, tile * LANES : (tile + 1) * LANES]
                block = pltpu.roll(block, lax.bitwise_and(looks * (chunk - group), LANES - 1), 1)
                out_ref[part, lag] = jnp.where(lane == chunk, block, out_ref[part, lag])


def tiled_body(slc, offsets, kernel_index, range_shift):
    dates, rng_count = (lax.axis_size(a) for a in ("date", "rng"))
    lines, columns = slc.shape[2], slc.shape[3]
    chunk = columns // dates
    looks = chunk // LOOK_RG
    groups = lines // LOOK_AZ
    out_width = up(min(LAGS, dates - 1) * 2 * looks, LANES)
    vmem = pl.BlockSpec(memory_space=pltpu.VMEM)
    smem = pl.BlockSpec(memory_space=pltpu.SMEM)
    anywhere = pl.BlockSpec(memory_space=pl.ANY)
    limit = pltpu.CompilerParams(vmem_limit_bytes=32 * 1024 * 1024)
    bf16 = jnp.bfloat16
    cells = slc.reshape(2, lines, columns)

    moves = slots(rng_count)
    shapes = [(2, HALO_LINES, columns)] + [(2, lines, LANES)] * len(moves) + [(2, HALO_LINES, LANES)] * len(moves)
    edges = pl.pallas_call(
        edge_kernel,
        out_shape=[jax.ShapeDtypeStruct(s, bf16) for s in shapes],
        in_specs=[anywhere],
        out_specs=[vmem] * len(shapes),
        scratch_shapes=[pltpu.SemaphoreType.DMA((len(shapes),))],
        compiler_params=limit,
    )(cells)
    swap = [(0, 1), (1, 0)]
    sides = [lax.ppermute(edges[1 + i], "rng", move) for i, move in enumerate(moves)]
    corners = [
        lax.ppermute(edges[1 + len(moves) + i], ("rng", "az"), [(2 * a + c, 2 * b + d) for a, b in move for c, d in swap])
        for i, move in enumerate(moves)
    ]
    halo_lines = lax.ppermute(edges[0], "az", swap)

    line_taps, column_taps, held = pl.pallas_call(
        taps_kernel,
        out_shape=[
            jax.ShapeDtypeStruct((2 * lines, lines + HALO_LINES), bf16),
            jax.ShapeDtypeStruct((2 * LANES, 2 * LANES), bf16),
            jax.ShapeDtypeStruct(cells.shape, bf16),
        ],
        in_specs=[smem, smem, vmem, anywhere],
        out_specs=[vmem] * 3,
        scratch_shapes=[pltpu.SemaphoreType.DMA],
        compiler_params=limit,
    )(offsets, kernel_index, jnp.asarray(kernel_table()), cells)

    tiles = chunk // LANES + 1
    sent = pl.pallas_call(
        functools.partial(resample_kernel, rng_count - 1),
        out_shape=[jax.ShapeDtypeStruct((tiles, 2 * lines, LANES), bf16)] * dates,
        in_specs=[vmem] * 8,
        out_specs=[vmem] * dates,
        scratch_shapes=[pltpu.VMEM((columns // LANES + 1, 2 * lines, LANES), bf16)],
        compiler_params=limit,
    )(held, halo_lines, sides[0], sides[-1], corners[0], corners[-1], line_taps, column_taps)

    def exchanged(values):
        arrived = {0: values[0]}
        for step in range(dates - 1, 0, -1):
            arrived[step] = lax.ppermute(values[step], "date", [(i, i ^ step) for i in range(dates)])
        return [arrived[step] for step in range(dates)]

    chunks = exchanged(sent)
    pairs = [(first, second) for first in range(dates) for second in range(first + 1, dates)]
    weights = pl.pallas_call(
        functools.partial(filter_kernel, pairs),
        out_shape=jax.ShapeDtypeStruct((len(pairs), 2, 2 * LANES, 2 * LANES), bf16),
        in_specs=[smem, vmem],
        out_specs=vmem,
        compiler_params=limit,
    )(range_shift, jnp.asarray(lowpass_row(2 * LANES)))
    looked = pl.pallas_call(
        functools.partial(looks_kernel, pairs, dates),
        out_shape=[jax.ShapeDtypeStruct((groups, out_width), jnp.float32)] * dates,
        in_specs=[vmem] * (1 + dates),
        out_specs=[vmem] * dates,
        scratch_shapes=[
            pltpu.VMEM((dates, (tiles - 1) * 2 * lines, 2 * LANES), bf16),
            pltpu.VMEM((len(pairs) * 2 * groups, chunk), jnp.float32),
        ],
        compiler_params=limit,
    )(weights, *chunks)
    out = pl.pallas_call(
        functools.partial(place_kernel, min(LAGS, dates - 1), looks),
        out_shape=jax.ShapeDtypeStruct((2, LAGS, groups, looks * dates), jnp.float32),
        in_specs=[vmem] * dates,
        out_specs=vmem,
        compiler_params=limit,
    )(*exchanged(looked))
    return out[:, None]


def body(slc, offsets, kernel_index, range_shift):
    dates, az_count = (lax.axis_size(a) for a in ("date", "az"))
    lines, columns = slc.shape[2], slc.shape[3]
    whole_tiles = columns % (dates * LANES) == 0 and columns % (dates * LOOK_RG) == 0
    one_row = columns // LOOK_RG == LANES and range_shift.shape[0] == dates
    few = dates & (dates - 1) == 0 and dates - 1 <= LAGS
    if az_count == 2 and whole_tiles and one_row and few and lines % 32 == 0:
        return tiled_body(slc, offsets, kernel_index, range_shift)
    return chunked_body(slc, offsets, kernel_index, range_shift)


def solution(mesh):
    return jax.shard_map(
        body,
        mesh=mesh,
        in_specs=(
            P(None, ("groups", "date"), "az", "rng"),
            P(("groups", "date"), None),
            P(("groups", "date"), None),
            P("groups"),
        ),
        out_specs=P(None, ("groups", "date"), None, "az", "rng"),
        check_vma=False,
    )
```

```python
import functools

import jax
import jax.numpy as jnp
import numpy as np
from jax import lax
from jax.experimental import pallas as pl
from jax.experimental.pallas import tpu as pltpu
from jax.sharding import PartitionSpec as P

LAGS = 8
KERNELS = 16
TAPS = 8
FILTER_HALF = 8
FILTER_TAPS = 2 * FILTER_HALF + 1
LOOK_AZ = 4
LOOK_RG = 20
LANES = 128
META = 3
UNROLLED_PAIRS = 12


def up(value, unit):
    return -(-value // unit) * unit


def kernel_table():
    position = np.arange(TAPS) - 3.0 - np.arange(KERNELS)[:, None] / KERNELS
    shaped = np.sinc(position) * (0.5 + 0.5 * np.cos(np.pi * position / 5.0))
    table = np.zeros((KERNELS, LANES), np.float32)
    table[:, :TAPS] = shaped / shaped.sum(1, keepdims=True)
    return table


def lowpass_row(width):
    t = np.arange(FILTER_TAPS) - FILTER_HALF
    row = np.zeros((1, width), np.float32)
    row[0, :FILTER_TAPS] = 0.4 * np.sinc(0.4 * t) * (0.54 + 0.46 * np.cos(np.pi * t / (FILTER_HALF + 1)))
    return row


def halves(value):
    high = value.astype(jnp.bfloat16)
    return high, (value - high.astype(jnp.float32)).astype(jnp.bfloat16)


def dot(a, b):
    return jnp.dot(a, b, preferred_element_type=jnp.float32)


def dot_nt(a, b):
    return lax.dot_general(a, b, (((1,), (1,)), ((), ())), preferred_element_type=jnp.float32)


def pack_kernel(chunk, place_ref, offsets_ref, index_ref, slc_ref, before_ref, after_ref, out_ref, wide_ref):
    columns = slc_ref.shape[1]
    wide = out_ref.shape[2]
    first = place_ref[0] == 0
    last = place_ref[0] == place_ref[1] - 1
    zero = jnp.zeros_like(before_ref[...])
    wide_ref[:, :LANES] = jnp.where(first, zero, before_ref[...])
    wide_ref[:, LANES : LANES + columns] = slc_ref[...]
    wide_ref[:, LANES + columns :] = jnp.where(last, zero, after_ref[...])
    lane = lax.broadcasted_iota(jnp.int32, (slc_ref.shape[0], wide), 1)
    numbers = [offsets_ref[0, 0], index_ref[0, 0], index_ref[0, 1]]
    for j in range(out_ref.shape[0]):
        start = LANES + chunk * j - FILTER_HALF - 3 + offsets_ref[0, 1]
        tile = lax.shift_right_logical(start, 7)
        within = lax.bitwise_and(start, LANES - 1)
        window = wide_ref[:, pl.ds(pl.multiple_of(tile * LANES, LANES), wide + LANES)].astype(jnp.float32)
        moved = pltpu.roll(window, wide + LANES - within, 1)[:, :wide]
        for slot, number in enumerate(numbers):
            moved = jnp.where(lane == wide - META + slot, number.astype(jnp.float32), moved)
        out_ref[j] = moved.astype(jnp.bfloat16)


def picked_taps(table, index):
    row = lax.broadcasted_iota(jnp.int32, table.shape, 0).astype(jnp.float32)
    return jnp.sum(jnp.where(row == index, table, 0.0), axis=0, keepdims=True)


def banded(taps, distance):
    out = jnp.zeros(distance.shape, jnp.float32)
    for q in range(TAPS):
        out = jnp.where(distance == q, taps[:, q : q + 1], out)
    return out


def pairs_kernel(chunk, pairs, *refs):
    if isinstance(pairs, int):
        table_of_pairs, refs = refs[0], refs[1:]
    shift_ref, table_ref, lowpass_ref, recv_ref, out_ref, resampled_ref, weight_ref, product_ref = refs
    sources, rows, wide = recv_ref.shape
    dates = shift_ref.shape[0]
    az_count = sources // dates
    own_lines = rows // 2
    lines = own_lines * az_count
    groups = lines // LOOK_AZ
    looks = chunk // LOOK_RG
    table = table_ref[...]
    held = resampled_ref.shape[2]

    out_row = lax.broadcasted_iota(jnp.int32, (lines, lines), 0)
    in_row = lax.broadcasted_iota(jnp.int32, (lines, lines), 1)
    line = LOOK_AZ * (out_row % groups) + out_row // groups
    line_distance = (in_row - line + 3).astype(jnp.float32)
    span = min(2 * LANES, wide)
    column_distance = (
        lax.broadcasted_iota(jnp.int32, (span, LANES), 0) - lax.broadcasted_iota(jnp.int32, (span, LANES), 1)
    ).astype(jnp.float32)
    for date in range(dates):
        numbers = recv_ref[date * az_count, 0:16, wide - LANES :].astype(jnp.float32)[0:1, LANES - META :]
        line_offset, line_index, column_index = (numbers[:, s : s + 1] for s in range(META))
        line_taps = banded(picked_taps(table, line_index), line_distance - line_offset)
        line_taps = jnp.concatenate(halves(line_taps), axis=0)
        column_high, column_low = halves(banded(picked_taps(table, column_index), column_distance))
        moved = []
        for plane in range(2):
            rows_of = slice(plane * own_lines, (plane + 1) * own_lines)
            source = jnp.concatenate([recv_ref[date * az_count + a, rows_of, :] for a in range(az_count)], axis=0)
            both = dot(line_taps, source)
            moved.append(both[:lines] + both[lines:])
        moved_high, moved_low = halves(jnp.concatenate(moved, axis=0))
        for begin in range(0, held, LANES):
            end = min(begin + span, wide)
            taken = end - begin
            total = dot(moved_high[:, begin:end], column_high[:taken])
            total += dot(moved_low[:, begin:end], column_high[:taken])
            total += dot(moved_high[:, begin:end], column_low[:taken])
            resampled_ref[date, :, begin : begin + LANES] = total.astype(jnp.bfloat16)

    window = lowpass_ref[...]
    spacing = lax.broadcasted_iota(jnp.int32, window.shape, 1).astype(jnp.float32) - FILTER_HALF
    span = min(2 * LANES, held)

    def one_pair(place, own, other):
        gap = shift_ref[own] - shift_ref[other]
        angle = jnp.where(jnp.abs(spacing) <= FILTER_HALF, jnp.pi * gap * spacing, 0.0)
        for part, taps in enumerate((window * jnp.cos(angle), window * jnp.sin(angle))):
            spread = jnp.broadcast_to(taps, (LANES, 2 * LANES))
            spread = pltpu.roll(spread, 0, 1, stride=1, stride_axis=0)
            high, low = halves(spread)
            weight_ref[0, part * LANES : (part + 1) * LANES, :] = high
            weight_ref[1, part * LANES : (part + 1) * LANES, :] = low
        both = jnp.concatenate([resampled_ref[own], resampled_ref[other]], axis=0)
        for begin in range(0, up(chunk, LANES), LANES):
            end = min(begin + span, held)
            taken = end - begin
            total = dot_nt(both[:, begin:end], weight_ref[0, :, :taken])
            total += dot_nt(both[:, begin:end], weight_ref[1, :, :taken])
            cos, sin = total[:, :LANES], total[:, LANES:]
            re, im = slice(0, lines), slice(lines, 2 * lines)
            master_re = cos[re] + sin[im]
            master_im = cos[im] - sin[re]
            re, im = slice(2 * lines, 3 * lines), slice(3 * lines, 4 * lines)
            partner_re = cos[re] - sin[im]
            partner_im = cos[im] + sin[re]
            for part, product in enumerate(
                (
                    master_re * partner_re + master_im * partner_im,
                    master_im * partner_re - master_re * partner_im,
                )
            ):
                summed = sum(product[k * groups : (k + 1) * groups] for k in range(LOOK_AZ))
                product_ref[place, part, :, begin : begin + LANES] = summed

    if isinstance(pairs, int):
        count = pairs

        def step(place, carry):
            one_pair(place, table_of_pairs[place, 0], table_of_pairs[place, 1])
            return carry

        lax.fori_loop(0, count, step, 0)
    else:
        count = len(pairs)
        for place, (own, other) in enumerate(pairs):
            one_pair(place, own, other)

    out_width = out_ref.shape[2]
    column = lax.broadcasted_iota(jnp.int32, (product_ref.shape[3], out_width), 0)
    lane = lax.broadcasted_iota(jnp.int32, (product_ref.shape[3], out_width), 1)
    collect = jnp.where(column // LOOK_RG == lane % looks, 1.0, 0.0).astype(jnp.bfloat16)
    high, low = halves(product_ref[...].reshape(count * 2 * groups, product_ref.shape[3]))
    total = (dot(high, collect) + dot(low, collect)) * (1.0 / (LOOK_AZ * LOOK_RG))
    total = total.reshape(count, 2, groups, out_width)
    own_lane = lax.broadcasted_iota(jnp.int32, (groups, out_width), 1) // looks
    place = 0
    for own in range(dates):
        value = jnp.zeros((groups, out_width), jnp.float32)
        for lag in range(min(LAGS, dates - 1 - own)):
            for part in range(2):
                value = jnp.where(own_lane == lag * 2 + part, total[place, part], value)
            place += 1
        out_ref[own * az_count : (own + 1) * az_count] = value.reshape(az_count, groups // az_count, out_width)


def unpack_kernel(used_lags, looks, recv_ref, out_ref):
    sources, groups, width = recv_ref.shape
    columns = out_ref.shape[-1]
    lane = lax.broadcasted_iota(jnp.int32, (groups, columns), 1) // looks
    out_ref[...] = jnp.zeros_like(out_ref)
    for lag in range(used_lags):
        for part in range(2):
            value = jnp.zeros((groups, columns), jnp.float32)
            for source in range(sources):
                block = recv_ref[source]
                if width != columns:
                    block = block[:, :columns]
                shift = looks * (source - lag * 2 - part) % columns
                if shift:
                    block = pltpu.roll(block, shift, 1)
                value = jnp.where(lane == source, block, value)
            out_ref[part, lag] = value


def chunked_body(slc, offsets, kernel_index, range_shift):
    axes = ("date", "az")
    date_count, az_count, rng_count = (lax.axis_size(a) for a in ("date", "az", "rng"))
    peers = date_count * az_count
    lines, columns = slc.shape[2], slc.shape[3]
    dates = range_shift.shape[0]
    chunk = columns // peers
    looks = chunk // LOOK_RG
    groups = lines * az_count // LOOK_AZ
    wide = up(chunk + 2 * FILTER_HALF + TAPS - 1 + META, LANES)
    held = up(chunk + 2 * FILTER_HALF, LANES)
    used_lags = min(LAGS, dates - 1)
    out_width = up(used_lags * 2 * looks, LANES)
    vmem = pl.BlockSpec(memory_space=pltpu.VMEM)
    smem = pl.BlockSpec(memory_space=pltpu.SMEM)
    limit = pltpu.CompilerParams(vmem_limit_bytes=32 * 1024 * 1024)

    cells = slc.reshape(2 * lines, columns)
    place = lax.axis_index("rng")
    if rng_count == 2:
        edge = jnp.where(place == 0, cells[:, columns - LANES :], cells[:, :LANES])
        before = after = lax.ppermute(edge, "rng", [(0, 1), (1, 0)])
    else:
        forth = [(i, i + 1) for i in range(rng_count - 1)]
        before = lax.ppermute(cells[:, columns - LANES :], "rng", forth)
        after = lax.ppermute(cells[:, :LANES], "rng", [(b, a) for a, b in forth])

    packed = pl.pallas_call(
        functools.partial(pack_kernel, chunk),
        out_shape=jax.ShapeDtypeStruct((peers, 2 * lines, wide), jnp.bfloat16),
        in_specs=[smem] * 3 + [vmem] * 3,
        out_specs=vmem,
        scratch_shapes=[pltpu.VMEM((2 * lines, columns + 2 * LANES), jnp.bfloat16)],
        compiler_params=limit,
    )(jnp.stack([place, rng_count]).astype(jnp.int32), offsets, kernel_index, cells, before, after)
    arrived = lax.all_to_all(packed, axes, 0, 0, tiled=True)

    pairs = [(own, own + lag) for own in range(dates) for lag in range(1, LAGS + 1) if own + lag < dates]
    count = len(pairs)
    first = [jnp.asarray(np.array(pairs, np.int32))] if count > UNROLLED_PAIRS else []
    looked = pl.pallas_call(
        functools.partial(pairs_kernel, chunk, count if first else pairs),
        out_shape=jax.ShapeDtypeStruct((peers, groups // az_count, out_width), jnp.float32),
        in_specs=[smem] * len(first) + [smem] + [vmem] * 3,
        out_specs=vmem,
        scratch_shapes=[
            pltpu.VMEM((dates, 4 * (groups * LOOK_AZ) // 2, held), jnp.bfloat16),
            pltpu.VMEM((2, 2 * LANES, 2 * LANES), jnp.bfloat16),
            pltpu.VMEM((count, 2, groups, up(chunk, LANES)), jnp.float32),
        ],
        compiler_params=limit,
    )(*first, range_shift, jnp.asarray(kernel_table()), jnp.asarray(lowpass_row(2 * LANES)), arrived)
    returned = lax.all_to_all(looked, axes, 0, 0, tiled=True)

    out = pl.pallas_call(
        functools.partial(unpack_kernel, used_lags, looks),
        out_shape=jax.ShapeDtypeStruct((2, LAGS, groups // az_count, looks * peers), jnp.float32),
        in_specs=[vmem],
        out_specs=vmem,
        compiler_params=limit,
    )(returned)
    return out[:, None]


HALO_LINES = 16
LEAD = 32


def slots(count):
    if count == 2:
        return [[(0, 1), (1, 0)]]
    return [[(i, i + 1) for i in range(count - 1)], [(i + 1, i) for i in range(count - 1)]]


def edge_kernel(slc_ref, *refs):
    outs, semaphores = refs[:-1], refs[-1]
    lines, columns = slc_ref.shape[1:]
    row = pl.multiple_of((1 - lax.axis_index("az")) * (lines - HALO_LINES), HALO_LINES)
    if len(outs) == 3:
        starts = [pl.multiple_of((1 - lax.axis_index("rng")) * (columns - LANES), LANES)]
    else:
        starts = [columns - LANES, 0]
    wanted = [slc_ref.at[:, pl.ds(row, HALO_LINES), :]]
    wanted += [slc_ref.at[:, :, pl.ds(start, LANES)] for start in starts]
    wanted += [slc_ref.at[:, pl.ds(row, HALO_LINES), pl.ds(start, LANES)] for start in starts]
    copies = [pltpu.make_async_copy(w, o, semaphores.at[i]) for i, (w, o) in enumerate(zip(wanted, outs))]
    for copy in copies:
        copy.start()
    for copy in copies:
        copy.wait()


def sinc(value):
    angle = jnp.pi * value
    return jnp.where(angle == 0.0, 1.0, jnp.sin(angle) / jnp.where(angle == 0.0, 1.0, angle))


def tap_row(index):
    lane = lax.broadcasted_iota(jnp.int32, (1, LANES), 1)
    position = lane.astype(jnp.float32) - 3.0 - index.astype(jnp.float32) / KERNELS
    shaped = sinc(position) * (0.5 + 0.5 * jnp.cos(jnp.pi * position / 5.0))
    shaped = jnp.where(lane < TAPS, shaped, 0.0)
    return shaped / jnp.sum(shaped, axis=1, keepdims=True)


def taps_kernel(offsets_hbm, index_hbm, slc_ref, line_ref, column_ref, held_ref, offsets_ref, index_ref, semaphores):
    copy = pltpu.make_async_copy(slc_ref, held_ref, semaphores.at[0])
    numbers = [
        pltpu.make_async_copy(offsets_hbm, offsets_ref, semaphores.at[1]),
        pltpu.make_async_copy(index_hbm, index_ref, semaphores.at[2]),
    ]
    for each in numbers:
        each.start()
    copy.start()
    for each in numbers:
        each.wait()
    lines = slc_ref.shape[1]
    groups = lines // LOOK_AZ
    shape = (lines, lines + HALO_LINES)
    row = lax.broadcasted_iota(jnp.int32, shape, 0)
    place = lax.broadcasted_iota(jnp.int32, shape, 1)
    beyond = jnp.where(lax.axis_index("az") == 0, 0, -lines - HALO_LINES)
    source = jnp.where(place < lines, place, place + beyond)
    line = LOOK_AZ * (row % groups) + row // groups
    taps = banded(tap_row(index_ref[0, 0]), source - line - offsets_ref[0, 0] + 3)
    line_ref[...] = jnp.concatenate(halves(taps), axis=0)
    shape = (2 * LANES, LANES)
    distance = lax.broadcasted_iota(jnp.int32, shape, 0) - lax.broadcasted_iota(jnp.int32, shape, 1)
    distance = distance - (LANES - LEAD - 3) - offsets_ref[0, 1]
    taps = banded(tap_row(index_ref[0, 1]), distance)
    column_ref[...] = jnp.concatenate(halves(taps), axis=1)
    copy.wait()


def resample_kernel(last_block, slc_ref, lines_ref, left_ref, right_ref, left_corner, right_corner, line_ref, column_ref, *outs):
    outs, tiles_ref = outs[:-1], outs[-1]
    lines = slc_ref.shape[1]
    block = lax.axis_index("rng")
    moved = []
    for plane in range(2):
        own = jnp.concatenate([left_ref[plane], slc_ref[plane], right_ref[plane]], axis=1)
        halo = jnp.concatenate([left_corner[plane], lines_ref[plane], right_corner[plane]], axis=1)
        both = dot(line_ref[...], jnp.concatenate([own, halo], axis=0))
        moved.append(both[:lines] + both[lines:])
    moved = jnp.concatenate(moved, axis=0)
    width = moved.shape[1]
    left = jnp.where(block > 0, moved[:, :LANES], 0.0)
    right = jnp.where(block < last_block, moved[:, width - LANES :], 0.0)
    moved = jnp.concatenate([left, moved[:, LANES : width - LANES], right], axis=1)
    high, low = halves(moved)
    starts = range(0, width - LANES, LANES)
    high = jnp.concatenate([high[:, s : s + 2 * LANES] for s in starts], axis=0)
    low = jnp.concatenate([low[:, s : s + 2 * LANES] for s in starts], axis=0)
    total = dot(high, column_ref[...])
    total = total[:, :LANES] + total[:, LANES:] + dot(low, column_ref[:, :LANES])
    tiles_ref[...] = total.astype(jnp.bfloat16).reshape(tiles_ref.shape)
    date = lax.axis_index("date")
    each = outs[0].shape[0]
    for step, out_ref in enumerate(outs):
        out_ref[...] = tiles_ref[pl.ds((date ^ step) * (each - 1), each)]


def filter_kernel(pairs, shift_hbm, out_ref, shift_ref, semaphore):
    copy = pltpu.make_async_copy(shift_hbm, shift_ref, semaphore)
    copy.start()
    date = lax.axis_index("date")
    spacing = lax.broadcasted_iota(jnp.int32, (1, 2 * LANES), 1).astype(jnp.float32) - FILTER_HALF
    window = 0.4 * sinc(0.4 * spacing) * (0.54 + 0.46 * jnp.cos(jnp.pi * spacing / (FILTER_HALF + 1)))
    window = jnp.where(jnp.abs(spacing) <= FILTER_HALF, window, 0.0)
    copy.wait()
    for place, (first, second) in enumerate(pairs):
        gap = shift_ref[date ^ first] - shift_ref[date ^ second]
        angle = jnp.where(jnp.abs(spacing) <= FILTER_HALF, jnp.pi * gap * spacing, 0.0)
        for part, taps in enumerate((window * jnp.cos(angle), window * jnp.sin(angle))):
            spread = jnp.broadcast_to(taps, (LANES, 2 * LANES))
            spread = pltpu.roll(spread, LEAD - FILTER_HALF, 1, stride=1, stride_axis=0)
            high, low = halves(spread)
            out_ref[place, 0, part * LANES : (part + 1) * LANES, :] = high
            out_ref[place, 1, part * LANES : (part + 1) * LANES, :] = low


def looks_kernel(pairs, dates, weight_ref, *refs):
    chunks, outs, window_ref, product_ref = refs[:dates], refs[dates : 2 * dates], refs[-2], refs[-1]
    blocks, rows = chunks[0].shape[0] - 1, chunks[0].shape[1]
    lines = rows // 2
    groups = lines // LOOK_AZ
    looks = blocks * LANES // LOOK_RG
    date = lax.axis_index("date")
    for step, chunk_ref in enumerate(chunks):
        for k in range(blocks):
            at = pl.ds(k * rows, rows)
            window_ref[step, at, :LANES] = chunk_ref[k]
            window_ref[step, at, LANES:] = chunk_ref[k + 1]
    for place, (first, second) in enumerate(pairs):
        def filtered(step):
            total = dot_nt(window_ref[step], weight_ref[place, 0]) + dot_nt(window_ref[step], weight_ref[place, 1])
            total = total.reshape(blocks, 2, lines, 2 * LANES)
            return total[:, 0, :, :LANES], total[:, 1, :, :LANES], total[:, 0, :, LANES:], total[:, 1, :, LANES:]

        cos_re, cos_im, sin_re, sin_im = filtered(first)
        master_re, master_im = cos_re + sin_im, cos_im - sin_re
        cos_re, cos_im, sin_re, sin_im = filtered(second)
        partner_re, partner_im = cos_re - sin_im, cos_im + sin_re
        for part, product in enumerate(
            (
                master_re * partner_re + master_im * partner_im,
                master_im * partner_re - master_re * partner_im,
            )
        ):
            summed = sum(product[:, k * groups : (k + 1) * groups] for k in range(LOOK_AZ))
            at = pl.ds((place * 2 + part) * groups, groups)
            for k in range(blocks):
                product_ref[at, k * LANES : (k + 1) * LANES] = summed[k]

    out_width = outs[0].shape[1]
    column = lax.broadcasted_iota(jnp.int32, (product_ref.shape[1], out_width), 0)
    lane = lax.broadcasted_iota(jnp.int32, (product_ref.shape[1], out_width), 1)
    collect = jnp.where(column // LOOK_RG == lane % looks, 1.0, 0.0).astype(jnp.bfloat16)
    high, low = halves(product_ref[...])
    total = (dot(high, collect) + dot(low, collect)) * (1.0 / (LOOK_AZ * LOOK_RG))
    total = total.reshape(len(pairs), 2, groups, out_width)
    own_lane = lax.broadcasted_iota(jnp.int32, (groups, out_width), 1) // looks
    for step, out_ref in enumerate(outs):
        value = jnp.zeros((groups, out_width), jnp.float32)
        for place, pair in enumerate(pairs):
            if step in pair:
                other = pair[1] if pair[0] == step else pair[0]
                lag = (date ^ other) - (date ^ step)
                for part in range(2):
                    signed = -total[place, part] if part == 1 and pair[1] == step else total[place, part]
                    value = jnp.where(own_lane == (lag - 1) * 2 + part, signed, value)
        out_ref[...] = value


def place_kernel(used_lags, looks, *refs):
    out_ref = refs[-1]
    groups, columns = out_ref.shape[2:]
    date = lax.axis_index("date")
    lane = lax.broadcasted_iota(jnp.int32, (groups, LANES), 1) // looks
    out_ref[...] = jnp.zeros_like(out_ref)
    each = LANES // looks
    for step, recv_ref in enumerate(refs[:-1]):
        chunk = date ^ step
        for lag in range(used_lags):
            for part in range(2):
                tile, group = divmod(lag * 2 + part, each)
                block = recv_ref[:, tile * LANES : (tile + 1) * LANES]
                block = pltpu.roll(block, lax.bitwise_and(looks * (chunk - group), LANES - 1), 1)
                out_ref[part, lag] = jnp.where(lane == chunk, block, out_ref[part, lag])


def tiled_body(slc, offsets, kernel_index, range_shift):
    dates, rng_count = (lax.axis_size(a) for a in ("date", "rng"))
    lines, columns = slc.shape[2], slc.shape[3]
    chunk = columns // dates
    looks = chunk // LOOK_RG
    groups = lines // LOOK_AZ
    out_width = up(min(LAGS, dates - 1) * 2 * looks, LANES)
    vmem = pl.BlockSpec(memory_space=pltpu.VMEM)
    hbm = pl.BlockSpec(memory_space=pltpu.HBM)
    limit = pltpu.CompilerParams(vmem_limit_bytes=32 * 1024 * 1024)
    bf16 = jnp.bfloat16
    cells, offsets, kernel_index, range_shift = (
        pltpu.with_memory_space_constraint(value, pltpu.HBM)
        for value in (slc.reshape(2, lines, columns), offsets, kernel_index, range_shift)
    )

    moves = slots(rng_count)
    shapes = [(2, HALO_LINES, columns)] + [(2, lines, LANES)] * len(moves) + [(2, HALO_LINES, LANES)] * len(moves)
    edges = pl.pallas_call(
        edge_kernel,
        out_shape=[jax.ShapeDtypeStruct(s, bf16) for s in shapes],
        in_specs=[hbm],
        out_specs=[vmem] * len(shapes),
        scratch_shapes=[pltpu.SemaphoreType.DMA((len(shapes),))],
        compiler_params=limit,
    )(cells)
    swap = [(0, 1), (1, 0)]
    sides = [lax.ppermute(edges[1 + i], "rng", move) for i, move in enumerate(moves)]
    corners = [
        lax.ppermute(edges[1 + len(moves) + i], ("rng", "az"), [(2 * a + c, 2 * b + d) for a, b in move for c, d in swap])
        for i, move in enumerate(moves)
    ]
    halo_lines = lax.ppermute(edges[0], "az", swap)

    line_taps, column_taps, held = pl.pallas_call(
        taps_kernel,
        out_shape=[
            jax.ShapeDtypeStruct((2 * lines, lines + HALO_LINES), bf16),
            jax.ShapeDtypeStruct((2 * LANES, 2 * LANES), bf16),
            jax.ShapeDtypeStruct(cells.shape, bf16),
        ],
        in_specs=[hbm] * 3,
        out_specs=[vmem] * 3,
        scratch_shapes=[
            pltpu.SMEM(offsets.shape, jnp.int32),
            pltpu.SMEM(kernel_index.shape, jnp.int32),
            pltpu.SemaphoreType.DMA((3,)),
        ],
        compiler_params=limit,
    )(offsets, kernel_index, cells)

    tiles = chunk // LANES + 1
    sent = pl.pallas_call(
        functools.partial(resample_kernel, rng_count - 1),
        out_shape=[jax.ShapeDtypeStruct((tiles, 2 * lines, LANES), bf16)] * dates,
        in_specs=[vmem] * 8,
        out_specs=[vmem] * dates,
        scratch_shapes=[pltpu.VMEM((columns // LANES + 1, 2 * lines, LANES), bf16)],
        compiler_params=limit,
    )(held, halo_lines, sides[0], sides[-1], corners[0], corners[-1], line_taps, column_taps)

    def exchanged(values):
        arrived = {0: values[0]}
        for step in range(dates - 1, 0, -1):
            arrived[step] = lax.ppermute(values[step], "date", [(i, i ^ step) for i in range(dates)])
        return [arrived[step] for step in range(dates)]

    chunks = exchanged(sent)
    pairs = [(first, second) for first in range(dates) for second in range(first + 1, dates)]
    weights = pl.pallas_call(
        functools.partial(filter_kernel, pairs),
        out_shape=jax.ShapeDtypeStruct((len(pairs), 2, 2 * LANES, 2 * LANES), bf16),
        in_specs=[hbm],
        out_specs=vmem,
        scratch_shapes=[pltpu.SMEM(range_shift.shape, jnp.float32), pltpu.SemaphoreType.DMA],
        compiler_params=limit,
    )(range_shift)
    looked = pl.pallas_call(
        functools.partial(looks_kernel, pairs, dates),
        out_shape=[jax.ShapeDtypeStruct((groups, out_width), jnp.float32)] * dates,
        in_specs=[vmem] * (1 + dates),
        out_specs=[vmem] * dates,
        scratch_shapes=[
            pltpu.VMEM((dates, (tiles - 1) * 2 * lines, 2 * LANES), bf16),
            pltpu.VMEM((len(pairs) * 2 * groups, chunk), jnp.float32),
        ],
        compiler_params=limit,
    )(weights, *chunks)
    out = pl.pallas_call(
        functools.partial(place_kernel, min(LAGS, dates - 1), looks),
        out_shape=jax.ShapeDtypeStruct((2, LAGS, groups, looks * dates), jnp.float32),
        in_specs=[vmem] * dates,
        out_specs=vmem,
        compiler_params=limit,
    )(*exchanged(looked))
    return out[:, None]


def body(slc, offsets, kernel_index, range_shift):
    dates, az_count = (lax.axis_size(a) for a in ("date", "az"))
    lines, columns = slc.shape[2], slc.shape[3]
    whole_tiles = columns % (dates * LANES) == 0 and columns % (dates * LOOK_RG) == 0
    one_row = columns // LOOK_RG == LANES and range_shift.shape[0] == dates
    few = dates & (dates - 1) == 0 and dates - 1 <= LAGS
    if az_count == 2 and whole_tiles and one_row and few and lines % 32 == 0:
        return tiled_body(slc, offsets, kernel_index, range_shift)
    return chunked_body(slc, offsets, kernel_index, range_shift)


def solution(mesh):
    return jax.shard_map(
        body,
        mesh=mesh,
        in_specs=(
            P(None, ("groups", "date"), "az", "rng"),
            P(("groups", "date"), None),
            P(("groups", "date"), None),
            P("groups"),
        ),
        out_specs=P(None, ("groups", "date"), None, "az", "rng"),
        check_vma=False,
    )
```

```python
import functools

import jax
import jax.numpy as jnp
import numpy as np
from jax import lax
from jax.experimental import pallas as pl
from jax.experimental.pallas import tpu as pltpu
from jax.sharding import PartitionSpec as P

LAGS = 8
KERNELS = 16
TAPS = 8
FILTER_HALF = 8
FILTER_TAPS = 2 * FILTER_HALF + 1
LOOK_AZ = 4
LOOK_RG = 20
LANES = 128
META = 3
UNROLLED_PAIRS = 12


def up(value, unit):
    return -(-value // unit) * unit


def kernel_table():
    position = np.arange(TAPS) - 3.0 - np.arange(KERNELS)[:, None] / KERNELS
    shaped = np.sinc(position) * (0.5 + 0.5 * np.cos(np.pi * position / 5.0))
    table = np.zeros((KERNELS, LANES), np.float32)
    table[:, :TAPS] = shaped / shaped.sum(1, keepdims=True)
    return table


def lowpass_row(width):
    t = np.arange(FILTER_TAPS) - FILTER_HALF
    row = np.zeros((1, width), np.float32)
    row[0, :FILTER_TAPS] = 0.4 * np.sinc(0.4 * t) * (0.54 + 0.46 * np.cos(np.pi * t / (FILTER_HALF + 1)))
    return row


def halves(value):
    high = value.astype(jnp.bfloat16)
    return high, (value - high.astype(jnp.float32)).astype(jnp.bfloat16)


def dot(a, b):
    return jnp.dot(a, b, preferred_element_type=jnp.float32)


def dot_nt(a, b):
    return lax.dot_general(a, b, (((1,), (1,)), ((), ())), preferred_element_type=jnp.float32)


def pack_kernel(chunk, place_ref, offsets_ref, index_ref, slc_ref, before_ref, after_ref, out_ref, wide_ref):
    columns = slc_ref.shape[1]
    wide = out_ref.shape[2]
    first = place_ref[0] == 0
    last = place_ref[0] == place_ref[1] - 1
    zero = jnp.zeros_like(before_ref[...])
    wide_ref[:, :LANES] = jnp.where(first, zero, before_ref[...])
    wide_ref[:, LANES : LANES + columns] = slc_ref[...]
    wide_ref[:, LANES + columns :] = jnp.where(last, zero, after_ref[...])
    lane = lax.broadcasted_iota(jnp.int32, (slc_ref.shape[0], wide), 1)
    numbers = [offsets_ref[0, 0], index_ref[0, 0], index_ref[0, 1]]
    for j in range(out_ref.shape[0]):
        start = LANES + chunk * j - FILTER_HALF - 3 + offsets_ref[0, 1]
        tile = lax.shift_right_logical(start, 7)
        within = lax.bitwise_and(start, LANES - 1)
        window = wide_ref[:, pl.ds(pl.multiple_of(tile * LANES, LANES), wide + LANES)].astype(jnp.float32)
        moved = pltpu.roll(window, wide + LANES - within, 1)[:, :wide]
        for slot, number in enumerate(numbers):
            moved = jnp.where(lane == wide - META + slot, number.astype(jnp.float32), moved)
        out_ref[j] = moved.astype(jnp.bfloat16)


def picked_taps(table, index):
    row = lax.broadcasted_iota(jnp.int32, table.shape, 0).astype(jnp.float32)
    return jnp.sum(jnp.where(row == index, table, 0.0), axis=0, keepdims=True)


def banded(taps, distance):
    out = jnp.zeros(distance.shape, jnp.float32)
    for q in range(TAPS):
        out = jnp.where(distance == q, taps[:, q : q + 1], out)
    return out


def pairs_kernel(chunk, pairs, *refs):
    if isinstance(pairs, int):
        table_of_pairs, refs = refs[0], refs[1:]
    shift_ref, table_ref, lowpass_ref, recv_ref, out_ref, resampled_ref, weight_ref, product_ref = refs
    sources, rows, wide = recv_ref.shape
    dates = shift_ref.shape[0]
    az_count = sources // dates
    own_lines = rows // 2
    lines = own_lines * az_count
    groups = lines // LOOK_AZ
    looks = chunk // LOOK_RG
    table = table_ref[...]
    held = resampled_ref.shape[2]

    out_row = lax.broadcasted_iota(jnp.int32, (lines, lines), 0)
    in_row = lax.broadcasted_iota(jnp.int32, (lines, lines), 1)
    line = LOOK_AZ * (out_row % groups) + out_row // groups
    line_distance = (in_row - line + 3).astype(jnp.float32)
    span = min(2 * LANES, wide)
    column_distance = (
        lax.broadcasted_iota(jnp.int32, (span, LANES), 0) - lax.broadcasted_iota(jnp.int32, (span, LANES), 1)
    ).astype(jnp.float32)
    for date in range(dates):
        numbers = recv_ref[date * az_count, 0:16, wide - LANES :].astype(jnp.float32)[0:1, LANES - META :]
        line_offset, line_index, column_index = (numbers[:, s : s + 1] for s in range(META))
        line_taps = banded(picked_taps(table, line_index), line_distance - line_offset)
        line_taps = jnp.concatenate(halves(line_taps), axis=0)
        column_high, column_low = halves(banded(picked_taps(table, column_index), column_distance))
        moved = []
        for plane in range(2):
            rows_of = slice(plane * own_lines, (plane + 1) * own_lines)
            source = jnp.concatenate([recv_ref[date * az_count + a, rows_of, :] for a in range(az_count)], axis=0)
            both = dot(line_taps, source)
            moved.append(both[:lines] + both[lines:])
        moved_high, moved_low = halves(jnp.concatenate(moved, axis=0))
        for begin in range(0, held, LANES):
            end = min(begin + span, wide)
            taken = end - begin
            total = dot(moved_high[:, begin:end], column_high[:taken])
            total += dot(moved_low[:, begin:end], column_high[:taken])
            total += dot(moved_high[:, begin:end], column_low[:taken])
            resampled_ref[date, :, begin : begin + LANES] = total.astype(jnp.bfloat16)

    window = lowpass_ref[...]
    spacing = lax.broadcasted_iota(jnp.int32, window.shape, 1).astype(jnp.float32) - FILTER_HALF
    span = min(2 * LANES, held)

    def one_pair(place, own, other):
        gap = shift_ref[own] - shift_ref[other]
        angle = jnp.where(jnp.abs(spacing) <= FILTER_HALF, jnp.pi * gap * spacing, 0.0)
        for part, taps in enumerate((window * jnp.cos(angle), window * jnp.sin(angle))):
            spread = jnp.broadcast_to(taps, (LANES, 2 * LANES))
            spread = pltpu.roll(spread, 0, 1, stride=1, stride_axis=0)
            high, low = halves(spread)
            weight_ref[0, part * LANES : (part + 1) * LANES, :] = high
            weight_ref[1, part * LANES : (part + 1) * LANES, :] = low
        both = jnp.concatenate([resampled_ref[own], resampled_ref[other]], axis=0)
        for begin in range(0, up(chunk, LANES), LANES):
            end = min(begin + span, held)
            taken = end - begin
            total = dot_nt(both[:, begin:end], weight_ref[0, :, :taken])
            total += dot_nt(both[:, begin:end], weight_ref[1, :, :taken])
            cos, sin = total[:, :LANES], total[:, LANES:]
            re, im = slice(0, lines), slice(lines, 2 * lines)
            master_re = cos[re] + sin[im]
            master_im = cos[im] - sin[re]
            re, im = slice(2 * lines, 3 * lines), slice(3 * lines, 4 * lines)
            partner_re = cos[re] - sin[im]
            partner_im = cos[im] + sin[re]
            for part, product in enumerate(
                (
                    master_re * partner_re + master_im * partner_im,
                    master_im * partner_re - master_re * partner_im,
                )
            ):
                summed = sum(product[k * groups : (k + 1) * groups] for k in range(LOOK_AZ))
                product_ref[place, part, :, begin : begin + LANES] = summed

    if isinstance(pairs, int):
        count = pairs

        def step(place, carry):
            one_pair(place, table_of_pairs[place, 0], table_of_pairs[place, 1])
            return carry

        lax.fori_loop(0, count, step, 0)
    else:
        count = len(pairs)
        for place, (own, other) in enumerate(pairs):
            one_pair(place, own, other)

    out_width = out_ref.shape[2]
    column = lax.broadcasted_iota(jnp.int32, (product_ref.shape[3], out_width), 0)
    lane = lax.broadcasted_iota(jnp.int32, (product_ref.shape[3], out_width), 1)
    collect = jnp.where(column // LOOK_RG == lane % looks, 1.0, 0.0).astype(jnp.bfloat16)
    high, low = halves(product_ref[...].reshape(count * 2 * groups, product_ref.shape[3]))
    total = (dot(high, collect) + dot(low, collect)) * (1.0 / (LOOK_AZ * LOOK_RG))
    total = total.reshape(count, 2, groups, out_width)
    own_lane = lax.broadcasted_iota(jnp.int32, (groups, out_width), 1) // looks
    place = 0
    for own in range(dates):
        value = jnp.zeros((groups, out_width), jnp.float32)
        for lag in range(min(LAGS, dates - 1 - own)):
            for part in range(2):
                value = jnp.where(own_lane == lag * 2 + part, total[place, part], value)
            place += 1
        out_ref[own * az_count : (own + 1) * az_count] = value.reshape(az_count, groups // az_count, out_width)


def unpack_kernel(used_lags, looks, recv_ref, out_ref):
    sources, groups, width = recv_ref.shape
    columns = out_ref.shape[-1]
    lane = lax.broadcasted_iota(jnp.int32, (groups, columns), 1) // looks
    out_ref[...] = jnp.zeros_like(out_ref)
    for lag in range(used_lags):
        for part in range(2):
            value = jnp.zeros((groups, columns), jnp.float32)
            for source in range(sources):
                block = recv_ref[source]
                if width != columns:
                    block = block[:, :columns]
                shift = looks * (source - lag * 2 - part) % columns
                if shift:
                    block = pltpu.roll(block, shift, 1)
                value = jnp.where(lane == source, block, value)
            out_ref[part, lag] = value


def chunked_body(slc, offsets, kernel_index, range_shift):
    axes = ("date", "az")
    date_count, az_count, rng_count = (lax.axis_size(a) for a in ("date", "az", "rng"))
    peers = date_count * az_count
    lines, columns = slc.shape[2], slc.shape[3]
    dates = range_shift.shape[0]
    chunk = columns // peers
    looks = chunk // LOOK_RG
    groups = lines * az_count // LOOK_AZ
    wide = up(chunk + 2 * FILTER_HALF + TAPS - 1 + META, LANES)
    held = up(chunk + 2 * FILTER_HALF, LANES)
    used_lags = min(LAGS, dates - 1)
    out_width = up(used_lags * 2 * looks, LANES)
    vmem = pl.BlockSpec(memory_space=pltpu.VMEM)
    smem = pl.BlockSpec(memory_space=pltpu.SMEM)
    limit = pltpu.CompilerParams(vmem_limit_bytes=32 * 1024 * 1024)

    cells = slc.reshape(2 * lines, columns)
    place = lax.axis_index("rng")
    if rng_count == 2:
        edge = jnp.where(place == 0, cells[:, columns - LANES :], cells[:, :LANES])
        before = after = lax.ppermute(edge, "rng", [(0, 1), (1, 0)])
    else:
        forth = [(i, i + 1) for i in range(rng_count - 1)]
        before = lax.ppermute(cells[:, columns - LANES :], "rng", forth)
        after = lax.ppermute(cells[:, :LANES], "rng", [(b, a) for a, b in forth])

    packed = pl.pallas_call(
        functools.partial(pack_kernel, chunk),
        out_shape=jax.ShapeDtypeStruct((peers, 2 * lines, wide), jnp.bfloat16),
        in_specs=[smem] * 3 + [vmem] * 3,
        out_specs=vmem,
        scratch_shapes=[pltpu.VMEM((2 * lines, columns + 2 * LANES), jnp.bfloat16)],
        compiler_params=limit,
    )(jnp.stack([place, rng_count]).astype(jnp.int32), offsets, kernel_index, cells, before, after)
    arrived = lax.all_to_all(packed, axes, 0, 0, tiled=True)

    pairs = [(own, own + lag) for own in range(dates) for lag in range(1, LAGS + 1) if own + lag < dates]
    count = len(pairs)
    first = [jnp.asarray(np.array(pairs, np.int32))] if count > UNROLLED_PAIRS else []
    looked = pl.pallas_call(
        functools.partial(pairs_kernel, chunk, count if first else pairs),
        out_shape=jax.ShapeDtypeStruct((peers, groups // az_count, out_width), jnp.float32),
        in_specs=[smem] * len(first) + [smem] + [vmem] * 3,
        out_specs=vmem,
        scratch_shapes=[
            pltpu.VMEM((dates, 4 * (groups * LOOK_AZ) // 2, held), jnp.bfloat16),
            pltpu.VMEM((2, 2 * LANES, 2 * LANES), jnp.bfloat16),
            pltpu.VMEM((count, 2, groups, up(chunk, LANES)), jnp.float32),
        ],
        compiler_params=limit,
    )(*first, range_shift, jnp.asarray(kernel_table()), jnp.asarray(lowpass_row(2 * LANES)), arrived)
    returned = lax.all_to_all(looked, axes, 0, 0, tiled=True)

    out = pl.pallas_call(
        functools.partial(unpack_kernel, used_lags, looks),
        out_shape=jax.ShapeDtypeStruct((2, LAGS, groups // az_count, looks * peers), jnp.float32),
        in_specs=[vmem],
        out_specs=vmem,
        compiler_params=limit,
    )(returned)
    return out[:, None]


HALO_LINES = 16
LEAD = 32


def slots(count):
    if count == 2:
        return [[(0, 1), (1, 0)]]
    return [[(i, i + 1) for i in range(count - 1)], [(i + 1, i) for i in range(count - 1)]]


def edge_kernel(slc_ref, *refs):
    outs, semaphores = refs[:-1], refs[-1]
    lines, columns = slc_ref.shape[1:]
    row = pl.multiple_of((1 - lax.axis_index("az")) * (lines - HALO_LINES), HALO_LINES)
    if len(outs) == 3:
        starts = [pl.multiple_of((1 - lax.axis_index("rng")) * (columns - LANES), LANES)]
    else:
        starts = [columns - LANES, 0]
    wanted = [slc_ref.at[:, pl.ds(row, HALO_LINES), :]]
    wanted += [slc_ref.at[:, :, pl.ds(start, LANES)] for start in starts]
    wanted += [slc_ref.at[:, pl.ds(row, HALO_LINES), pl.ds(start, LANES)] for start in starts]
    copies = [pltpu.make_async_copy(w, o, semaphores.at[i]) for i, (w, o) in enumerate(zip(wanted, outs))]
    for copy in copies:
        copy.start()
    for copy in copies:
        copy.wait()


def sinc(value):
    angle = jnp.pi * value
    return jnp.where(angle == 0.0, 1.0, jnp.sin(angle) / jnp.where(angle == 0.0, 1.0, angle))


def tap_row(index):
    lane = lax.broadcasted_iota(jnp.int32, (1, LANES), 1)
    position = lane.astype(jnp.float32) - 3.0 - index.astype(jnp.float32) / KERNELS
    shaped = sinc(position) * (0.5 + 0.5 * jnp.cos(jnp.pi * position / 5.0))
    shaped = jnp.where(lane < TAPS, shaped, 0.0)
    return shaped / jnp.sum(shaped, axis=1, keepdims=True)


def taps_kernel(offsets_hbm, index_hbm, slc_ref, line_ref, column_ref, held_ref, offsets_ref, index_ref, semaphores):
    copy = pltpu.make_async_copy(slc_ref, held_ref, semaphores.at[0])
    numbers = [
        pltpu.make_async_copy(offsets_hbm, offsets_ref, semaphores.at[1]),
        pltpu.make_async_copy(index_hbm, index_ref, semaphores.at[2]),
    ]
    for each in numbers:
        each.start()
    copy.start()
    for each in numbers:
        each.wait()
    lines = slc_ref.shape[1]
    groups = lines // LOOK_AZ
    shape = (lines, lines + HALO_LINES)
    row = lax.broadcasted_iota(jnp.int32, shape, 0)
    place = lax.broadcasted_iota(jnp.int32, shape, 1)
    beyond = jnp.where(lax.axis_index("az") == 0, 0, -lines - HALO_LINES)
    source = jnp.where(place < lines, place, place + beyond)
    line = LOOK_AZ * (row % groups) + row // groups
    taps = banded(tap_row(index_ref[0, 0]), source - line - offsets_ref[0, 0] + 3)
    line_ref[...] = jnp.concatenate(halves(taps), axis=0)
    shape = (2 * LANES, LANES)
    distance = lax.broadcasted_iota(jnp.int32, shape, 0) - lax.broadcasted_iota(jnp.int32, shape, 1)
    distance = distance - (LANES - LEAD - 3) - offsets_ref[0, 1]
    taps = banded(tap_row(index_ref[0, 1]), distance)
    column_ref[...] = jnp.concatenate(halves(taps), axis=1)
    copy.wait()


def resample_kernel(last_block, slc_ref, lines_ref, left_ref, right_ref, left_corner, right_corner, line_ref, column_ref, *outs):
    outs, tiles_ref = outs[:-1], outs[-1]
    lines = slc_ref.shape[1]
    block = lax.axis_index("rng")
    moved = []
    for plane in range(2):
        own = jnp.concatenate([left_ref[plane], slc_ref[plane], right_ref[plane]], axis=1)
        halo = jnp.concatenate([left_corner[plane], lines_ref[plane], right_corner[plane]], axis=1)
        both = dot(line_ref[...], jnp.concatenate([own, halo], axis=0))
        moved.append(both[:lines] + both[lines:])
    moved = jnp.concatenate(moved, axis=0)
    width = moved.shape[1]
    left = jnp.where(block > 0, moved[:, :LANES], 0.0)
    right = jnp.where(block < last_block, moved[:, width - LANES :], 0.0)
    moved = jnp.concatenate([left, moved[:, LANES : width - LANES], right], axis=1)
    high, low = halves(moved)
    starts = range(0, width - LANES, LANES)
    high = jnp.concatenate([high[:, s : s + 2 * LANES] for s in starts], axis=0)
    low = jnp.concatenate([low[:, s : s + 2 * LANES] for s in starts], axis=0)
    total = dot(high, column_ref[...])
    total = total[:, :LANES] + total[:, LANES:] + dot(low, column_ref[:, :LANES])
    tiles_ref[...] = total.astype(jnp.bfloat16).reshape(tiles_ref.shape)
    date = lax.axis_index("date")
    each = outs[0].shape[0]
    for step, out_ref in enumerate(outs):
        out_ref[...] = tiles_ref[pl.ds((date ^ step) * (each - 1), each)]


def filter_kernel(pairs, shift_hbm, out_ref, shift_ref, semaphore):
    copy = pltpu.make_async_copy(shift_hbm, shift_ref, semaphore)
    copy.start()
    date = lax.axis_index("date")
    spacing = lax.broadcasted_iota(jnp.int32, (1, 2 * LANES), 1).astype(jnp.float32) - FILTER_HALF
    window = 0.4 * sinc(0.4 * spacing) * (0.54 + 0.46 * jnp.cos(jnp.pi * spacing / (FILTER_HALF + 1)))
    window = jnp.where(jnp.abs(spacing) <= FILTER_HALF, window, 0.0)
    copy.wait()
    for place, (first, second) in enumerate(pairs):
        gap = shift_ref[date ^ first] - shift_ref[date ^ second]
        angle = jnp.where(jnp.abs(spacing) <= FILTER_HALF, jnp.pi * gap * spacing, 0.0)
        for part, taps in enumerate((window * jnp.cos(angle), window * jnp.sin(angle))):
            spread = jnp.broadcast_to(taps, (LANES, 2 * LANES))
            spread = pltpu.roll(spread, LEAD - FILTER_HALF, 1, stride=1, stride_axis=0)
            high, low = halves(spread)
            out_ref[place, 0, part * LANES : (part + 1) * LANES, :] = high
            out_ref[place, 1, part * LANES : (part + 1) * LANES, :] = low


def looks_kernel(pairs, dates, weight_ref, *refs):
    chunks, out_ref, window_ref, product_ref = refs[:dates], refs[dates], refs[-2], refs[-1]
    blocks, rows = chunks[0].shape[0] - 1, chunks[0].shape[1]
    lines = rows // 2
    groups = lines // LOOK_AZ
    looks = blocks * LANES // LOOK_RG
    date = lax.axis_index("date")
    for step, chunk_ref in enumerate(chunks):
        for k in range(blocks):
            at = pl.ds(k * rows, rows)
            window_ref[step, at, :LANES] = chunk_ref[k]
            window_ref[step, at, LANES:] = chunk_ref[k + 1]
    for place, (first, second) in enumerate(pairs):
        def filtered(step):
            total = dot_nt(window_ref[step], weight_ref[place, 0]) + dot_nt(window_ref[step], weight_ref[place, 1])
            total = total.reshape(blocks, 2, lines, 2 * LANES)
            return total[:, 0, :, :LANES], total[:, 1, :, :LANES], total[:, 0, :, LANES:], total[:, 1, :, LANES:]

        cos_re, cos_im, sin_re, sin_im = filtered(first)
        master_re, master_im = cos_re + sin_im, cos_im - sin_re
        cos_re, cos_im, sin_re, sin_im = filtered(second)
        partner_re, partner_im = cos_re - sin_im, cos_im + sin_re
        for part, product in enumerate(
            (
                master_re * partner_re + master_im * partner_im,
                master_im * partner_re - master_re * partner_im,
            )
        ):
            summed = sum(product[:, k * groups : (k + 1) * groups] for k in range(LOOK_AZ))
            at = pl.ds((place * 2 + part) * groups, groups)
            for k in range(blocks):
                product_ref[at, k * LANES : (k + 1) * LANES] = summed[k]

    out_width = out_ref.shape[2]
    column = lax.broadcasted_iota(jnp.int32, (product_ref.shape[1], out_width), 0)
    lane = lax.broadcasted_iota(jnp.int32, (product_ref.shape[1], out_width), 1)
    collect = jnp.where(column // LOOK_RG == lane % looks, 1.0, 0.0).astype(jnp.bfloat16)
    high, low = halves(product_ref[...])
    total = (dot(high, collect) + dot(low, collect)) * (1.0 / (LOOK_AZ * LOOK_RG))
    total = total.reshape(len(pairs), 2, groups, out_width)
    own_lane = lax.broadcasted_iota(jnp.int32, (groups, out_width), 1) // looks
    for step in range(dates):
        value = jnp.zeros((groups, out_width), jnp.float32)
        for place, pair in enumerate(pairs):
            if step in pair:
                other = pair[1] if pair[0] == step else pair[0]
                lag = (date ^ other) - (date ^ step)
                for part in range(2):
                    signed = -total[place, part] if part == 1 and pair[1] == step else total[place, part]
                    value = jnp.where(own_lane == (lag - 1) * 2 + part, signed, value)
        out_ref[date ^ step] = value


def place_kernel(used_lags, looks, recv_ref, out_ref):
    groups, columns = out_ref.shape[2:]
    lane = lax.broadcasted_iota(jnp.int32, (groups, LANES), 1) // looks
    out_ref[...] = jnp.zeros_like(out_ref)
    each = LANES // looks
    for lag in range(used_lags):
        for part in range(2):
            tile, group = divmod(lag * 2 + part, each)
            value = jnp.zeros((groups, columns), jnp.float32)
            for chunk in range(recv_ref.shape[0]):
                block = recv_ref[chunk, :, tile * LANES : (tile + 1) * LANES]
                shift = looks * (chunk - group) % LANES
                if shift:
                    block = pltpu.roll(block, shift, 1)
                value = jnp.where(lane == chunk, block, value)
            out_ref[part, lag] = value


def tiled_body(slc, offsets, kernel_index, range_shift):
    dates, rng_count = (lax.axis_size(a) for a in ("date", "rng"))
    lines, columns = slc.shape[2], slc.shape[3]
    chunk = columns // dates
    looks = chunk // LOOK_RG
    groups = lines // LOOK_AZ
    out_width = up(min(LAGS, dates - 1) * 2 * looks, LANES)
    vmem = pl.BlockSpec(memory_space=pltpu.VMEM)
    hbm = pl.BlockSpec(memory_space=pltpu.HBM)
    limit = pltpu.CompilerParams(vmem_limit_bytes=32 * 1024 * 1024)
    bf16 = jnp.bfloat16
    cells, offsets, kernel_index, range_shift = (
        pltpu.with_memory_space_constraint(value, pltpu.HBM)
        for value in (slc.reshape(2, lines, columns), offsets, kernel_index, range_shift)
    )

    moves = slots(rng_count)
    shapes = [(2, HALO_LINES, columns)] + [(2, lines, LANES)] * len(moves) + [(2, HALO_LINES, LANES)] * len(moves)
    edges = pl.pallas_call(
        edge_kernel,
        out_shape=[jax.ShapeDtypeStruct(s, bf16) for s in shapes],
        in_specs=[hbm],
        out_specs=[vmem] * len(shapes),
        scratch_shapes=[pltpu.SemaphoreType.DMA((len(shapes),))],
        compiler_params=limit,
    )(cells)
    swap = [(0, 1), (1, 0)]
    sides = [lax.ppermute(edges[1 + i], "rng", move) for i, move in enumerate(moves)]
    corners = [
        lax.ppermute(edges[1 + len(moves) + i], ("rng", "az"), [(2 * a + c, 2 * b + d) for a, b in move for c, d in swap])
        for i, move in enumerate(moves)
    ]
    halo_lines = lax.ppermute(edges[0], "az", swap)

    line_taps, column_taps, held = pl.pallas_call(
        taps_kernel,
        out_shape=[
            jax.ShapeDtypeStruct((2 * lines, lines + HALO_LINES), bf16),
            jax.ShapeDtypeStruct((2 * LANES, 2 * LANES), bf16),
            jax.ShapeDtypeStruct(cells.shape, bf16),
        ],
        in_specs=[hbm] * 3,
        out_specs=[vmem] * 3,
        scratch_shapes=[
            pltpu.SMEM(offsets.shape, jnp.int32),
            pltpu.SMEM(kernel_index.shape, jnp.int32),
            pltpu.SemaphoreType.DMA((3,)),
        ],
        compiler_params=limit,
    )(offsets, kernel_index, cells)

    tiles = chunk // LANES + 1
    sent = pl.pallas_call(
        functools.partial(resample_kernel, rng_count - 1),
        out_shape=[jax.ShapeDtypeStruct((tiles, 2 * lines, LANES), bf16)] * dates,
        in_specs=[vmem] * 8,
        out_specs=[vmem] * dates,
        scratch_shapes=[pltpu.VMEM((columns // LANES + 1, 2 * lines, LANES), bf16)],
        compiler_params=limit,
    )(held, halo_lines, sides[0], sides[-1], corners[0], corners[-1], line_taps, column_taps)

    def exchanged(values):
        arrived = {0: values[0]}
        for step in range(dates - 1, 0, -1):
            arrived[step] = lax.ppermute(values[step], "date", [(i, i ^ step) for i in range(dates)])
        return [arrived[step] for step in range(dates)]

    chunks = exchanged(sent)
    pairs = [(first, second) for first in range(dates) for second in range(first + 1, dates)]
    weights = pl.pallas_call(
        functools.partial(filter_kernel, pairs),
        out_shape=jax.ShapeDtypeStruct((len(pairs), 2, 2 * LANES, 2 * LANES), bf16),
        in_specs=[hbm],
        out_specs=vmem,
        scratch_shapes=[pltpu.SMEM(range_shift.shape, jnp.float32), pltpu.SemaphoreType.DMA],
        compiler_params=limit,
    )(range_shift)
    looked = pl.pallas_call(
        functools.partial(looks_kernel, pairs, dates),
        out_shape=jax.ShapeDtypeStruct((dates, groups, out_width), jnp.float32),
        in_specs=[vmem] * (1 + dates),
        out_specs=vmem,
        scratch_shapes=[
            pltpu.VMEM((dates, (tiles - 1) * 2 * lines, 2 * LANES), bf16),
            pltpu.VMEM((len(pairs) * 2 * groups, chunk), jnp.float32),
        ],
        compiler_params=limit,
    )(weights, *chunks)
    out = pl.pallas_call(
        functools.partial(place_kernel, min(LAGS, dates - 1), looks),
        out_shape=jax.ShapeDtypeStruct((2, LAGS, groups, looks * dates), jnp.float32),
        in_specs=[vmem],
        out_specs=vmem,
        compiler_params=limit,
    )(lax.all_to_all(looked, "date", 0, 0, tiled=True))
    return out[:, None]


def body(slc, offsets, kernel_index, range_shift):
    dates, az_count = (lax.axis_size(a) for a in ("date", "az"))
    lines, columns = slc.shape[2], slc.shape[3]
    whole_tiles = columns % (dates * LANES) == 0 and columns % (dates * LOOK_RG) == 0
    one_row = columns // LOOK_RG == LANES and range_shift.shape[0] == dates
    few = dates & (dates - 1) == 0 and dates - 1 <= LAGS
    if az_count == 2 and whole_tiles and one_row and few and lines % 32 == 0:
        return tiled_body(slc, offsets, kernel_index, range_shift)
    return chunked_body(slc, offsets, kernel_index, range_shift)


def solution(mesh):
    return jax.shard_map(
        body,
        mesh=mesh,
        in_specs=(
            P(None, ("groups", "date"), "az", "rng"),
            P(("groups", "date"), None),
            P(("groups", "date"), None),
            P("groups"),
        ),
        out_specs=P(None, ("groups", "date"), None, "az", "rng"),
        check_vma=False,
    )
```

```python
import functools

import jax
import jax.numpy as jnp
import numpy as np
from jax import lax
from jax.experimental import pallas as pl
from jax.experimental.pallas import tpu as pltpu
from jax.sharding import PartitionSpec as P

LAGS = 8
KERNELS = 16
TAPS = 8
FILTER_HALF = 8
FILTER_TAPS = 2 * FILTER_HALF + 1
LOOK_AZ = 4
LOOK_RG = 20
LANES = 128
META = 3
UNROLLED_PAIRS = 12


def up(value, unit):
    return -(-value // unit) * unit


def kernel_table():
    position = np.arange(TAPS) - 3.0 - np.arange(KERNELS)[:, None] / KERNELS
    shaped = np.sinc(position) * (0.5 + 0.5 * np.cos(np.pi * position / 5.0))
    table = np.zeros((KERNELS, LANES), np.float32)
    table[:, :TAPS] = shaped / shaped.sum(1, keepdims=True)
    return table


def lowpass_row(width):
    t = np.arange(FILTER_TAPS) - FILTER_HALF
    row = np.zeros((1, width), np.float32)
    row[0, :FILTER_TAPS] = 0.4 * np.sinc(0.4 * t) * (0.54 + 0.46 * np.cos(np.pi * t / (FILTER_HALF + 1)))
    return row


def halves(value):
    high = value.astype(jnp.bfloat16)
    return high, (value - high.astype(jnp.float32)).astype(jnp.bfloat16)


def dot(a, b):
    return jnp.dot(a, b, preferred_element_type=jnp.float32)


def dot_nt(a, b):
    return lax.dot_general(a, b, (((1,), (1,)), ((), ())), preferred_element_type=jnp.float32)


def pack_kernel(chunk, place_ref, offsets_ref, index_ref, slc_ref, before_ref, after_ref, out_ref, wide_ref):
    columns = slc_ref.shape[1]
    wide = out_ref.shape[2]
    first = place_ref[0] == 0
    last = place_ref[0] == place_ref[1] - 1
    zero = jnp.zeros_like(before_ref[...])
    wide_ref[:, :LANES] = jnp.where(first, zero, before_ref[...])
    wide_ref[:, LANES : LANES + columns] = slc_ref[...]
    wide_ref[:, LANES + columns :] = jnp.where(last, zero, after_ref[...])
    lane = lax.broadcasted_iota(jnp.int32, (slc_ref.shape[0], wide), 1)
    numbers = [offsets_ref[0, 0], index_ref[0, 0], index_ref[0, 1]]
    for j in range(out_ref.shape[0]):
        start = LANES + chunk * j - FILTER_HALF - 3 + offsets_ref[0, 1]
        tile = lax.shift_right_logical(start, 7)
        within = lax.bitwise_and(start, LANES - 1)
        window = wide_ref[:, pl.ds(pl.multiple_of(tile * LANES, LANES), wide + LANES)].astype(jnp.float32)
        moved = pltpu.roll(window, wide + LANES - within, 1)[:, :wide]
        for slot, number in enumerate(numbers):
            moved = jnp.where(lane == wide - META + slot, number.astype(jnp.float32), moved)
        out_ref[j] = moved.astype(jnp.bfloat16)


def picked_taps(table, index):
    row = lax.broadcasted_iota(jnp.int32, table.shape, 0).astype(jnp.float32)
    return jnp.sum(jnp.where(row == index, table, 0.0), axis=0, keepdims=True)


def banded(taps, distance):
    out = jnp.zeros(distance.shape, jnp.float32)
    for q in range(TAPS):
        out = jnp.where(distance == q, taps[:, q : q + 1], out)
    return out


def pairs_kernel(chunk, pairs, *refs):
    if isinstance(pairs, int):
        table_of_pairs, refs = refs[0], refs[1:]
    shift_ref, table_ref, lowpass_ref, recv_ref, out_ref, resampled_ref, weight_ref, product_ref = refs
    sources, rows, wide = recv_ref.shape
    dates = shift_ref.shape[0]
    az_count = sources // dates
    own_lines = rows // 2
    lines = own_lines * az_count
    groups = lines // LOOK_AZ
    looks = chunk // LOOK_RG
    table = table_ref[...]
    held = resampled_ref.shape[2]

    out_row = lax.broadcasted_iota(jnp.int32, (lines, lines), 0)
    in_row = lax.broadcasted_iota(jnp.int32, (lines, lines), 1)
    line = LOOK_AZ * (out_row % groups) + out_row // groups
    line_distance = (in_row - line + 3).astype(jnp.float32)
    span = min(2 * LANES, wide)
    column_distance = (
        lax.broadcasted_iota(jnp.int32, (span, LANES), 0) - lax.broadcasted_iota(jnp.int32, (span, LANES), 1)
    ).astype(jnp.float32)
    for date in range(dates):
        numbers = recv_ref[date * az_count, 0:16, wide - LANES :].astype(jnp.float32)[0:1, LANES - META :]
        line_offset, line_index, column_index = (numbers[:, s : s + 1] for s in range(META))
        line_taps = banded(picked_taps(table, line_index), line_distance - line_offset)
        line_taps = jnp.concatenate(halves(line_taps), axis=0)
        column_high, column_low = halves(banded(picked_taps(table, column_index), column_distance))
        moved = []
        for plane in range(2):
            rows_of = slice(plane * own_lines, (plane + 1) * own_lines)
            source = jnp.concatenate([recv_ref[date * az_count + a, rows_of, :] for a in range(az_count)], axis=0)
            both = dot(line_taps, source)
            moved.append(both[:lines] + both[lines:])
        moved_high, moved_low = halves(jnp.concatenate(moved, axis=0))
        for begin in range(0, held, LANES):
            end = min(begin + span, wide)
            taken = end - begin
            total = dot(moved_high[:, begin:end], column_high[:taken])
            total += dot(moved_low[:, begin:end], column_high[:taken])
            total += dot(moved_high[:, begin:end], column_low[:taken])
            resampled_ref[date, :, begin : begin + LANES] = total.astype(jnp.bfloat16)

    window = lowpass_ref[...]
    spacing = lax.broadcasted_iota(jnp.int32, window.shape, 1).astype(jnp.float32) - FILTER_HALF
    span = min(2 * LANES, held)

    def one_pair(place, own, other):
        gap = shift_ref[own] - shift_ref[other]
        angle = jnp.where(jnp.abs(spacing) <= FILTER_HALF, jnp.pi * gap * spacing, 0.0)
        for part, taps in enumerate((window * jnp.cos(angle), window * jnp.sin(angle))):
            spread = jnp.broadcast_to(taps, (LANES, 2 * LANES))
            spread = pltpu.roll(spread, 0, 1, stride=1, stride_axis=0)
            high, low = halves(spread)
            weight_ref[0, part * LANES : (part + 1) * LANES, :] = high
            weight_ref[1, part * LANES : (part + 1) * LANES, :] = low
        both = jnp.concatenate([resampled_ref[own], resampled_ref[other]], axis=0)
        for begin in range(0, up(chunk, LANES), LANES):
            end = min(begin + span, held)
            taken = end - begin
            total = dot_nt(both[:, begin:end], weight_ref[0, :, :taken])
            total += dot_nt(both[:, begin:end], weight_ref[1, :, :taken])
            cos, sin = total[:, :LANES], total[:, LANES:]
            re, im = slice(0, lines), slice(lines, 2 * lines)
            master_re = cos[re] + sin[im]
            master_im = cos[im] - sin[re]
            re, im = slice(2 * lines, 3 * lines), slice(3 * lines, 4 * lines)
            partner_re = cos[re] - sin[im]
            partner_im = cos[im] + sin[re]
            for part, product in enumerate(
                (
                    master_re * partner_re + master_im * partner_im,
                    master_im * partner_re - master_re * partner_im,
                )
            ):
                summed = sum(product[k * groups : (k + 1) * groups] for k in range(LOOK_AZ))
                product_ref[place, part, :, begin : begin + LANES] = summed

    if isinstance(pairs, int):
        count = pairs

        def step(place, carry):
            one_pair(place, table_of_pairs[place, 0], table_of_pairs[place, 1])
            return carry

        lax.fori_loop(0, count, step, 0)
    else:
        count = len(pairs)
        for place, (own, other) in enumerate(pairs):
            one_pair(place, own, other)

    out_width = out_ref.shape[2]
    column = lax.broadcasted_iota(jnp.int32, (product_ref.shape[3], out_width), 0)
    lane = lax.broadcasted_iota(jnp.int32, (product_ref.shape[3], out_width), 1)
    collect = jnp.where(column // LOOK_RG == lane % looks, 1.0, 0.0).astype(jnp.bfloat16)
    high, low = halves(product_ref[...].reshape(count * 2 * groups, product_ref.shape[3]))
    total = (dot(high, collect) + dot(low, collect)) * (1.0 / (LOOK_AZ * LOOK_RG))
    total = total.reshape(count, 2, groups, out_width)
    own_lane = lax.broadcasted_iota(jnp.int32, (groups, out_width), 1) // looks
    place = 0
    for own in range(dates):
        value = jnp.zeros((groups, out_width), jnp.float32)
        for lag in range(min(LAGS, dates - 1 - own)):
            for part in range(2):
                value = jnp.where(own_lane == lag * 2 + part, total[place, part], value)
            place += 1
        out_ref[own * az_count : (own + 1) * az_count] = value.reshape(az_count, groups // az_count, out_width)


def unpack_kernel(used_lags, looks, recv_ref, out_ref):
    sources, groups, width = recv_ref.shape
    columns = out_ref.shape[-1]
    lane = lax.broadcasted_iota(jnp.int32, (groups, columns), 1) // looks
    out_ref[...] = jnp.zeros_like(out_ref)
    for lag in range(used_lags):
        for part in range(2):
            value = jnp.zeros((groups, columns), jnp.float32)
            for source in range(sources):
                block = recv_ref[source]
                if width != columns:
                    block = block[:, :columns]
                shift = looks * (source - lag * 2 - part) % columns
                if shift:
                    block = pltpu.roll(block, shift, 1)
                value = jnp.where(lane == source, block, value)
            out_ref[part, lag] = value


def chunked_body(slc, offsets, kernel_index, range_shift):
    axes = ("date", "az")
    date_count, az_count, rng_count = (lax.axis_size(a) for a in ("date", "az", "rng"))
    peers = date_count * az_count
    lines, columns = slc.shape[2], slc.shape[3]
    dates = range_shift.shape[0]
    chunk = columns // peers
    looks = chunk // LOOK_RG
    groups = lines * az_count // LOOK_AZ
    wide = up(chunk + 2 * FILTER_HALF + TAPS - 1 + META, LANES)
    held = up(chunk + 2 * FILTER_HALF, LANES)
    used_lags = min(LAGS, dates - 1)
    out_width = up(used_lags * 2 * looks, LANES)
    vmem = pl.BlockSpec(memory_space=pltpu.VMEM)
    smem = pl.BlockSpec(memory_space=pltpu.SMEM)
    limit = pltpu.CompilerParams(vmem_limit_bytes=32 * 1024 * 1024)

    cells = slc.reshape(2 * lines, columns)
    place = lax.axis_index("rng")
    if rng_count == 2:
        edge = jnp.where(place == 0, cells[:, columns - LANES :], cells[:, :LANES])
        before = after = lax.ppermute(edge, "rng", [(0, 1), (1, 0)])
    else:
        forth = [(i, i + 1) for i in range(rng_count - 1)]
        before = lax.ppermute(cells[:, columns - LANES :], "rng", forth)
        after = lax.ppermute(cells[:, :LANES], "rng", [(b, a) for a, b in forth])

    packed = pl.pallas_call(
        functools.partial(pack_kernel, chunk),
        out_shape=jax.ShapeDtypeStruct((peers, 2 * lines, wide), jnp.bfloat16),
        in_specs=[smem] * 3 + [vmem] * 3,
        out_specs=vmem,
        scratch_shapes=[pltpu.VMEM((2 * lines, columns + 2 * LANES), jnp.bfloat16)],
        compiler_params=limit,
    )(jnp.stack([place, rng_count]).astype(jnp.int32), offsets, kernel_index, cells, before, after)
    arrived = lax.all_to_all(packed, axes, 0, 0, tiled=True)

    pairs = [(own, own + lag) for own in range(dates) for lag in range(1, LAGS + 1) if own + lag < dates]
    count = len(pairs)
    first = [jnp.asarray(np.array(pairs, np.int32))] if count > UNROLLED_PAIRS else []
    looked = pl.pallas_call(
        functools.partial(pairs_kernel, chunk, count if first else pairs),
        out_shape=jax.ShapeDtypeStruct((peers, groups // az_count, out_width), jnp.float32),
        in_specs=[smem] * len(first) + [smem] + [vmem] * 3,
        out_specs=vmem,
        scratch_shapes=[
            pltpu.VMEM((dates, 4 * (groups * LOOK_AZ) // 2, held), jnp.bfloat16),
            pltpu.VMEM((2, 2 * LANES, 2 * LANES), jnp.bfloat16),
            pltpu.VMEM((count, 2, groups, up(chunk, LANES)), jnp.float32),
        ],
        compiler_params=limit,
    )(*first, range_shift, jnp.asarray(kernel_table()), jnp.asarray(lowpass_row(2 * LANES)), arrived)
    returned = lax.all_to_all(looked, axes, 0, 0, tiled=True)

    out = pl.pallas_call(
        functools.partial(unpack_kernel, used_lags, looks),
        out_shape=jax.ShapeDtypeStruct((2, LAGS, groups // az_count, looks * peers), jnp.float32),
        in_specs=[vmem],
        out_specs=vmem,
        compiler_params=limit,
    )(returned)
    return out[:, None]


HALO_LINES = 16
LEAD = 32


def slots(count):
    if count == 2:
        return [[(0, 1), (1, 0)]]
    return [[(i, i + 1) for i in range(count - 1)], [(i + 1, i) for i in range(count - 1)]]


def edge_kernel(slc_ref, *refs):
    outs, semaphores = refs[:-1], refs[-1]
    lines, columns = slc_ref.shape[1:]
    row = pl.multiple_of((1 - lax.axis_index("az")) * (lines - HALO_LINES), HALO_LINES)
    if len(outs) == 3:
        starts = [pl.multiple_of((1 - lax.axis_index("rng")) * (columns - LANES), LANES)]
    else:
        starts = [columns - LANES, 0]
    wanted = [slc_ref.at[:, pl.ds(row, HALO_LINES), :]]
    wanted += [slc_ref.at[:, :, pl.ds(start, LANES)] for start in starts]
    wanted += [slc_ref.at[:, pl.ds(row, HALO_LINES), pl.ds(start, LANES)] for start in starts]
    copies = [pltpu.make_async_copy(w, o, semaphores.at[i]) for i, (w, o) in enumerate(zip(wanted, outs))]
    for copy in copies:
        copy.start()
    for copy in copies:
        copy.wait()


def sinc(value):
    angle = jnp.pi * value
    return jnp.where(angle == 0.0, 1.0, jnp.sin(angle) / jnp.where(angle == 0.0, 1.0, angle))


def tap_row(index):
    lane = lax.broadcasted_iota(jnp.int32, (1, LANES), 1)
    position = lane.astype(jnp.float32) - 3.0 - index.astype(jnp.float32) / KERNELS
    shaped = sinc(position) * (0.5 + 0.5 * jnp.cos(jnp.pi * position / 5.0))
    shaped = jnp.where(lane < TAPS, shaped, 0.0)
    return shaped / jnp.sum(shaped, axis=1, keepdims=True)


def taps_kernel(offsets_hbm, index_hbm, slc_ref, line_ref, column_ref, held_ref, offsets_ref, index_ref, semaphores):
    copy = pltpu.make_async_copy(slc_ref, held_ref, semaphores.at[0])
    numbers = [
        pltpu.make_async_copy(offsets_hbm, offsets_ref, semaphores.at[1]),
        pltpu.make_async_copy(index_hbm, index_ref, semaphores.at[2]),
    ]
    for each in numbers:
        each.start()
    copy.start()
    for each in numbers:
        each.wait()
    lines = slc_ref.shape[1]
    groups = lines // LOOK_AZ
    shape = (lines, lines + HALO_LINES)
    row = lax.broadcasted_iota(jnp.int32, shape, 0)
    place = lax.broadcasted_iota(jnp.int32, shape, 1)
    beyond = jnp.where(lax.axis_index("az") == 0, 0, -lines - HALO_LINES)
    source = jnp.where(place < lines, place, place + beyond)
    line = LOOK_AZ * (row % groups) + row // groups
    taps = banded(tap_row(index_ref[0, 0]), source - line - offsets_ref[0, 0] + 3)
    line_ref[...] = jnp.concatenate(halves(taps), axis=0)
    shape = (2 * LANES, LANES)
    distance = lax.broadcasted_iota(jnp.int32, shape, 0) - lax.broadcasted_iota(jnp.int32, shape, 1)
    distance = distance - (LANES - LEAD - 3) - offsets_ref[0, 1]
    taps = banded(tap_row(index_ref[0, 1]), distance)
    column_ref[...] = jnp.concatenate(halves(taps), axis=1)
    copy.wait()


def resample_kernel(last_block, left_ref, right_ref, left_corner, right_corner, lines_ref, slc_ref, line_ref, column_ref, *outs):
    outs, tiles_ref = outs[:-1], outs[-1]
    lines = slc_ref.shape[1]
    block = lax.axis_index("rng")
    moved = []
    for plane in range(2):
        own = jnp.concatenate([left_ref[plane], slc_ref[plane], right_ref[plane]], axis=1)
        halo = jnp.concatenate([left_corner[plane], lines_ref[plane], right_corner[plane]], axis=1)
        both = dot(line_ref[...], jnp.concatenate([own, halo], axis=0))
        moved.append(both[:lines] + both[lines:])
    moved = jnp.concatenate(moved, axis=0)
    width = moved.shape[1]
    left = jnp.where(block > 0, moved[:, :LANES], 0.0)
    right = jnp.where(block < last_block, moved[:, width - LANES :], 0.0)
    moved = jnp.concatenate([left, moved[:, LANES : width - LANES], right], axis=1)
    high, low = halves(moved)
    starts = range(0, width - LANES, LANES)
    high = jnp.concatenate([high[:, s : s + 2 * LANES] for s in starts], axis=0)
    low = jnp.concatenate([low[:, s : s + 2 * LANES] for s in starts], axis=0)
    total = dot(high, column_ref[...])
    total = total[:, :LANES] + total[:, LANES:] + dot(low, column_ref[:, :LANES])
    tiles_ref[...] = total.astype(jnp.bfloat16).reshape(tiles_ref.shape)
    date = lax.axis_index("date")
    each = outs[0].shape[0]
    for step, out_ref in enumerate(outs):
        out_ref[...] = tiles_ref[pl.ds((date ^ step) * (each - 1), each)]


def filter_kernel(pairs, shift_hbm, out_ref, shift_ref, semaphore):
    copy = pltpu.make_async_copy(shift_hbm, shift_ref, semaphore)
    copy.start()
    date = lax.axis_index("date")
    spacing = lax.broadcasted_iota(jnp.int32, (1, 2 * LANES), 1).astype(jnp.float32) - FILTER_HALF
    window = 0.4 * sinc(0.4 * spacing) * (0.54 + 0.46 * jnp.cos(jnp.pi * spacing / (FILTER_HALF + 1)))
    window = jnp.where(jnp.abs(spacing) <= FILTER_HALF, window, 0.0)
    copy.wait()
    for place, (first, second) in enumerate(pairs):
        gap = shift_ref[date ^ first] - shift_ref[date ^ second]
        angle = jnp.where(jnp.abs(spacing) <= FILTER_HALF, jnp.pi * gap * spacing, 0.0)
        for part, taps in enumerate((window * jnp.cos(angle), window * jnp.sin(angle))):
            spread = jnp.broadcast_to(taps, (LANES, 2 * LANES))
            spread = pltpu.roll(spread, LEAD - FILTER_HALF, 1, stride=1, stride_axis=0)
            high, low = halves(spread)
            out_ref[place, 0, part * LANES : (part + 1) * LANES, :] = high
            out_ref[place, 1, part * LANES : (part + 1) * LANES, :] = low


def looks_kernel(pairs, dates, weight_ref, *refs):
    chunks, outs, window_ref, product_ref = refs[:dates][::-1], refs[dates : 2 * dates], refs[-2], refs[-1]
    blocks, rows = chunks[0].shape[0] - 1, chunks[0].shape[1]
    lines = rows // 2
    groups = lines // LOOK_AZ
    looks = blocks * LANES // LOOK_RG
    date = lax.axis_index("date")
    for step, chunk_ref in enumerate(chunks):
        for k in range(blocks):
            at = pl.ds(k * rows, rows)
            window_ref[step, at, :LANES] = chunk_ref[k]
            window_ref[step, at, LANES:] = chunk_ref[k + 1]
    for place, (first, second) in enumerate(pairs):
        def filtered(step):
            total = dot_nt(window_ref[step], weight_ref[place, 0]) + dot_nt(window_ref[step], weight_ref[place, 1])
            total = total.reshape(blocks, 2, lines, 2 * LANES)
            return total[:, 0, :, :LANES], total[:, 1, :, :LANES], total[:, 0, :, LANES:], total[:, 1, :, LANES:]

        cos_re, cos_im, sin_re, sin_im = filtered(first)
        master_re, master_im = cos_re + sin_im, cos_im - sin_re
        cos_re, cos_im, sin_re, sin_im = filtered(second)
        partner_re, partner_im = cos_re - sin_im, cos_im + sin_re
        for part, product in enumerate(
            (
                master_re * partner_re + master_im * partner_im,
                master_im * partner_re - master_re * partner_im,
            )
        ):
            summed = sum(product[:, k * groups : (k + 1) * groups] for k in range(LOOK_AZ))
            at = pl.ds((place * 2 + part) * groups, groups)
            for k in range(blocks):
                product_ref[at, k * LANES : (k + 1) * LANES] = summed[k]

    out_width = outs[0].shape[1]
    column = lax.broadcasted_iota(jnp.int32, (product_ref.shape[1], out_width), 0)
    lane = lax.broadcasted_iota(jnp.int32, (product_ref.shape[1], out_width), 1)
    collect = jnp.where(column // LOOK_RG == lane % looks, 1.0, 0.0).astype(jnp.bfloat16)
    high, low = halves(product_ref[...])
    total = (dot(high, collect) + dot(low, collect)) * (1.0 / (LOOK_AZ * LOOK_RG))
    total = total.reshape(len(pairs), 2, groups, out_width)
    own_lane = lax.broadcasted_iota(jnp.int32, (groups, out_width), 1) // looks
    for step, out_ref in enumerate(outs):
        value = jnp.zeros((groups, out_width), jnp.float32)
        for place, pair in enumerate(pairs):
            if step in pair:
                other = pair[1] if pair[0] == step else pair[0]
                lag = (date ^ other) - (date ^ step)
                for part in range(2):
                    signed = -total[place, part] if part == 1 and pair[1] == step else total[place, part]
                    value = jnp.where(own_lane == (lag - 1) * 2 + part, signed, value)
        out_ref[...] = value


def place_kernel(used_lags, looks, *refs):
    out_ref = refs[-1]
    groups, columns = out_ref.shape[2:]
    date = lax.axis_index("date")
    lane = lax.broadcasted_iota(jnp.int32, (groups, LANES), 1) // looks
    out_ref[...] = jnp.zeros_like(out_ref)
    each = LANES // looks
    for step, recv_ref in enumerate(refs[:-1][::-1]):
        chunk = date ^ step
        for lag in range(used_lags):
            for part in range(2):
                tile, group = divmod(lag * 2 + part, each)
                block = recv_ref[:, tile * LANES : (tile + 1) * LANES]
                block = pltpu.roll(block, lax.bitwise_and(looks * (chunk - group), LANES - 1), 1)
                out_ref[part, lag] = jnp.where(lane == chunk, block, out_ref[part, lag])


def tiled_body(slc, offsets, kernel_index, range_shift):
    dates, rng_count = (lax.axis_size(a) for a in ("date", "rng"))
    lines, columns = slc.shape[2], slc.shape[3]
    chunk = columns // dates
    looks = chunk // LOOK_RG
    groups = lines // LOOK_AZ
    out_width = up(min(LAGS, dates - 1) * 2 * looks, LANES)
    vmem = pl.BlockSpec(memory_space=pltpu.VMEM)
    hbm = pl.BlockSpec(memory_space=pltpu.HBM)
    limit = pltpu.CompilerParams(vmem_limit_bytes=32 * 1024 * 1024)
    bf16 = jnp.bfloat16
    cells, offsets, kernel_index, range_shift = (
        pltpu.with_memory_space_constraint(value, pltpu.HBM)
        for value in (slc.reshape(2, lines, columns), offsets, kernel_index, range_shift)
    )

    moves = slots(rng_count)
    shapes = [(2, HALO_LINES, columns)] + [(2, lines, LANES)] * len(moves) + [(2, HALO_LINES, LANES)] * len(moves)
    edges = pl.pallas_call(
        edge_kernel,
        out_shape=[jax.ShapeDtypeStruct(s, bf16) for s in shapes],
        in_specs=[hbm],
        out_specs=[vmem] * len(shapes),
        scratch_shapes=[pltpu.SemaphoreType.DMA((len(shapes),))],
        compiler_params=limit,
    )(cells)
    swap = [(0, 1), (1, 0)]
    sides = [lax.ppermute(edges[1 + i], "rng", move) for i, move in enumerate(moves)]
    corners = [
        lax.ppermute(edges[1 + len(moves) + i], ("rng", "az"), [(2 * a + c, 2 * b + d) for a, b in move for c, d in swap])
        for i, move in enumerate(moves)
    ]
    halo_lines = lax.ppermute(edges[0], "az", swap)

    line_taps, column_taps, held = pl.pallas_call(
        taps_kernel,
        out_shape=[
            jax.ShapeDtypeStruct((2 * lines, lines + HALO_LINES), bf16),
            jax.ShapeDtypeStruct((2 * LANES, 2 * LANES), bf16),
            jax.ShapeDtypeStruct(cells.shape, bf16),
        ],
        in_specs=[hbm] * 3,
        out_specs=[vmem] * 3,
        scratch_shapes=[
            pltpu.SMEM(offsets.shape, jnp.int32),
            pltpu.SMEM(kernel_index.shape, jnp.int32),
            pltpu.SemaphoreType.DMA((3,)),
        ],
        compiler_params=limit,
    )(offsets, kernel_index, cells)

    tiles = chunk // LANES + 1
    sent = pl.pallas_call(
        functools.partial(resample_kernel, rng_count - 1),
        out_shape=[jax.ShapeDtypeStruct((tiles, 2 * lines, LANES), bf16)] * dates,
        in_specs=[vmem] * 8,
        out_specs=[vmem] * dates,
        scratch_shapes=[pltpu.VMEM((columns // LANES + 1, 2 * lines, LANES), bf16)],
        compiler_params=limit,
    )(sides[0], sides[-1], corners[0], corners[-1], halo_lines, held, line_taps, column_taps)

    def exchanged(values):
        arrived = {0: values[0]}
        for step in range(dates - 1, 0, -1):
            arrived[step] = lax.ppermute(values[step], "date", [(i, i ^ step) for i in range(dates)])
        return [arrived[step] for step in reversed(range(dates))]

    chunks = exchanged(sent)
    pairs = [(first, second) for first in range(dates) for second in range(first + 1, dates)]
    weights = pl.pallas_call(
        functools.partial(filter_kernel, pairs),
        out_shape=jax.ShapeDtypeStruct((len(pairs), 2, 2 * LANES, 2 * LANES), bf16),
        in_specs=[hbm],
        out_specs=vmem,
        scratch_shapes=[pltpu.SMEM(range_shift.shape, jnp.float32), pltpu.SemaphoreType.DMA],
        compiler_params=limit,
    )(range_shift)
    looked = pl.pallas_call(
        functools.partial(looks_kernel, pairs, dates),
        out_shape=[jax.ShapeDtypeStruct((groups, out_width), jnp.float32)] * dates,
        in_specs=[vmem] * (1 + dates),
        out_specs=[vmem] * dates,
        scratch_shapes=[
            pltpu.VMEM((dates, (tiles - 1) * 2 * lines, 2 * LANES), bf16),
            pltpu.VMEM((len(pairs) * 2 * groups, chunk), jnp.float32),
        ],
        compiler_params=limit,
    )(weights, *chunks)
    out = pl.pallas_call(
        functools.partial(place_kernel, min(LAGS, dates - 1), looks),
        out_shape=jax.ShapeDtypeStruct((2, LAGS, groups, looks * dates), jnp.float32),
        in_specs=[vmem] * dates,
        out_specs=vmem,
        compiler_params=limit,
    )(*exchanged(looked))
    return out[:, None]


def body(slc, offsets, kernel_index, range_shift):
    dates, az_count = (lax.axis_size(a) for a in ("date", "az"))
    lines, columns = slc.shape[2], slc.shape[3]
    whole_tiles = columns % (dates * LANES) == 0 and columns % (dates * LOOK_RG) == 0
    one_row = columns // LOOK_RG == LANES and range_shift.shape[0] == dates
    few = dates & (dates - 1) == 0 and dates - 1 <= LAGS
    if az_count == 2 and whole_tiles and one_row and few and lines % 32 == 0:
        return tiled_body(slc, offsets, kernel_index, range_shift)
    return chunked_body(slc, offsets, kernel_index, range_shift)


def solution(mesh):
    return jax.shard_map(
        body,
        mesh=mesh,
        in_specs=(
            P(None, ("groups", "date"), "az", "rng"),
            P(("groups", "date"), None),
            P(("groups", "date"), None),
            P("groups"),
        ),
        out_specs=P(None, ("groups", "date"), None, "az", "rng"),
        check_vma=False,
    )
```

```python
import functools

import jax
import jax.numpy as jnp
import numpy as np
from jax import lax
from jax.experimental import pallas as pl
from jax.experimental.pallas import tpu as pltpu
from jax.sharding import PartitionSpec as P

LAGS = 8
KERNELS = 16
TAPS = 8
FILTER_HALF = 8
FILTER_TAPS = 2 * FILTER_HALF + 1
LOOK_AZ = 4
LOOK_RG = 20
LANES = 128
META = 3
UNROLLED_PAIRS = 12


def up(value, unit):
    return -(-value // unit) * unit


def kernel_table():
    position = np.arange(TAPS) - 3.0 - np.arange(KERNELS)[:, None] / KERNELS
    shaped = np.sinc(position) * (0.5 + 0.5 * np.cos(np.pi * position / 5.0))
    table = np.zeros((KERNELS, LANES), np.float32)
    table[:, :TAPS] = shaped / shaped.sum(1, keepdims=True)
    return table


def lowpass_row(width):
    t = np.arange(FILTER_TAPS) - FILTER_HALF
    row = np.zeros((1, width), np.float32)
    row[0, :FILTER_TAPS] = 0.4 * np.sinc(0.4 * t) * (0.54 + 0.46 * np.cos(np.pi * t / (FILTER_HALF + 1)))
    return row


def halves(value):
    high = value.astype(jnp.bfloat16)
    return high, (value - high.astype(jnp.float32)).astype(jnp.bfloat16)


def dot(a, b):
    return jnp.dot(a, b, preferred_element_type=jnp.float32)


def dot_nt(a, b):
    return lax.dot_general(a, b, (((1,), (1,)), ((), ())), preferred_element_type=jnp.float32)


def pack_kernel(chunk, place_ref, offsets_ref, index_ref, slc_ref, before_ref, after_ref, out_ref, wide_ref):
    columns = slc_ref.shape[1]
    wide = out_ref.shape[2]
    first = place_ref[0] == 0
    last = place_ref[0] == place_ref[1] - 1
    zero = jnp.zeros_like(before_ref[...])
    wide_ref[:, :LANES] = jnp.where(first, zero, before_ref[...])
    wide_ref[:, LANES : LANES + columns] = slc_ref[...]
    wide_ref[:, LANES + columns :] = jnp.where(last, zero, after_ref[...])
    lane = lax.broadcasted_iota(jnp.int32, (slc_ref.shape[0], wide), 1)
    numbers = [offsets_ref[0, 0], index_ref[0, 0], index_ref[0, 1]]
    for j in range(out_ref.shape[0]):
        start = LANES + chunk * j - FILTER_HALF - 3 + offsets_ref[0, 1]
        tile = lax.shift_right_logical(start, 7)
        within = lax.bitwise_and(start, LANES - 1)
        window = wide_ref[:, pl.ds(pl.multiple_of(tile * LANES, LANES), wide + LANES)].astype(jnp.float32)
        moved = pltpu.roll(window, wide + LANES - within, 1)[:, :wide]
        for slot, number in enumerate(numbers):
            moved = jnp.where(lane == wide - META + slot, number.astype(jnp.float32), moved)
        out_ref[j] = moved.astype(jnp.bfloat16)


def picked_taps(table, index):
    row = lax.broadcasted_iota(jnp.int32, table.shape, 0).astype(jnp.float32)
    return jnp.sum(jnp.where(row == index, table, 0.0), axis=0, keepdims=True)


def banded(taps, distance):
    out = jnp.zeros(distance.shape, jnp.float32)
    for q in range(TAPS):
        out = jnp.where(distance == q, taps[:, q : q + 1], out)
    return out


def pairs_kernel(chunk, pairs, *refs):
    if isinstance(pairs, int):
        table_of_pairs, refs = refs[0], refs[1:]
    shift_ref, table_ref, lowpass_ref, recv_ref, out_ref, resampled_ref, weight_ref, product_ref = refs
    sources, rows, wide = recv_ref.shape
    dates = shift_ref.shape[0]
    az_count = sources // dates
    own_lines = rows // 2
    lines = own_lines * az_count
    groups = lines // LOOK_AZ
    looks = chunk // LOOK_RG
    table = table_ref[...]
    held = resampled_ref.shape[2]

    out_row = lax.broadcasted_iota(jnp.int32, (lines, lines), 0)
    in_row = lax.broadcasted_iota(jnp.int32, (lines, lines), 1)
    line = LOOK_AZ * (out_row % groups) + out_row // groups
    line_distance = (in_row - line + 3).astype(jnp.float32)
    span = min(2 * LANES, wide)
    column_distance = (
        lax.broadcasted_iota(jnp.int32, (span, LANES), 0) - lax.broadcasted_iota(jnp.int32, (span, LANES), 1)
    ).astype(jnp.float32)
    for date in range(dates):
        numbers = recv_ref[date * az_count, 0:16, wide - LANES :].astype(jnp.float32)[0:1, LANES - META :]
        line_offset, line_index, column_index = (numbers[:, s : s + 1] for s in range(META))
        line_taps = banded(picked_taps(table, line_index), line_distance - line_offset)
        line_taps = jnp.concatenate(halves(line_taps), axis=0)
        column_high, column_low = halves(banded(picked_taps(table, column_index), column_distance))
        moved = []
        for plane in range(2):
            rows_of = slice(plane * own_lines, (plane + 1) * own_lines)
            source = jnp.concatenate([recv_ref[date * az_count + a, rows_of, :] for a in range(az_count)], axis=0)
            both = dot(line_taps, source)
            moved.append(both[:lines] + both[lines:])
        moved_high, moved_low = halves(jnp.concatenate(moved, axis=0))
        for begin in range(0, held, LANES):
            end = min(begin + span, wide)
            taken = end - begin
            total = dot(moved_high[:, begin:end], column_high[:taken])
            total += dot(moved_low[:, begin:end], column_high[:taken])
            total += dot(moved_high[:, begin:end], column_low[:taken])
            resampled_ref[date, :, begin : begin + LANES] = total.astype(jnp.bfloat16)

    window = lowpass_ref[...]
    spacing = lax.broadcasted_iota(jnp.int32, window.shape, 1).astype(jnp.float32) - FILTER_HALF
    span = min(2 * LANES, held)

    def one_pair(place, own, other):
        gap = shift_ref[own] - shift_ref[other]
        angle = jnp.where(jnp.abs(spacing) <= FILTER_HALF, jnp.pi * gap * spacing, 0.0)
        for part, taps in enumerate((window * jnp.cos(angle), window * jnp.sin(angle))):
            spread = jnp.broadcast_to(taps, (LANES, 2 * LANES))
            spread = pltpu.roll(spread, 0, 1, stride=1, stride_axis=0)
            high, low = halves(spread)
            weight_ref[0, part * LANES : (part + 1) * LANES, :] = high
            weight_ref[1, part * LANES : (part + 1) * LANES, :] = low
        both = jnp.concatenate([resampled_ref[own], resampled_ref[other]], axis=0)
        for begin in range(0, up(chunk, LANES), LANES):
            end = min(begin + span, held)
            taken = end - begin
            total = dot_nt(both[:, begin:end], weight_ref[0, :, :taken])
            total += dot_nt(both[:, begin:end], weight_ref[1, :, :taken])
            cos, sin = total[:, :LANES], total[:, LANES:]
            re, im = slice(0, lines), slice(lines, 2 * lines)
            master_re = cos[re] + sin[im]
            master_im = cos[im] - sin[re]
            re, im = slice(2 * lines, 3 * lines), slice(3 * lines, 4 * lines)
            partner_re = cos[re] - sin[im]
            partner_im = cos[im] + sin[re]
            for part, product in enumerate(
                (
                    master_re * partner_re + master_im * partner_im,
                    master_im * partner_re - master_re * partner_im,
                )
            ):
                summed = sum(product[k * groups : (k + 1) * groups] for k in range(LOOK_AZ))
                product_ref[place, part, :, begin : begin + LANES] = summed

    if isinstance(pairs, int):
        count = pairs

        def step(place, carry):
            one_pair(place, table_of_pairs[place, 0], table_of_pairs[place, 1])
            return carry

        lax.fori_loop(0, count, step, 0)
    else:
        count = len(pairs)
        for place, (own, other) in enumerate(pairs):
            one_pair(place, own, other)

    out_width = out_ref.shape[2]
    column = lax.broadcasted_iota(jnp.int32, (product_ref.shape[3], out_width), 0)
    lane = lax.broadcasted_iota(jnp.int32, (product_ref.shape[3], out_width), 1)
    collect = jnp.where(column // LOOK_RG == lane % looks, 1.0, 0.0).astype(jnp.bfloat16)
    high, low = halves(product_ref[...].reshape(count * 2 * groups, product_ref.shape[3]))
    total = (dot(high, collect) + dot(low, collect)) * (1.0 / (LOOK_AZ * LOOK_RG))
    total = total.reshape(count, 2, groups, out_width)
    own_lane = lax.broadcasted_iota(jnp.int32, (groups, out_width), 1) // looks
    place = 0
    for own in range(dates):
        value = jnp.zeros((groups, out_width), jnp.float32)
        for lag in range(min(LAGS, dates - 1 - own)):
            for part in range(2):
                value = jnp.where(own_lane == lag * 2 + part, total[place, part], value)
            place += 1
        out_ref[own * az_count : (own + 1) * az_count] = value.reshape(az_count, groups // az_count, out_width)


def unpack_kernel(used_lags, looks, recv_ref, out_ref):
    sources, groups, width = recv_ref.shape
    columns = out_ref.shape[-1]
    lane = lax.broadcasted_iota(jnp.int32, (groups, columns), 1) // looks
    out_ref[...] = jnp.zeros_like(out_ref)
    for lag in range(used_lags):
        for part in range(2):
            value = jnp.zeros((groups, columns), jnp.float32)
            for source in range(sources):
                block = recv_ref[source]
                if width != columns:
                    block = block[:, :columns]
                shift = looks * (source - lag * 2 - part) % columns
                if shift:
                    block = pltpu.roll(block, shift, 1)
                value = jnp.where(lane == source, block, value)
            out_ref[part, lag] = value


def chunked_body(slc, offsets, kernel_index, range_shift):
    axes = ("date", "az")
    date_count, az_count, rng_count = (lax.axis_size(a) for a in ("date", "az", "rng"))
    peers = date_count * az_count
    lines, columns = slc.shape[2], slc.shape[3]
    dates = range_shift.shape[0]
    chunk = columns // peers
    looks = chunk // LOOK_RG
    groups = lines * az_count // LOOK_AZ
    wide = up(chunk + 2 * FILTER_HALF + TAPS - 1 + META, LANES)
    held = up(chunk + 2 * FILTER_HALF, LANES)
    used_lags = min(LAGS, dates - 1)
    out_width = up(used_lags * 2 * looks, LANES)
    vmem = pl.BlockSpec(memory_space=pltpu.VMEM)
    smem = pl.BlockSpec(memory_space=pltpu.SMEM)
    limit = pltpu.CompilerParams(vmem_limit_bytes=32 * 1024 * 1024)

    cells = slc.reshape(2 * lines, columns)
    place = lax.axis_index("rng")
    if rng_count == 2:
        edge = jnp.where(place == 0, cells[:, columns - LANES :], cells[:, :LANES])
        before = after = lax.ppermute(edge, "rng", [(0, 1), (1, 0)])
    else:
        forth = [(i, i + 1) for i in range(rng_count - 1)]
        before = lax.ppermute(cells[:, columns - LANES :], "rng", forth)
        after = lax.ppermute(cells[:, :LANES], "rng", [(b, a) for a, b in forth])

    packed = pl.pallas_call(
        functools.partial(pack_kernel, chunk),
        out_shape=jax.ShapeDtypeStruct((peers, 2 * lines, wide), jnp.bfloat16),
        in_specs=[smem] * 3 + [vmem] * 3,
        out_specs=vmem,
        scratch_shapes=[pltpu.VMEM((2 * lines, columns + 2 * LANES), jnp.bfloat16)],
        compiler_params=limit,
    )(jnp.stack([place, rng_count]).astype(jnp.int32), offsets, kernel_index, cells, before, after)
    arrived = lax.all_to_all(packed, axes, 0, 0, tiled=True)

    pairs = [(own, own + lag) for own in range(dates) for lag in range(1, LAGS + 1) if own + lag < dates]
    count = len(pairs)
    first = [jnp.asarray(np.array(pairs, np.int32))] if count > UNROLLED_PAIRS else []
    looked = pl.pallas_call(
        functools.partial(pairs_kernel, chunk, count if first else pairs),
        out_shape=jax.ShapeDtypeStruct((peers, groups // az_count, out_width), jnp.float32),
        in_specs=[smem] * len(first) + [smem] + [vmem] * 3,
        out_specs=vmem,
        scratch_shapes=[
            pltpu.VMEM((dates, 4 * (groups * LOOK_AZ) // 2, held), jnp.bfloat16),
            pltpu.VMEM((2, 2 * LANES, 2 * LANES), jnp.bfloat16),
            pltpu.VMEM((count, 2, groups, up(chunk, LANES)), jnp.float32),
        ],
        compiler_params=limit,
    )(*first, range_shift, jnp.asarray(kernel_table()), jnp.asarray(lowpass_row(2 * LANES)), arrived)
    returned = lax.all_to_all(looked, axes, 0, 0, tiled=True)

    out = pl.pallas_call(
        functools.partial(unpack_kernel, used_lags, looks),
        out_shape=jax.ShapeDtypeStruct((2, LAGS, groups // az_count, looks * peers), jnp.float32),
        in_specs=[vmem],
        out_specs=vmem,
        compiler_params=limit,
    )(returned)
    return out[:, None]


HALO_LINES = 16
FOLD = 16
TAIL = 2 * FILTER_HALF


def slots(count):
    if count == 2:
        return [[(0, 1), (1, 0)]]
    return [[(i, i + 1) for i in range(count - 1)], [(i + 1, i) for i in range(count - 1)]]


def edge_kernel(slc_ref, *refs):
    outs, semaphores = refs[:-1], refs[-1]
    lines, columns = slc_ref.shape[1:]
    row = pl.multiple_of((1 - lax.axis_index("az")) * (lines - HALO_LINES), HALO_LINES)
    if len(outs) == 3:
        starts = [pl.multiple_of((1 - lax.axis_index("rng")) * (columns - LANES), LANES)]
    else:
        starts = [columns - LANES, 0]
    wanted = [slc_ref.at[:, pl.ds(row, HALO_LINES), :]]
    wanted += [slc_ref.at[:, :, pl.ds(start, LANES)] for start in starts]
    wanted += [slc_ref.at[:, pl.ds(row, HALO_LINES), pl.ds(start, LANES)] for start in starts]
    copies = [pltpu.make_async_copy(w, o, semaphores.at[i]) for i, (w, o) in enumerate(zip(wanted, outs))]
    for copy in copies:
        copy.start()
    for copy in copies:
        copy.wait()


def sinc(value):
    angle = jnp.pi * value
    return jnp.where(angle == 0.0, 1.0, jnp.sin(angle) / jnp.where(angle == 0.0, 1.0, angle))


def tap_row(index):
    lane = lax.broadcasted_iota(jnp.int32, (1, LANES), 1)
    position = lane.astype(jnp.float32) - 3.0 - index.astype(jnp.float32) / KERNELS
    shaped = sinc(position) * (0.5 + 0.5 * jnp.cos(jnp.pi * position / 5.0))
    shaped = jnp.where(lane < TAPS, shaped, 0.0)
    return shaped / jnp.sum(shaped, axis=1, keepdims=True)


def taps_kernel(offsets_hbm, index_hbm, slc_ref, line_ref, column_ref, held_ref, offsets_ref, index_ref, semaphores):
    copy = pltpu.make_async_copy(slc_ref, held_ref, semaphores.at[0])
    numbers = [
        pltpu.make_async_copy(offsets_hbm, offsets_ref, semaphores.at[1]),
        pltpu.make_async_copy(index_hbm, index_ref, semaphores.at[2]),
    ]
    for each in numbers:
        each.start()
    copy.start()
    for each in numbers:
        each.wait()
    lines = slc_ref.shape[1]
    groups = lines // LOOK_AZ
    shape = (lines, lines + HALO_LINES)
    row = lax.broadcasted_iota(jnp.int32, shape, 0)
    place = lax.broadcasted_iota(jnp.int32, shape, 1)
    beyond = jnp.where(lax.axis_index("az") == 0, 0, -lines - HALO_LINES)
    source = jnp.where(place < lines, place, place + beyond)
    line = LOOK_AZ * (row % groups) + row // groups
    taps = banded(tap_row(index_ref[0, 0]), source - line - offsets_ref[0, 0] + 3)
    line_ref[...] = jnp.concatenate(halves(taps), axis=0)
    shape = (3 * LANES, LANES)
    distance = lax.broadcasted_iota(jnp.int32, shape, 0) - lax.broadcasted_iota(jnp.int32, shape, 1)
    distance = distance - (LANES - FILTER_HALF - 3) - offsets_ref[0, 1]
    taps = banded(tap_row(index_ref[0, 1]), distance)
    column_ref[...] = jnp.concatenate(halves(taps), axis=1)
    copy.wait()


def resample_kernel(last_block, left_ref, right_ref, left_corner, right_corner, lines_ref, slc_ref, line_ref, column_ref, *outs):
    outs, tiles_ref, tails_ref = outs[:-2], outs[-2], outs[-1]
    lines = slc_ref.shape[1]
    block = lax.axis_index("rng")
    moved = []
    for plane in range(2):
        own = jnp.concatenate([left_ref[plane], slc_ref[plane], right_ref[plane]], axis=1)
        halo = jnp.concatenate([left_corner[plane], lines_ref[plane], right_corner[plane]], axis=1)
        both = dot(line_ref[...], jnp.concatenate([own, halo], axis=0))
        moved.append(both[:lines] + both[lines:])
    moved = jnp.concatenate(moved, axis=0)
    width = moved.shape[1]
    left = jnp.where(block > 0, moved[:, :LANES], 0.0)
    right = jnp.where(block < last_block, moved[:, width - LANES :], 0.0)
    moved = jnp.concatenate([left, moved[:, LANES : width - LANES], right, jnp.zeros_like(right)], axis=1)
    high, low = halves(moved)
    starts = range(0, width - LANES, LANES)
    high = jnp.concatenate([high[:, s : s + 3 * LANES] for s in starts], axis=0)
    low = jnp.concatenate([low[:, s : s + 3 * LANES] for s in starts], axis=0)
    total = dot(high, column_ref[...])
    total = total[:, :LANES] + total[:, LANES:] + dot(low, column_ref[:, :LANES])
    rows = 2 * lines
    tiles_ref[...] = total.astype(jnp.bfloat16)
    chunk_rows = outs[0].shape[0] - FOLD
    lane = lax.broadcasted_iota(jnp.int32, (FOLD, LANES), 1) // TAIL
    for chunk in range(len(outs)):
        begin = (chunk + 1) * chunk_rows
        folded = total[begin : begin + FOLD]
        for part in range(1, rows // FOLD):
            value = pltpu.roll(total[begin + part * FOLD : begin + (part + 1) * FOLD], part * TAIL, 1)
            folded = jnp.where(lane == part, value, folded)
        tails_ref[chunk] = folded.astype(jnp.bfloat16)
    date = lax.axis_index("date")
    for step, out_ref in enumerate(outs):
        chunk = date ^ step
        out_ref[:chunk_rows] = tiles_ref[pl.ds(pl.multiple_of(chunk * chunk_rows, FOLD), chunk_rows), :]
        out_ref[chunk_rows:] = tails_ref[chunk]


def filter_kernel(pairs, shift_hbm, out_ref, shift_ref, semaphore):
    copy = pltpu.make_async_copy(shift_hbm, shift_ref, semaphore)
    copy.start()
    date = lax.axis_index("date")
    spacing = lax.broadcasted_iota(jnp.int32, (1, 2 * LANES), 1).astype(jnp.float32) - FILTER_HALF
    window = 0.4 * sinc(0.4 * spacing) * (0.54 + 0.46 * jnp.cos(jnp.pi * spacing / (FILTER_HALF + 1)))
    window = jnp.where(jnp.abs(spacing) <= FILTER_HALF, window, 0.0)
    copy.wait()
    for place, (first, second) in enumerate(pairs):
        gap = shift_ref[date ^ first] - shift_ref[date ^ second]
        angle = jnp.where(jnp.abs(spacing) <= FILTER_HALF, jnp.pi * gap * spacing, 0.0)
        for part, taps in enumerate((window * jnp.cos(angle), window * jnp.sin(angle))):
            spread = jnp.broadcast_to(taps, (LANES, 2 * LANES))
            spread = pltpu.roll(spread, 0, 1, stride=1, stride_axis=0)
            high, low = halves(spread)
            out_ref[place, 0, part * LANES : (part + 1) * LANES, :] = high
            out_ref[place, 1, part * LANES : (part + 1) * LANES, :] = low


def looks_kernel(pairs, dates, weight_ref, *refs):
    chunks, outs, window_ref, product_ref = refs[:dates][::-1], refs[dates : 2 * dates], refs[-2], refs[-1]
    groups, lines = outs[0].shape[0], outs[0].shape[0] * LOOK_AZ
    rows = 2 * lines
    blocks = (chunks[0].shape[0] - FOLD) // rows
    looks = blocks * LANES // LOOK_RG
    date = lax.axis_index("date")
    for step, chunk_ref in enumerate(chunks):
        window_ref[step, :, :LANES] = chunk_ref[: blocks * rows]
        window_ref[step, : (blocks - 1) * rows, LANES:] = chunk_ref[rows : blocks * rows]
        folded = chunk_ref[blocks * rows :].astype(jnp.float32)
        for part in range(rows // FOLD):
            value = pltpu.roll(folded, LANES - part * TAIL, 1) if part else folded
            at = pl.ds((blocks - 1) * rows + part * FOLD, FOLD)
            window_ref[step, at, LANES:] = value.astype(jnp.bfloat16)
    for place, (first, second) in enumerate(pairs):
        def filtered(step):
            total = dot_nt(window_ref[step], weight_ref[place, 0]) + dot_nt(window_ref[step], weight_ref[place, 1])
            total = total.reshape(blocks, 2, lines, 2 * LANES)
            return total[:, 0, :, :LANES], total[:, 1, :, :LANES], total[:, 0, :, LANES:], total[:, 1, :, LANES:]

        cos_re, cos_im, sin_re, sin_im = filtered(first)
        master_re, master_im = cos_re + sin_im, cos_im - sin_re
        cos_re, cos_im, sin_re, sin_im = filtered(second)
        partner_re, partner_im = cos_re - sin_im, cos_im + sin_re
        for part, product in enumerate(
            (
                master_re * partner_re + master_im * partner_im,
                master_im * partner_re - master_re * partner_im,
            )
        ):
            summed = sum(product[:, k * groups : (k + 1) * groups] for k in range(LOOK_AZ))
            at = pl.ds((place * 2 + part) * groups, groups)
            for k in range(blocks):
                product_ref[at, k * LANES : (k + 1) * LANES] = summed[k]

    out_width = outs[0].shape[1]
    column = lax.broadcasted_iota(jnp.int32, (product_ref.shape[1], out_width), 0)
    lane = lax.broadcasted_iota(jnp.int32, (product_ref.shape[1], out_width), 1)
    collect = jnp.where(column // LOOK_RG == lane % looks, 1.0, 0.0).astype(jnp.bfloat16)
    high, low = halves(product_ref[...])
    total = (dot(high, collect) + dot(low, collect)) * (1.0 / (LOOK_AZ * LOOK_RG))
    total = total.reshape(len(pairs), 2, groups, out_width)
    own_lane = lax.broadcasted_iota(jnp.int32, (groups, out_width), 1) // looks
    for step, out_ref in enumerate(outs):
        value = jnp.zeros((groups, out_width), jnp.float32)
        for place, pair in enumerate(pairs):
            if step in pair:
                other = pair[1] if pair[0] == step else pair[0]
                lag = (date ^ other) - (date ^ step)
                for part in range(2):
                    signed = -total[place, part] if part == 1 and pair[1] == step else total[place, part]
                    value = jnp.where(own_lane == (lag - 1) * 2 + part, signed, value)
        out_ref[...] = value


def place_kernel(used_lags, looks, *refs):
    out_ref = refs[-1]
    groups, columns = out_ref.shape[2:]
    date = lax.axis_index("date")
    lane = lax.broadcasted_iota(jnp.int32, (groups, LANES), 1) // looks
    out_ref[...] = jnp.zeros_like(out_ref)
    each = LANES // looks
    for step, recv_ref in enumerate(refs[:-1][::-1]):
        chunk = date ^ step
        for lag in range(used_lags):
            for part in range(2):
                tile, group = divmod(lag * 2 + part, each)
                block = recv_ref[:, tile * LANES : (tile + 1) * LANES]
                block = pltpu.roll(block, lax.bitwise_and(looks * (chunk - group), LANES - 1), 1)
                out_ref[part, lag] = jnp.where(lane == chunk, block, out_ref[part, lag])


def tiled_body(slc, offsets, kernel_index, range_shift):
    dates, rng_count = (lax.axis_size(a) for a in ("date", "rng"))
    lines, columns = slc.shape[2], slc.shape[3]
    chunk = columns // dates
    looks = chunk // LOOK_RG
    groups = lines // LOOK_AZ
    out_width = up(min(LAGS, dates - 1) * 2 * looks, LANES)
    vmem = pl.BlockSpec(memory_space=pltpu.VMEM)
    hbm = pl.BlockSpec(memory_space=pltpu.HBM)
    limit = pltpu.CompilerParams(vmem_limit_bytes=32 * 1024 * 1024)
    bf16 = jnp.bfloat16
    cells, offsets, kernel_index, range_shift = (
        pltpu.with_memory_space_constraint(value, pltpu.HBM)
        for value in (slc.reshape(2, lines, columns), offsets, kernel_index, range_shift)
    )

    moves = slots(rng_count)
    shapes = [(2, HALO_LINES, columns)] + [(2, lines, LANES)] * len(moves) + [(2, HALO_LINES, LANES)] * len(moves)
    edges = pl.pallas_call(
        edge_kernel,
        out_shape=[jax.ShapeDtypeStruct(s, bf16) for s in shapes],
        in_specs=[hbm],
        out_specs=[vmem] * len(shapes),
        scratch_shapes=[pltpu.SemaphoreType.DMA((len(shapes),))],
        compiler_params=limit,
    )(cells)
    swap = [(0, 1), (1, 0)]
    sides = [lax.ppermute(edges[1 + i], "rng", move) for i, move in enumerate(moves)]
    corners = [
        lax.ppermute(edges[1 + len(moves) + i], ("rng", "az"), [(2 * a + c, 2 * b + d) for a, b in move for c, d in swap])
        for i, move in enumerate(moves)
    ]
    halo_lines = lax.ppermute(edges[0], "az", swap)

    line_taps, column_taps, held = pl.pallas_call(
        taps_kernel,
        out_shape=[
            jax.ShapeDtypeStruct((2 * lines, lines + HALO_LINES), bf16),
            jax.ShapeDtypeStruct((3 * LANES, 2 * LANES), bf16),
            jax.ShapeDtypeStruct(cells.shape, bf16),
        ],
        in_specs=[hbm] * 3,
        out_specs=[vmem] * 3,
        scratch_shapes=[
            pltpu.SMEM(offsets.shape, jnp.int32),
            pltpu.SMEM(kernel_index.shape, jnp.int32),
            pltpu.SemaphoreType.DMA((3,)),
        ],
        compiler_params=limit,
    )(offsets, kernel_index, cells)

    chunk_rows = chunk // LANES * 2 * lines
    sent = pl.pallas_call(
        functools.partial(resample_kernel, rng_count - 1),
        out_shape=[jax.ShapeDtypeStruct((chunk_rows + FOLD, LANES), bf16)] * dates,
        in_specs=[vmem] * 8,
        out_specs=[vmem] * dates,
        scratch_shapes=[
            pltpu.VMEM(((columns // LANES + 1) * 2 * lines, LANES), bf16),
            pltpu.VMEM((dates, FOLD, LANES), bf16),
        ],
        compiler_params=limit,
    )(sides[0], sides[-1], corners[0], corners[-1], halo_lines, held, line_taps, column_taps)

    def exchanged(values):
        arrived = {0: values[0]}
        for step in range(dates - 1, 0, -1):
            arrived[step] = lax.ppermute(values[step], "date", [(i, i ^ step) for i in range(dates)])
        return [arrived[step] for step in reversed(range(dates))]

    chunks = exchanged(sent)
    pairs = [(first, second) for first in range(dates) for second in range(first + 1, dates)]
    weights = pl.pallas_call(
        functools.partial(filter_kernel, pairs),
        out_shape=jax.ShapeDtypeStruct((len(pairs), 2, 2 * LANES, 2 * LANES), bf16),
        in_specs=[hbm],
        out_specs=vmem,
        scratch_shapes=[pltpu.SMEM(range_shift.shape, jnp.float32), pltpu.SemaphoreType.DMA],
        compiler_params=limit,
    )(range_shift)
    looked = pl.pallas_call(
        functools.partial(looks_kernel, pairs, dates),
        out_shape=[jax.ShapeDtypeStruct((groups, out_width), jnp.float32)] * dates,
        in_specs=[vmem] * (1 + dates),
        out_specs=[vmem] * dates,
        scratch_shapes=[
            pltpu.VMEM((dates, chunk_rows, 2 * LANES), bf16),
            pltpu.VMEM((len(pairs) * 2 * groups, chunk), jnp.float32),
        ],
        compiler_params=limit,
    )(weights, *chunks)
    out = pl.pallas_call(
        functools.partial(place_kernel, min(LAGS, dates - 1), looks),
        out_shape=jax.ShapeDtypeStruct((2, LAGS, groups, looks * dates), jnp.float32),
        in_specs=[vmem] * dates,
        out_specs=vmem,
        compiler_params=limit,
    )(*exchanged(looked))
    return out[:, None]


def body(slc, offsets, kernel_index, range_shift):
    dates, az_count = (lax.axis_size(a) for a in ("date", "az"))
    lines, columns = slc.shape[2], slc.shape[3]
    whole_tiles = columns % (dates * LANES) == 0 and columns % (dates * LOOK_RG) == 0
    one_row = columns // LOOK_RG == LANES and range_shift.shape[0] == dates
    few = dates & (dates - 1) == 0 and dates - 1 <= LAGS
    folds = lines % (2 * HALO_LINES) == 0 and 2 * lines // FOLD * TAIL <= LANES
    if az_count == 2 and whole_tiles and one_row and few and folds:
        return tiled_body(slc, offsets, kernel_index, range_shift)
    return chunked_body(slc, offsets, kernel_index, range_shift)


def solution(mesh):
    return jax.shard_map(
        body,
        mesh=mesh,
        in_specs=(
            P(None, ("groups", "date"), "az", "rng"),
            P(("groups", "date"), None),
            P(("groups", "date"), None),
            P("groups"),
        ),
        out_specs=P(None, ("groups", "date"), None, "az", "rng"),
        check_vma=False,
    )
```

```python
import functools

import jax
import jax.numpy as jnp
import numpy as np
from jax import lax
from jax.experimental import pallas as pl
from jax.experimental.pallas import tpu as pltpu
from jax.sharding import PartitionSpec as P

LAGS = 8
KERNELS = 16
TAPS = 8
FILTER_HALF = 8
FILTER_TAPS = 2 * FILTER_HALF + 1
LOOK_AZ = 4
LOOK_RG = 20
LANES = 128
META = 3
UNROLLED_PAIRS = 12


def up(value, unit):
    return -(-value // unit) * unit


def kernel_table():
    position = np.arange(TAPS) - 3.0 - np.arange(KERNELS)[:, None] / KERNELS
    shaped = np.sinc(position) * (0.5 + 0.5 * np.cos(np.pi * position / 5.0))
    table = np.zeros((KERNELS, LANES), np.float32)
    table[:, :TAPS] = shaped / shaped.sum(1, keepdims=True)
    return table


def lowpass_row(width):
    t = np.arange(FILTER_TAPS) - FILTER_HALF
    row = np.zeros((1, width), np.float32)
    row[0, :FILTER_TAPS] = 0.4 * np.sinc(0.4 * t) * (0.54 + 0.46 * np.cos(np.pi * t / (FILTER_HALF + 1)))
    return row


def halves(value):
    high = value.astype(jnp.bfloat16)
    return high, (value - high.astype(jnp.float32)).astype(jnp.bfloat16)


def dot(a, b):
    return jnp.dot(a, b, preferred_element_type=jnp.float32)


def dot_nt(a, b):
    return lax.dot_general(a, b, (((1,), (1,)), ((), ())), preferred_element_type=jnp.float32)


def pack_kernel(chunk, place_ref, offsets_ref, index_ref, slc_ref, before_ref, after_ref, out_ref, wide_ref):
    columns = slc_ref.shape[1]
    wide = out_ref.shape[2]
    first = place_ref[0] == 0
    last = place_ref[0] == place_ref[1] - 1
    zero = jnp.zeros_like(before_ref[...])
    wide_ref[:, :LANES] = jnp.where(first, zero, before_ref[...])
    wide_ref[:, LANES : LANES + columns] = slc_ref[...]
    wide_ref[:, LANES + columns :] = jnp.where(last, zero, after_ref[...])
    lane = lax.broadcasted_iota(jnp.int32, (slc_ref.shape[0], wide), 1)
    numbers = [offsets_ref[0, 0], index_ref[0, 0], index_ref[0, 1]]
    for j in range(out_ref.shape[0]):
        start = LANES + chunk * j - FILTER_HALF - 3 + offsets_ref[0, 1]
        tile = lax.shift_right_logical(start, 7)
        within = lax.bitwise_and(start, LANES - 1)
        window = wide_ref[:, pl.ds(pl.multiple_of(tile * LANES, LANES), wide + LANES)].astype(jnp.float32)
        moved = pltpu.roll(window, wide + LANES - within, 1)[:, :wide]
        for slot, number in enumerate(numbers):
            moved = jnp.where(lane == wide - META + slot, number.astype(jnp.float32), moved)
        out_ref[j] = moved.astype(jnp.bfloat16)


def picked_taps(table, index):
    row = lax.broadcasted_iota(jnp.int32, table.shape, 0).astype(jnp.float32)
    return jnp.sum(jnp.where(row == index, table, 0.0), axis=0, keepdims=True)


def banded(taps, distance):
    out = jnp.zeros(distance.shape, jnp.float32)
    for q in range(TAPS):
        out = jnp.where(distance == q, taps[:, q : q + 1], out)
    return out


def pairs_kernel(chunk, pairs, *refs):
    if isinstance(pairs, int):
        table_of_pairs, refs = refs[0], refs[1:]
    shift_ref, table_ref, lowpass_ref, recv_ref, out_ref, resampled_ref, weight_ref, product_ref = refs
    sources, rows, wide = recv_ref.shape
    dates = shift_ref.shape[0]
    az_count = sources // dates
    own_lines = rows // 2
    lines = own_lines * az_count
    groups = lines // LOOK_AZ
    looks = chunk // LOOK_RG
    table = table_ref[...]
    held = resampled_ref.shape[2]

    out_row = lax.broadcasted_iota(jnp.int32, (lines, lines), 0)
    in_row = lax.broadcasted_iota(jnp.int32, (lines, lines), 1)
    line = LOOK_AZ * (out_row % groups) + out_row // groups
    line_distance = (in_row - line + 3).astype(jnp.float32)
    span = min(2 * LANES, wide)
    column_distance = (
        lax.broadcasted_iota(jnp.int32, (span, LANES), 0) - lax.broadcasted_iota(jnp.int32, (span, LANES), 1)
    ).astype(jnp.float32)
    for date in range(dates):
        numbers = recv_ref[date * az_count, 0:16, wide - LANES :].astype(jnp.float32)[0:1, LANES - META :]
        line_offset, line_index, column_index = (numbers[:, s : s + 1] for s in range(META))
        line_taps = banded(picked_taps(table, line_index), line_distance - line_offset)
        line_taps = jnp.concatenate(halves(line_taps), axis=0)
        column_high, column_low = halves(banded(picked_taps(table, column_index), column_distance))
        moved = []
        for plane in range(2):
            rows_of = slice(plane * own_lines, (plane + 1) * own_lines)
            source = jnp.concatenate([recv_ref[date * az_count + a, rows_of, :] for a in range(az_count)], axis=0)
            both = dot(line_taps, source)
            moved.append(both[:lines] + both[lines:])
        moved_high, moved_low = halves(jnp.concatenate(moved, axis=0))
        for begin in range(0, held, LANES):
            end = min(begin + span, wide)
            taken = end - begin
            total = dot(moved_high[:, begin:end], column_high[:taken])
            total += dot(moved_low[:, begin:end], column_high[:taken])
            total += dot(moved_high[:, begin:end], column_low[:taken])
            resampled_ref[date, :, begin : begin + LANES] = total.astype(jnp.bfloat16)

    window = lowpass_ref[...]
    spacing = lax.broadcasted_iota(jnp.int32, window.shape, 1).astype(jnp.float32) - FILTER_HALF
    span = min(2 * LANES, held)

    def one_pair(place, own, other):
        gap = shift_ref[own] - shift_ref[other]
        angle = jnp.where(jnp.abs(spacing) <= FILTER_HALF, jnp.pi * gap * spacing, 0.0)
        for part, taps in enumerate((window * jnp.cos(angle), window * jnp.sin(angle))):
            spread = jnp.broadcast_to(taps, (LANES, 2 * LANES))
            spread = pltpu.roll(spread, 0, 1, stride=1, stride_axis=0)
            high, low = halves(spread)
            weight_ref[0, part * LANES : (part + 1) * LANES, :] = high
            weight_ref[1, part * LANES : (part + 1) * LANES, :] = low
        both = jnp.concatenate([resampled_ref[own], resampled_ref[other]], axis=0)
        for begin in range(0, up(chunk, LANES), LANES):
            end = min(begin + span, held)
            taken = end - begin
            total = dot_nt(both[:, begin:end], weight_ref[0, :, :taken])
            total += dot_nt(both[:, begin:end], weight_ref[1, :, :taken])
            cos, sin = total[:, :LANES], total[:, LANES:]
            re, im = slice(0, lines), slice(lines, 2 * lines)
            master_re = cos[re] + sin[im]
            master_im = cos[im] - sin[re]
            re, im = slice(2 * lines, 3 * lines), slice(3 * lines, 4 * lines)
            partner_re = cos[re] - sin[im]
            partner_im = cos[im] + sin[re]
            for part, product in enumerate(
                (
                    master_re * partner_re + master_im * partner_im,
                    master_im * partner_re - master_re * partner_im,
                )
            ):
                summed = sum(product[k * groups : (k + 1) * groups] for k in range(LOOK_AZ))
                product_ref[place, part, :, begin : begin + LANES] = summed

    if isinstance(pairs, int):
        count = pairs

        def step(place, carry):
            one_pair(place, table_of_pairs[place, 0], table_of_pairs[place, 1])
            return carry

        lax.fori_loop(0, count, step, 0)
    else:
        count = len(pairs)
        for place, (own, other) in enumerate(pairs):
            one_pair(place, own, other)

    out_width = out_ref.shape[2]
    column = lax.broadcasted_iota(jnp.int32, (product_ref.shape[3], out_width), 0)
    lane = lax.broadcasted_iota(jnp.int32, (product_ref.shape[3], out_width), 1)
    collect = jnp.where(column // LOOK_RG == lane % looks, 1.0, 0.0).astype(jnp.bfloat16)
    high, low = halves(product_ref[...].reshape(count * 2 * groups, product_ref.shape[3]))
    total = (dot(high, collect) + dot(low, collect)) * (1.0 / (LOOK_AZ * LOOK_RG))
    total = total.reshape(count, 2, groups, out_width)
    own_lane = lax.broadcasted_iota(jnp.int32, (groups, out_width), 1) // looks
    place = 0
    for own in range(dates):
        value = jnp.zeros((groups, out_width), jnp.float32)
        for lag in range(min(LAGS, dates - 1 - own)):
            for part in range(2):
                value = jnp.where(own_lane == lag * 2 + part, total[place, part], value)
            place += 1
        out_ref[own * az_count : (own + 1) * az_count] = value.reshape(az_count, groups // az_count, out_width)


def unpack_kernel(used_lags, looks, recv_ref, out_ref):
    sources, groups, width = recv_ref.shape
    columns = out_ref.shape[-1]
    lane = lax.broadcasted_iota(jnp.int32, (groups, columns), 1) // looks
    out_ref[...] = jnp.zeros_like(out_ref)
    for lag in range(used_lags):
        for part in range(2):
            value = jnp.zeros((groups, columns), jnp.float32)
            for source in range(sources):
                block = recv_ref[source]
                if width != columns:
                    block = block[:, :columns]
                shift = looks * (source - lag * 2 - part) % columns
                if shift:
                    block = pltpu.roll(block, shift, 1)
                value = jnp.where(lane == source, block, value)
            out_ref[part, lag] = value


def chunked_body(slc, offsets, kernel_index, range_shift):
    axes = ("date", "az")
    date_count, az_count, rng_count = (lax.axis_size(a) for a in ("date", "az", "rng"))
    peers = date_count * az_count
    lines, columns = slc.shape[2], slc.shape[3]
    dates = range_shift.shape[0]
    chunk = columns // peers
    looks = chunk // LOOK_RG
    groups = lines * az_count // LOOK_AZ
    wide = up(chunk + 2 * FILTER_HALF + TAPS - 1 + META, LANES)
    held = up(chunk + 2 * FILTER_HALF, LANES)
    used_lags = min(LAGS, dates - 1)
    out_width = up(used_lags * 2 * looks, LANES)
    vmem = pl.BlockSpec(memory_space=pltpu.VMEM)
    smem = pl.BlockSpec(memory_space=pltpu.SMEM)
    limit = pltpu.CompilerParams(vmem_limit_bytes=32 * 1024 * 1024)

    cells = slc.reshape(2 * lines, columns)
    place = lax.axis_index("rng")
    if rng_count == 2:
        edge = jnp.where(place == 0, cells[:, columns - LANES :], cells[:, :LANES])
        before = after = lax.ppermute(edge, "rng", [(0, 1), (1, 0)])
    else:
        forth = [(i, i + 1) for i in range(rng_count - 1)]
        before = lax.ppermute(cells[:, columns - LANES :], "rng", forth)
        after = lax.ppermute(cells[:, :LANES], "rng", [(b, a) for a, b in forth])

    packed = pl.pallas_call(
        functools.partial(pack_kernel, chunk),
        out_shape=jax.ShapeDtypeStruct((peers, 2 * lines, wide), jnp.bfloat16),
        in_specs=[smem] * 3 + [vmem] * 3,
        out_specs=vmem,
        scratch_shapes=[pltpu.VMEM((2 * lines, columns + 2 * LANES), jnp.bfloat16)],
        compiler_params=limit,
    )(jnp.stack([place, rng_count]).astype(jnp.int32), offsets, kernel_index, cells, before, after)
    arrived = lax.all_to_all(packed, axes, 0, 0, tiled=True)

    pairs = [(own, own + lag) for own in range(dates) for lag in range(1, LAGS + 1) if own + lag < dates]
    count = len(pairs)
    first = [jnp.asarray(np.array(pairs, np.int32))] if count > UNROLLED_PAIRS else []
    looked = pl.pallas_call(
        functools.partial(pairs_kernel, chunk, count if first else pairs),
        out_shape=jax.ShapeDtypeStruct((peers, groups // az_count, out_width), jnp.float32),
        in_specs=[smem] * len(first) + [smem] + [vmem] * 3,
        out_specs=vmem,
        scratch_shapes=[
            pltpu.VMEM((dates, 4 * (groups * LOOK_AZ) // 2, held), jnp.bfloat16),
            pltpu.VMEM((2, 2 * LANES, 2 * LANES), jnp.bfloat16),
            pltpu.VMEM((count, 2, groups, up(chunk, LANES)), jnp.float32),
        ],
        compiler_params=limit,
    )(*first, range_shift, jnp.asarray(kernel_table()), jnp.asarray(lowpass_row(2 * LANES)), arrived)
    returned = lax.all_to_all(looked, axes, 0, 0, tiled=True)

    out = pl.pallas_call(
        functools.partial(unpack_kernel, used_lags, looks),
        out_shape=jax.ShapeDtypeStruct((2, LAGS, groups // az_count, looks * peers), jnp.float32),
        in_specs=[vmem],
        out_specs=vmem,
        compiler_params=limit,
    )(returned)
    return out[:, None]


HALO_LINES = 16
FOLD = 16
TAIL = 2 * FILTER_HALF


def slots(count):
    if count == 2:
        return [[(0, 1), (1, 0)]]
    return [[(i, i + 1) for i in range(count - 1)], [(i + 1, i) for i in range(count - 1)]]


def edge_kernel(slc_ref, *refs):
    outs, semaphores = refs[:-1], refs[-1]
    lines, columns = slc_ref.shape[1:]
    row = pl.multiple_of((1 - lax.axis_index("az")) * (lines - HALO_LINES), HALO_LINES)
    if len(outs) == 3:
        starts = [pl.multiple_of((1 - lax.axis_index("rng")) * (columns - LANES), LANES)]
    else:
        starts = [columns - LANES, 0]
    wanted = [slc_ref.at[:, pl.ds(row, HALO_LINES), :]]
    wanted += [slc_ref.at[:, :, pl.ds(start, LANES)] for start in starts]
    wanted += [slc_ref.at[:, pl.ds(row, HALO_LINES), pl.ds(start, LANES)] for start in starts]
    copies = [pltpu.make_async_copy(w, o, semaphores.at[i]) for i, (w, o) in enumerate(zip(wanted, outs))]
    for copy in copies:
        copy.start()
    for copy in copies:
        copy.wait()


def sinc(value):
    angle = jnp.pi * value
    return jnp.where(angle == 0.0, 1.0, jnp.sin(angle) / jnp.where(angle == 0.0, 1.0, angle))


def tap_row(index):
    lane = lax.broadcasted_iota(jnp.int32, (1, LANES), 1)
    position = lane.astype(jnp.float32) - 3.0 - index.astype(jnp.float32) / KERNELS
    shaped = sinc(position) * (0.5 + 0.5 * jnp.cos(jnp.pi * position / 5.0))
    shaped = jnp.where(lane < TAPS, shaped, 0.0)
    return shaped / jnp.sum(shaped, axis=1, keepdims=True)


def taps_kernel(offsets_hbm, index_hbm, slc_ref, line_ref, column_ref, held_ref, offsets_ref, index_ref, semaphores):
    copy = pltpu.make_async_copy(slc_ref, held_ref, semaphores.at[0])
    numbers = [
        pltpu.make_async_copy(offsets_hbm, offsets_ref, semaphores.at[1]),
        pltpu.make_async_copy(index_hbm, index_ref, semaphores.at[2]),
    ]
    for each in numbers:
        each.start()
    copy.start()
    for each in numbers:
        each.wait()
    lines = slc_ref.shape[1]
    groups = lines // LOOK_AZ
    shape = (lines, lines + HALO_LINES)
    row = lax.broadcasted_iota(jnp.int32, shape, 0)
    place = lax.broadcasted_iota(jnp.int32, shape, 1)
    beyond = jnp.where(lax.axis_index("az") == 0, 0, -lines - HALO_LINES)
    source = jnp.where(place < lines, place, place + beyond)
    line = LOOK_AZ * (row % groups) + row // groups
    taps = banded(tap_row(index_ref[0, 0]), source - line - offsets_ref[0, 0] + 3)
    line_ref[...] = jnp.concatenate(halves(taps), axis=0)
    shape = (2 * LANES, LANES)
    distance = lax.broadcasted_iota(jnp.int32, shape, 0) - lax.broadcasted_iota(jnp.int32, shape, 1)
    taps = banded(tap_row(index_ref[0, 1]), distance)
    column_ref[...] = jnp.concatenate(halves(taps), axis=1)
    copy.wait()


def resample_kernel(last_block, offsets_hbm, left_ref, right_ref, left_corner, right_corner, lines_ref, slc_ref, line_ref, column_ref, *outs):
    outs, (tiles_ref, tails_ref, moved_ref, offsets_ref, semaphore) = outs[:-5], outs[-5:]
    copy = pltpu.make_async_copy(offsets_hbm, offsets_ref, semaphore)
    copy.start()
    lines, columns = slc_ref.shape[1:]
    block = lax.axis_index("rng")
    width = columns + 2 * LANES
    for plane in range(2):
        own = jnp.concatenate([left_ref[plane], slc_ref[plane], right_ref[plane]], axis=1)
        halo = jnp.concatenate([left_corner[plane], lines_ref[plane], right_corner[plane]], axis=1)
        both = dot(line_ref[...], jnp.concatenate([own, halo], axis=0))
        both = both[:lines] + both[lines:]
        at = slice(plane * lines, (plane + 1) * lines)
        moved_ref[at, :LANES] = jnp.where(block > 0, both[:, :LANES], 0.0)
        moved_ref[at, LANES : width - LANES] = both[:, LANES : width - LANES]
        moved_ref[at, width - LANES : width] = jnp.where(block < last_block, both[:, width - LANES :], 0.0)
        moved_ref[at, width:] = jnp.zeros((lines, 2 * LANES), jnp.float32)
    copy.wait()
    start = LANES - FILTER_HALF - 3 + offsets_ref[0, 1]
    within = lax.bitwise_and(start, LANES - 1)
    first = lax.shift_right_logical(start, 7) * LANES
    lane = lax.broadcasted_iota(jnp.int32, (2 * lines, LANES), 1)
    turned = [
        pltpu.roll(moved_ref[:, pl.ds(pl.multiple_of(first + begin, LANES), LANES)], LANES - within, 1)
        for begin in range(0, width + LANES, LANES)
    ]
    kept = lane < LANES - within
    tiles = [halves(jnp.where(kept, a, b)) for a, b in zip(turned, turned[1:])]
    high = jnp.concatenate([jnp.concatenate([a[0], b[0]], axis=1) for a, b in zip(tiles, tiles[1:])], axis=0)
    low = jnp.concatenate([jnp.concatenate([a[1], b[1]], axis=1) for a, b in zip(tiles, tiles[1:])], axis=0)
    total = dot(high, column_ref[...])
    total = total[:, :LANES] + total[:, LANES:] + dot(low, column_ref[:, :LANES])
    rows = 2 * lines
    tiles_ref[...] = total.astype(jnp.bfloat16)
    chunk_rows = outs[0].shape[0] - FOLD
    lane = lax.broadcasted_iota(jnp.int32, (FOLD, LANES), 1) // TAIL
    for chunk in range(len(outs)):
        begin = (chunk + 1) * chunk_rows
        folded = total[begin : begin + FOLD]
        for part in range(1, rows // FOLD):
            value = pltpu.roll(total[begin + part * FOLD : begin + (part + 1) * FOLD], part * TAIL, 1)
            folded = jnp.where(lane == part, value, folded)
        tails_ref[chunk] = folded.astype(jnp.bfloat16)
    date = lax.axis_index("date")
    for step, out_ref in enumerate(outs):
        chunk = date ^ step
        out_ref[:chunk_rows] = tiles_ref[pl.ds(pl.multiple_of(chunk * chunk_rows, FOLD), chunk_rows), :]
        out_ref[chunk_rows:] = tails_ref[chunk]


def filter_kernel(pairs, shift_hbm, out_ref, shift_ref, semaphore):
    copy = pltpu.make_async_copy(shift_hbm, shift_ref, semaphore)
    copy.start()
    date = lax.axis_index("date")
    spacing = lax.broadcasted_iota(jnp.int32, (1, 2 * LANES), 1).astype(jnp.float32) - FILTER_HALF
    window = 0.4 * sinc(0.4 * spacing) * (0.54 + 0.46 * jnp.cos(jnp.pi * spacing / (FILTER_HALF + 1)))
    window = jnp.where(jnp.abs(spacing) <= FILTER_HALF, window, 0.0)
    copy.wait()
    for place, (first, second) in enumerate(pairs):
        gap = shift_ref[date ^ first] - shift_ref[date ^ second]
        angle = jnp.where(jnp.abs(spacing) <= FILTER_HALF, jnp.pi * gap * spacing, 0.0)
        for part, taps in enumerate((window * jnp.cos(angle), window * jnp.sin(angle))):
            spread = jnp.broadcast_to(taps, (LANES, 2 * LANES))
            spread = pltpu.roll(spread, 0, 1, stride=1, stride_axis=0)
            high, low = halves(spread)
            out_ref[place, 0, part * LANES : (part + 1) * LANES, :] = high
            out_ref[place, 1, part * LANES : (part + 1) * LANES, :] = low


def looks_kernel(pairs, dates, weight_ref, *refs):
    chunks, outs, window_ref, product_ref = refs[:dates][::-1], refs[dates : 2 * dates], refs[-2], refs[-1]
    groups, lines = outs[0].shape[0], outs[0].shape[0] * LOOK_AZ
    rows = 2 * lines
    blocks = (chunks[0].shape[0] - FOLD) // rows
    looks = blocks * LANES // LOOK_RG
    date = lax.axis_index("date")
    for step, chunk_ref in enumerate(chunks):
        window_ref[step, :, :LANES] = chunk_ref[: blocks * rows]
        window_ref[step, : (blocks - 1) * rows, LANES:] = chunk_ref[rows : blocks * rows]
        folded = chunk_ref[blocks * rows :].astype(jnp.float32)
        for part in range(rows // FOLD):
            value = pltpu.roll(folded, LANES - part * TAIL, 1) if part else folded
            at = pl.ds((blocks - 1) * rows + part * FOLD, FOLD)
            window_ref[step, at, LANES:] = value.astype(jnp.bfloat16)
    for place, (first, second) in enumerate(pairs):
        def filtered(step):
            total = dot_nt(window_ref[step], weight_ref[place, 0]) + dot_nt(window_ref[step], weight_ref[place, 1])
            total = total.reshape(blocks, 2, lines, 2 * LANES)
            return total[:, 0, :, :LANES], total[:, 1, :, :LANES], total[:, 0, :, LANES:], total[:, 1, :, LANES:]

        cos_re, cos_im, sin_re, sin_im = filtered(first)
        master_re, master_im = cos_re + sin_im, cos_im - sin_re
        cos_re, cos_im, sin_re, sin_im = filtered(second)
        partner_re, partner_im = cos_re - sin_im, cos_im + sin_re
        for part, product in enumerate(
            (
                master_re * partner_re + master_im * partner_im,
                master_im * partner_re - master_re * partner_im,
            )
        ):
            summed = sum(product[:, k * groups : (k + 1) * groups] for k in range(LOOK_AZ))
            at = pl.ds((place * 2 + part) * groups, groups)
            for k in range(blocks):
                product_ref[at, k * LANES : (k + 1) * LANES] = summed[k]

    out_width = outs[0].shape[1]
    column = lax.broadcasted_iota(jnp.int32, (product_ref.shape[1], out_width), 0)
    lane = lax.broadcasted_iota(jnp.int32, (product_ref.shape[1], out_width), 1)
    collect = jnp.where(column // LOOK_RG == lane % looks, 1.0, 0.0).astype(jnp.bfloat16)
    high, low = halves(product_ref[...])
    total = (dot(high, collect) + dot(low, collect)) * (1.0 / (LOOK_AZ * LOOK_RG))
    total = total.reshape(len(pairs), 2, groups, out_width)
    own_lane = lax.broadcasted_iota(jnp.int32, (groups, out_width), 1) // looks
    for step, out_ref in enumerate(outs):
        value = jnp.zeros((groups, out_width), jnp.float32)
        for place, pair in enumerate(pairs):
            if step in pair:
                other = pair[1] if pair[0] == step else pair[0]
                lag = (date ^ other) - (date ^ step)
                for part in range(2):
                    signed = -total[place, part] if part == 1 and pair[1] == step else total[place, part]
                    value = jnp.where(own_lane == (lag - 1) * 2 + part, signed, value)
        out_ref[...] = value


def place_kernel(used_lags, looks, *refs):
    out_ref = refs[-1]
    groups, columns = out_ref.shape[2:]
    date = lax.axis_index("date")
    lane = lax.broadcasted_iota(jnp.int32, (groups, LANES), 1) // looks
    out_ref[...] = jnp.zeros_like(out_ref)
    each = LANES // looks
    for step, recv_ref in enumerate(refs[:-1][::-1]):
        chunk = date ^ step
        for lag in range(used_lags):
            for part in range(2):
                tile, group = divmod(lag * 2 + part, each)
                block = recv_ref[:, tile * LANES : (tile + 1) * LANES]
                block = pltpu.roll(block, lax.bitwise_and(looks * (chunk - group), LANES - 1), 1)
                out_ref[part, lag] = jnp.where(lane == chunk, block, out_ref[part, lag])


def tiled_body(slc, offsets, kernel_index, range_shift):
    dates, rng_count = (lax.axis_size(a) for a in ("date", "rng"))
    lines, columns = slc.shape[2], slc.shape[3]
    chunk = columns // dates
    looks = chunk // LOOK_RG
    groups = lines // LOOK_AZ
    out_width = up(min(LAGS, dates - 1) * 2 * looks, LANES)
    vmem = pl.BlockSpec(memory_space=pltpu.VMEM)
    hbm = pl.BlockSpec(memory_space=pltpu.HBM)
    limit = pltpu.CompilerParams(vmem_limit_bytes=32 * 1024 * 1024)
    bf16 = jnp.bfloat16
    cells, offsets, kernel_index, range_shift = (
        pltpu.with_memory_space_constraint(value, pltpu.HBM)
        for value in (slc.reshape(2, lines, columns), offsets, kernel_index, range_shift)
    )

    moves = slots(rng_count)
    shapes = [(2, HALO_LINES, columns)] + [(2, lines, LANES)] * len(moves) + [(2, HALO_LINES, LANES)] * len(moves)
    edges = pl.pallas_call(
        edge_kernel,
        out_shape=[jax.ShapeDtypeStruct(s, bf16) for s in shapes],
        in_specs=[hbm],
        out_specs=[vmem] * len(shapes),
        scratch_shapes=[pltpu.SemaphoreType.DMA((len(shapes),))],
        compiler_params=limit,
    )(cells)
    swap = [(0, 1), (1, 0)]
    sides = [lax.ppermute(edges[1 + i], "rng", move) for i, move in enumerate(moves)]
    corners = [
        lax.ppermute(edges[1 + len(moves) + i], ("rng", "az"), [(2 * a + c, 2 * b + d) for a, b in move for c, d in swap])
        for i, move in enumerate(moves)
    ]
    halo_lines = lax.ppermute(edges[0], "az", swap)

    line_taps, column_taps, held = pl.pallas_call(
        taps_kernel,
        out_shape=[
            jax.ShapeDtypeStruct((2 * lines, lines + HALO_LINES), bf16),
            jax.ShapeDtypeStruct((2 * LANES, 2 * LANES), bf16),
            jax.ShapeDtypeStruct(cells.shape, bf16),
        ],
        in_specs=[hbm] * 3,
        out_specs=[vmem] * 3,
        scratch_shapes=[
            pltpu.SMEM(offsets.shape, jnp.int32),
            pltpu.SMEM(kernel_index.shape, jnp.int32),
            pltpu.SemaphoreType.DMA((3,)),
        ],
        compiler_params=limit,
    )(offsets, kernel_index, cells)

    chunk_rows = chunk // LANES * 2 * lines
    sent = pl.pallas_call(
        functools.partial(resample_kernel, rng_count - 1),
        out_shape=[jax.ShapeDtypeStruct((chunk_rows + FOLD, LANES), bf16)] * dates,
        in_specs=[hbm] + [vmem] * 8,
        out_specs=[vmem] * dates,
        scratch_shapes=[
            pltpu.VMEM(((columns // LANES + 1) * 2 * lines, LANES), bf16),
            pltpu.VMEM((dates, FOLD, LANES), bf16),
            pltpu.VMEM((2 * lines, columns + 4 * LANES), jnp.float32),
            pltpu.SMEM(offsets.shape, jnp.int32),
            pltpu.SemaphoreType.DMA,
        ],
        compiler_params=limit,
    )(offsets, sides[0], sides[-1], corners[0], corners[-1], halo_lines, held, line_taps, column_taps)

    def exchanged(values, targets=dates):
        arrived = {0: values[0]}
        for step in range(dates - 1, 0, -1):
            moves = [(i, i ^ step) for i in range(dates) if i ^ step < targets]
            arrived[step] = lax.ppermute(values[step], "date", moves)
        return [arrived[step] for step in reversed(range(dates))]

    chunks = exchanged(sent)
    pairs = [(first, second) for first in range(dates) for second in range(first + 1, dates)]
    weights = pl.pallas_call(
        functools.partial(filter_kernel, pairs),
        out_shape=jax.ShapeDtypeStruct((len(pairs), 2, 2 * LANES, 2 * LANES), bf16),
        in_specs=[hbm],
        out_specs=vmem,
        scratch_shapes=[pltpu.SMEM(range_shift.shape, jnp.float32), pltpu.SemaphoreType.DMA],
        compiler_params=limit,
    )(range_shift)
    looked = pl.pallas_call(
        functools.partial(looks_kernel, pairs, dates),
        out_shape=[jax.ShapeDtypeStruct((groups, out_width), jnp.float32)] * dates,
        in_specs=[vmem] * (1 + dates),
        out_specs=[vmem] * dates,
        scratch_shapes=[
            pltpu.VMEM((dates, chunk_rows, 2 * LANES), bf16),
            pltpu.VMEM((len(pairs) * 2 * groups, chunk), jnp.float32),
        ],
        compiler_params=limit,
    )(weights, *chunks)
    out = pl.pallas_call(
        functools.partial(place_kernel, min(LAGS, dates - 1), looks),
        out_shape=jax.ShapeDtypeStruct((2, LAGS, groups, looks * dates), jnp.float32),
        in_specs=[vmem] * dates,
        out_specs=vmem,
        compiler_params=limit,
    )(*exchanged(looked, dates - 1))
    return out[:, None]


def body(slc, offsets, kernel_index, range_shift):
    dates, az_count = (lax.axis_size(a) for a in ("date", "az"))
    lines, columns = slc.shape[2], slc.shape[3]
    whole_tiles = columns % (dates * LANES) == 0 and columns % (dates * LOOK_RG) == 0
    one_row = columns // LOOK_RG == LANES and range_shift.shape[0] == dates
    few = dates & (dates - 1) == 0 and dates - 1 <= LAGS
    folds = lines % (2 * HALO_LINES) == 0 and 2 * lines // FOLD * TAIL <= LANES
    if az_count == 2 and whole_tiles and one_row and few and folds:
        return tiled_body(slc, offsets, kernel_index, range_shift)
    return chunked_body(slc, offsets, kernel_index, range_shift)


def solution(mesh):
    return jax.shard_map(
        body,
        mesh=mesh,
        in_specs=(
            P(None, ("groups", "date"), "az", "rng"),
            P(("groups", "date"), None),
            P(("groups", "date"), None),
            P("groups"),
        ),
        out_specs=P(None, ("groups", "date"), None, "az", "rng"),
        check_vma=False,
    )
```

```python
import functools

import jax
import jax.numpy as jnp
import numpy as np
from jax import lax
from jax.experimental import pallas as pl
from jax.experimental.pallas import tpu as pltpu
from jax.sharding import PartitionSpec as P

LAGS = 8
KERNELS = 16
TAPS = 8
FILTER_HALF = 8
FILTER_TAPS = 2 * FILTER_HALF + 1
LOOK_AZ = 4
LOOK_RG = 20
LANES = 128
META = 3
UNROLLED_PAIRS = 12


def up(value, unit):
    return -(-value // unit) * unit


def kernel_table():
    position = np.arange(TAPS) - 3.0 - np.arange(KERNELS)[:, None] / KERNELS
    shaped = np.sinc(position) * (0.5 + 0.5 * np.cos(np.pi * position / 5.0))
    table = np.zeros((KERNELS, LANES), np.float32)
    table[:, :TAPS] = shaped / shaped.sum(1, keepdims=True)
    return table


def lowpass_row(width):
    t = np.arange(FILTER_TAPS) - FILTER_HALF
    row = np.zeros((1, width), np.float32)
    row[0, :FILTER_TAPS] = 0.4 * np.sinc(0.4 * t) * (0.54 + 0.46 * np.cos(np.pi * t / (FILTER_HALF + 1)))
    return row


def halves(value):
    high = value.astype(jnp.bfloat16)
    return high, (value - high.astype(jnp.float32)).astype(jnp.bfloat16)


def dot(a, b):
    return jnp.dot(a, b, preferred_element_type=jnp.float32)


def dot_nt(a, b):
    return lax.dot_general(a, b, (((1,), (1,)), ((), ())), preferred_element_type=jnp.float32)


def pack_kernel(chunk, place_ref, offsets_ref, index_ref, slc_ref, before_ref, after_ref, out_ref, wide_ref):
    columns = slc_ref.shape[1]
    wide = out_ref.shape[2]
    first = place_ref[0] == 0
    last = place_ref[0] == place_ref[1] - 1
    zero = jnp.zeros_like(before_ref[...])
    wide_ref[:, :LANES] = jnp.where(first, zero, before_ref[...])
    wide_ref[:, LANES : LANES + columns] = slc_ref[...]
    wide_ref[:, LANES + columns :] = jnp.where(last, zero, after_ref[...])
    lane = lax.broadcasted_iota(jnp.int32, (slc_ref.shape[0], wide), 1)
    numbers = [offsets_ref[0, 0], index_ref[0, 0], index_ref[0, 1]]
    for j in range(out_ref.shape[0]):
        start = LANES + chunk * j - FILTER_HALF - 3 + offsets_ref[0, 1]
        tile = lax.shift_right_logical(start, 7)
        within = lax.bitwise_and(start, LANES - 1)
        window = wide_ref[:, pl.ds(pl.multiple_of(tile * LANES, LANES), wide + LANES)].astype(jnp.float32)
        moved = pltpu.roll(window, wide + LANES - within, 1)[:, :wide]
        for slot, number in enumerate(numbers):
            moved = jnp.where(lane == wide - META + slot, number.astype(jnp.float32), moved)
        out_ref[j] = moved.astype(jnp.bfloat16)


def picked_taps(table, index):
    row = lax.broadcasted_iota(jnp.int32, table.shape, 0).astype(jnp.float32)
    return jnp.sum(jnp.where(row == index, table, 0.0), axis=0, keepdims=True)


def banded(taps, distance):
    out = jnp.zeros(distance.shape, jnp.float32)
    for q in range(TAPS):
        out = jnp.where(distance == q, taps[:, q : q + 1], out)
    return out


def pairs_kernel(chunk, pairs, *refs):
    if isinstance(pairs, int):
        table_of_pairs, refs = refs[0], refs[1:]
    shift_ref, table_ref, lowpass_ref, recv_ref, out_ref, resampled_ref, weight_ref, product_ref = refs
    sources, rows, wide = recv_ref.shape
    dates = shift_ref.shape[0]
    az_count = sources // dates
    own_lines = rows // 2
    lines = own_lines * az_count
    groups = lines // LOOK_AZ
    looks = chunk // LOOK_RG
    table = table_ref[...]
    held = resampled_ref.shape[2]

    out_row = lax.broadcasted_iota(jnp.int32, (lines, lines), 0)
    in_row = lax.broadcasted_iota(jnp.int32, (lines, lines), 1)
    line = LOOK_AZ * (out_row % groups) + out_row // groups
    line_distance = (in_row - line + 3).astype(jnp.float32)
    span = min(2 * LANES, wide)
    column_distance = (
        lax.broadcasted_iota(jnp.int32, (span, LANES), 0) - lax.broadcasted_iota(jnp.int32, (span, LANES), 1)
    ).astype(jnp.float32)
    for date in range(dates):
        numbers = recv_ref[date * az_count, 0:16, wide - LANES :].astype(jnp.float32)[0:1, LANES - META :]
        line_offset, line_index, column_index = (numbers[:, s : s + 1] for s in range(META))
        line_taps = banded(picked_taps(table, line_index), line_distance - line_offset)
        line_taps = jnp.concatenate(halves(line_taps), axis=0)
        column_high, column_low = halves(banded(picked_taps(table, column_index), column_distance))
        moved = []
        for plane in range(2):
            rows_of = slice(plane * own_lines, (plane + 1) * own_lines)
            source = jnp.concatenate([recv_ref[date * az_count + a, rows_of, :] for a in range(az_count)], axis=0)
            both = dot(line_taps, source)
            moved.append(both[:lines] + both[lines:])
        moved_high, moved_low = halves(jnp.concatenate(moved, axis=0))
        for begin in range(0, held, LANES):
            end = min(begin + span, wide)
            taken = end - begin
            total = dot(moved_high[:, begin:end], column_high[:taken])
            total += dot(moved_low[:, begin:end], column_high[:taken])
            total += dot(moved_high[:, begin:end], column_low[:taken])
            resampled_ref[date, :, begin : begin + LANES] = total.astype(jnp.bfloat16)

    window = lowpass_ref[...]
    spacing = lax.broadcasted_iota(jnp.int32, window.shape, 1).astype(jnp.float32) - FILTER_HALF
    span = min(2 * LANES, held)

    def one_pair(place, own, other):
        gap = shift_ref[own] - shift_ref[other]
        angle = jnp.where(jnp.abs(spacing) <= FILTER_HALF, jnp.pi * gap * spacing, 0.0)
        for part, taps in enumerate((window * jnp.cos(angle), window * jnp.sin(angle))):
            spread = jnp.broadcast_to(taps, (LANES, 2 * LANES))
            spread = pltpu.roll(spread, 0, 1, stride=1, stride_axis=0)
            high, low = halves(spread)
            weight_ref[0, part * LANES : (part + 1) * LANES, :] = high
            weight_ref[1, part * LANES : (part + 1) * LANES, :] = low
        both = jnp.concatenate([resampled_ref[own], resampled_ref[other]], axis=0)
        for begin in range(0, up(chunk, LANES), LANES):
            end = min(begin + span, held)
            taken = end - begin
            total = dot_nt(both[:, begin:end], weight_ref[0, :, :taken])
            total += dot_nt(both[:, begin:end], weight_ref[1, :, :taken])
            cos, sin = total[:, :LANES], total[:, LANES:]
            re, im = slice(0, lines), slice(lines, 2 * lines)
            master_re = cos[re] + sin[im]
            master_im = cos[im] - sin[re]
            re, im = slice(2 * lines, 3 * lines), slice(3 * lines, 4 * lines)
            partner_re = cos[re] - sin[im]
            partner_im = cos[im] + sin[re]
            for part, product in enumerate(
                (
                    master_re * partner_re + master_im * partner_im,
                    master_im * partner_re - master_re * partner_im,
                )
            ):
                summed = sum(product[k * groups : (k + 1) * groups] for k in range(LOOK_AZ))
                product_ref[place, part, :, begin : begin + LANES] = summed

    if isinstance(pairs, int):
        count = pairs

        def step(place, carry):
            one_pair(place, table_of_pairs[place, 0], table_of_pairs[place, 1])
            return carry

        lax.fori_loop(0, count, step, 0)
    else:
        count = len(pairs)
        for place, (own, other) in enumerate(pairs):
            one_pair(place, own, other)

    out_width = out_ref.shape[2]
    column = lax.broadcasted_iota(jnp.int32, (product_ref.shape[3], out_width), 0)
    lane = lax.broadcasted_iota(jnp.int32, (product_ref.shape[3], out_width), 1)
    collect = jnp.where(column // LOOK_RG == lane % looks, 1.0, 0.0).astype(jnp.bfloat16)
    high, low = halves(product_ref[...].reshape(count * 2 * groups, product_ref.shape[3]))
    total = (dot(high, collect) + dot(low, collect)) * (1.0 / (LOOK_AZ * LOOK_RG))
    total = total.reshape(count, 2, groups, out_width)
    own_lane = lax.broadcasted_iota(jnp.int32, (groups, out_width), 1) // looks
    place = 0
    for own in range(dates):
        value = jnp.zeros((groups, out_width), jnp.float32)
        for lag in range(min(LAGS, dates - 1 - own)):
            for part in range(2):
                value = jnp.where(own_lane == lag * 2 + part, total[place, part], value)
            place += 1
        out_ref[own * az_count : (own + 1) * az_count] = value.reshape(az_count, groups // az_count, out_width)


def unpack_kernel(used_lags, looks, recv_ref, out_ref):
    sources, groups, width = recv_ref.shape
    columns = out_ref.shape[-1]
    lane = lax.broadcasted_iota(jnp.int32, (groups, columns), 1) // looks
    out_ref[...] = jnp.zeros_like(out_ref)
    for lag in range(used_lags):
        for part in range(2):
            value = jnp.zeros((groups, columns), jnp.float32)
            for source in range(sources):
                block = recv_ref[source]
                if width != columns:
                    block = block[:, :columns]
                shift = looks * (source - lag * 2 - part) % columns
                if shift:
                    block = pltpu.roll(block, shift, 1)
                value = jnp.where(lane == source, block, value)
            out_ref[part, lag] = value


def chunked_body(slc, offsets, kernel_index, range_shift):
    axes = ("date", "az")
    date_count, az_count, rng_count = (lax.axis_size(a) for a in ("date", "az", "rng"))
    peers = date_count * az_count
    lines, columns = slc.shape[2], slc.shape[3]
    dates = range_shift.shape[0]
    chunk = columns // peers
    looks = chunk // LOOK_RG
    groups = lines * az_count // LOOK_AZ
    wide = up(chunk + 2 * FILTER_HALF + TAPS - 1 + META, LANES)
    held = up(chunk + 2 * FILTER_HALF, LANES)
    used_lags = min(LAGS, dates - 1)
    out_width = up(used_lags * 2 * looks, LANES)
    vmem = pl.BlockSpec(memory_space=pltpu.VMEM)
    smem = pl.BlockSpec(memory_space=pltpu.SMEM)
    limit = pltpu.CompilerParams(vmem_limit_bytes=32 * 1024 * 1024)

    cells = slc.reshape(2 * lines, columns)
    place = lax.axis_index("rng")
    if rng_count == 2:
        edge = jnp.where(place == 0, cells[:, columns - LANES :], cells[:, :LANES])
        before = after = lax.ppermute(edge, "rng", [(0, 1), (1, 0)])
    else:
        forth = [(i, i + 1) for i in range(rng_count - 1)]
        before = lax.ppermute(cells[:, columns - LANES :], "rng", forth)
        after = lax.ppermute(cells[:, :LANES], "rng", [(b, a) for a, b in forth])

    packed = pl.pallas_call(
        functools.partial(pack_kernel, chunk),
        out_shape=jax.ShapeDtypeStruct((peers, 2 * lines, wide), jnp.bfloat16),
        in_specs=[smem] * 3 + [vmem] * 3,
        out_specs=vmem,
        scratch_shapes=[pltpu.VMEM((2 * lines, columns + 2 * LANES), jnp.bfloat16)],
        compiler_params=limit,
    )(jnp.stack([place, rng_count]).astype(jnp.int32), offsets, kernel_index, cells, before, after)
    arrived = lax.all_to_all(packed, axes, 0, 0, tiled=True)

    pairs = [(own, own + lag) for own in range(dates) for lag in range(1, LAGS + 1) if own + lag < dates]
    count = len(pairs)
    first = [jnp.asarray(np.array(pairs, np.int32))] if count > UNROLLED_PAIRS else []
    looked = pl.pallas_call(
        functools.partial(pairs_kernel, chunk, count if first else pairs),
        out_shape=jax.ShapeDtypeStruct((peers, groups // az_count, out_width), jnp.float32),
        in_specs=[smem] * len(first) + [smem] + [vmem] * 3,
        out_specs=vmem,
        scratch_shapes=[
            pltpu.VMEM((dates, 4 * (groups * LOOK_AZ) // 2, held), jnp.bfloat16),
            pltpu.VMEM((2, 2 * LANES, 2 * LANES), jnp.bfloat16),
            pltpu.VMEM((count, 2, groups, up(chunk, LANES)), jnp.float32),
        ],
        compiler_params=limit,
    )(*first, range_shift, jnp.asarray(kernel_table()), jnp.asarray(lowpass_row(2 * LANES)), arrived)
    returned = lax.all_to_all(looked, axes, 0, 0, tiled=True)

    out = pl.pallas_call(
        functools.partial(unpack_kernel, used_lags, looks),
        out_shape=jax.ShapeDtypeStruct((2, LAGS, groups // az_count, looks * peers), jnp.float32),
        in_specs=[vmem],
        out_specs=vmem,
        compiler_params=limit,
    )(returned)
    return out[:, None]


HALO_LINES = 16
FOLD = 16
TAIL = 2 * FILTER_HALF


def sinc(value):
    angle = jnp.pi * value
    return jnp.where(angle == 0.0, 1.0, jnp.sin(angle) / jnp.where(angle == 0.0, 1.0, angle))


def tap_row(index):
    lane = lax.broadcasted_iota(jnp.int32, (1, LANES), 1)
    position = lane.astype(jnp.float32) - 3.0 - index.astype(jnp.float32) / KERNELS
    shaped = sinc(position) * (0.5 + 0.5 * jnp.cos(jnp.pi * position / 5.0))
    shaped = jnp.where(lane < TAPS, shaped, 0.0)
    return shaped / jnp.sum(shaped, axis=1, keepdims=True)


def row_line(row, az):
    quarter = HALO_LINES // LOOK_AZ
    within = row % HALO_LINES
    return HALO_LINES * ((row // HALO_LINES) ^ az) + LOOK_AZ * (within % quarter) + within // quarter


def prepare_kernel(offsets_hbm, index_hbm, slc_ref, side_ref, corner_ref, lines_ref, line_ref, column_ref, held_ref, offsets_ref, index_ref, semaphores):
    lines, columns = slc_ref.shape[1:]
    az = lax.axis_index("az")
    row = pl.multiple_of((1 - az) * (lines - HALO_LINES), HALO_LINES)
    edge = pl.multiple_of((1 - lax.axis_index("rng")) * (columns - LANES), LANES)
    nearest, outermost = pl.ds(row, HALO_LINES), pl.ds(edge, LANES)
    moves = [
        (offsets_hbm, offsets_ref),
        (index_hbm, index_ref),
        (slc_ref.at[:, :, outermost], side_ref),
        (slc_ref.at[:, nearest, outermost], corner_ref),
        (slc_ref.at[:, nearest, :], lines_ref),
        (slc_ref, held_ref.at[:, :, pl.ds(LANES, columns)]),
    ]
    copies = [pltpu.make_async_copy(a, b, semaphores.at[i]) for i, (a, b) in enumerate(moves)]
    for copy in copies:
        copy.start()
    held_ref[:, :, :LANES] = jnp.zeros((2, lines, LANES), held_ref.dtype)
    held_ref[:, :, LANES + columns :] = jnp.zeros((2, lines, 2 * LANES), held_ref.dtype)
    copies[0].wait()
    copies[1].wait()
    for half in range(2):
        shape = (HALO_LINES, lines + HALO_LINES)
        line = row_line(lax.broadcasted_iota(jnp.int32, shape, 0) + half * HALO_LINES, az)
        place = lax.broadcasted_iota(jnp.int32, shape, 1)
        source = jnp.where(place < lines, place, place + jnp.where(az == 0, 0, -lines - HALO_LINES))
        taps = banded(tap_row(index_ref[0, 0]), source - line - offsets_ref[0, 0] + 3)
        line_ref[half] = jnp.concatenate(halves(taps), axis=0)
    shape = (3 * LANES, LANES)
    distance = lax.broadcasted_iota(jnp.int32, shape, 0) - lax.broadcasted_iota(jnp.int32, shape, 1)
    distance = distance - (LANES - FILTER_HALF - 3) - offsets_ref[0, 1]
    taps = banded(tap_row(index_ref[0, 1]), distance)
    column_ref[...] = jnp.concatenate(halves(taps), axis=1)
    for copy in copies[2:]:
        copy.wait()


def along_range(moved, column_ref, tiles):
    high, low = halves(moved)
    starts = range(0, tiles * LANES, LANES)
    high = jnp.concatenate([high[:, s : s + 3 * LANES] for s in starts], axis=0)
    low = jnp.concatenate([low[:, s : s + 3 * LANES] for s in starts], axis=0)
    total = dot(high, column_ref[...])
    return total[:, :LANES] + total[:, LANES:] + dot(low, column_ref[:, :LANES])


def early_kernel(tiles, held_ref, line_ref, column_ref, out_ref):
    lines = held_ref.shape[1]
    early = out_ref.shape[0] // (2 * HALO_LINES)
    chunk = lax.axis_index("date") ^ (lax.axis_size("date") - 1)
    begin = pl.multiple_of((chunk * tiles + lax.axis_index("rng")) * LANES, LANES)
    moved = []
    for plane in range(2):
        both = dot(line_ref[0, :, :lines], held_ref[plane, :, pl.ds(begin, (early + 2) * LANES)])
        moved.append(both[:HALO_LINES] + both[HALO_LINES:])
    moved = jnp.concatenate(moved, axis=0)
    out_ref[...] = along_range(moved, column_ref, early).astype(jnp.bfloat16)


def resample_kernel(side_ref, corner_ref, lines_ref, held_ref, line_ref, column_ref, *outs):
    outs, tiles_ref, tails_ref = outs[:-2], outs[-2], outs[-1]
    lines, width = held_ref.shape[1:]
    width -= LANES
    block = lax.axis_index("rng")
    taps = jnp.concatenate([line_ref[0], line_ref[1]], axis=0)
    moved = [[], []]
    for plane in range(2):
        own = jnp.concatenate([side_ref[plane], held_ref[plane, :, LANES : width - LANES], side_ref[plane]], axis=1)
        halo = jnp.concatenate([corner_ref[plane], lines_ref[plane], corner_ref[plane]], axis=1)
        both = dot(taps, jnp.concatenate([own, halo], axis=0))
        for half in range(2):
            at = 2 * half * HALO_LINES
            moved[half].append(both[at : at + HALO_LINES] + both[at + HALO_LINES : at + 2 * HALO_LINES])
    moved = jnp.concatenate(moved[0] + moved[1], axis=0)
    left = jnp.where(block > 0, moved[:, :LANES], 0.0)
    right = jnp.where(block == 0, moved[:, width - LANES :], 0.0)
    moved = jnp.concatenate([left, moved[:, LANES : width - LANES], right, jnp.zeros_like(right)], axis=1)
    total = along_range(moved, column_ref, width // LANES - 1)
    rows = 2 * lines
    tiles_ref[...] = total.astype(jnp.bfloat16)
    chunk_rows = outs[0].shape[0] - FOLD
    lane = lax.broadcasted_iota(jnp.int32, (FOLD, LANES), 1) // TAIL
    for chunk in range(len(outs)):
        begin = (chunk + 1) * chunk_rows
        folded = total[begin : begin + FOLD]
        for part in range(1, rows // FOLD):
            value = pltpu.roll(total[begin + part * FOLD : begin + (part + 1) * FOLD], part * TAIL, 1)
            folded = jnp.where(lane == part, value, folded)
        tails_ref[chunk] = folded.astype(jnp.bfloat16)
    date = lax.axis_index("date")
    for step, out_ref in enumerate(outs[:-1]):
        chunk = date ^ step
        out_ref[:chunk_rows] = tiles_ref[pl.ds(pl.multiple_of(chunk * chunk_rows, FOLD), chunk_rows), :]
        out_ref[chunk_rows:] = tails_ref[chunk]
    out_ref = outs[-1]
    chunk = date ^ (len(outs) - 1)
    early = chunk_rows // rows - 1
    for tile in range(early):
        begin = pl.multiple_of(chunk * chunk_rows + (tile + block) * rows + lines, FOLD)
        out_ref[tile * lines : (tile + 1) * lines] = tiles_ref[pl.ds(begin, lines), :]
    begin = pl.multiple_of(chunk * chunk_rows + (1 - block) * early * rows, FOLD)
    out_ref[early * lines : early * lines + rows] = tiles_ref[pl.ds(begin, rows), :]
    out_ref[early * lines + rows :] = tails_ref[chunk]


def filter_kernel(pairs, shift_hbm, early_ref, out_ref, spread_ref, shift_ref, semaphore):
    copy = pltpu.make_async_copy(shift_hbm, shift_ref, semaphore)
    copy.start()
    lines = 2 * HALO_LINES
    spread_ref[...] = jnp.zeros_like(spread_ref)
    for tile in range(early_ref.shape[0] // lines):
        begin = pl.multiple_of((tile + lax.axis_index("rng")) * 2 * lines, FOLD)
        spread_ref[pl.ds(begin, lines), :] = early_ref[tile * lines : (tile + 1) * lines]
    date = lax.axis_index("date")
    spacing = lax.broadcasted_iota(jnp.int32, (1, 2 * LANES), 1).astype(jnp.float32) - FILTER_HALF
    window = 0.4 * sinc(0.4 * spacing) * (0.54 + 0.46 * jnp.cos(jnp.pi * spacing / (FILTER_HALF + 1)))
    window = jnp.where(jnp.abs(spacing) <= FILTER_HALF, window, 0.0)
    copy.wait()
    for place, (first, second) in enumerate(pairs):
        gap = shift_ref[date ^ first] - shift_ref[date ^ second]
        angle = jnp.where(jnp.abs(spacing) <= FILTER_HALF, jnp.pi * gap * spacing, 0.0)
        for part, taps in enumerate((window * jnp.cos(angle), window * jnp.sin(angle))):
            spread = jnp.broadcast_to(taps, (LANES, 2 * LANES))
            spread = pltpu.roll(spread, 0, 1, stride=1, stride_axis=0)
            high, low = halves(spread)
            out_ref[place, 0, part * LANES : (part + 1) * LANES, :] = high
            out_ref[place, 1, part * LANES : (part + 1) * LANES, :] = low


def looks_kernel(pairs, dates, weight_ref, *refs):
    early_ref, chunks, outs = refs[0], list(refs[1 : dates + 1][::-1]), refs[dates + 1 : 2 * dates + 1]
    whole_ref, window_ref, product_ref = refs[-3:]
    groups, lines = outs[0].shape[0], outs[0].shape[0] * LOOK_AZ
    rows = 2 * lines
    blocks = (chunks[0].shape[0] - FOLD) // rows
    looks = blocks * LANES // LOOK_RG
    date = lax.axis_index("date")
    block = lax.axis_index("rng")
    early = blocks - 1
    whole_ref[: blocks * rows] = early_ref[...]
    for tile in range(early):
        begin = pl.multiple_of((tile + block) * rows, FOLD)
        whole_ref[pl.ds(begin + lines, lines), :] = chunks[-1][tile * lines : (tile + 1) * lines]
    begin = pl.multiple_of((1 - block) * early * rows, FOLD)
    whole_ref[pl.ds(begin, rows), :] = chunks[-1][early * lines : early * lines + rows]
    whole_ref[blocks * rows :] = chunks[-1][early * lines + rows :]
    chunks[-1] = whole_ref
    az = lax.axis_index("az")
    upper = lax.broadcasted_iota(jnp.int32, (groups, LANES), 0) // (groups // 2) == az
    for step, chunk_ref in enumerate(chunks):
        window_ref[step, :, :LANES] = chunk_ref[: blocks * rows]
        window_ref[step, : (blocks - 1) * rows, LANES:] = chunk_ref[rows : blocks * rows]
        folded = chunk_ref[blocks * rows :].astype(jnp.float32)
        for part in range(rows // FOLD):
            value = pltpu.roll(folded, LANES - part * TAIL, 1) if part else folded
            at = pl.ds((blocks - 1) * rows + part * FOLD, FOLD)
            window_ref[step, at, LANES:] = value.astype(jnp.bfloat16)
    for place, (first, second) in enumerate(pairs):
        def filtered(step):
            total = dot_nt(window_ref[step], weight_ref[place, 0]) + dot_nt(window_ref[step], weight_ref[place, 1])
            total = total.reshape(blocks, 2, 2, HALO_LINES, 2 * LANES)
            re, im = total[:, :, 0], total[:, :, 1]
            return re[..., :LANES], im[..., :LANES], re[..., LANES:], im[..., LANES:]

        cos_re, cos_im, sin_re, sin_im = filtered(first)
        master_re, master_im = cos_re + sin_im, cos_im - sin_re
        cos_re, cos_im, sin_re, sin_im = filtered(second)
        partner_re, partner_im = cos_re - sin_im, cos_im + sin_re
        for part, product in enumerate(
            (
                master_re * partner_re + master_im * partner_im,
                master_im * partner_re - master_re * partner_im,
            )
        ):
            summed = product[:, :, :groups] + product[:, :, groups:]
            at = pl.ds((place * 2 + part) * groups, groups)
            for k in range(blocks):
                both = [summed[k, half] + pltpu.roll(summed[k, half], groups // 2, 0) for half in range(2)]
                product_ref[at, k * LANES : (k + 1) * LANES] = jnp.where(upper, both[0], both[1])

    out_width = outs[0].shape[1]
    column = lax.broadcasted_iota(jnp.int32, (product_ref.shape[1], out_width), 0)
    lane = lax.broadcasted_iota(jnp.int32, (product_ref.shape[1], out_width), 1)
    collect = jnp.where(column // LOOK_RG == lane % looks, 1.0, 0.0).astype(jnp.bfloat16)
    high, low = halves(product_ref[...])
    total = (dot(high, collect) + dot(low, collect)) * (1.0 / (LOOK_AZ * LOOK_RG))
    total = total.reshape(len(pairs), 2, groups, out_width)
    own_lane = lax.broadcasted_iota(jnp.int32, (groups, out_width), 1) // looks
    for step, out_ref in enumerate(outs):
        value = jnp.zeros((groups, out_width), jnp.float32)
        for place, pair in enumerate(pairs):
            if step in pair:
                other = pair[1] if pair[0] == step else pair[0]
                lag = (date ^ other) - (date ^ step)
                for part in range(2):
                    signed = -total[place, part] if part == 1 and pair[1] == step else total[place, part]
                    value = jnp.where(own_lane == (lag - 1) * 2 + part, signed, value)
        out_ref[...] = value


def place_kernel(used_lags, looks, *refs):
    out_ref = refs[-1]
    groups, columns = out_ref.shape[2:]
    date = lax.axis_index("date")
    lane = lax.broadcasted_iota(jnp.int32, (groups, LANES), 1) // looks
    out_ref[...] = jnp.zeros_like(out_ref)
    each = LANES // looks
    for step, recv_ref in enumerate(refs[:-1][::-1]):
        chunk = date ^ step
        for lag in range(used_lags):
            for part in range(2):
                tile, group = divmod(lag * 2 + part, each)
                block = recv_ref[:, tile * LANES : (tile + 1) * LANES]
                block = pltpu.roll(block, lax.bitwise_and(looks * (chunk - group), LANES - 1), 1)
                out_ref[part, lag] = jnp.where(lane == chunk, block, out_ref[part, lag])


def tiled_body(slc, offsets, kernel_index, range_shift):
    dates = lax.axis_size("date")
    lines, columns = slc.shape[2], slc.shape[3]
    chunk = columns // dates
    looks = chunk // LOOK_RG
    groups = lines // LOOK_AZ
    out_width = up(min(LAGS, dates - 1) * 2 * looks, LANES)
    vmem = pl.BlockSpec(memory_space=pltpu.VMEM)
    hbm = pl.BlockSpec(memory_space=pltpu.HBM)
    limit = pltpu.CompilerParams(vmem_limit_bytes=32 * 1024 * 1024)
    bf16 = jnp.bfloat16
    cells, offsets, kernel_index, range_shift = (
        pltpu.with_memory_space_constraint(value, pltpu.HBM)
        for value in (slc.reshape(2, lines, columns), offsets, kernel_index, range_shift)
    )
    tiles = chunk // LANES
    chunk_rows = tiles * 2 * lines

    side, corner, halo_lines, line_taps, column_taps, held = pl.pallas_call(
        prepare_kernel,
        out_shape=[
            jax.ShapeDtypeStruct((2, lines, LANES), bf16),
            jax.ShapeDtypeStruct((2, HALO_LINES, LANES), bf16),
            jax.ShapeDtypeStruct((2, HALO_LINES, columns), bf16),
            jax.ShapeDtypeStruct((2, 2 * HALO_LINES, lines + HALO_LINES), bf16),
            jax.ShapeDtypeStruct((3 * LANES, 2 * LANES), bf16),
            jax.ShapeDtypeStruct((2, lines, columns + 3 * LANES), bf16),
        ],
        in_specs=[hbm] * 3,
        out_specs=[vmem] * 6,
        scratch_shapes=[
            pltpu.SMEM(offsets.shape, jnp.int32),
            pltpu.SMEM(kernel_index.shape, jnp.int32),
            pltpu.SemaphoreType.DMA((6,)),
        ],
        compiler_params=limit,
    )(offsets, kernel_index, cells)
    swap = [(0, 1), (1, 0)]
    side = lax.ppermute(side, "rng", swap)
    corner = lax.ppermute(corner, ("rng", "az"), [(0, 3), (1, 2), (2, 1), (3, 0)])
    halo_lines = lax.ppermute(halo_lines, "az", swap)

    early_rows = (tiles - 1) * lines
    early = pl.pallas_call(
        functools.partial(early_kernel, tiles),
        out_shape=jax.ShapeDtypeStruct((early_rows, LANES), bf16),
        in_specs=[vmem] * 3,
        out_specs=vmem,
        compiler_params=limit,
    )(held, line_taps, column_taps)
    early = lax.ppermute(early, "date", [(i, i ^ (dates - 1)) for i in range(dates)])
    out_rows = [chunk_rows + FOLD] * (dates - 1) + [chunk_rows + FOLD - early_rows]
    sent = pl.pallas_call(
        resample_kernel,
        out_shape=[jax.ShapeDtypeStruct((rows, LANES), bf16) for rows in out_rows],
        in_specs=[vmem] * 6,
        out_specs=[vmem] * dates,
        scratch_shapes=[
            pltpu.VMEM(((columns // LANES + 1) * 2 * lines, LANES), bf16),
            pltpu.VMEM((dates, FOLD, LANES), bf16),
        ],
        compiler_params=limit,
    )(side, corner, halo_lines, held, line_taps, column_taps)

    def exchanged(values, order):
        arrived = {0: values[0]}
        for step in order:
            arrived[step] = lax.ppermute(values[step], "date", [(i, i ^ step) for i in range(dates)])
        return [arrived[step] for step in reversed(range(dates))]

    steps = range(dates - 1, 0, -1)

    chunks = exchanged(sent, steps)
    pairs = [(first, second) for first in range(dates) for second in range(first + 1, dates)]
    weights, early = pl.pallas_call(
        functools.partial(filter_kernel, pairs),
        out_shape=[
            jax.ShapeDtypeStruct((len(pairs), 2, 2 * LANES, 2 * LANES), bf16),
            jax.ShapeDtypeStruct((chunk_rows, LANES), bf16),
        ],
        in_specs=[hbm, vmem],
        out_specs=[vmem] * 2,
        scratch_shapes=[pltpu.SMEM(range_shift.shape, jnp.float32), pltpu.SemaphoreType.DMA],
        compiler_params=limit,
        cost_estimate=pl.CostEstimate(flops=600_000_000, bytes_accessed=0, transcendentals=0),
    )(range_shift, early)
    looked = pl.pallas_call(
        functools.partial(looks_kernel, pairs, dates),
        out_shape=[jax.ShapeDtypeStruct((groups, out_width), jnp.float32)] * dates,
        in_specs=[vmem] * (2 + dates),
        out_specs=[vmem] * dates,
        scratch_shapes=[
            pltpu.VMEM((chunk_rows + FOLD, LANES), bf16),
            pltpu.VMEM((dates, chunk_rows, 2 * LANES), bf16),
            pltpu.VMEM((len(pairs) * 2 * groups, chunk), jnp.float32),
        ],
        compiler_params=limit,
    )(weights, early, *chunks)
    out = pl.pallas_call(
        functools.partial(place_kernel, min(LAGS, dates - 1), looks),
        out_shape=jax.ShapeDtypeStruct((2, LAGS, groups, looks * dates), jnp.float32),
        in_specs=[vmem] * dates,
        out_specs=vmem,
        compiler_params=limit,
    )(*exchanged(looked, steps))
    return out[:, None]


def body(slc, offsets, kernel_index, range_shift):
    dates, az_count = (lax.axis_size(a) for a in ("date", "az"))
    lines, columns = slc.shape[2], slc.shape[3]
    whole_tiles = columns % (dates * LANES) == 0 and columns % (dates * LOOK_RG) == 0
    one_row = columns // LOOK_RG == LANES and range_shift.shape[0] == dates
    few = dates & (dates - 1) == 0 and dates - 1 <= LAGS
    folds = lines == 2 * HALO_LINES and lax.axis_size("rng") == 2 and dates > 1 and 2 * lines // FOLD * TAIL <= LANES
    if az_count == 2 and whole_tiles and one_row and few and folds:
        return tiled_body(slc, offsets, kernel_index, range_shift)
    return chunked_body(slc, offsets, kernel_index, range_shift)


def solution(mesh):
    return jax.shard_map(
        body,
        mesh=mesh,
        in_specs=(
            P(None, ("groups", "date"), "az", "rng"),
            P(("groups", "date"), None),
            P(("groups", "date"), None),
            P("groups"),
        ),
        out_specs=P(None, ("groups", "date"), None, "az", "rng"),
        check_vma=False,
    )
```

```python
import functools

import jax
import jax.numpy as jnp
import numpy as np
from jax import lax
from jax.experimental import pallas as pl
from jax.experimental.pallas import tpu as pltpu
from jax.sharding import PartitionSpec as P

LAGS = 8
KERNELS = 16
TAPS = 8
FILTER_HALF = 8
FILTER_TAPS = 2 * FILTER_HALF + 1
LOOK_AZ = 4
LOOK_RG = 20
LANES = 128
META = 3
UNROLLED_PAIRS = 12


def up(value, unit):
    return -(-value // unit) * unit


def kernel_table():
    position = np.arange(TAPS) - 3.0 - np.arange(KERNELS)[:, None] / KERNELS
    shaped = np.sinc(position) * (0.5 + 0.5 * np.cos(np.pi * position / 5.0))
    table = np.zeros((KERNELS, LANES), np.float32)
    table[:, :TAPS] = shaped / shaped.sum(1, keepdims=True)
    return table


def lowpass_row(width):
    t = np.arange(FILTER_TAPS) - FILTER_HALF
    row = np.zeros((1, width), np.float32)
    row[0, :FILTER_TAPS] = 0.4 * np.sinc(0.4 * t) * (0.54 + 0.46 * np.cos(np.pi * t / (FILTER_HALF + 1)))
    return row


def halves(value):
    high = value.astype(jnp.bfloat16)
    return high, (value - high.astype(jnp.float32)).astype(jnp.bfloat16)


def dot(a, b):
    return jnp.dot(a, b, preferred_element_type=jnp.float32)


def dot_nt(a, b):
    return lax.dot_general(a, b, (((1,), (1,)), ((), ())), preferred_element_type=jnp.float32)


def pack_kernel(chunk, place_ref, offsets_ref, index_ref, slc_ref, before_ref, after_ref, out_ref, wide_ref):
    columns = slc_ref.shape[1]
    wide = out_ref.shape[2]
    first = place_ref[0] == 0
    last = place_ref[0] == place_ref[1] - 1
    zero = jnp.zeros_like(before_ref[...])
    wide_ref[:, :LANES] = jnp.where(first, zero, before_ref[...])
    wide_ref[:, LANES : LANES + columns] = slc_ref[...]
    wide_ref[:, LANES + columns :] = jnp.where(last, zero, after_ref[...])
    lane = lax.broadcasted_iota(jnp.int32, (slc_ref.shape[0], wide), 1)
    numbers = [offsets_ref[0, 0], index_ref[0, 0], index_ref[0, 1]]
    for j in range(out_ref.shape[0]):
        start = LANES + chunk * j - FILTER_HALF - 3 + offsets_ref[0, 1]
        tile = lax.shift_right_logical(start, 7)
        within = lax.bitwise_and(start, LANES - 1)
        window = wide_ref[:, pl.ds(pl.multiple_of(tile * LANES, LANES), wide + LANES)].astype(jnp.float32)
        moved = pltpu.roll(window, wide + LANES - within, 1)[:, :wide]
        for slot, number in enumerate(numbers):
            moved = jnp.where(lane == wide - META + slot, number.astype(jnp.float32), moved)
        out_ref[j] = moved.astype(jnp.bfloat16)


def picked_taps(table, index):
    row = lax.broadcasted_iota(jnp.int32, table.shape, 0).astype(jnp.float32)
    return jnp.sum(jnp.where(row == index, table, 0.0), axis=0, keepdims=True)


def banded(taps, distance):
    out = jnp.zeros(distance.shape, jnp.float32)
    for q in range(TAPS):
        out = jnp.where(distance == q, taps[:, q : q + 1], out)
    return out


def pairs_kernel(chunk, pairs, *refs):
    if isinstance(pairs, int):
        table_of_pairs, refs = refs[0], refs[1:]
    shift_ref, table_ref, lowpass_ref, recv_ref, out_ref, resampled_ref, weight_ref, product_ref = refs
    sources, rows, wide = recv_ref.shape
    dates = shift_ref.shape[0]
    az_count = sources // dates
    own_lines = rows // 2
    lines = own_lines * az_count
    groups = lines // LOOK_AZ
    looks = chunk // LOOK_RG
    table = table_ref[...]
    held = resampled_ref.shape[2]

    out_row = lax.broadcasted_iota(jnp.int32, (lines, lines), 0)
    in_row = lax.broadcasted_iota(jnp.int32, (lines, lines), 1)
    line = LOOK_AZ * (out_row % groups) + out_row // groups
    line_distance = (in_row - line + 3).astype(jnp.float32)
    span = min(2 * LANES, wide)
    column_distance = (
        lax.broadcasted_iota(jnp.int32, (span, LANES), 0) - lax.broadcasted_iota(jnp.int32, (span, LANES), 1)
    ).astype(jnp.float32)
    for date in range(dates):
        numbers = recv_ref[date * az_count, 0:16, wide - LANES :].astype(jnp.float32)[0:1, LANES - META :]
        line_offset, line_index, column_index = (numbers[:, s : s + 1] for s in range(META))
        line_taps = banded(picked_taps(table, line_index), line_distance - line_offset)
        line_taps = jnp.concatenate(halves(line_taps), axis=0)
        column_high, column_low = halves(banded(picked_taps(table, column_index), column_distance))
        moved = []
        for plane in range(2):
            rows_of = slice(plane * own_lines, (plane + 1) * own_lines)
            source = jnp.concatenate([recv_ref[date * az_count + a, rows_of, :] for a in range(az_count)], axis=0)
            both = dot(line_taps, source)
            moved.append(both[:lines] + both[lines:])
        moved_high, moved_low = halves(jnp.concatenate(moved, axis=0))
        for begin in range(0, held, LANES):
            end = min(begin + span, wide)
            taken = end - begin
            total = dot(moved_high[:, begin:end], column_high[:taken])
            total += dot(moved_low[:, begin:end], column_high[:taken])
            total += dot(moved_high[:, begin:end], column_low[:taken])
            resampled_ref[date, :, begin : begin + LANES] = total.astype(jnp.bfloat16)

    window = lowpass_ref[...]
    spacing = lax.broadcasted_iota(jnp.int32, window.shape, 1).astype(jnp.float32) - FILTER_HALF
    span = min(2 * LANES, held)

    def one_pair(place, own, other):
        gap = shift_ref[own] - shift_ref[other]
        angle = jnp.where(jnp.abs(spacing) <= FILTER_HALF, jnp.pi * gap * spacing, 0.0)
        for part, taps in enumerate((window * jnp.cos(angle), window * jnp.sin(angle))):
            spread = jnp.broadcast_to(taps, (LANES, 2 * LANES))
            spread = pltpu.roll(spread, 0, 1, stride=1, stride_axis=0)
            high, low = halves(spread)
            weight_ref[0, part * LANES : (part + 1) * LANES, :] = high
            weight_ref[1, part * LANES : (part + 1) * LANES, :] = low
        both = jnp.concatenate([resampled_ref[own], resampled_ref[other]], axis=0)
        for begin in range(0, up(chunk, LANES), LANES):
            end = min(begin + span, held)
            taken = end - begin
            total = dot_nt(both[:, begin:end], weight_ref[0, :, :taken])
            total += dot_nt(both[:, begin:end], weight_ref[1, :, :taken])
            cos, sin = total[:, :LANES], total[:, LANES:]
            re, im = slice(0, lines), slice(lines, 2 * lines)
            master_re = cos[re] + sin[im]
            master_im = cos[im] - sin[re]
            re, im = slice(2 * lines, 3 * lines), slice(3 * lines, 4 * lines)
            partner_re = cos[re] - sin[im]
            partner_im = cos[im] + sin[re]
            for part, product in enumerate(
                (
                    master_re * partner_re + master_im * partner_im,
                    master_im * partner_re - master_re * partner_im,
                )
            ):
                summed = sum(product[k * groups : (k + 1) * groups] for k in range(LOOK_AZ))
                product_ref[place, part, :, begin : begin + LANES] = summed

    if isinstance(pairs, int):
        count = pairs

        def step(place, carry):
            one_pair(place, table_of_pairs[place, 0], table_of_pairs[place, 1])
            return carry

        lax.fori_loop(0, count, step, 0)
    else:
        count = len(pairs)
        for place, (own, other) in enumerate(pairs):
            one_pair(place, own, other)

    out_width = out_ref.shape[2]
    column = lax.broadcasted_iota(jnp.int32, (product_ref.shape[3], out_width), 0)
    lane = lax.broadcasted_iota(jnp.int32, (product_ref.shape[3], out_width), 1)
    collect = jnp.where(column // LOOK_RG == lane % looks, 1.0, 0.0).astype(jnp.bfloat16)
    high, low = halves(product_ref[...].reshape(count * 2 * groups, product_ref.shape[3]))
    total = (dot(high, collect) + dot(low, collect)) * (1.0 / (LOOK_AZ * LOOK_RG))
    total = total.reshape(count, 2, groups, out_width)
    own_lane = lax.broadcasted_iota(jnp.int32, (groups, out_width), 1) // looks
    place = 0
    for own in range(dates):
        value = jnp.zeros((groups, out_width), jnp.float32)
        for lag in range(min(LAGS, dates - 1 - own)):
            for part in range(2):
                value = jnp.where(own_lane == lag * 2 + part, total[place, part], value)
            place += 1
        out_ref[own * az_count : (own + 1) * az_count] = value.reshape(az_count, groups // az_count, out_width)


def unpack_kernel(used_lags, looks, recv_ref, out_ref):
    sources, groups, width = recv_ref.shape
    columns = out_ref.shape[-1]
    lane = lax.broadcasted_iota(jnp.int32, (groups, columns), 1) // looks
    out_ref[...] = jnp.zeros_like(out_ref)
    for lag in range(used_lags):
        for part in range(2):
            value = jnp.zeros((groups, columns), jnp.float32)
            for source in range(sources):
                block = recv_ref[source]
                if width != columns:
                    block = block[:, :columns]
                shift = looks * (source - lag * 2 - part) % columns
                if shift:
                    block = pltpu.roll(block, shift, 1)
                value = jnp.where(lane == source, block, value)
            out_ref[part, lag] = value


def chunked_body(slc, offsets, kernel_index, range_shift):
    axes = ("date", "az")
    date_count, az_count, rng_count = (lax.axis_size(a) for a in ("date", "az", "rng"))
    peers = date_count * az_count
    lines, columns = slc.shape[2], slc.shape[3]
    dates = range_shift.shape[0]
    chunk = columns // peers
    looks = chunk // LOOK_RG
    groups = lines * az_count // LOOK_AZ
    wide = up(chunk + 2 * FILTER_HALF + TAPS - 1 + META, LANES)
    held = up(chunk + 2 * FILTER_HALF, LANES)
    used_lags = min(LAGS, dates - 1)
    out_width = up(used_lags * 2 * looks, LANES)
    vmem = pl.BlockSpec(memory_space=pltpu.VMEM)
    smem = pl.BlockSpec(memory_space=pltpu.SMEM)
    limit = pltpu.CompilerParams(vmem_limit_bytes=32 * 1024 * 1024)

    cells = slc.reshape(2 * lines, columns)
    place = lax.axis_index("rng")
    if rng_count == 2:
        edge = jnp.where(place == 0, cells[:, columns - LANES :], cells[:, :LANES])
        before = after = lax.ppermute(edge, "rng", [(0, 1), (1, 0)])
    else:
        forth = [(i, i + 1) for i in range(rng_count - 1)]
        before = lax.ppermute(cells[:, columns - LANES :], "rng", forth)
        after = lax.ppermute(cells[:, :LANES], "rng", [(b, a) for a, b in forth])

    packed = pl.pallas_call(
        functools.partial(pack_kernel, chunk),
        out_shape=jax.ShapeDtypeStruct((peers, 2 * lines, wide), jnp.bfloat16),
        in_specs=[smem] * 3 + [vmem] * 3,
        out_specs=vmem,
        scratch_shapes=[pltpu.VMEM((2 * lines, columns + 2 * LANES), jnp.bfloat16)],
        compiler_params=limit,
    )(jnp.stack([place, rng_count]).astype(jnp.int32), offsets, kernel_index, cells, before, after)
    arrived = lax.all_to_all(packed, axes, 0, 0, tiled=True)

    pairs = [(own, own + lag) for own in range(dates) for lag in range(1, LAGS + 1) if own + lag < dates]
    count = len(pairs)
    first = [jnp.asarray(np.array(pairs, np.int32))] if count > UNROLLED_PAIRS else []
    looked = pl.pallas_call(
        functools.partial(pairs_kernel, chunk, count if first else pairs),
        out_shape=jax.ShapeDtypeStruct((peers, groups // az_count, out_width), jnp.float32),
        in_specs=[smem] * len(first) + [smem] + [vmem] * 3,
        out_specs=vmem,
        scratch_shapes=[
            pltpu.VMEM((dates, 4 * (groups * LOOK_AZ) // 2, held), jnp.bfloat16),
            pltpu.VMEM((2, 2 * LANES, 2 * LANES), jnp.bfloat16),
            pltpu.VMEM((count, 2, groups, up(chunk, LANES)), jnp.float32),
        ],
        compiler_params=limit,
    )(*first, range_shift, jnp.asarray(kernel_table()), jnp.asarray(lowpass_row(2 * LANES)), arrived)
    returned = lax.all_to_all(looked, axes, 0, 0, tiled=True)

    out = pl.pallas_call(
        functools.partial(unpack_kernel, used_lags, looks),
        out_shape=jax.ShapeDtypeStruct((2, LAGS, groups // az_count, looks * peers), jnp.float32),
        in_specs=[vmem],
        out_specs=vmem,
        compiler_params=limit,
    )(returned)
    return out[:, None]


HALO_LINES = 16
FOLD = 16
TAIL = 2 * FILTER_HALF


def sinc(value):
    angle = jnp.pi * value
    return jnp.where(angle == 0.0, 1.0, jnp.sin(angle) / jnp.where(angle == 0.0, 1.0, angle))


def tap_row(index):
    lane = lax.broadcasted_iota(jnp.int32, (1, LANES), 1)
    position = lane.astype(jnp.float32) - 3.0 - index.astype(jnp.float32) / KERNELS
    shaped = sinc(position) * (0.5 + 0.5 * jnp.cos(jnp.pi * position / 5.0))
    shaped = jnp.where(lane < TAPS, shaped, 0.0)
    return shaped / jnp.sum(shaped, axis=1, keepdims=True)


def row_line(row, az):
    quarter = HALO_LINES // LOOK_AZ
    within = row % HALO_LINES
    return HALO_LINES * ((row // HALO_LINES) ^ az) + LOOK_AZ * (within % quarter) + within // quarter


def prepare_kernel(offsets_hbm, index_hbm, slc_ref, side_ref, corner_ref, lines_ref, line_ref, column_ref, held_ref, offsets_ref, index_ref, semaphores):
    lines, columns = slc_ref.shape[1:]
    az = lax.axis_index("az")
    row = pl.multiple_of((1 - az) * (lines - HALO_LINES), HALO_LINES)
    edge = pl.multiple_of((1 - lax.axis_index("rng")) * (columns - LANES), LANES)
    nearest, outermost = pl.ds(row, HALO_LINES), pl.ds(edge, LANES)
    moves = [
        (offsets_hbm, offsets_ref),
        (index_hbm, index_ref),
        (slc_ref.at[:, :, outermost], side_ref),
        (slc_ref.at[:, nearest, outermost], corner_ref),
        (slc_ref.at[:, nearest, :], lines_ref),
        (slc_ref, held_ref.at[:, :, pl.ds(LANES, columns)]),
    ]
    copies = [pltpu.make_async_copy(a, b, semaphores.at[i]) for i, (a, b) in enumerate(moves)]
    for copy in copies:
        copy.start()
    held_ref[:, :, :LANES] = jnp.zeros((2, lines, LANES), held_ref.dtype)
    held_ref[:, :, LANES + columns :] = jnp.zeros((2, lines, 2 * LANES), held_ref.dtype)
    copies[0].wait()
    copies[1].wait()
    for half in range(2):
        shape = (HALO_LINES, lines + HALO_LINES)
        line = row_line(lax.broadcasted_iota(jnp.int32, shape, 0) + half * HALO_LINES, az)
        place = lax.broadcasted_iota(jnp.int32, shape, 1)
        source = jnp.where(place < lines, place, place + jnp.where(az == 0, 0, -lines - HALO_LINES))
        taps = banded(tap_row(index_ref[0, 0]), source - line - offsets_ref[0, 0] + 3)
        line_ref[half] = jnp.concatenate(halves(taps), axis=0)
    shape = (3 * LANES, LANES)
    distance = lax.broadcasted_iota(jnp.int32, shape, 0) - lax.broadcasted_iota(jnp.int32, shape, 1)
    distance = distance - (LANES - FILTER_HALF - 3) - offsets_ref[0, 1]
    taps = banded(tap_row(index_ref[0, 1]), distance)
    column_ref[...] = jnp.concatenate(halves(taps), axis=1)
    for copy in copies[2:]:
        copy.wait()


def along_range(blocks, column_ref, tiles):
    blocks = [halves(moved) for moved in blocks]
    starts = range(0, tiles * LANES, LANES)
    high = jnp.concatenate([high[:, s : s + 3 * LANES] for high, _ in blocks for s in starts], axis=0)
    low = jnp.concatenate([low[:, s : s + 3 * LANES] for _, low in blocks for s in starts], axis=0)
    total = dot(high, column_ref[...])
    return total[:, :LANES] + total[:, LANES:] + dot(low, column_ref[:, :LANES])


def early_kernel(tiles, steps, held_ref, line_ref, column_ref, *outs):
    lines = held_ref.shape[1]
    early = tiles - 1
    moved = []
    for step in steps:
        chunk = lax.axis_index("date") ^ step
        begin = pl.multiple_of((chunk * tiles + lax.axis_index("rng")) * LANES, LANES)
        moved += [held_ref[plane, :, pl.ds(begin, (early + 2) * LANES)] for plane in range(2)]
    both = dot(line_ref[0, :, :lines], jnp.concatenate(moved, axis=1))
    both = both[:HALO_LINES] + both[HALO_LINES:]
    width = (early + 2) * LANES
    moved = [
        jnp.concatenate([both[:, (2 * i + plane) * width : (2 * i + plane + 1) * width] for plane in range(2)], axis=0)
        for i in range(len(outs))
    ]
    total = along_range(moved, column_ref, early).astype(jnp.bfloat16)
    rows = early * lines
    for i, out_ref in enumerate(outs):
        out_ref[...] = total[i * rows : (i + 1) * rows]


def resample_kernel(side_ref, corner_ref, lines_ref, held_ref, line_ref, column_ref, *outs):
    outs, tiles_ref, tails_ref = outs[:-2], outs[-2], outs[-1]
    lines, width = held_ref.shape[1:]
    width -= LANES
    block = lax.axis_index("rng")
    taps = jnp.concatenate([line_ref[0], line_ref[1]], axis=0)
    moved = [[], []]
    for plane in range(2):
        own = jnp.concatenate([side_ref[plane], held_ref[plane, :, LANES : width - LANES], side_ref[plane]], axis=1)
        halo = jnp.concatenate([corner_ref[plane], lines_ref[plane], corner_ref[plane]], axis=1)
        both = dot(taps, jnp.concatenate([own, halo], axis=0))
        for half in range(2):
            at = 2 * half * HALO_LINES
            moved[half].append(both[at : at + HALO_LINES] + both[at + HALO_LINES : at + 2 * HALO_LINES])
    moved = jnp.concatenate(moved[0] + moved[1], axis=0)
    left = jnp.where(block > 0, moved[:, :LANES], 0.0)
    right = jnp.where(block == 0, moved[:, width - LANES :], 0.0)
    moved = jnp.concatenate([left, moved[:, LANES : width - LANES], right, jnp.zeros_like(right)], axis=1)
    total = along_range([moved], column_ref, width // LANES - 1)
    rows = 2 * lines
    tiles_ref[...] = total.astype(jnp.bfloat16)
    chunk_rows = outs[0].shape[0] - FOLD
    lane = lax.broadcasted_iota(jnp.int32, (FOLD, LANES), 1) // TAIL
    for chunk in range(len(outs)):
        begin = (chunk + 1) * chunk_rows
        folded = total[begin : begin + FOLD]
        for part in range(1, rows // FOLD):
            value = pltpu.roll(total[begin + part * FOLD : begin + (part + 1) * FOLD], part * TAIL, 1)
            folded = jnp.where(lane == part, value, folded)
        tails_ref[chunk] = folded.astype(jnp.bfloat16)
    date = lax.axis_index("date")
    early = chunk_rows // rows - 1
    for step, out_ref in enumerate(outs):
        chunk = date ^ step
        if out_ref.shape[0] == outs[0].shape[0]:
            out_ref[:chunk_rows] = tiles_ref[pl.ds(pl.multiple_of(chunk * chunk_rows, FOLD), chunk_rows), :]
            out_ref[chunk_rows:] = tails_ref[chunk]
            continue
        for tile in range(early):
            begin = pl.multiple_of(chunk * chunk_rows + (tile + block) * rows + lines, FOLD)
            out_ref[tile * lines : (tile + 1) * lines] = tiles_ref[pl.ds(begin, lines), :]
        begin = pl.multiple_of(chunk * chunk_rows + (1 - block) * early * rows, FOLD)
        out_ref[early * lines : early * lines + rows] = tiles_ref[pl.ds(begin, rows), :]
        out_ref[early * lines + rows :] = tails_ref[chunk]


def filter_kernel(pairs, shift_hbm, *refs):
    count = (len(refs) - 3) // 2
    earlies, out_ref, spreads, (shift_ref, semaphore) = refs[:count], refs[count], refs[count + 1 : -2], refs[-2:]
    copy = pltpu.make_async_copy(shift_hbm, shift_ref, semaphore)
    copy.start()
    lines = 2 * HALO_LINES
    for early_ref, spread_ref in zip(earlies, spreads):
        spread_ref[...] = jnp.zeros_like(spread_ref)
        for tile in range(early_ref.shape[0] // lines):
            begin = pl.multiple_of((tile + lax.axis_index("rng")) * 2 * lines, FOLD)
            spread_ref[pl.ds(begin, lines), :] = early_ref[tile * lines : (tile + 1) * lines]
    date = lax.axis_index("date")
    spacing = lax.broadcasted_iota(jnp.int32, (1, 2 * LANES), 1).astype(jnp.float32) - FILTER_HALF
    window = 0.4 * sinc(0.4 * spacing) * (0.54 + 0.46 * jnp.cos(jnp.pi * spacing / (FILTER_HALF + 1)))
    window = jnp.where(jnp.abs(spacing) <= FILTER_HALF, window, 0.0)
    copy.wait()
    for place, (first, second) in enumerate(pairs):
        gap = shift_ref[date ^ first] - shift_ref[date ^ second]
        angle = jnp.where(jnp.abs(spacing) <= FILTER_HALF, jnp.pi * gap * spacing, 0.0)
        for part, taps in enumerate((window * jnp.cos(angle), window * jnp.sin(angle))):
            spread = jnp.broadcast_to(taps, (LANES, 2 * LANES))
            spread = pltpu.roll(spread, 0, 1, stride=1, stride_axis=0)
            high, low = halves(spread)
            out_ref[place, 0, part * LANES : (part + 1) * LANES, :] = high
            out_ref[place, 1, part * LANES : (part + 1) * LANES, :] = low


def set_window(window_ref, chunk_ref, tail):
    chunk_rows = window_ref.shape[0]
    rows = 4 * HALO_LINES
    window_ref[:, :LANES] = chunk_ref[:chunk_rows]
    window_ref[: chunk_rows - rows, LANES:] = chunk_ref[rows:chunk_rows]
    folded = tail.astype(jnp.float32)
    for part in range(rows // FOLD):
        value = pltpu.roll(folded, LANES - part * TAIL, 1) if part else folded
        at = pl.ds(chunk_rows - rows + part * FOLD, FOLD)
        window_ref[at, LANES:] = value.astype(jnp.bfloat16)


def pair_totals(pairs, places, windows, weight_ref, product_ref, out_width):
    lines, rows = 2 * HALO_LINES, 4 * HALO_LINES
    groups = lines // LOOK_AZ
    blocks = windows[pairs[0][0]].shape[0] // rows
    looks = blocks * LANES // LOOK_RG
    upper = lax.broadcasted_iota(jnp.int32, (groups, LANES), 0) // (groups // 2) == lax.axis_index("az")
    for i, (first, second) in enumerate(pairs):
        def filtered(step):
            window = windows[step][...]
            total = dot_nt(window, weight_ref[places[i], 0]) + dot_nt(window, weight_ref[places[i], 1])
            total = total.reshape(blocks, 2, 2, HALO_LINES, 2 * LANES)
            re, im = total[:, :, 0], total[:, :, 1]
            return re[..., :LANES], im[..., :LANES], re[..., LANES:], im[..., LANES:]

        cos_re, cos_im, sin_re, sin_im = filtered(first)
        master_re, master_im = cos_re + sin_im, cos_im - sin_re
        cos_re, cos_im, sin_re, sin_im = filtered(second)
        partner_re, partner_im = cos_re - sin_im, cos_im + sin_re
        for part, product in enumerate(
            (
                master_re * partner_re + master_im * partner_im,
                master_im * partner_re - master_re * partner_im,
            )
        ):
            summed = product[:, :, :groups] + product[:, :, groups:]
            at = pl.ds((i * 2 + part) * groups, groups)
            for k in range(blocks):
                both = [summed[k, half] + pltpu.roll(summed[k, half], groups // 2, 0) for half in range(2)]
                product_ref[at, k * LANES : (k + 1) * LANES] = jnp.where(upper, both[0], both[1])
    column = lax.broadcasted_iota(jnp.int32, (product_ref.shape[1], out_width), 0)
    lane = lax.broadcasted_iota(jnp.int32, (product_ref.shape[1], out_width), 1)
    collect = jnp.where(column // LOOK_RG == lane % looks, 1.0, 0.0).astype(jnp.bfloat16)
    high, low = halves(product_ref[...])
    total = (dot(high, collect) + dot(low, collect)) * (1.0 / (LOOK_AZ * LOOK_RG))
    return total.reshape(len(pairs), 2, groups, out_width)


def far_kernel(pairs, places, far, weight_ref, *refs):
    wholes, rests = refs[:far], refs[far : 2 * far]
    own_ref, totals_ref, window_ref, product_ref, whole_ref = refs[2 * far :]
    lines, rows = 2 * HALO_LINES, 4 * HALO_LINES
    chunk_rows = window_ref.shape[1]
    early = chunk_rows // rows - 1
    block = lax.axis_index("rng")
    set_window(window_ref.at[0], own_ref, own_ref[chunk_rows:])
    for i, (early_ref, rest_ref) in enumerate(zip(wholes, rests)):
        whole_ref[...] = early_ref[...]
        for tile in range(early):
            begin = pl.multiple_of((tile + block) * rows, FOLD)
            whole_ref[pl.ds(begin + lines, lines), :] = rest_ref[tile * lines : (tile + 1) * lines]
        begin = pl.multiple_of((1 - block) * early * rows, FOLD)
        whole_ref[pl.ds(begin, rows), :] = rest_ref[early * lines : early * lines + rows]
        set_window(window_ref.at[i + 1], whole_ref, rest_ref[early * lines + rows :])
    windows = {step: window_ref.at[i] for i, step in enumerate([0] + list(range(far + 1, 1, -1)))}
    totals_ref[...] = pair_totals(pairs, places, windows, weight_ref, product_ref, totals_ref.shape[3])


def near_kernel(pairs, places, far, all_pairs, weight_ref, held_ref, totals_ref, near_ref, *refs):
    outs, window_ref, product_ref = refs[:-2], refs[-2], refs[-1]
    groups, out_width = outs[0].shape
    chunk_rows = window_ref.shape[0]
    looks = chunk_rows // (4 * HALO_LINES) * LANES // LOOK_RG
    date = lax.axis_index("date")
    set_window(window_ref, near_ref, near_ref[chunk_rows:])
    windows = {step: held_ref.at[i] for i, step in enumerate([0] + list(range(far + 1, 1, -1)))}
    windows[1] = window_ref
    near = pair_totals(pairs, places, windows, weight_ref, product_ref, out_width)
    total = {pair: near[i] for i, pair in enumerate(pairs)}
    for i, pair in enumerate(pair for pair in all_pairs if pair not in pairs):
        total[pair] = totals_ref[i]
    own_lane = lax.broadcasted_iota(jnp.int32, (groups, out_width), 1) // looks
    for step, out_ref in enumerate(outs):
        value = jnp.zeros((groups, out_width), jnp.float32)
        for pair in all_pairs:
            if step in pair:
                other = pair[1] if pair[0] == step else pair[0]
                lag = (date ^ other) - (date ^ step)
                for part in range(2):
                    signed = -total[pair][part] if part == 1 and pair[1] == step else total[pair][part]
                    value = jnp.where(own_lane == (lag - 1) * 2 + part, signed, value)
        out_ref[...] = value


def place_kernel(used_lags, looks, *refs):
    out_ref = refs[-1]
    groups, columns = out_ref.shape[2:]
    date = lax.axis_index("date")
    lane = lax.broadcasted_iota(jnp.int32, (groups, LANES), 1) // looks
    out_ref[...] = jnp.zeros_like(out_ref)
    each = LANES // looks
    for step, recv_ref in enumerate(refs[:-1][::-1]):
        chunk = date ^ step
        for lag in range(used_lags):
            for part in range(2):
                tile, group = divmod(lag * 2 + part, each)
                block = recv_ref[:, tile * LANES : (tile + 1) * LANES]
                block = pltpu.roll(block, lax.bitwise_and(looks * (chunk - group), LANES - 1), 1)
                out_ref[part, lag] = jnp.where(lane == chunk, block, out_ref[part, lag])


def tiled_body(slc, offsets, kernel_index, range_shift):
    dates = lax.axis_size("date")
    lines, columns = slc.shape[2], slc.shape[3]
    chunk = columns // dates
    looks = chunk // LOOK_RG
    groups = lines // LOOK_AZ
    out_width = up(min(LAGS, dates - 1) * 2 * looks, LANES)
    vmem = pl.BlockSpec(memory_space=pltpu.VMEM)
    hbm = pl.BlockSpec(memory_space=pltpu.HBM)
    limit = pltpu.CompilerParams(vmem_limit_bytes=32 * 1024 * 1024)
    bf16 = jnp.bfloat16
    cells, offsets, kernel_index, range_shift = (
        pltpu.with_memory_space_constraint(value, pltpu.HBM)
        for value in (slc.reshape(2, lines, columns), offsets, kernel_index, range_shift)
    )
    tiles = chunk // LANES
    chunk_rows = tiles * 2 * lines

    side, corner, halo_lines, line_taps, column_taps, held = pl.pallas_call(
        prepare_kernel,
        out_shape=[
            jax.ShapeDtypeStruct((2, lines, LANES), bf16),
            jax.ShapeDtypeStruct((2, HALO_LINES, LANES), bf16),
            jax.ShapeDtypeStruct((2, HALO_LINES, columns), bf16),
            jax.ShapeDtypeStruct((2, 2 * HALO_LINES, lines + HALO_LINES), bf16),
            jax.ShapeDtypeStruct((3 * LANES, 2 * LANES), bf16),
            jax.ShapeDtypeStruct((2, lines, columns + 3 * LANES), bf16),
        ],
        in_specs=[hbm] * 3,
        out_specs=[vmem] * 6,
        scratch_shapes=[
            pltpu.SMEM(offsets.shape, jnp.int32),
            pltpu.SMEM(kernel_index.shape, jnp.int32),
            pltpu.SemaphoreType.DMA((6,)),
        ],
        compiler_params=limit,
    )(offsets, kernel_index, cells)
    swap = [(0, 1), (1, 0)]
    side = lax.ppermute(side, "rng", swap)
    corner = lax.ppermute(corner, ("rng", "az"), [(0, 3), (1, 2), (2, 1), (3, 0)])
    halo_lines = lax.ppermute(halo_lines, "az", swap)

    steps = range(dates - 1, 0, -1)
    far = dates - 2

    def swapped(value, step):
        return lax.ppermute(value, "date", [(i, i ^ step) for i in range(dates)])

    early_rows = (tiles - 1) * lines
    early = pl.pallas_call(
        functools.partial(early_kernel, tiles, steps[:far]),
        out_shape=[jax.ShapeDtypeStruct((early_rows, LANES), bf16)] * far,
        in_specs=[vmem] * 3,
        out_specs=[vmem] * far,
        compiler_params=limit,
    )(held, line_taps, column_taps)
    early = [swapped(rows, step) for rows, step in zip(early, steps)]
    out_rows = [chunk_rows + FOLD] * 2 + [chunk_rows + FOLD - early_rows] * far
    own, near, *rests = pl.pallas_call(
        resample_kernel,
        out_shape=[jax.ShapeDtypeStruct((rows, LANES), bf16) for rows in out_rows],
        in_specs=[vmem] * 6,
        out_specs=[vmem] * dates,
        scratch_shapes=[
            pltpu.VMEM(((columns // LANES + 1) * 2 * lines, LANES), bf16),
            pltpu.VMEM((dates, FOLD, LANES), bf16),
        ],
        compiler_params=limit,
    )(side, corner, halo_lines, held, line_taps, column_taps)
    rests = [swapped(rows, step) for rows, step in zip(rests[::-1], steps)]
    near = swapped(near, 1)

    pairs = [(first, second) for first in range(dates) for second in range(first + 1, dates)]
    weights, *wholes = pl.pallas_call(
        functools.partial(filter_kernel, pairs),
        out_shape=[jax.ShapeDtypeStruct((len(pairs), 2, 2 * LANES, 2 * LANES), bf16)]
        + [jax.ShapeDtypeStruct((chunk_rows, LANES), bf16)] * far,
        in_specs=[hbm] + [vmem] * far,
        out_specs=[vmem] * (1 + far),
        scratch_shapes=[pltpu.SMEM(range_shift.shape, jnp.float32), pltpu.SemaphoreType.DMA],
        compiler_params=limit,
        cost_estimate=pl.CostEstimate(flops=275_000_000, bytes_accessed=0, transcendentals=0),
    )(range_shift, *early)
    far_pairs = [pair for pair in pairs if 1 not in pair]
    near_pairs = [pair for pair in pairs if 1 in pair]
    totals, windows = pl.pallas_call(
        functools.partial(far_kernel, far_pairs, [pairs.index(pair) for pair in far_pairs], far),
        out_shape=[
            jax.ShapeDtypeStruct((len(far_pairs), 2, groups, out_width), jnp.float32),
            jax.ShapeDtypeStruct((1 + far, chunk_rows, 2 * LANES), bf16),
        ],
        in_specs=[vmem] * (2 + 2 * far),
        out_specs=[vmem] * 2,
        scratch_shapes=[
            pltpu.VMEM((len(far_pairs) * 2 * groups, chunk), jnp.float32),
            pltpu.VMEM((chunk_rows, LANES), bf16),
        ],
        compiler_params=limit,
        cost_estimate=pl.CostEstimate(flops=500_000_000, bytes_accessed=0, transcendentals=0),
    )(weights, *wholes, *rests, own)
    looked = pl.pallas_call(
        functools.partial(near_kernel, near_pairs, [pairs.index(pair) for pair in near_pairs], far, pairs),
        out_shape=[jax.ShapeDtypeStruct((groups, out_width), jnp.float32)] * dates,
        in_specs=[vmem] * 4,
        out_specs=[vmem] * dates,
        scratch_shapes=[
            pltpu.VMEM((chunk_rows, 2 * LANES), bf16),
            pltpu.VMEM((len(near_pairs) * 2 * groups, chunk), jnp.float32),
        ],
        compiler_params=limit,
    )(weights, windows, totals, near)
    returned = [swapped(looked[step], step) for step in steps] + [looked[0]]
    out = pl.pallas_call(
        functools.partial(place_kernel, min(LAGS, dates - 1), looks),
        out_shape=jax.ShapeDtypeStruct((2, LAGS, groups, looks * dates), jnp.float32),
        in_specs=[vmem] * dates,
        out_specs=vmem,
        compiler_params=limit,
    )(*returned)
    return out[:, None]


def body(slc, offsets, kernel_index, range_shift):
    dates, az_count = (lax.axis_size(a) for a in ("date", "az"))
    lines, columns = slc.shape[2], slc.shape[3]
    whole_tiles = columns % (dates * LANES) == 0 and columns % (dates * LOOK_RG) == 0
    one_row = columns // LOOK_RG == LANES and range_shift.shape[0] == dates
    few = dates & (dates - 1) == 0 and dates - 1 <= LAGS
    folds = lines == 2 * HALO_LINES and lax.axis_size("rng") == 2 and dates >= 4 and 2 * lines // FOLD * TAIL <= LANES
    if az_count == 2 and whole_tiles and one_row and few and folds:
        return tiled_body(slc, offsets, kernel_index, range_shift)
    return chunked_body(slc, offsets, kernel_index, range_shift)


def solution(mesh):
    return jax.shard_map(
        body,
        mesh=mesh,
        in_specs=(
            P(None, ("groups", "date"), "az", "rng"),
            P(("groups", "date"), None),
            P(("groups", "date"), None),
            P("groups"),
        ),
        out_specs=P(None, ("groups", "date"), None, "az", "rng"),
        check_vma=False,
    )
```

```python
import functools

import jax
import jax.numpy as jnp
import numpy as np
from jax import lax
from jax.experimental import pallas as pl
from jax.experimental.pallas import tpu as pltpu
from jax.sharding import PartitionSpec as P

LAGS = 8
KERNELS = 16
TAPS = 8
FILTER_HALF = 8
FILTER_TAPS = 2 * FILTER_HALF + 1
LOOK_AZ = 4
LOOK_RG = 20
LANES = 128
META = 3
UNROLLED_PAIRS = 12


def up(value, unit):
    return -(-value // unit) * unit


def kernel_table():
    position = np.arange(TAPS) - 3.0 - np.arange(KERNELS)[:, None] / KERNELS
    shaped = np.sinc(position) * (0.5 + 0.5 * np.cos(np.pi * position / 5.0))
    table = np.zeros((KERNELS, LANES), np.float32)
    table[:, :TAPS] = shaped / shaped.sum(1, keepdims=True)
    return table


def lowpass_row(width):
    t = np.arange(FILTER_TAPS) - FILTER_HALF
    row = np.zeros((1, width), np.float32)
    row[0, :FILTER_TAPS] = 0.4 * np.sinc(0.4 * t) * (0.54 + 0.46 * np.cos(np.pi * t / (FILTER_HALF + 1)))
    return row


def halves(value):
    high = value.astype(jnp.bfloat16)
    return high, (value - high.astype(jnp.float32)).astype(jnp.bfloat16)


def dot(a, b):
    return jnp.dot(a, b, preferred_element_type=jnp.float32)


def dot_nt(a, b):
    return lax.dot_general(a, b, (((1,), (1,)), ((), ())), preferred_element_type=jnp.float32)


def pack_kernel(chunk, place_ref, offsets_ref, index_ref, slc_ref, before_ref, after_ref, out_ref, wide_ref):
    columns = slc_ref.shape[1]
    wide = out_ref.shape[2]
    first = place_ref[0] == 0
    last = place_ref[0] == place_ref[1] - 1
    zero = jnp.zeros_like(before_ref[...])
    wide_ref[:, :LANES] = jnp.where(first, zero, before_ref[...])
    wide_ref[:, LANES : LANES + columns] = slc_ref[...]
    wide_ref[:, LANES + columns :] = jnp.where(last, zero, after_ref[...])
    lane = lax.broadcasted_iota(jnp.int32, (slc_ref.shape[0], wide), 1)
    numbers = [offsets_ref[0, 0], index_ref[0, 0], index_ref[0, 1]]
    for j in range(out_ref.shape[0]):
        start = LANES + chunk * j - FILTER_HALF - 3 + offsets_ref[0, 1]
        tile = lax.shift_right_logical(start, 7)
        within = lax.bitwise_and(start, LANES - 1)
        window = wide_ref[:, pl.ds(pl.multiple_of(tile * LANES, LANES), wide + LANES)].astype(jnp.float32)
        moved = pltpu.roll(window, wide + LANES - within, 1)[:, :wide]
        for slot, number in enumerate(numbers):
            moved = jnp.where(lane == wide - META + slot, number.astype(jnp.float32), moved)
        out_ref[j] = moved.astype(jnp.bfloat16)


def picked_taps(table, index):
    row = lax.broadcasted_iota(jnp.int32, table.shape, 0).astype(jnp.float32)
    return jnp.sum(jnp.where(row == index, table, 0.0), axis=0, keepdims=True)


def banded(taps, distance):
    out = jnp.zeros(distance.shape, jnp.float32)
    for q in range(TAPS):
        out = jnp.where(distance == q, taps[:, q : q + 1], out)
    return out


def pairs_kernel(chunk, pairs, *refs):
    if isinstance(pairs, int):
        table_of_pairs, refs = refs[0], refs[1:]
    shift_ref, table_ref, lowpass_ref, recv_ref, out_ref, resampled_ref, weight_ref, product_ref = refs
    sources, rows, wide = recv_ref.shape
    dates = shift_ref.shape[0]
    az_count = sources // dates
    own_lines = rows // 2
    lines = own_lines * az_count
    groups = lines // LOOK_AZ
    looks = chunk // LOOK_RG
    table = table_ref[...]
    held = resampled_ref.shape[2]

    out_row = lax.broadcasted_iota(jnp.int32, (lines, lines), 0)
    in_row = lax.broadcasted_iota(jnp.int32, (lines, lines), 1)
    line = LOOK_AZ * (out_row % groups) + out_row // groups
    line_distance = (in_row - line + 3).astype(jnp.float32)
    span = min(2 * LANES, wide)
    column_distance = (
        lax.broadcasted_iota(jnp.int32, (span, LANES), 0) - lax.broadcasted_iota(jnp.int32, (span, LANES), 1)
    ).astype(jnp.float32)
    for date in range(dates):
        numbers = recv_ref[date * az_count, 0:16, wide - LANES :].astype(jnp.float32)[0:1, LANES - META :]
        line_offset, line_index, column_index = (numbers[:, s : s + 1] for s in range(META))
        line_taps = banded(picked_taps(table, line_index), line_distance - line_offset)
        line_taps = jnp.concatenate(halves(line_taps), axis=0)
        column_high, column_low = halves(banded(picked_taps(table, column_index), column_distance))
        moved = []
        for plane in range(2):
            rows_of = slice(plane * own_lines, (plane + 1) * own_lines)
            source = jnp.concatenate([recv_ref[date * az_count + a, rows_of, :] for a in range(az_count)], axis=0)
            both = dot(line_taps, source)
            moved.append(both[:lines] + both[lines:])
        moved_high, moved_low = halves(jnp.concatenate(moved, axis=0))
        for begin in range(0, held, LANES):
            end = min(begin + span, wide)
            taken = end - begin
            total = dot(moved_high[:, begin:end], column_high[:taken])
            total += dot(moved_low[:, begin:end], column_high[:taken])
            total += dot(moved_high[:, begin:end], column_low[:taken])
            resampled_ref[date, :, begin : begin + LANES] = total.astype(jnp.bfloat16)

    window = lowpass_ref[...]
    spacing = lax.broadcasted_iota(jnp.int32, window.shape, 1).astype(jnp.float32) - FILTER_HALF
    span = min(2 * LANES, held)

    def one_pair(place, own, other):
        gap = shift_ref[own] - shift_ref[other]
        angle = jnp.where(jnp.abs(spacing) <= FILTER_HALF, jnp.pi * gap * spacing, 0.0)
        for part, taps in enumerate((window * jnp.cos(angle), window * jnp.sin(angle))):
            spread = jnp.broadcast_to(taps, (LANES, 2 * LANES))
            spread = pltpu.roll(spread, 0, 1, stride=1, stride_axis=0)
            high, low = halves(spread)
            weight_ref[0, part * LANES : (part + 1) * LANES, :] = high
            weight_ref[1, part * LANES : (part + 1) * LANES, :] = low
        both = jnp.concatenate([resampled_ref[own], resampled_ref[other]], axis=0)
        for begin in range(0, up(chunk, LANES), LANES):
            end = min(begin + span, held)
            taken = end - begin
            total = dot_nt(both[:, begin:end], weight_ref[0, :, :taken])
            total += dot_nt(both[:, begin:end], weight_ref[1, :, :taken])
            cos, sin = total[:, :LANES], total[:, LANES:]
            re, im = slice(0, lines), slice(lines, 2 * lines)
            master_re = cos[re] + sin[im]
            master_im = cos[im] - sin[re]
            re, im = slice(2 * lines, 3 * lines), slice(3 * lines, 4 * lines)
            partner_re = cos[re] - sin[im]
            partner_im = cos[im] + sin[re]
            for part, product in enumerate(
                (
                    master_re * partner_re + master_im * partner_im,
                    master_im * partner_re - master_re * partner_im,
                )
            ):
                summed = sum(product[k * groups : (k + 1) * groups] for k in range(LOOK_AZ))
                product_ref[place, part, :, begin : begin + LANES] = summed

    if isinstance(pairs, int):
        count = pairs

        def step(place, carry):
            one_pair(place, table_of_pairs[place, 0], table_of_pairs[place, 1])
            return carry

        lax.fori_loop(0, count, step, 0)
    else:
        count = len(pairs)
        for place, (own, other) in enumerate(pairs):
            one_pair(place, own, other)

    out_width = out_ref.shape[2]
    column = lax.broadcasted_iota(jnp.int32, (product_ref.shape[3], out_width), 0)
    lane = lax.broadcasted_iota(jnp.int32, (product_ref.shape[3], out_width), 1)
    collect = jnp.where(column // LOOK_RG == lane % looks, 1.0, 0.0).astype(jnp.bfloat16)
    high, low = halves(product_ref[...].reshape(count * 2 * groups, product_ref.shape[3]))
    total = (dot(high, collect) + dot(low, collect)) * (1.0 / (LOOK_AZ * LOOK_RG))
    total = total.reshape(count, 2, groups, out_width)
    own_lane = lax.broadcasted_iota(jnp.int32, (groups, out_width), 1) // looks
    place = 0
    for own in range(dates):
        value = jnp.zeros((groups, out_width), jnp.float32)
        for lag in range(min(LAGS, dates - 1 - own)):
            for part in range(2):
                value = jnp.where(own_lane == lag * 2 + part, total[place, part], value)
            place += 1
        out_ref[own * az_count : (own + 1) * az_count] = value.reshape(az_count, groups // az_count, out_width)


def unpack_kernel(used_lags, looks, recv_ref, out_ref):
    sources, groups, width = recv_ref.shape
    columns = out_ref.shape[-1]
    lane = lax.broadcasted_iota(jnp.int32, (groups, columns), 1) // looks
    out_ref[...] = jnp.zeros_like(out_ref)
    for lag in range(used_lags):
        for part in range(2):
            value = jnp.zeros((groups, columns), jnp.float32)
            for source in range(sources):
                block = recv_ref[source]
                if width != columns:
                    block = block[:, :columns]
                shift = looks * (source - lag * 2 - part) % columns
                if shift:
                    block = pltpu.roll(block, shift, 1)
                value = jnp.where(lane == source, block, value)
            out_ref[part, lag] = value


def chunked_body(slc, offsets, kernel_index, range_shift):
    axes = ("date", "az")
    date_count, az_count, rng_count = (lax.axis_size(a) for a in ("date", "az", "rng"))
    peers = date_count * az_count
    lines, columns = slc.shape[2], slc.shape[3]
    dates = range_shift.shape[0]
    chunk = columns // peers
    looks = chunk // LOOK_RG
    groups = lines * az_count // LOOK_AZ
    wide = up(chunk + 2 * FILTER_HALF + TAPS - 1 + META, LANES)
    held = up(chunk + 2 * FILTER_HALF, LANES)
    used_lags = min(LAGS, dates - 1)
    out_width = up(used_lags * 2 * looks, LANES)
    vmem = pl.BlockSpec(memory_space=pltpu.VMEM)
    smem = pl.BlockSpec(memory_space=pltpu.SMEM)
    limit = pltpu.CompilerParams(vmem_limit_bytes=32 * 1024 * 1024)

    cells = slc.reshape(2 * lines, columns)
    place = lax.axis_index("rng")
    if rng_count == 2:
        edge = jnp.where(place == 0, cells[:, columns - LANES :], cells[:, :LANES])
        before = after = lax.ppermute(edge, "rng", [(0, 1), (1, 0)])
    else:
        forth = [(i, i + 1) for i in range(rng_count - 1)]
        before = lax.ppermute(cells[:, columns - LANES :], "rng", forth)
        after = lax.ppermute(cells[:, :LANES], "rng", [(b, a) for a, b in forth])

    packed = pl.pallas_call(
        functools.partial(pack_kernel, chunk),
        out_shape=jax.ShapeDtypeStruct((peers, 2 * lines, wide), jnp.bfloat16),
        in_specs=[smem] * 3 + [vmem] * 3,
        out_specs=vmem,
        scratch_shapes=[pltpu.VMEM((2 * lines, columns + 2 * LANES), jnp.bfloat16)],
        compiler_params=limit,
    )(jnp.stack([place, rng_count]).astype(jnp.int32), offsets, kernel_index, cells, before, after)
    arrived = lax.all_to_all(packed, axes, 0, 0, tiled=True)

    pairs = [(own, own + lag) for own in range(dates) for lag in range(1, LAGS + 1) if own + lag < dates]
    count = len(pairs)
    first = [jnp.asarray(np.array(pairs, np.int32))] if count > UNROLLED_PAIRS else []
    looked = pl.pallas_call(
        functools.partial(pairs_kernel, chunk, count if first else pairs),
        out_shape=jax.ShapeDtypeStruct((peers, groups // az_count, out_width), jnp.float32),
        in_specs=[smem] * len(first) + [smem] + [vmem] * 3,
        out_specs=vmem,
        scratch_shapes=[
            pltpu.VMEM((dates, 4 * (groups * LOOK_AZ) // 2, held), jnp.bfloat16),
            pltpu.VMEM((2, 2 * LANES, 2 * LANES), jnp.bfloat16),
            pltpu.VMEM((count, 2, groups, up(chunk, LANES)), jnp.float32),
        ],
        compiler_params=limit,
    )(*first, range_shift, jnp.asarray(kernel_table()), jnp.asarray(lowpass_row(2 * LANES)), arrived)
    returned = lax.all_to_all(looked, axes, 0, 0, tiled=True)

    out = pl.pallas_call(
        functools.partial(unpack_kernel, used_lags, looks),
        out_shape=jax.ShapeDtypeStruct((2, LAGS, groups // az_count, looks * peers), jnp.float32),
        in_specs=[vmem],
        out_specs=vmem,
        compiler_params=limit,
    )(returned)
    return out[:, None]


HALO_LINES = 16
FOLD = 16
TAIL = 2 * FILTER_HALF


def sinc(value):
    angle = jnp.pi * value
    return jnp.where(angle == 0.0, 1.0, jnp.sin(angle) / jnp.where(angle == 0.0, 1.0, angle))


def tap_row(index):
    lane = lax.broadcasted_iota(jnp.int32, (1, LANES), 1)
    position = lane.astype(jnp.float32) - 3.0 - index.astype(jnp.float32) / KERNELS
    shaped = sinc(position) * (0.5 + 0.5 * jnp.cos(jnp.pi * position / 5.0))
    shaped = jnp.where(lane < TAPS, shaped, 0.0)
    return shaped / jnp.sum(shaped, axis=1, keepdims=True)


def row_line(row, az):
    quarter = HALO_LINES // LOOK_AZ
    within = row % HALO_LINES
    return HALO_LINES * ((row // HALO_LINES) ^ az) + LOOK_AZ * (within % quarter) + within // quarter


def prepare_kernel(offsets_hbm, index_hbm, slc_ref, side_ref, corner_ref, lines_ref, offsets_ref, index_ref, held_ref, semaphores):
    lines, columns = slc_ref.shape[1:]
    row = pl.multiple_of((1 - lax.axis_index("az")) * (lines - HALO_LINES), HALO_LINES)
    edge = pl.multiple_of((1 - lax.axis_index("rng")) * (columns - LANES), LANES)
    nearest, outermost = pl.ds(row, HALO_LINES), pl.ds(edge, LANES)
    moves = [
        (slc_ref.at[:, nearest, :], lines_ref),
        (slc_ref.at[:, :, outermost], side_ref),
        (slc_ref.at[:, nearest, outermost], corner_ref),
        (slc_ref, held_ref.at[:, :, pl.ds(LANES, columns)]),
        (offsets_hbm, offsets_ref),
        (index_hbm, index_ref),
    ]
    copies = [pltpu.make_async_copy(a, b, semaphores.at[i]) for i, (a, b) in enumerate(moves)]
    for copy in copies:
        copy.start()
    held_ref[:, :, :LANES] = jnp.zeros((2, lines, LANES), held_ref.dtype)
    held_ref[:, :, LANES + columns :] = jnp.zeros((2, lines, 2 * LANES), held_ref.dtype)
    for copy in copies:
        copy.wait()


def set_taps(offsets_ref, index_ref, line_ref, column_ref):
    az = lax.axis_index("az")
    lines = line_ref.shape[2] - HALO_LINES
    offsets, index = offsets_ref[...], index_ref[...]
    for half in range(2):
        shape = (HALO_LINES, lines + HALO_LINES)
        line = row_line(lax.broadcasted_iota(jnp.int32, shape, 0) + half * HALO_LINES, az)
        place = lax.broadcasted_iota(jnp.int32, shape, 1)
        source = jnp.where(place < lines, place, place + jnp.where(az == 0, 0, -lines - HALO_LINES))
        taps = banded(tap_row(index[:, 0:1]), source - line - offsets[:, 0:1] + 3)
        line_ref[half] = jnp.concatenate(halves(taps), axis=0)
    shape = (3 * LANES, LANES)
    distance = lax.broadcasted_iota(jnp.int32, shape, 0) - lax.broadcasted_iota(jnp.int32, shape, 1)
    distance = distance - (LANES - FILTER_HALF - 3) - offsets[:, 1:2]
    taps = banded(tap_row(index[:, 1:2]), distance)
    column_ref[...] = jnp.concatenate(halves(taps), axis=1)


def along_range(moved, column_ref, tiles):
    high, low = halves(moved)
    starts = range(0, tiles * LANES, LANES)
    high = jnp.concatenate([high[:, s : s + 3 * LANES] for s in starts], axis=0)
    low = jnp.concatenate([low[:, s : s + 3 * LANES] for s in starts], axis=0)
    total = dot(high, column_ref[...])
    return total[:, :LANES] + total[:, LANES:] + dot(low, column_ref[:, :LANES])


def early_kernel(tiles, offsets_ref, index_ref, held_ref, line_ref, column_ref, out_ref):
    set_taps(offsets_ref, index_ref, line_ref, column_ref)
    lines = held_ref.shape[1]
    early = out_ref.shape[0] // (2 * HALO_LINES)
    chunk = lax.axis_index("date") ^ (lax.axis_size("date") - 1)
    begin = pl.multiple_of((chunk * tiles + lax.axis_index("rng")) * LANES, LANES)
    moved = []
    for plane in range(2):
        both = dot(line_ref[0, :, :lines], held_ref[plane, :, pl.ds(begin, (early + 2) * LANES)])
        moved.append(both[:HALO_LINES] + both[HALO_LINES:])
    out_ref[...] = along_range(jnp.concatenate(moved, axis=0), column_ref, early).astype(jnp.bfloat16)


def whole_lines(taps, sources):
    moved = [[], []]
    for source in sources:
        both = dot(taps, source)
        for half in range(2):
            at = 2 * half * HALO_LINES
            moved[half].append(both[at : at + HALO_LINES] + both[at + HALO_LINES : at + 2 * HALO_LINES])
    return jnp.concatenate(moved[0] + moved[1], axis=0)


def folded_tail(tile):
    lane = lax.broadcasted_iota(jnp.int32, (FOLD, LANES), 1) // TAIL
    folded = tile[:FOLD]
    for part in range(1, tile.shape[0] // FOLD):
        folded = jnp.where(lane == part, pltpu.roll(tile[part * FOLD : (part + 1) * FOLD], part * TAIL, 1), folded)
    return folded.astype(jnp.bfloat16)


def first_kernel(tiles, step, side_ref, corner_ref, lines_ref, held_ref, line_ref, column_ref, out_ref, wide_ref):
    lines, width = held_ref.shape[1:]
    block = lax.axis_index("rng")
    zero = jnp.zeros((lines, LANES), wide_ref.dtype)
    for plane in range(2):
        side, corner = side_ref[plane], corner_ref[plane]
        right = width - 2 * LANES
        wide_ref[plane, :lines, :LANES] = jnp.where(block > 0, side, zero)
        wide_ref[plane, :lines, LANES:right] = held_ref[plane, :, LANES:right]
        wide_ref[plane, :lines, right : right + LANES] = jnp.where(block == 0, side, zero)
        wide_ref[plane, :lines, right + LANES :] = zero
        wide_ref[plane, lines:, :LANES] = jnp.where(block > 0, corner, zero[:HALO_LINES])
        wide_ref[plane, lines:, LANES:right] = lines_ref[plane]
        wide_ref[plane, lines:, right : right + LANES] = jnp.where(block == 0, corner, zero[:HALO_LINES])
        wide_ref[plane, lines:, right + LANES :] = zero[:HALO_LINES]
    taps = jnp.concatenate([line_ref[0], line_ref[1]], axis=0)
    chunk = lax.axis_index("date") ^ step
    read = pl.ds(pl.multiple_of(chunk * tiles * LANES, LANES), (tiles + 3) * LANES)
    moved = whole_lines(taps, [wide_ref[plane, :, read] for plane in range(2)])
    total = along_range(moved, column_ref, tiles + 1)
    rows = tiles * 2 * lines
    out_ref[:rows] = total[:rows].astype(jnp.bfloat16)
    out_ref[rows : rows + FOLD] = folded_tail(total[rows:])
    out_ref[rows + FOLD :] = jnp.zeros((out_ref.shape[0] - rows - FOLD, LANES), out_ref.dtype)


def rest_kernel(tiles, steps, wide_ref, line_ref, column_ref, *outs):
    lines = wide_ref.shape[1] - HALO_LINES
    block = lax.axis_index("rng")
    date = lax.axis_index("date")
    taps = jnp.concatenate([line_ref[0], line_ref[1]], axis=0)
    rows = 2 * lines
    for step, out_ref in zip(steps, outs):
        read = pl.ds(pl.multiple_of((date ^ step) * tiles * LANES, LANES), (tiles + 3) * LANES)
        moved = whole_lines(taps, [wide_ref[plane, :, read] for plane in range(2)])
        total = along_range(moved, column_ref, tiles + 1)
        tail = folded_tail(total[tiles * rows :])
        total = total.astype(jnp.bfloat16)
        if out_ref.shape[0] == tiles * rows + FOLD:
            out_ref[: tiles * rows] = total[: tiles * rows]
            out_ref[tiles * rows :] = tail
            continue
        for tile in range(tiles - 1):
            near, far = (total[at * rows + lines : (at + 1) * rows] for at in (tile, tile + 1))
            out_ref[tile * lines : (tile + 1) * lines] = jnp.where(block == 0, near, far)
        begin = (tiles - 1) * rows
        out_ref[begin // 2 : begin // 2 + rows] = jnp.where(block == 0, total[begin : begin + rows], total[:rows])
        out_ref[begin // 2 + rows :] = tail


def filter_kernel(pairs, shift_hbm, early_ref, out_ref, spread_ref, shift_ref, semaphore):
    copy = pltpu.make_async_copy(shift_hbm, shift_ref, semaphore)
    copy.start()
    lines = 2 * HALO_LINES
    spread_ref[...] = jnp.zeros_like(spread_ref)
    for tile in range(early_ref.shape[0] // lines):
        begin = pl.multiple_of((tile + lax.axis_index("rng")) * 2 * lines, FOLD)
        spread_ref[pl.ds(begin, lines), :] = early_ref[tile * lines : (tile + 1) * lines]
    date = lax.axis_index("date")
    spacing = lax.broadcasted_iota(jnp.int32, (1, 2 * LANES), 1).astype(jnp.float32) - FILTER_HALF
    window = 0.4 * sinc(0.4 * spacing) * (0.54 + 0.46 * jnp.cos(jnp.pi * spacing / (FILTER_HALF + 1)))
    window = jnp.where(jnp.abs(spacing) <= FILTER_HALF, window, 0.0)
    copy.wait()
    for place, (first, second) in enumerate(pairs):
        gap = shift_ref[date ^ first] - shift_ref[date ^ second]
        angle = jnp.where(jnp.abs(spacing) <= FILTER_HALF, jnp.pi * gap * spacing, 0.0)
        for part, taps in enumerate((window * jnp.cos(angle), window * jnp.sin(angle))):
            spread = jnp.broadcast_to(taps, (LANES, 2 * LANES))
            spread = pltpu.roll(spread, 0, 1, stride=1, stride_axis=0)
            high, low = halves(spread)
            out_ref[place, 0, part * LANES : (part + 1) * LANES, :] = high
            out_ref[place, 1, part * LANES : (part + 1) * LANES, :] = low


def looks_kernel(pairs, dates, weight_ref, *refs):
    early_ref, chunks, outs = refs[0], list(refs[1 : dates + 1][::-1]), refs[dates + 1 : 2 * dates + 1]
    whole_ref, window_ref, product_ref = refs[-3:]
    groups, lines = outs[0].shape[0], outs[0].shape[0] * LOOK_AZ
    rows = 2 * lines
    blocks = (chunks[0].shape[0] - FOLD) // rows
    looks = blocks * LANES // LOOK_RG
    date = lax.axis_index("date")
    block = lax.axis_index("rng")
    early = blocks - 1
    whole_ref[: blocks * rows] = early_ref[...]
    for tile in range(early):
        begin = pl.multiple_of((tile + block) * rows, FOLD)
        whole_ref[pl.ds(begin + lines, lines), :] = chunks[-1][tile * lines : (tile + 1) * lines]
    begin = pl.multiple_of((1 - block) * early * rows, FOLD)
    whole_ref[pl.ds(begin, rows), :] = chunks[-1][early * lines : early * lines + rows]
    whole_ref[blocks * rows :] = chunks[-1][early * lines + rows :]
    chunks[-1] = whole_ref
    az = lax.axis_index("az")
    upper = lax.broadcasted_iota(jnp.int32, (groups, LANES), 0) // (groups // 2) == az
    for step, chunk_ref in enumerate(chunks):
        window_ref[step, :, :LANES] = chunk_ref[: blocks * rows]
        window_ref[step, : (blocks - 1) * rows, LANES:] = chunk_ref[rows : blocks * rows]
        folded = chunk_ref[blocks * rows : blocks * rows + FOLD].astype(jnp.float32)
        for part in range(rows // FOLD):
            value = pltpu.roll(folded, LANES - part * TAIL, 1) if part else folded
            at = pl.ds((blocks - 1) * rows + part * FOLD, FOLD)
            window_ref[step, at, LANES:] = value.astype(jnp.bfloat16)
    for place, (first, second) in enumerate(pairs):
        def filtered(step):
            total = dot_nt(window_ref[step], weight_ref[place, 0]) + dot_nt(window_ref[step], weight_ref[place, 1])
            total = total.reshape(blocks, 2, 2, HALO_LINES, 2 * LANES)
            re, im = total[:, :, 0], total[:, :, 1]
            return re[..., :LANES], im[..., :LANES], re[..., LANES:], im[..., LANES:]

        cos_re, cos_im, sin_re, sin_im = filtered(first)
        master_re, master_im = cos_re + sin_im, cos_im - sin_re
        cos_re, cos_im, sin_re, sin_im = filtered(second)
        partner_re, partner_im = cos_re - sin_im, cos_im + sin_re
        for part, product in enumerate(
            (
                master_re * partner_re + master_im * partner_im,
                master_im * partner_re - master_re * partner_im,
            )
        ):
            summed = product[:, :, :groups] + product[:, :, groups:]
            at = pl.ds((place * 2 + part) * groups, groups)
            for k in range(blocks):
                both = [summed[k, half] + pltpu.roll(summed[k, half], groups // 2, 0) for half in range(2)]
                product_ref[at, k * LANES : (k + 1) * LANES] = jnp.where(upper, both[0], both[1])

    out_width = outs[0].shape[1]
    column = lax.broadcasted_iota(jnp.int32, (product_ref.shape[1], out_width), 0)
    lane = lax.broadcasted_iota(jnp.int32, (product_ref.shape[1], out_width), 1)
    collect = jnp.where(column // LOOK_RG == lane % looks, 1.0, 0.0).astype(jnp.bfloat16)
    high, low = halves(product_ref[...])
    total = (dot(high, collect) + dot(low, collect)) * (1.0 / (LOOK_AZ * LOOK_RG))
    total = total.reshape(len(pairs), 2, groups, out_width)
    own_lane = lax.broadcasted_iota(jnp.int32, (groups, out_width), 1) // looks
    for step, out_ref in enumerate(outs):
        value = jnp.zeros((groups, out_width), jnp.float32)
        for place, pair in enumerate(pairs):
            if step in pair:
                other = pair[1] if pair[0] == step else pair[0]
                lag = (date ^ other) - (date ^ step)
                for part in range(2):
                    signed = -total[place, part] if part == 1 and pair[1] == step else total[place, part]
                    value = jnp.where(own_lane == (lag - 1) * 2 + part, signed, value)
        out_ref[...] = value


def place_kernel(used_lags, looks, *refs):
    out_ref = refs[-1]
    groups, columns = out_ref.shape[2:]
    date = lax.axis_index("date")
    lane = lax.broadcasted_iota(jnp.int32, (groups, LANES), 1) // looks
    out_ref[...] = jnp.zeros_like(out_ref)
    each = LANES // looks
    for step, recv_ref in enumerate(refs[:-1][::-1]):
        chunk = date ^ step
        for lag in range(used_lags):
            for part in range(2):
                tile, group = divmod(lag * 2 + part, each)
                block = recv_ref[:, tile * LANES : (tile + 1) * LANES]
                block = pltpu.roll(block, lax.bitwise_and(looks * (chunk - group), LANES - 1), 1)
                out_ref[part, lag] = jnp.where(lane == chunk, block, out_ref[part, lag])


def tiled_body(slc, offsets, kernel_index, range_shift):
    dates = lax.axis_size("date")
    lines, columns = slc.shape[2], slc.shape[3]
    chunk = columns // dates
    looks = chunk // LOOK_RG
    groups = lines // LOOK_AZ
    out_width = up(min(LAGS, dates - 1) * 2 * looks, LANES)
    vmem = pl.BlockSpec(memory_space=pltpu.VMEM)
    hbm = pl.BlockSpec(memory_space=pltpu.HBM)
    limit = pltpu.CompilerParams(vmem_limit_bytes=32 * 1024 * 1024)
    bf16 = jnp.bfloat16
    cells, offsets, kernel_index, range_shift = (
        pltpu.with_memory_space_constraint(value, pltpu.HBM)
        for value in (slc.reshape(2, lines, columns), offsets, kernel_index, range_shift)
    )
    tiles = chunk // LANES
    chunk_rows = tiles * 2 * lines

    side, corner, halo_lines, offsets, kernel_index, held = pl.pallas_call(
        prepare_kernel,
        out_shape=[
            jax.ShapeDtypeStruct((2, lines, LANES), bf16),
            jax.ShapeDtypeStruct((2, HALO_LINES, LANES), bf16),
            jax.ShapeDtypeStruct((2, HALO_LINES, columns), bf16),
            jax.ShapeDtypeStruct(offsets.shape, jnp.int32),
            jax.ShapeDtypeStruct(kernel_index.shape, jnp.int32),
            jax.ShapeDtypeStruct((2, lines, columns + 3 * LANES), bf16),
        ],
        in_specs=[hbm] * 3,
        out_specs=[vmem] * 6,
        scratch_shapes=[pltpu.SemaphoreType.DMA((6,))],
        compiler_params=limit,
    )(offsets, kernel_index, cells)
    swap = [(0, 1), (1, 0)]
    side = lax.ppermute(side, "rng", swap)
    corner = lax.ppermute(corner, ("rng", "az"), [(0, 3), (1, 2), (2, 1), (3, 0)])
    halo_lines = lax.ppermute(halo_lines, "az", swap)

    def swapped(value, step):
        return lax.ppermute(value, "date", [(i, i ^ step) for i in range(dates)])

    steps = range(dates - 1, 0, -1)
    early_rows = (tiles - 1) * lines
    line_taps, column_taps, early = pl.pallas_call(
        functools.partial(early_kernel, tiles),
        out_shape=[
            jax.ShapeDtypeStruct((2, 2 * HALO_LINES, lines + HALO_LINES), bf16),
            jax.ShapeDtypeStruct((3 * LANES, 2 * LANES), bf16),
            jax.ShapeDtypeStruct((early_rows, LANES), bf16),
        ],
        in_specs=[vmem] * 3,
        out_specs=[vmem] * 3,
        compiler_params=limit,
    )(offsets, kernel_index, held)
    early = swapped(early, steps[0])
    first, wide = pl.pallas_call(
        functools.partial(first_kernel, tiles, steps[1]),
        out_shape=[
            jax.ShapeDtypeStruct((chunk_rows + 2 * FOLD, LANES), bf16),
            jax.ShapeDtypeStruct((2, lines + HALO_LINES, columns + 3 * LANES), bf16),
        ],
        in_specs=[vmem] * 6,
        out_specs=[vmem] * 2,
        compiler_params=limit,
    )(side, corner, halo_lines, held, line_taps, column_taps)
    first = swapped(first, steps[1])
    others = [steps[0], *steps[2:], 0]
    rest = pl.pallas_call(
        functools.partial(rest_kernel, tiles, others),
        out_shape=[
            jax.ShapeDtypeStruct((chunk_rows + FOLD - (early_rows if step == steps[0] else 0), LANES), bf16)
            for step in others
        ],
        in_specs=[vmem] * 3,
        out_specs=[vmem] * (dates - 1),
        compiler_params=limit,
    )(wide, line_taps, column_taps)
    rest = [swapped(rows, step) if step else rows for rows, step in zip(rest, others)]
    chunks = [rest[0], first, *rest[1:]]

    pairs = [(first, second) for first in range(dates) for second in range(first + 1, dates)]
    weights, early = pl.pallas_call(
        functools.partial(filter_kernel, pairs),
        out_shape=[
            jax.ShapeDtypeStruct((len(pairs), 2, 2 * LANES, 2 * LANES), bf16),
            jax.ShapeDtypeStruct((chunk_rows, LANES), bf16),
        ],
        in_specs=[hbm, vmem],
        out_specs=[vmem] * 2,
        scratch_shapes=[pltpu.SMEM(range_shift.shape, jnp.float32), pltpu.SemaphoreType.DMA],
        compiler_params=limit,
        cost_estimate=pl.CostEstimate(flops=700_000_000, bytes_accessed=0, transcendentals=0),
    )(range_shift, early)
    looked = pl.pallas_call(
        functools.partial(looks_kernel, pairs, dates),
        out_shape=[jax.ShapeDtypeStruct((groups, out_width), jnp.float32)] * dates,
        in_specs=[vmem] * (2 + dates),
        out_specs=[vmem] * dates,
        scratch_shapes=[
            pltpu.VMEM((chunk_rows + FOLD, LANES), bf16),
            pltpu.VMEM((dates, chunk_rows, 2 * LANES), bf16),
            pltpu.VMEM((len(pairs) * 2 * groups, chunk), jnp.float32),
        ],
        compiler_params=limit,
    )(weights, early, *chunks)
    out = pl.pallas_call(
        functools.partial(place_kernel, min(LAGS, dates - 1), looks),
        out_shape=jax.ShapeDtypeStruct((2, LAGS, groups, looks * dates), jnp.float32),
        in_specs=[vmem] * dates,
        out_specs=vmem,
        compiler_params=limit,
    )(*[swapped(looked[step], step) for step in steps], looked[0])
    return out[:, None]


def body(slc, offsets, kernel_index, range_shift):
    dates, az_count = (lax.axis_size(a) for a in ("date", "az"))
    lines, columns = slc.shape[2], slc.shape[3]
    whole_tiles = columns % (dates * LANES) == 0 and columns % (dates * LOOK_RG) == 0
    one_row = columns // LOOK_RG == LANES and range_shift.shape[0] == dates
    few = dates & (dates - 1) == 0 and dates - 1 <= LAGS
    folds = lines == 2 * HALO_LINES and lax.axis_size("rng") == 2 and dates >= 4 and 2 * lines // FOLD * TAIL <= LANES
    if az_count == 2 and whole_tiles and one_row and few and folds:
        return tiled_body(slc, offsets, kernel_index, range_shift)
    return chunked_body(slc, offsets, kernel_index, range_shift)


def solution(mesh):
    return jax.shard_map(
        body,
        mesh=mesh,
        in_specs=(
            P(None, ("groups", "date"), "az", "rng"),
            P(("groups", "date"), None),
            P(("groups", "date"), None),
            P("groups"),
        ),
        out_specs=P(None, ("groups", "date"), None, "az", "rng"),
        check_vma=False,
    )
```

```python
import functools

import jax
import jax.numpy as jnp
import numpy as np
from jax import lax
from jax.experimental import pallas as pl
from jax.experimental.pallas import tpu as pltpu
from jax.sharding import PartitionSpec as P

LAGS = 8
KERNELS = 16
TAPS = 8
FILTER_HALF = 8
FILTER_TAPS = 2 * FILTER_HALF + 1
LOOK_AZ = 4
LOOK_RG = 20
LANES = 128
META = 3
UNROLLED_PAIRS = 12


def up(value, unit):
    return -(-value // unit) * unit


def kernel_table():
    position = np.arange(TAPS) - 3.0 - np.arange(KERNELS)[:, None] / KERNELS
    shaped = np.sinc(position) * (0.5 + 0.5 * np.cos(np.pi * position / 5.0))
    table = np.zeros((KERNELS, LANES), np.float32)
    table[:, :TAPS] = shaped / shaped.sum(1, keepdims=True)
    return table


def lowpass_row(width):
    t = np.arange(FILTER_TAPS) - FILTER_HALF
    row = np.zeros((1, width), np.float32)
    row[0, :FILTER_TAPS] = 0.4 * np.sinc(0.4 * t) * (0.54 + 0.46 * np.cos(np.pi * t / (FILTER_HALF + 1)))
    return row


def halves(value):
    high = value.astype(jnp.bfloat16)
    return high, (value - high.astype(jnp.float32)).astype(jnp.bfloat16)


def dot(a, b):
    return jnp.dot(a, b, preferred_element_type=jnp.float32)


def dot_nt(a, b):
    return lax.dot_general(a, b, (((1,), (1,)), ((), ())), preferred_element_type=jnp.float32)


def pack_kernel(chunk, place_ref, offsets_ref, index_ref, slc_ref, before_ref, after_ref, out_ref, wide_ref):
    columns = slc_ref.shape[1]
    wide = out_ref.shape[2]
    first = place_ref[0] == 0
    last = place_ref[0] == place_ref[1] - 1
    zero = jnp.zeros_like(before_ref[...])
    wide_ref[:, :LANES] = jnp.where(first, zero, before_ref[...])
    wide_ref[:, LANES : LANES + columns] = slc_ref[...]
    wide_ref[:, LANES + columns :] = jnp.where(last, zero, after_ref[...])
    lane = lax.broadcasted_iota(jnp.int32, (slc_ref.shape[0], wide), 1)
    numbers = [offsets_ref[0, 0], index_ref[0, 0], index_ref[0, 1]]
    for j in range(out_ref.shape[0]):
        start = LANES + chunk * j - FILTER_HALF - 3 + offsets_ref[0, 1]
        tile = lax.shift_right_logical(start, 7)
        within = lax.bitwise_and(start, LANES - 1)
        window = wide_ref[:, pl.ds(pl.multiple_of(tile * LANES, LANES), wide + LANES)].astype(jnp.float32)
        moved = pltpu.roll(window, wide + LANES - within, 1)[:, :wide]
        for slot, number in enumerate(numbers):
            moved = jnp.where(lane == wide - META + slot, number.astype(jnp.float32), moved)
        out_ref[j] = moved.astype(jnp.bfloat16)


def picked_taps(table, index):
    row = lax.broadcasted_iota(jnp.int32, table.shape, 0).astype(jnp.float32)
    return jnp.sum(jnp.where(row == index, table, 0.0), axis=0, keepdims=True)


def banded(taps, distance):
    out = jnp.zeros(distance.shape, jnp.float32)
    for q in range(TAPS):
        out = jnp.where(distance == q, taps[:, q : q + 1], out)
    return out


def pairs_kernel(chunk, pairs, *refs):
    if isinstance(pairs, int):
        table_of_pairs, refs = refs[0], refs[1:]
    shift_ref, table_ref, lowpass_ref, recv_ref, out_ref, resampled_ref, weight_ref, product_ref = refs
    sources, rows, wide = recv_ref.shape
    dates = shift_ref.shape[0]
    az_count = sources // dates
    own_lines = rows // 2
    lines = own_lines * az_count
    groups = lines // LOOK_AZ
    looks = chunk // LOOK_RG
    table = table_ref[...]
    held = resampled_ref.shape[2]

    out_row = lax.broadcasted_iota(jnp.int32, (lines, lines), 0)
    in_row = lax.broadcasted_iota(jnp.int32, (lines, lines), 1)
    line = LOOK_AZ * (out_row % groups) + out_row // groups
    line_distance = (in_row - line + 3).astype(jnp.float32)
    span = min(2 * LANES, wide)
    column_distance = (
        lax.broadcasted_iota(jnp.int32, (span, LANES), 0) - lax.broadcasted_iota(jnp.int32, (span, LANES), 1)
    ).astype(jnp.float32)
    for date in range(dates):
        numbers = recv_ref[date * az_count, 0:16, wide - LANES :].astype(jnp.float32)[0:1, LANES - META :]
        line_offset, line_index, column_index = (numbers[:, s : s + 1] for s in range(META))
        line_taps = banded(picked_taps(table, line_index), line_distance - line_offset)
        line_taps = jnp.concatenate(halves(line_taps), axis=0)
        column_high, column_low = halves(banded(picked_taps(table, column_index), column_distance))
        moved = []
        for plane in range(2):
            rows_of = slice(plane * own_lines, (plane + 1) * own_lines)
            source = jnp.concatenate([recv_ref[date * az_count + a, rows_of, :] for a in range(az_count)], axis=0)
            both = dot(line_taps, source)
            moved.append(both[:lines] + both[lines:])
        moved_high, moved_low = halves(jnp.concatenate(moved, axis=0))
        for begin in range(0, held, LANES):
            end = min(begin + span, wide)
            taken = end - begin
            total = dot(moved_high[:, begin:end], column_high[:taken])
            total += dot(moved_low[:, begin:end], column_high[:taken])
            total += dot(moved_high[:, begin:end], column_low[:taken])
            resampled_ref[date, :, begin : begin + LANES] = total.astype(jnp.bfloat16)

    window = lowpass_ref[...]
    spacing = lax.broadcasted_iota(jnp.int32, window.shape, 1).astype(jnp.float32) - FILTER_HALF
    span = min(2 * LANES, held)

    def one_pair(place, own, other):
        gap = shift_ref[own] - shift_ref[other]
        angle = jnp.where(jnp.abs(spacing) <= FILTER_HALF, jnp.pi * gap * spacing, 0.0)
        for part, taps in enumerate((window * jnp.cos(angle), window * jnp.sin(angle))):
            spread = jnp.broadcast_to(taps, (LANES, 2 * LANES))
            spread = pltpu.roll(spread, 0, 1, stride=1, stride_axis=0)
            high, low = halves(spread)
            weight_ref[0, part * LANES : (part + 1) * LANES, :] = high
            weight_ref[1, part * LANES : (part + 1) * LANES, :] = low
        both = jnp.concatenate([resampled_ref[own], resampled_ref[other]], axis=0)
        for begin in range(0, up(chunk, LANES), LANES):
            end = min(begin + span, held)
            taken = end - begin
            total = dot_nt(both[:, begin:end], weight_ref[0, :, :taken])
            total += dot_nt(both[:, begin:end], weight_ref[1, :, :taken])
            cos, sin = total[:, :LANES], total[:, LANES:]
            re, im = slice(0, lines), slice(lines, 2 * lines)
            master_re = cos[re] + sin[im]
            master_im = cos[im] - sin[re]
            re, im = slice(2 * lines, 3 * lines), slice(3 * lines, 4 * lines)
            partner_re = cos[re] - sin[im]
            partner_im = cos[im] + sin[re]
            for part, product in enumerate(
                (
                    master_re * partner_re + master_im * partner_im,
                    master_im * partner_re - master_re * partner_im,
                )
            ):
                summed = sum(product[k * groups : (k + 1) * groups] for k in range(LOOK_AZ))
                product_ref[place, part, :, begin : begin + LANES] = summed

    if isinstance(pairs, int):
        count = pairs

        def step(place, carry):
            one_pair(place, table_of_pairs[place, 0], table_of_pairs[place, 1])
            return carry

        lax.fori_loop(0, count, step, 0)
    else:
        count = len(pairs)
        for place, (own, other) in enumerate(pairs):
            one_pair(place, own, other)

    out_width = out_ref.shape[2]
    column = lax.broadcasted_iota(jnp.int32, (product_ref.shape[3], out_width), 0)
    lane = lax.broadcasted_iota(jnp.int32, (product_ref.shape[3], out_width), 1)
    collect = jnp.where(column // LOOK_RG == lane % looks, 1.0, 0.0).astype(jnp.bfloat16)
    high, low = halves(product_ref[...].reshape(count * 2 * groups, product_ref.shape[3]))
    total = (dot(high, collect) + dot(low, collect)) * (1.0 / (LOOK_AZ * LOOK_RG))
    total = total.reshape(count, 2, groups, out_width)
    own_lane = lax.broadcasted_iota(jnp.int32, (groups, out_width), 1) // looks
    place = 0
    for own in range(dates):
        value = jnp.zeros((groups, out_width), jnp.float32)
        for lag in range(min(LAGS, dates - 1 - own)):
            for part in range(2):
                value = jnp.where(own_lane == lag * 2 + part, total[place, part], value)
            place += 1
        out_ref[own * az_count : (own + 1) * az_count] = value.reshape(az_count, groups // az_count, out_width)


def unpack_kernel(used_lags, looks, recv_ref, out_ref):
    sources, groups, width = recv_ref.shape
    columns = out_ref.shape[-1]
    lane = lax.broadcasted_iota(jnp.int32, (groups, columns), 1) // looks
    out_ref[...] = jnp.zeros_like(out_ref)
    for lag in range(used_lags):
        for part in range(2):
            value = jnp.zeros((groups, columns), jnp.float32)
            for source in range(sources):
                block = recv_ref[source]
                if width != columns:
                    block = block[:, :columns]
                shift = looks * (source - lag * 2 - part) % columns
                if shift:
                    block = pltpu.roll(block, shift, 1)
                value = jnp.where(lane == source, block, value)
            out_ref[part, lag] = value


def chunked_body(slc, offsets, kernel_index, range_shift):
    axes = ("date", "az")
    date_count, az_count, rng_count = (lax.axis_size(a) for a in ("date", "az", "rng"))
    peers = date_count * az_count
    lines, columns = slc.shape[2], slc.shape[3]
    dates = range_shift.shape[0]
    chunk = columns // peers
    looks = chunk // LOOK_RG
    groups = lines * az_count // LOOK_AZ
    wide = up(chunk + 2 * FILTER_HALF + TAPS - 1 + META, LANES)
    held = up(chunk + 2 * FILTER_HALF, LANES)
    used_lags = min(LAGS, dates - 1)
    out_width = up(used_lags * 2 * looks, LANES)
    vmem = pl.BlockSpec(memory_space=pltpu.VMEM)
    smem = pl.BlockSpec(memory_space=pltpu.SMEM)
    limit = pltpu.CompilerParams(vmem_limit_bytes=32 * 1024 * 1024)

    cells = slc.reshape(2 * lines, columns)
    place = lax.axis_index("rng")
    if rng_count == 2:
        edge = jnp.where(place == 0, cells[:, columns - LANES :], cells[:, :LANES])
        before = after = lax.ppermute(edge, "rng", [(0, 1), (1, 0)])
    else:
        forth = [(i, i + 1) for i in range(rng_count - 1)]
        before = lax.ppermute(cells[:, columns - LANES :], "rng", forth)
        after = lax.ppermute(cells[:, :LANES], "rng", [(b, a) for a, b in forth])

    packed = pl.pallas_call(
        functools.partial(pack_kernel, chunk),
        out_shape=jax.ShapeDtypeStruct((peers, 2 * lines, wide), jnp.bfloat16),
        in_specs=[smem] * 3 + [vmem] * 3,
        out_specs=vmem,
        scratch_shapes=[pltpu.VMEM((2 * lines, columns + 2 * LANES), jnp.bfloat16)],
        compiler_params=limit,
    )(jnp.stack([place, rng_count]).astype(jnp.int32), offsets, kernel_index, cells, before, after)
    arrived = lax.all_to_all(packed, axes, 0, 0, tiled=True)

    pairs = [(own, own + lag) for own in range(dates) for lag in range(1, LAGS + 1) if own + lag < dates]
    count = len(pairs)
    first = [jnp.asarray(np.array(pairs, np.int32))] if count > UNROLLED_PAIRS else []
    looked = pl.pallas_call(
        functools.partial(pairs_kernel, chunk, count if first else pairs),
        out_shape=jax.ShapeDtypeStruct((peers, groups // az_count, out_width), jnp.float32),
        in_specs=[smem] * len(first) + [smem] + [vmem] * 3,
        out_specs=vmem,
        scratch_shapes=[
            pltpu.VMEM((dates, 4 * (groups * LOOK_AZ) // 2, held), jnp.bfloat16),
            pltpu.VMEM((2, 2 * LANES, 2 * LANES), jnp.bfloat16),
            pltpu.VMEM((count, 2, groups, up(chunk, LANES)), jnp.float32),
        ],
        compiler_params=limit,
    )(*first, range_shift, jnp.asarray(kernel_table()), jnp.asarray(lowpass_row(2 * LANES)), arrived)
    returned = lax.all_to_all(looked, axes, 0, 0, tiled=True)

    out = pl.pallas_call(
        functools.partial(unpack_kernel, used_lags, looks),
        out_shape=jax.ShapeDtypeStruct((2, LAGS, groups // az_count, looks * peers), jnp.float32),
        in_specs=[vmem],
        out_specs=vmem,
        compiler_params=limit,
    )(returned)
    return out[:, None]


HALO_LINES = 16
FOLD = 16
TAIL = 2 * FILTER_HALF


def sinc(value):
    angle = jnp.pi * value
    return jnp.where(angle == 0.0, 1.0, jnp.sin(angle) / jnp.where(angle == 0.0, 1.0, angle))


def tap_row(index):
    lane = lax.broadcasted_iota(jnp.int32, (1, LANES), 1)
    position = lane.astype(jnp.float32) - 3.0 - index.astype(jnp.float32) / KERNELS
    shaped = sinc(position) * (0.5 + 0.5 * jnp.cos(jnp.pi * position / 5.0))
    shaped = jnp.where(lane < TAPS, shaped, 0.0)
    return shaped / jnp.sum(shaped, axis=1, keepdims=True)


def row_line(row, az):
    quarter = HALO_LINES // LOOK_AZ
    within = row % HALO_LINES
    return HALO_LINES * ((row // HALO_LINES) ^ az) + LOOK_AZ * (within % quarter) + within // quarter


def prepare_kernel(offsets_hbm, index_hbm, slc_ref, side_ref, corner_ref, lines_ref, line_ref, column_ref, held_ref, offsets_ref, index_ref, semaphores):
    lines, columns = slc_ref.shape[1:]
    az = lax.axis_index("az")
    row = pl.multiple_of((1 - az) * (lines - HALO_LINES), HALO_LINES)
    edge = pl.multiple_of((1 - lax.axis_index("rng")) * (columns - LANES), LANES)
    nearest, outermost = pl.ds(row, HALO_LINES), pl.ds(edge, LANES)
    moves = [
        (offsets_hbm, offsets_ref),
        (index_hbm, index_ref),
        (slc_ref.at[:, :, outermost], side_ref),
        (slc_ref.at[:, nearest, outermost], corner_ref),
        (slc_ref.at[:, nearest, :], lines_ref),
        (slc_ref, held_ref.at[:, :, pl.ds(LANES, columns)]),
    ]
    copies = [pltpu.make_async_copy(a, b, semaphores.at[i]) for i, (a, b) in enumerate(moves)]
    for copy in copies:
        copy.start()
    held_ref[:, :, :LANES] = jnp.zeros((2, lines, LANES), held_ref.dtype)
    held_ref[:, :, LANES + columns :] = jnp.zeros((2, lines, 2 * LANES), held_ref.dtype)
    copies[0].wait()
    copies[1].wait()
    for half in range(2):
        shape = (HALO_LINES, lines + HALO_LINES)
        line = row_line(lax.broadcasted_iota(jnp.int32, shape, 0) + half * HALO_LINES, az)
        place = lax.broadcasted_iota(jnp.int32, shape, 1)
        source = jnp.where(place < lines, place, place + jnp.where(az == 0, 0, -lines - HALO_LINES))
        taps = banded(tap_row(index_ref[0, 0]), source - line - offsets_ref[0, 0] + 3)
        line_ref[half] = jnp.concatenate(halves(taps), axis=0)
    shape = (3 * LANES, LANES)
    distance = lax.broadcasted_iota(jnp.int32, shape, 0) - lax.broadcasted_iota(jnp.int32, shape, 1)
    distance = distance - (LANES - FILTER_HALF - 3) - offsets_ref[0, 1]
    taps = banded(tap_row(index_ref[0, 1]), distance)
    column_ref[...] = jnp.concatenate(halves(taps), axis=1)
    for copy in copies[2:]:
        copy.wait()


def along_range(moved, column_ref, tiles):
    high, low = halves(moved)
    starts = range(0, tiles * LANES, LANES)
    high = jnp.concatenate([high[:, s : s + 3 * LANES] for s in starts], axis=0)
    low = jnp.concatenate([low[:, s : s + 3 * LANES] for s in starts], axis=0)
    total = dot(high, column_ref[...])
    return total[:, :LANES] + total[:, LANES:] + dot(low, column_ref[:, :LANES])


def early_kernel(tiles, held_ref, line_ref, column_ref, out_ref):
    lines = held_ref.shape[1]
    early = out_ref.shape[0] // (2 * HALO_LINES)
    chunk = lax.axis_index("date") ^ (lax.axis_size("date") - 1)
    begin = pl.multiple_of((chunk * tiles + lax.axis_index("rng")) * LANES, LANES)
    moved = []
    for plane in range(2):
        both = dot(line_ref[0, :, :lines], held_ref[plane, :, pl.ds(begin, (early + 2) * LANES)])
        moved.append(both[:HALO_LINES] + both[HALO_LINES:])
    moved = jnp.concatenate(moved, axis=0)
    out_ref[...] = along_range(moved, column_ref, early).astype(jnp.bfloat16)


def whole_lines(taps, sources):
    moved = [[], []]
    for source in sources:
        both = dot(taps, source)
        for half in range(2):
            at = 2 * half * HALO_LINES
            moved[half].append(both[at : at + HALO_LINES] + both[at + HALO_LINES : at + 2 * HALO_LINES])
    return jnp.concatenate(moved[0] + moved[1], axis=0)


def folded_tail(tile):
    lane = lax.broadcasted_iota(jnp.int32, (FOLD, LANES), 1) // TAIL
    folded = tile[:FOLD]
    for part in range(1, tile.shape[0] // FOLD):
        folded = jnp.where(lane == part, pltpu.roll(tile[part * FOLD : (part + 1) * FOLD], part * TAIL, 1), folded)
    return folded.astype(jnp.bfloat16)


def first_kernel(tiles, step, side_ref, corner_ref, lines_ref, held_ref, line_ref, column_ref, out_ref, wide_ref):
    lines, width = held_ref.shape[1:]
    block = lax.axis_index("rng")
    zero = jnp.zeros((lines, LANES), wide_ref.dtype)
    for plane in range(2):
        side, corner = side_ref[plane], corner_ref[plane]
        right = width - 2 * LANES
        wide_ref[plane, :lines, :LANES] = jnp.where(block > 0, side, zero)
        wide_ref[plane, :lines, LANES:right] = held_ref[plane, :, LANES:right]
        wide_ref[plane, :lines, right : right + LANES] = jnp.where(block == 0, side, zero)
        wide_ref[plane, :lines, right + LANES :] = zero
        wide_ref[plane, lines:, :LANES] = jnp.where(block > 0, corner, zero[:HALO_LINES])
        wide_ref[plane, lines:, LANES:right] = lines_ref[plane]
        wide_ref[plane, lines:, right : right + LANES] = jnp.where(block == 0, corner, zero[:HALO_LINES])
        wide_ref[plane, lines:, right + LANES :] = zero[:HALO_LINES]
    taps = jnp.concatenate([line_ref[0], line_ref[1]], axis=0)
    chunk = lax.axis_index("date") ^ step
    read = pl.ds(pl.multiple_of(chunk * tiles * LANES, LANES), (tiles + 3) * LANES)
    moved = whole_lines(taps, [wide_ref[plane, :, read] for plane in range(2)])
    total = along_range(moved, column_ref, tiles + 1)
    rows = tiles * 2 * lines
    out_ref[:rows] = total[:rows].astype(jnp.bfloat16)
    out_ref[rows : rows + FOLD] = folded_tail(total[rows:])
    out_ref[rows + FOLD :] = jnp.zeros((out_ref.shape[0] - rows - FOLD, LANES), out_ref.dtype)


def rest_kernel(tiles, steps, wide_ref, line_ref, column_ref, *outs):
    lines = wide_ref.shape[1] - HALO_LINES
    block = lax.axis_index("rng")
    date = lax.axis_index("date")
    taps = jnp.concatenate([line_ref[0], line_ref[1]], axis=0)
    rows = 2 * lines
    for step, out_ref in zip(steps, outs):
        read = pl.ds(pl.multiple_of((date ^ step) * tiles * LANES, LANES), (tiles + 3) * LANES)
        moved = whole_lines(taps, [wide_ref[plane, :, read] for plane in range(2)])
        total = along_range(moved, column_ref, tiles + 1)
        tail = folded_tail(total[tiles * rows :])
        total = total.astype(jnp.bfloat16)
        if out_ref.shape[0] == tiles * rows + FOLD:
            out_ref[: tiles * rows] = total[: tiles * rows]
            out_ref[tiles * rows :] = tail
            continue
        for tile in range(tiles - 1):
            near, far = (total[at * rows + lines : (at + 1) * rows] for at in (tile, tile + 1))
            out_ref[tile * lines : (tile + 1) * lines] = jnp.where(block == 0, near, far)
        begin = (tiles - 1) * rows
        out_ref[begin // 2 : begin // 2 + rows] = jnp.where(block == 0, total[begin : begin + rows], total[:rows])
        out_ref[begin // 2 + rows :] = tail


def filter_kernel(pairs, shift_hbm, early_ref, out_ref, spread_ref, shift_ref, semaphore):
    copy = pltpu.make_async_copy(shift_hbm, shift_ref, semaphore)
    copy.start()
    lines = 2 * HALO_LINES
    spread_ref[...] = jnp.zeros_like(spread_ref)
    for tile in range(early_ref.shape[0] // lines):
        begin = pl.multiple_of((tile + lax.axis_index("rng")) * 2 * lines, FOLD)
        spread_ref[pl.ds(begin, lines), :] = early_ref[tile * lines : (tile + 1) * lines]
    date = lax.axis_index("date")
    spacing = lax.broadcasted_iota(jnp.int32, (1, 2 * LANES), 1).astype(jnp.float32) - FILTER_HALF
    window = 0.4 * sinc(0.4 * spacing) * (0.54 + 0.46 * jnp.cos(jnp.pi * spacing / (FILTER_HALF + 1)))
    window = jnp.where(jnp.abs(spacing) <= FILTER_HALF, window, 0.0)
    copy.wait()
    for place, (first, second) in enumerate(pairs):
        gap = shift_ref[date ^ first] - shift_ref[date ^ second]
        angle = jnp.where(jnp.abs(spacing) <= FILTER_HALF, jnp.pi * gap * spacing, 0.0)
        for part, taps in enumerate((window * jnp.cos(angle), window * jnp.sin(angle))):
            spread = jnp.broadcast_to(taps, (LANES, 2 * LANES))
            spread = pltpu.roll(spread, 0, 1, stride=1, stride_axis=0)
            high, low = halves(spread)
            out_ref[place, 0, part * LANES : (part + 1) * LANES, :] = high
            out_ref[place, 1, part * LANES : (part + 1) * LANES, :] = low


def looks_kernel(pairs, dates, weight_ref, *refs):
    early_ref, chunks, outs = refs[0], list(refs[1 : dates + 1][::-1]), refs[dates + 1 : 2 * dates + 1]
    whole_ref, window_ref, product_ref = refs[-3:]
    groups, lines = outs[0].shape[0], outs[0].shape[0] * LOOK_AZ
    rows = 2 * lines
    blocks = (chunks[0].shape[0] - FOLD) // rows
    looks = blocks * LANES // LOOK_RG
    date = lax.axis_index("date")
    block = lax.axis_index("rng")
    early = blocks - 1
    whole_ref[: blocks * rows] = early_ref[...]
    for tile in range(early):
        begin = pl.multiple_of((tile + block) * rows, FOLD)
        whole_ref[pl.ds(begin + lines, lines), :] = chunks[-1][tile * lines : (tile + 1) * lines]
    begin = pl.multiple_of((1 - block) * early * rows, FOLD)
    whole_ref[pl.ds(begin, rows), :] = chunks[-1][early * lines : early * lines + rows]
    whole_ref[blocks * rows :] = chunks[-1][early * lines + rows :]
    chunks[-1] = whole_ref
    az = lax.axis_index("az")
    upper = lax.broadcasted_iota(jnp.int32, (groups, LANES), 0) // (groups // 2) == az
    for step, chunk_ref in enumerate(chunks):
        window_ref[step, :, :LANES] = chunk_ref[: blocks * rows]
        window_ref[step, : (blocks - 1) * rows, LANES:] = chunk_ref[rows : blocks * rows]
        folded = chunk_ref[blocks * rows : blocks * rows + FOLD].astype(jnp.float32)
        for part in range(rows // FOLD):
            value = pltpu.roll(folded, LANES - part * TAIL, 1) if part else folded
            at = pl.ds((blocks - 1) * rows + part * FOLD, FOLD)
            window_ref[step, at, LANES:] = value.astype(jnp.bfloat16)
    for place, (first, second) in enumerate(pairs):
        def filtered(step):
            total = dot_nt(window_ref[step], weight_ref[place, 0]) + dot_nt(window_ref[step], weight_ref[place, 1])
            total = total.reshape(blocks, 2, 2, HALO_LINES, 2 * LANES)
            re, im = total[:, :, 0], total[:, :, 1]
            return re[..., :LANES], im[..., :LANES], re[..., LANES:], im[..., LANES:]

        cos_re, cos_im, sin_re, sin_im = filtered(first)
        master_re, master_im = cos_re + sin_im, cos_im - sin_re
        cos_re, cos_im, sin_re, sin_im = filtered(second)
        partner_re, partner_im = cos_re - sin_im, cos_im + sin_re
        for part, product in enumerate(
            (
                master_re * partner_re + master_im * partner_im,
                master_im * partner_re - master_re * partner_im,
            )
        ):
            summed = product[:, :, :groups] + product[:, :, groups:]
            at = pl.ds((place * 2 + part) * groups, groups)
            for k in range(blocks):
                both = [summed[k, half] + pltpu.roll(summed[k, half], groups // 2, 0) for half in range(2)]
                product_ref[at, k * LANES : (k + 1) * LANES] = jnp.where(upper, both[0], both[1])

    out_width = outs[0].shape[1]
    column = lax.broadcasted_iota(jnp.int32, (product_ref.shape[1], out_width), 0)
    lane = lax.broadcasted_iota(jnp.int32, (product_ref.shape[1], out_width), 1)
    collect = jnp.where(column // LOOK_RG == lane % looks, 1.0, 0.0).astype(jnp.bfloat16)
    high, low = halves(product_ref[...])
    total = (dot(high, collect) + dot(low, collect)) * (1.0 / (LOOK_AZ * LOOK_RG))
    total = total.reshape(len(pairs), 2, groups, out_width)
    own_lane = lax.broadcasted_iota(jnp.int32, (groups, out_width), 1) // looks
    for step, out_ref in enumerate(outs):
        value = jnp.zeros((groups, out_width), jnp.float32)
        for place, pair in enumerate(pairs):
            if step in pair:
                other = pair[1] if pair[0] == step else pair[0]
                lag = (date ^ other) - (date ^ step)
                for part in range(2):
                    signed = -total[place, part] if part == 1 and pair[1] == step else total[place, part]
                    value = jnp.where(own_lane == (lag - 1) * 2 + part, signed, value)
        out_ref[...] = value


def place_kernel(used_lags, looks, *refs):
    out_ref = refs[-1]
    groups, columns = out_ref.shape[2:]
    date = lax.axis_index("date")
    lane = lax.broadcasted_iota(jnp.int32, (groups, LANES), 1) // looks
    out_ref[...] = jnp.zeros_like(out_ref)
    each = LANES // looks
    for step, recv_ref in enumerate(refs[:-1][::-1]):
        chunk = date ^ step
        for lag in range(used_lags):
            for part in range(2):
                tile, group = divmod(lag * 2 + part, each)
                block = recv_ref[:, tile * LANES : (tile + 1) * LANES]
                block = pltpu.roll(block, lax.bitwise_and(looks * (chunk - group), LANES - 1), 1)
                out_ref[part, lag] = jnp.where(lane == chunk, block, out_ref[part, lag])


def tiled_body(slc, offsets, kernel_index, range_shift):
    dates = lax.axis_size("date")
    lines, columns = slc.shape[2], slc.shape[3]
    chunk = columns // dates
    looks = chunk // LOOK_RG
    groups = lines // LOOK_AZ
    out_width = up(min(LAGS, dates - 1) * 2 * looks, LANES)
    vmem = pl.BlockSpec(memory_space=pltpu.VMEM)
    hbm = pl.BlockSpec(memory_space=pltpu.HBM)
    limit = pltpu.CompilerParams(vmem_limit_bytes=32 * 1024 * 1024)
    bf16 = jnp.bfloat16
    cells, offsets, kernel_index, range_shift = (
        pltpu.with_memory_space_constraint(value, pltpu.HBM)
        for value in (slc.reshape(2, lines, columns), offsets, kernel_index, range_shift)
    )
    tiles = chunk // LANES
    chunk_rows = tiles * 2 * lines

    side, corner, halo_lines, line_taps, column_taps, held = pl.pallas_call(
        prepare_kernel,
        out_shape=[
            jax.ShapeDtypeStruct((2, lines, LANES), bf16),
            jax.ShapeDtypeStruct((2, HALO_LINES, LANES), bf16),
            jax.ShapeDtypeStruct((2, HALO_LINES, columns), bf16),
            jax.ShapeDtypeStruct((2, 2 * HALO_LINES, lines + HALO_LINES), bf16),
            jax.ShapeDtypeStruct((3 * LANES, 2 * LANES), bf16),
            jax.ShapeDtypeStruct((2, lines, columns + 3 * LANES), bf16),
        ],
        in_specs=[hbm] * 3,
        out_specs=[vmem] * 6,
        scratch_shapes=[
            pltpu.SMEM(offsets.shape, jnp.int32),
            pltpu.SMEM(kernel_index.shape, jnp.int32),
            pltpu.SemaphoreType.DMA((6,)),
        ],
        compiler_params=limit,
    )(offsets, kernel_index, cells)
    swap = [(0, 1), (1, 0)]
    side = lax.ppermute(side, "rng", swap)
    corner = lax.ppermute(corner, ("rng", "az"), [(0, 3), (1, 2), (2, 1), (3, 0)])
    halo_lines = lax.ppermute(halo_lines, "az", swap)

    def swapped(value, step):
        return lax.ppermute(value, "date", [(i, i ^ step) for i in range(dates)])

    steps = range(dates - 1, 0, -1)
    early_rows = (tiles - 1) * lines
    early = pl.pallas_call(
        functools.partial(early_kernel, tiles),
        out_shape=jax.ShapeDtypeStruct((early_rows, LANES), bf16),
        in_specs=[vmem] * 3,
        out_specs=vmem,
        compiler_params=limit,
    )(held, line_taps, column_taps)
    early = swapped(early, steps[0])
    first, wide = pl.pallas_call(
        functools.partial(first_kernel, tiles, steps[1]),
        out_shape=[
            jax.ShapeDtypeStruct((chunk_rows + 2 * FOLD, LANES), bf16),
            jax.ShapeDtypeStruct((2, lines + HALO_LINES, columns + 3 * LANES), bf16),
        ],
        in_specs=[vmem] * 6,
        out_specs=[vmem] * 2,
        compiler_params=limit,
    )(side, corner, halo_lines, held, line_taps, column_taps)
    first = swapped(first, steps[1])
    others = [steps[0], *steps[2:], 0]
    rest = pl.pallas_call(
        functools.partial(rest_kernel, tiles, others),
        out_shape=[
            jax.ShapeDtypeStruct((chunk_rows + FOLD - (early_rows if step == steps[0] else 0), LANES), bf16)
            for step in others
        ],
        in_specs=[vmem] * 3,
        out_specs=[vmem] * (dates - 1),
        compiler_params=limit,
        cost_estimate=pl.CostEstimate(flops=400_000_000, bytes_accessed=0, transcendentals=0),
    )(wide, line_taps, column_taps)
    rest = [swapped(rows, step) if step else rows for rows, step in zip(rest, others)]
    chunks = [rest[0], first, *rest[1:]]

    pairs = [(first, second) for first in range(dates) for second in range(first + 1, dates)]
    weights, early = pl.pallas_call(
        functools.partial(filter_kernel, pairs),
        out_shape=[
            jax.ShapeDtypeStruct((len(pairs), 2, 2 * LANES, 2 * LANES), bf16),
            jax.ShapeDtypeStruct((chunk_rows, LANES), bf16),
        ],
        in_specs=[hbm, vmem],
        out_specs=[vmem] * 2,
        scratch_shapes=[pltpu.SMEM(range_shift.shape, jnp.float32), pltpu.SemaphoreType.DMA],
        compiler_params=limit,
        cost_estimate=pl.CostEstimate(flops=935_000_000, bytes_accessed=0, transcendentals=0),
    )(range_shift, early)
    looked = pl.pallas_call(
        functools.partial(looks_kernel, pairs, dates),
        out_shape=[jax.ShapeDtypeStruct((groups, out_width), jnp.float32)] * dates,
        in_specs=[vmem] * (2 + dates),
        out_specs=[vmem] * dates,
        scratch_shapes=[
            pltpu.VMEM((chunk_rows + FOLD, LANES), bf16),
            pltpu.VMEM((dates, chunk_rows, 2 * LANES), bf16),
            pltpu.VMEM((len(pairs) * 2 * groups, chunk), jnp.float32),
        ],
        compiler_params=limit,
    )(weights, early, *chunks)
    out = pl.pallas_call(
        functools.partial(place_kernel, min(LAGS, dates - 1), looks),
        out_shape=jax.ShapeDtypeStruct((2, LAGS, groups, looks * dates), jnp.float32),
        in_specs=[vmem] * dates,
        out_specs=vmem,
        compiler_params=limit,
    )(*[swapped(looked[step], step) for step in steps], looked[0])
    return out[:, None]


def body(slc, offsets, kernel_index, range_shift):
    dates, az_count = (lax.axis_size(a) for a in ("date", "az"))
    lines, columns = slc.shape[2], slc.shape[3]
    whole_tiles = columns % (dates * LANES) == 0 and columns % (dates * LOOK_RG) == 0
    one_row = columns // LOOK_RG == LANES and range_shift.shape[0] == dates
    few = dates & (dates - 1) == 0 and dates - 1 <= LAGS
    folds = lines == 2 * HALO_LINES and lax.axis_size("rng") == 2 and dates >= 4 and 2 * lines // FOLD * TAIL <= LANES
    if az_count == 2 and whole_tiles and one_row and few and folds:
        return tiled_body(slc, offsets, kernel_index, range_shift)
    return chunked_body(slc, offsets, kernel_index, range_shift)


def solution(mesh):
    return jax.shard_map(
        body,
        mesh=mesh,
        in_specs=(
            P(None, ("groups", "date"), "az", "rng"),
            P(("groups", "date"), None),
            P(("groups", "date"), None),
            P("groups"),
        ),
        out_specs=P(None, ("groups", "date"), None, "az", "rng"),
        check_vma=False,
    )
```

```python
import functools

import jax
import jax.numpy as jnp
import numpy as np
from jax import lax
from jax.experimental import pallas as pl
from jax.experimental.pallas import tpu as pltpu
from jax.sharding import PartitionSpec as P

LAGS = 8
KERNELS = 16
TAPS = 8
FILTER_HALF = 8
FILTER_TAPS = 2 * FILTER_HALF + 1
LOOK_AZ = 4
LOOK_RG = 20
LANES = 128
META = 3
UNROLLED_PAIRS = 12


def up(value, unit):
    return -(-value // unit) * unit


def kernel_table():
    position = np.arange(TAPS) - 3.0 - np.arange(KERNELS)[:, None] / KERNELS
    shaped = np.sinc(position) * (0.5 + 0.5 * np.cos(np.pi * position / 5.0))
    table = np.zeros((KERNELS, LANES), np.float32)
    table[:, :TAPS] = shaped / shaped.sum(1, keepdims=True)
    return table


def lowpass_row(width):
    t = np.arange(FILTER_TAPS) - FILTER_HALF
    row = np.zeros((1, width), np.float32)
    row[0, :FILTER_TAPS] = 0.4 * np.sinc(0.4 * t) * (0.54 + 0.46 * np.cos(np.pi * t / (FILTER_HALF + 1)))
    return row


def halves(value):
    high = value.astype(jnp.bfloat16)
    return high, (value - high.astype(jnp.float32)).astype(jnp.bfloat16)


def dot(a, b):
    return jnp.dot(a, b, preferred_element_type=jnp.float32)


def dot_nt(a, b):
    return lax.dot_general(a, b, (((1,), (1,)), ((), ())), preferred_element_type=jnp.float32)


def pack_kernel(chunk, place_ref, offsets_ref, index_ref, slc_ref, before_ref, after_ref, out_ref, wide_ref):
    columns = slc_ref.shape[1]
    wide = out_ref.shape[2]
    first = place_ref[0] == 0
    last = place_ref[0] == place_ref[1] - 1
    zero = jnp.zeros_like(before_ref[...])
    wide_ref[:, :LANES] = jnp.where(first, zero, before_ref[...])
    wide_ref[:, LANES : LANES + columns] = slc_ref[...]
    wide_ref[:, LANES + columns :] = jnp.where(last, zero, after_ref[...])
    lane = lax.broadcasted_iota(jnp.int32, (slc_ref.shape[0], wide), 1)
    numbers = [offsets_ref[0, 0], index_ref[0, 0], index_ref[0, 1]]
    for j in range(out_ref.shape[0]):
        start = LANES + chunk * j - FILTER_HALF - 3 + offsets_ref[0, 1]
        tile = lax.shift_right_logical(start, 7)
        within = lax.bitwise_and(start, LANES - 1)
        window = wide_ref[:, pl.ds(pl.multiple_of(tile * LANES, LANES), wide + LANES)].astype(jnp.float32)
        moved = pltpu.roll(window, wide + LANES - within, 1)[:, :wide]
        for slot, number in enumerate(numbers):
            moved = jnp.where(lane == wide - META + slot, number.astype(jnp.float32), moved)
        out_ref[j] = moved.astype(jnp.bfloat16)


def picked_taps(table, index):
    row = lax.broadcasted_iota(jnp.int32, table.shape, 0).astype(jnp.float32)
    return jnp.sum(jnp.where(row == index, table, 0.0), axis=0, keepdims=True)


def banded(taps, distance):
    out = jnp.zeros(distance.shape, jnp.float32)
    for q in range(TAPS):
        out = jnp.where(distance == q, taps[:, q : q + 1], out)
    return out


def pairs_kernel(chunk, pairs, *refs):
    if isinstance(pairs, int):
        table_of_pairs, refs = refs[0], refs[1:]
    shift_ref, table_ref, lowpass_ref, recv_ref, out_ref, resampled_ref, weight_ref, product_ref = refs
    sources, rows, wide = recv_ref.shape
    dates = shift_ref.shape[0]
    az_count = sources // dates
    own_lines = rows // 2
    lines = own_lines * az_count
    groups = lines // LOOK_AZ
    looks = chunk // LOOK_RG
    table = table_ref[...]
    held = resampled_ref.shape[2]

    out_row = lax.broadcasted_iota(jnp.int32, (lines, lines), 0)
    in_row = lax.broadcasted_iota(jnp.int32, (lines, lines), 1)
    line = LOOK_AZ * (out_row % groups) + out_row // groups
    line_distance = (in_row - line + 3).astype(jnp.float32)
    span = min(2 * LANES, wide)
    column_distance = (
        lax.broadcasted_iota(jnp.int32, (span, LANES), 0) - lax.broadcasted_iota(jnp.int32, (span, LANES), 1)
    ).astype(jnp.float32)
    for date in range(dates):
        numbers = recv_ref[date * az_count, 0:16, wide - LANES :].astype(jnp.float32)[0:1, LANES - META :]
        line_offset, line_index, column_index = (numbers[:, s : s + 1] for s in range(META))
        line_taps = banded(picked_taps(table, line_index), line_distance - line_offset)
        line_taps = jnp.concatenate(halves(line_taps), axis=0)
        column_high, column_low = halves(banded(picked_taps(table, column_index), column_distance))
        moved = []
        for plane in range(2):
            rows_of = slice(plane * own_lines, (plane + 1) * own_lines)
            source = jnp.concatenate([recv_ref[date * az_count + a, rows_of, :] for a in range(az_count)], axis=0)
            both = dot(line_taps, source)
            moved.append(both[:lines] + both[lines:])
        moved_high, moved_low = halves(jnp.concatenate(moved, axis=0))
        for begin in range(0, held, LANES):
            end = min(begin + span, wide)
            taken = end - begin
            total = dot(moved_high[:, begin:end], column_high[:taken])
            total += dot(moved_low[:, begin:end], column_high[:taken])
            total += dot(moved_high[:, begin:end], column_low[:taken])
            resampled_ref[date, :, begin : begin + LANES] = total.astype(jnp.bfloat16)

    window = lowpass_ref[...]
    spacing = lax.broadcasted_iota(jnp.int32, window.shape, 1).astype(jnp.float32) - FILTER_HALF
    span = min(2 * LANES, held)

    def one_pair(place, own, other):
        gap = shift_ref[own] - shift_ref[other]
        angle = jnp.where(jnp.abs(spacing) <= FILTER_HALF, jnp.pi * gap * spacing, 0.0)
        for part, taps in enumerate((window * jnp.cos(angle), window * jnp.sin(angle))):
            spread = jnp.broadcast_to(taps, (LANES, 2 * LANES))
            spread = pltpu.roll(spread, 0, 1, stride=1, stride_axis=0)
            high, low = halves(spread)
            weight_ref[0, part * LANES : (part + 1) * LANES, :] = high
            weight_ref[1, part * LANES : (part + 1) * LANES, :] = low
        both = jnp.concatenate([resampled_ref[own], resampled_ref[other]], axis=0)
        for begin in range(0, up(chunk, LANES), LANES):
            end = min(begin + span, held)
            taken = end - begin
            total = dot_nt(both[:, begin:end], weight_ref[0, :, :taken])
            total += dot_nt(both[:, begin:end], weight_ref[1, :, :taken])
            cos, sin = total[:, :LANES], total[:, LANES:]
            re, im = slice(0, lines), slice(lines, 2 * lines)
            master_re = cos[re] + sin[im]
            master_im = cos[im] - sin[re]
            re, im = slice(2 * lines, 3 * lines), slice(3 * lines, 4 * lines)
            partner_re = cos[re] - sin[im]
            partner_im = cos[im] + sin[re]
            for part, product in enumerate(
                (
                    master_re * partner_re + master_im * partner_im,
                    master_im * partner_re - master_re * partner_im,
                )
            ):
                summed = sum(product[k * groups : (k + 1) * groups] for k in range(LOOK_AZ))
                product_ref[place, part, :, begin : begin + LANES] = summed

    if isinstance(pairs, int):
        count = pairs

        def step(place, carry):
            one_pair(place, table_of_pairs[place, 0], table_of_pairs[place, 1])
            return carry

        lax.fori_loop(0, count, step, 0)
    else:
        count = len(pairs)
        for place, (own, other) in enumerate(pairs):
            one_pair(place, own, other)

    out_width = out_ref.shape[2]
    column = lax.broadcasted_iota(jnp.int32, (product_ref.shape[3], out_width), 0)
    lane = lax.broadcasted_iota(jnp.int32, (product_ref.shape[3], out_width), 1)
    collect = jnp.where(column // LOOK_RG == lane % looks, 1.0, 0.0).astype(jnp.bfloat16)
    high, low = halves(product_ref[...].reshape(count * 2 * groups, product_ref.shape[3]))
    total = (dot(high, collect) + dot(low, collect)) * (1.0 / (LOOK_AZ * LOOK_RG))
    total = total.reshape(count, 2, groups, out_width)
    own_lane = lax.broadcasted_iota(jnp.int32, (groups, out_width), 1) // looks
    place = 0
    for own in range(dates):
        value = jnp.zeros((groups, out_width), jnp.float32)
        for lag in range(min(LAGS, dates - 1 - own)):
            for part in range(2):
                value = jnp.where(own_lane == lag * 2 + part, total[place, part], value)
            place += 1
        out_ref[own * az_count : (own + 1) * az_count] = value.reshape(az_count, groups // az_count, out_width)


def unpack_kernel(used_lags, looks, recv_ref, out_ref):
    sources, groups, width = recv_ref.shape
    columns = out_ref.shape[-1]
    lane = lax.broadcasted_iota(jnp.int32, (groups, columns), 1) // looks
    out_ref[...] = jnp.zeros_like(out_ref)
    for lag in range(used_lags):
        for part in range(2):
            value = jnp.zeros((groups, columns), jnp.float32)
            for source in range(sources):
                block = recv_ref[source]
                if width != columns:
                    block = block[:, :columns]
                shift = looks * (source - lag * 2 - part) % columns
                if shift:
                    block = pltpu.roll(block, shift, 1)
                value = jnp.where(lane == source, block, value)
            out_ref[part, lag] = value


def chunked_body(slc, offsets, kernel_index, range_shift):
    axes = ("date", "az")
    date_count, az_count, rng_count = (lax.axis_size(a) for a in ("date", "az", "rng"))
    peers = date_count * az_count
    lines, columns = slc.shape[2], slc.shape[3]
    dates = range_shift.shape[0]
    chunk = columns // peers
    looks = chunk // LOOK_RG
    groups = lines * az_count // LOOK_AZ
    wide = up(chunk + 2 * FILTER_HALF + TAPS - 1 + META, LANES)
    held = up(chunk + 2 * FILTER_HALF, LANES)
    used_lags = min(LAGS, dates - 1)
    out_width = up(used_lags * 2 * looks, LANES)
    vmem = pl.BlockSpec(memory_space=pltpu.VMEM)
    smem = pl.BlockSpec(memory_space=pltpu.SMEM)
    limit = pltpu.CompilerParams(vmem_limit_bytes=32 * 1024 * 1024)

    cells = slc.reshape(2 * lines, columns)
    place = lax.axis_index("rng")
    if rng_count == 2:
        edge = jnp.where(place == 0, cells[:, columns - LANES :], cells[:, :LANES])
        before = after = lax.ppermute(edge, "rng", [(0, 1), (1, 0)])
    else:
        forth = [(i, i + 1) for i in range(rng_count - 1)]
        before = lax.ppermute(cells[:, columns - LANES :], "rng", forth)
        after = lax.ppermute(cells[:, :LANES], "rng", [(b, a) for a, b in forth])

    packed = pl.pallas_call(
        functools.partial(pack_kernel, chunk),
        out_shape=jax.ShapeDtypeStruct((peers, 2 * lines, wide), jnp.bfloat16),
        in_specs=[smem] * 3 + [vmem] * 3,
        out_specs=vmem,
        scratch_shapes=[pltpu.VMEM((2 * lines, columns + 2 * LANES), jnp.bfloat16)],
        compiler_params=limit,
    )(jnp.stack([place, rng_count]).astype(jnp.int32), offsets, kernel_index, cells, before, after)
    arrived = lax.all_to_all(packed, axes, 0, 0, tiled=True)

    pairs = [(own, own + lag) for own in range(dates) for lag in range(1, LAGS + 1) if own + lag < dates]
    count = len(pairs)
    first = [jnp.asarray(np.array(pairs, np.int32))] if count > UNROLLED_PAIRS else []
    looked = pl.pallas_call(
        functools.partial(pairs_kernel, chunk, count if first else pairs),
        out_shape=jax.ShapeDtypeStruct((peers, groups // az_count, out_width), jnp.float32),
        in_specs=[smem] * len(first) + [smem] + [vmem] * 3,
        out_specs=vmem,
        scratch_shapes=[
            pltpu.VMEM((dates, 4 * (groups * LOOK_AZ) // 2, held), jnp.bfloat16),
            pltpu.VMEM((2, 2 * LANES, 2 * LANES), jnp.bfloat16),
            pltpu.VMEM((count, 2, groups, up(chunk, LANES)), jnp.float32),
        ],
        compiler_params=limit,
    )(*first, range_shift, jnp.asarray(kernel_table()), jnp.asarray(lowpass_row(2 * LANES)), arrived)
    returned = lax.all_to_all(looked, axes, 0, 0, tiled=True)

    out = pl.pallas_call(
        functools.partial(unpack_kernel, used_lags, looks),
        out_shape=jax.ShapeDtypeStruct((2, LAGS, groups // az_count, looks * peers), jnp.float32),
        in_specs=[vmem],
        out_specs=vmem,
        compiler_params=limit,
    )(returned)
    return out[:, None]


HALO_LINES = 16
FOLD = 16
TAIL = 2 * FILTER_HALF


def core_step(step, az):
    if step in (1, 2):
        return step ^ (3 * az)
    return step


def sinc(value):
    angle = jnp.pi * value
    return jnp.where(angle == 0.0, 1.0, jnp.sin(angle) / jnp.where(angle == 0.0, 1.0, angle))


def tap_row(index):
    lane = lax.broadcasted_iota(jnp.int32, (1, LANES), 1)
    position = lane.astype(jnp.float32) - 3.0 - index.astype(jnp.float32) / KERNELS
    shaped = sinc(position) * (0.5 + 0.5 * jnp.cos(jnp.pi * position / 5.0))
    shaped = jnp.where(lane < TAPS, shaped, 0.0)
    return shaped / jnp.sum(shaped, axis=1, keepdims=True)


def row_line(row, az):
    quarter = HALO_LINES // LOOK_AZ
    within = row % HALO_LINES
    return HALO_LINES * ((row // HALO_LINES) ^ az) + LOOK_AZ * (within % quarter) + within // quarter


def prepare_kernel(offsets_hbm, index_hbm, slc_ref, side_ref, corner_ref, lines_ref, line_ref, column_ref, held_ref, offsets_ref, index_ref, semaphores):
    lines, columns = slc_ref.shape[1:]
    az = lax.axis_index("az")
    row = pl.multiple_of((1 - az) * (lines - HALO_LINES), HALO_LINES)
    edge = pl.multiple_of((1 - lax.axis_index("rng")) * (columns - LANES), LANES)
    nearest, outermost = pl.ds(row, HALO_LINES), pl.ds(edge, LANES)
    moves = [
        (offsets_hbm, offsets_ref),
        (index_hbm, index_ref),
        (slc_ref.at[:, :, outermost], side_ref),
        (slc_ref.at[:, nearest, outermost], corner_ref),
        (slc_ref.at[:, nearest, :], lines_ref),
        (slc_ref, held_ref.at[:, :, pl.ds(LANES, columns)]),
    ]
    copies = [pltpu.make_async_copy(a, b, semaphores.at[i]) for i, (a, b) in enumerate(moves)]
    for copy in copies:
        copy.start()
    held_ref[:, :, :LANES] = jnp.zeros((2, lines, LANES), held_ref.dtype)
    held_ref[:, :, LANES + columns :] = jnp.zeros((2, lines, 2 * LANES), held_ref.dtype)
    copies[0].wait()
    copies[1].wait()
    for half in range(2):
        shape = (HALO_LINES, lines + HALO_LINES)
        line = row_line(lax.broadcasted_iota(jnp.int32, shape, 0) + half * HALO_LINES, az)
        place = lax.broadcasted_iota(jnp.int32, shape, 1)
        source = jnp.where(place < lines, place, place + jnp.where(az == 0, 0, -lines - HALO_LINES))
        taps = banded(tap_row(index_ref[0, 0]), source - line - offsets_ref[0, 0] + 3)
        line_ref[half] = jnp.concatenate(halves(taps), axis=0)
    shape = (3 * LANES, LANES)
    distance = lax.broadcasted_iota(jnp.int32, shape, 0) - lax.broadcasted_iota(jnp.int32, shape, 1)
    distance = distance - (LANES - FILTER_HALF - 3) - offsets_ref[0, 1]
    taps = banded(tap_row(index_ref[0, 1]), distance)
    column_ref[...] = jnp.concatenate(halves(taps), axis=1)
    for copy in copies[2:]:
        copy.wait()


def along_range(moved, column_ref, tiles):
    high, low = halves(moved)
    starts = range(0, tiles * LANES, LANES)
    high = jnp.concatenate([high[:, s : s + 3 * LANES] for s in starts], axis=0)
    low = jnp.concatenate([low[:, s : s + 3 * LANES] for s in starts], axis=0)
    total = dot(high, column_ref[...])
    return total[:, :LANES] + total[:, LANES:] + dot(low, column_ref[:, :LANES])


def early_kernel(tiles, held_ref, line_ref, column_ref, out_ref):
    lines = held_ref.shape[1]
    early = out_ref.shape[0] // (2 * HALO_LINES)
    chunk = lax.axis_index("date") ^ (lax.axis_size("date") - 1)
    begin = pl.multiple_of((chunk * tiles + lax.axis_index("rng")) * LANES, LANES)
    moved = []
    for plane in range(2):
        both = dot(line_ref[0, :, :lines], held_ref[plane, :, pl.ds(begin, (early + 2) * LANES)])
        moved.append(both[:HALO_LINES] + both[HALO_LINES:])
    moved = jnp.concatenate(moved, axis=0)
    out_ref[...] = along_range(moved, column_ref, early).astype(jnp.bfloat16)


def resample_kernel(side_ref, corner_ref, lines_ref, held_ref, line_ref, column_ref, *outs):
    outs, tiles_ref, tails_ref = outs[:-2], outs[-2], outs[-1]
    lines, width = held_ref.shape[1:]
    width -= LANES
    block = lax.axis_index("rng")
    taps = jnp.concatenate([line_ref[0], line_ref[1]], axis=0)
    moved = [[], []]
    for plane in range(2):
        own = jnp.concatenate([side_ref[plane], held_ref[plane, :, LANES : width - LANES], side_ref[plane]], axis=1)
        halo = jnp.concatenate([corner_ref[plane], lines_ref[plane], corner_ref[plane]], axis=1)
        both = dot(taps, jnp.concatenate([own, halo], axis=0))
        for half in range(2):
            at = 2 * half * HALO_LINES
            moved[half].append(both[at : at + HALO_LINES] + both[at + HALO_LINES : at + 2 * HALO_LINES])
    moved = jnp.concatenate(moved[0] + moved[1], axis=0)
    left = jnp.where(block > 0, moved[:, :LANES], 0.0)
    right = jnp.where(block == 0, moved[:, width - LANES :], 0.0)
    moved = jnp.concatenate([left, moved[:, LANES : width - LANES], right, jnp.zeros_like(right)], axis=1)
    total = along_range(moved, column_ref, width // LANES - 1)
    rows = 2 * lines
    tiles_ref[...] = total.astype(jnp.bfloat16)
    chunk_rows = outs[0].shape[0] - FOLD
    lane = lax.broadcasted_iota(jnp.int32, (FOLD, LANES), 1) // TAIL
    for chunk in range(len(outs)):
        begin = (chunk + 1) * chunk_rows
        folded = total[begin : begin + FOLD]
        for part in range(1, rows // FOLD):
            value = pltpu.roll(total[begin + part * FOLD : begin + (part + 1) * FOLD], part * TAIL, 1)
            folded = jnp.where(lane == part, value, folded)
        tails_ref[chunk] = folded.astype(jnp.bfloat16)
    date = lax.axis_index("date")
    az = lax.axis_index("az")
    for step, out_ref in enumerate(outs[:-1]):
        chunk = date ^ core_step(step, az)
        out_ref[:chunk_rows] = tiles_ref[pl.ds(pl.multiple_of(chunk * chunk_rows, FOLD), chunk_rows), :]
        out_ref[chunk_rows:] = tails_ref[chunk]
    out_ref = outs[-1]
    chunk = date ^ (len(outs) - 1)
    early = chunk_rows // rows - 1
    for tile in range(early):
        begin = pl.multiple_of(chunk * chunk_rows + (tile + block) * rows + lines, FOLD)
        out_ref[tile * lines : (tile + 1) * lines] = tiles_ref[pl.ds(begin, lines), :]
    begin = pl.multiple_of(chunk * chunk_rows + (1 - block) * early * rows, FOLD)
    out_ref[early * lines : early * lines + rows] = tiles_ref[pl.ds(begin, rows), :]
    out_ref[early * lines + rows :] = tails_ref[chunk]


def filter_kernel(pairs, shift_hbm, early_ref, out_ref, spread_ref, shift_ref, semaphore):
    copy = pltpu.make_async_copy(shift_hbm, shift_ref, semaphore)
    copy.start()
    lines = 2 * HALO_LINES
    spread_ref[...] = jnp.zeros_like(spread_ref)
    for tile in range(early_ref.shape[0] // lines):
        begin = pl.multiple_of((tile + lax.axis_index("rng")) * 2 * lines, FOLD)
        spread_ref[pl.ds(begin, lines), :] = early_ref[tile * lines : (tile + 1) * lines]
    date = lax.axis_index("date")
    spacing = lax.broadcasted_iota(jnp.int32, (1, 2 * LANES), 1).astype(jnp.float32) - FILTER_HALF
    window = 0.4 * sinc(0.4 * spacing) * (0.54 + 0.46 * jnp.cos(jnp.pi * spacing / (FILTER_HALF + 1)))
    window = jnp.where(jnp.abs(spacing) <= FILTER_HALF, window, 0.0)
    copy.wait()
    for place, (first, second) in enumerate(pairs):
        gap = shift_ref[date ^ first] - shift_ref[date ^ second]
        angle = jnp.where(jnp.abs(spacing) <= FILTER_HALF, jnp.pi * gap * spacing, 0.0)
        for part, taps in enumerate((window * jnp.cos(angle), window * jnp.sin(angle))):
            spread = jnp.broadcast_to(taps, (LANES, 2 * LANES))
            spread = pltpu.roll(spread, 0, 1, stride=1, stride_axis=0)
            high, low = halves(spread)
            out_ref[place, 0, part * LANES : (part + 1) * LANES, :] = high
            out_ref[place, 1, part * LANES : (part + 1) * LANES, :] = low


def looks_kernel(pairs, dates, weight_ref, *refs):
    early_ref, chunks, outs = refs[0], list(refs[1 : dates + 1][::-1]), refs[dates + 1 : 2 * dates + 1]
    whole_ref, window_ref, product_ref = refs[-3:]
    groups, lines = outs[0].shape[0], outs[0].shape[0] * LOOK_AZ
    rows = 2 * lines
    blocks = (chunks[0].shape[0] - FOLD) // rows
    looks = blocks * LANES // LOOK_RG
    date = lax.axis_index("date")
    block = lax.axis_index("rng")
    early = blocks - 1
    whole_ref[: blocks * rows] = early_ref[...]
    for tile in range(early):
        begin = pl.multiple_of((tile + block) * rows, FOLD)
        whole_ref[pl.ds(begin + lines, lines), :] = chunks[-1][tile * lines : (tile + 1) * lines]
    begin = pl.multiple_of((1 - block) * early * rows, FOLD)
    whole_ref[pl.ds(begin, rows), :] = chunks[-1][early * lines : early * lines + rows]
    whole_ref[blocks * rows :] = chunks[-1][early * lines + rows :]
    chunks[-1] = whole_ref
    az = lax.axis_index("az")
    upper = lax.broadcasted_iota(jnp.int32, (groups, LANES), 0) // (groups // 2) == az
    for step, chunk_ref in enumerate(chunks):
        step = core_step(step, az)
        window_ref[step, :, :LANES] = chunk_ref[: blocks * rows]
        window_ref[step, : (blocks - 1) * rows, LANES:] = chunk_ref[rows : blocks * rows]
        folded = chunk_ref[blocks * rows :].astype(jnp.float32)
        for part in range(rows // FOLD):
            value = pltpu.roll(folded, LANES - part * TAIL, 1) if part else folded
            at = pl.ds((blocks - 1) * rows + part * FOLD, FOLD)
            window_ref[step, at, LANES:] = value.astype(jnp.bfloat16)
    for place, (first, second) in enumerate(pairs):
        def filtered(step):
            total = dot_nt(window_ref[step], weight_ref[place, 0]) + dot_nt(window_ref[step], weight_ref[place, 1])
            total = total.reshape(blocks, 2, 2, HALO_LINES, 2 * LANES)
            re, im = total[:, :, 0], total[:, :, 1]
            return re[..., :LANES], im[..., :LANES], re[..., LANES:], im[..., LANES:]

        cos_re, cos_im, sin_re, sin_im = filtered(first)
        master_re, master_im = cos_re + sin_im, cos_im - sin_re
        cos_re, cos_im, sin_re, sin_im = filtered(second)
        partner_re, partner_im = cos_re - sin_im, cos_im + sin_re
        for part, product in enumerate(
            (
                master_re * partner_re + master_im * partner_im,
                master_im * partner_re - master_re * partner_im,
            )
        ):
            summed = product[:, :, :groups] + product[:, :, groups:]
            at = pl.ds((place * 2 + part) * groups, groups)
            for k in range(blocks):
                both = [summed[k, half] + pltpu.roll(summed[k, half], groups // 2, 0) for half in range(2)]
                product_ref[at, k * LANES : (k + 1) * LANES] = jnp.where(upper, both[0], both[1])

    out_width = outs[0].shape[1]
    column = lax.broadcasted_iota(jnp.int32, (product_ref.shape[1], out_width), 0)
    lane = lax.broadcasted_iota(jnp.int32, (product_ref.shape[1], out_width), 1)
    collect = jnp.where(column // LOOK_RG == lane % looks, 1.0, 0.0).astype(jnp.bfloat16)
    high, low = halves(product_ref[...])
    total = (dot(high, collect) + dot(low, collect)) * (1.0 / (LOOK_AZ * LOOK_RG))
    total = total.reshape(len(pairs), 2, groups, out_width)
    own_lane = lax.broadcasted_iota(jnp.int32, (groups, out_width), 1) // looks
    for step, out_ref in enumerate(outs):
        value = jnp.zeros((groups, out_width), jnp.float32)
        for place, pair in enumerate(pairs):
            if step in pair:
                other = pair[1] if pair[0] == step else pair[0]
                lag = (date ^ other) - (date ^ step)
                for part in range(2):
                    signed = -total[place, part] if part == 1 and pair[1] == step else total[place, part]
                    value = jnp.where(own_lane == (lag - 1) * 2 + part, signed, value)
        out_ref[...] = value


def place_kernel(used_lags, looks, *refs):
    out_ref = refs[-1]
    groups, columns = out_ref.shape[2:]
    date = lax.axis_index("date")
    lane = lax.broadcasted_iota(jnp.int32, (groups, LANES), 1) // looks
    out_ref[...] = jnp.zeros_like(out_ref)
    each = LANES // looks
    for step, recv_ref in enumerate(refs[:-1][::-1]):
        chunk = date ^ step
        for lag in range(used_lags):
            for part in range(2):
                tile, group = divmod(lag * 2 + part, each)
                block = recv_ref[:, tile * LANES : (tile + 1) * LANES]
                block = pltpu.roll(block, lax.bitwise_and(looks * (chunk - group), LANES - 1), 1)
                out_ref[part, lag] = jnp.where(lane == chunk, block, out_ref[part, lag])


def tiled_body(slc, offsets, kernel_index, range_shift):
    dates = lax.axis_size("date")
    lines, columns = slc.shape[2], slc.shape[3]
    chunk = columns // dates
    looks = chunk // LOOK_RG
    groups = lines // LOOK_AZ
    out_width = up(min(LAGS, dates - 1) * 2 * looks, LANES)
    vmem = pl.BlockSpec(memory_space=pltpu.VMEM)
    hbm = pl.BlockSpec(memory_space=pltpu.HBM)
    limit = pltpu.CompilerParams(vmem_limit_bytes=32 * 1024 * 1024)
    bf16 = jnp.bfloat16
    cells, offsets, kernel_index, range_shift = (
        pltpu.with_memory_space_constraint(value, pltpu.HBM)
        for value in (slc.reshape(2, lines, columns), offsets, kernel_index, range_shift)
    )
    tiles = chunk // LANES
    chunk_rows = tiles * 2 * lines

    side, corner, halo_lines, line_taps, column_taps, held = pl.pallas_call(
        prepare_kernel,
        out_shape=[
            jax.ShapeDtypeStruct((2, lines, LANES), bf16),
            jax.ShapeDtypeStruct((2, HALO_LINES, LANES), bf16),
            jax.ShapeDtypeStruct((2, HALO_LINES, columns), bf16),
            jax.ShapeDtypeStruct((2, 2 * HALO_LINES, lines + HALO_LINES), bf16),
            jax.ShapeDtypeStruct((3 * LANES, 2 * LANES), bf16),
            jax.ShapeDtypeStruct((2, lines, columns + 3 * LANES), bf16),
        ],
        in_specs=[hbm] * 3,
        out_specs=[vmem] * 6,
        scratch_shapes=[
            pltpu.SMEM(offsets.shape, jnp.int32),
            pltpu.SMEM(kernel_index.shape, jnp.int32),
            pltpu.SemaphoreType.DMA((6,)),
        ],
        compiler_params=limit,
    )(offsets, kernel_index, cells)
    swap = [(0, 1), (1, 0)]
    side = lax.ppermute(side, "rng", swap)
    corner = lax.ppermute(corner, ("rng", "az"), [(0, 3), (1, 2), (2, 1), (3, 0)])
    halo_lines = lax.ppermute(halo_lines, "az", swap)

    early_rows = (tiles - 1) * lines
    early = pl.pallas_call(
        functools.partial(early_kernel, tiles),
        out_shape=jax.ShapeDtypeStruct((early_rows, LANES), bf16),
        in_specs=[vmem] * 3,
        out_specs=vmem,
        compiler_params=limit,
    )(held, line_taps, column_taps)
    early = lax.ppermute(early, "date", [(i, i ^ (dates - 1)) for i in range(dates)])
    out_rows = [chunk_rows + FOLD] * (dates - 1) + [chunk_rows + FOLD - early_rows]
    sent = pl.pallas_call(
        resample_kernel,
        out_shape=[jax.ShapeDtypeStruct((rows, LANES), bf16) for rows in out_rows],
        in_specs=[vmem] * 6,
        out_specs=[vmem] * dates,
        scratch_shapes=[
            pltpu.VMEM(((columns // LANES + 1) * 2 * lines, LANES), bf16),
            pltpu.VMEM((dates, FOLD, LANES), bf16),
        ],
        compiler_params=limit,
    )(side, corner, halo_lines, held, line_taps, column_taps)

    def exchanged(values, mixed):
        arrived = {0: values[0]}
        for step in steps:
            moves = [
                (2 * i + core, 2 * (i ^ (core_step(step, core) if mixed else step)) + core)
                for i in range(dates)
                for core in range(2)
            ]
            arrived[step] = lax.ppermute(values[step], ("date", "az"), moves)
        return [arrived[step] for step in reversed(range(dates))]

    steps = range(dates - 1, 0, -1)
    chunks = exchanged(sent, True)
    pairs = [(first, second) for first in range(dates) for second in range(first + 1, dates)]
    weights, early = pl.pallas_call(
        functools.partial(filter_kernel, pairs),
        out_shape=[
            jax.ShapeDtypeStruct((len(pairs), 2, 2 * LANES, 2 * LANES), bf16),
            jax.ShapeDtypeStruct((chunk_rows, LANES), bf16),
        ],
        in_specs=[hbm, vmem],
        out_specs=[vmem] * 2,
        scratch_shapes=[pltpu.SMEM(range_shift.shape, jnp.float32), pltpu.SemaphoreType.DMA],
        compiler_params=limit,
        cost_estimate=pl.CostEstimate(flops=600_000_000, bytes_accessed=0, transcendentals=0),
    )(range_shift, early)
    looked = pl.pallas_call(
        functools.partial(looks_kernel, pairs, dates),
        out_shape=[jax.ShapeDtypeStruct((groups, out_width), jnp.float32)] * dates,
        in_specs=[vmem] * (2 + dates),
        out_specs=[vmem] * dates,
        scratch_shapes=[
            pltpu.VMEM((chunk_rows + FOLD, LANES), bf16),
            pltpu.VMEM((dates, chunk_rows, 2 * LANES), bf16),
            pltpu.VMEM((len(pairs) * 2 * groups, chunk), jnp.float32),
        ],
        compiler_params=limit,
    )(weights, early, *chunks)
    out = pl.pallas_call(
        functools.partial(place_kernel, min(LAGS, dates - 1), looks),
        out_shape=jax.ShapeDtypeStruct((2, LAGS, groups, looks * dates), jnp.float32),
        in_specs=[vmem] * dates,
        out_specs=vmem,
        compiler_params=limit,
    )(*exchanged(looked, False))
    return out[:, None]


def body(slc, offsets, kernel_index, range_shift):
    dates, az_count = (lax.axis_size(a) for a in ("date", "az"))
    lines, columns = slc.shape[2], slc.shape[3]
    whole_tiles = columns % (dates * LANES) == 0 and columns % (dates * LOOK_RG) == 0
    one_row = columns // LOOK_RG == LANES and range_shift.shape[0] == dates
    few = dates & (dates - 1) == 0 and dates - 1 <= LAGS
    folds = lines == 2 * HALO_LINES and lax.axis_size("rng") == 2 and dates >= 4 and 2 * lines // FOLD * TAIL <= LANES
    if az_count == 2 and whole_tiles and one_row and few and folds:
        return tiled_body(slc, offsets, kernel_index, range_shift)
    return chunked_body(slc, offsets, kernel_index, range_shift)


def solution(mesh):
    return jax.shard_map(
        body,
        mesh=mesh,
        in_specs=(
            P(None, ("groups", "date"), "az", "rng"),
            P(("groups", "date"), None),
            P(("groups", "date"), None),
            P("groups"),
        ),
        out_specs=P(None, ("groups", "date"), None, "az", "rng"),
        check_vma=False,
    )
```

```python
import functools

import jax
import jax.numpy as jnp
import numpy as np
from jax import lax
from jax.experimental import pallas as pl
from jax.experimental.pallas import tpu as pltpu
from jax.sharding import PartitionSpec as P

LAGS = 8
KERNELS = 16
TAPS = 8
FILTER_HALF = 8
FILTER_TAPS = 2 * FILTER_HALF + 1
LOOK_AZ = 4
LOOK_RG = 20
LANES = 128
META = 3
UNROLLED_PAIRS = 12


def up(value, unit):
    return -(-value // unit) * unit


def kernel_table():
    position = np.arange(TAPS) - 3.0 - np.arange(KERNELS)[:, None] / KERNELS
    shaped = np.sinc(position) * (0.5 + 0.5 * np.cos(np.pi * position / 5.0))
    table = np.zeros((KERNELS, LANES), np.float32)
    table[:, :TAPS] = shaped / shaped.sum(1, keepdims=True)
    return table


def lowpass_row(width):
    t = np.arange(FILTER_TAPS) - FILTER_HALF
    row = np.zeros((1, width), np.float32)
    row[0, :FILTER_TAPS] = 0.4 * np.sinc(0.4 * t) * (0.54 + 0.46 * np.cos(np.pi * t / (FILTER_HALF + 1)))
    return row


def halves(value):
    high = value.astype(jnp.bfloat16)
    return high, (value - high.astype(jnp.float32)).astype(jnp.bfloat16)


def dot(a, b):
    return jnp.dot(a, b, preferred_element_type=jnp.float32)


def dot_nt(a, b):
    return lax.dot_general(a, b, (((1,), (1,)), ((), ())), preferred_element_type=jnp.float32)


def pack_kernel(chunk, place_ref, offsets_ref, index_ref, slc_ref, before_ref, after_ref, out_ref, wide_ref):
    columns = slc_ref.shape[1]
    wide = out_ref.shape[2]
    first = place_ref[0] == 0
    last = place_ref[0] == place_ref[1] - 1
    zero = jnp.zeros_like(before_ref[...])
    wide_ref[:, :LANES] = jnp.where(first, zero, before_ref[...])
    wide_ref[:, LANES : LANES + columns] = slc_ref[...]
    wide_ref[:, LANES + columns :] = jnp.where(last, zero, after_ref[...])
    lane = lax.broadcasted_iota(jnp.int32, (slc_ref.shape[0], wide), 1)
    numbers = [offsets_ref[0, 0], index_ref[0, 0], index_ref[0, 1]]
    for j in range(out_ref.shape[0]):
        start = LANES + chunk * j - FILTER_HALF - 3 + offsets_ref[0, 1]
        tile = lax.shift_right_logical(start, 7)
        within = lax.bitwise_and(start, LANES - 1)
        window = wide_ref[:, pl.ds(pl.multiple_of(tile * LANES, LANES), wide + LANES)].astype(jnp.float32)
        moved = pltpu.roll(window, wide + LANES - within, 1)[:, :wide]
        for slot, number in enumerate(numbers):
            moved = jnp.where(lane == wide - META + slot, number.astype(jnp.float32), moved)
        out_ref[j] = moved.astype(jnp.bfloat16)


def picked_taps(table, index):
    row = lax.broadcasted_iota(jnp.int32, table.shape, 0).astype(jnp.float32)
    return jnp.sum(jnp.where(row == index, table, 0.0), axis=0, keepdims=True)


def banded(taps, distance):
    out = jnp.zeros(distance.shape, jnp.float32)
    for q in range(TAPS):
        out = jnp.where(distance == q, taps[:, q : q + 1], out)
    return out


def pairs_kernel(chunk, pairs, *refs):
    if isinstance(pairs, int):
        table_of_pairs, refs = refs[0], refs[1:]
    shift_ref, table_ref, lowpass_ref, recv_ref, out_ref, resampled_ref, weight_ref, product_ref = refs
    sources, rows, wide = recv_ref.shape
    dates = shift_ref.shape[0]
    az_count = sources // dates
    own_lines = rows // 2
    lines = own_lines * az_count
    groups = lines // LOOK_AZ
    looks = chunk // LOOK_RG
    table = table_ref[...]
    held = resampled_ref.shape[2]

    out_row = lax.broadcasted_iota(jnp.int32, (lines, lines), 0)
    in_row = lax.broadcasted_iota(jnp.int32, (lines, lines), 1)
    line = LOOK_AZ * (out_row % groups) + out_row // groups
    line_distance = (in_row - line + 3).astype(jnp.float32)
    span = min(2 * LANES, wide)
    column_distance = (
        lax.broadcasted_iota(jnp.int32, (span, LANES), 0) - lax.broadcasted_iota(jnp.int32, (span, LANES), 1)
    ).astype(jnp.float32)
    for date in range(dates):
        numbers = recv_ref[date * az_count, 0:16, wide - LANES :].astype(jnp.float32)[0:1, LANES - META :]
        line_offset, line_index, column_index = (numbers[:, s : s + 1] for s in range(META))
        line_taps = banded(picked_taps(table, line_index), line_distance - line_offset)
        line_taps = jnp.concatenate(halves(line_taps), axis=0)
        column_high, column_low = halves(banded(picked_taps(table, column_index), column_distance))
        moved = []
        for plane in range(2):
            rows_of = slice(plane * own_lines, (plane + 1) * own_lines)
            source = jnp.concatenate([recv_ref[date * az_count + a, rows_of, :] for a in range(az_count)], axis=0)
            both = dot(line_taps, source)
            moved.append(both[:lines] + both[lines:])
        moved_high, moved_low = halves(jnp.concatenate(moved, axis=0))
        for begin in range(0, held, LANES):
            end = min(begin + span, wide)
            taken = end - begin
            total = dot(moved_high[:, begin:end], column_high[:taken])
            total += dot(moved_low[:, begin:end], column_high[:taken])
            total += dot(moved_high[:, begin:end], column_low[:taken])
            resampled_ref[date, :, begin : begin + LANES] = total.astype(jnp.bfloat16)

    window = lowpass_ref[...]
    spacing = lax.broadcasted_iota(jnp.int32, window.shape, 1).astype(jnp.float32) - FILTER_HALF
    span = min(2 * LANES, held)

    def one_pair(place, own, other):
        gap = shift_ref[own] - shift_ref[other]
        angle = jnp.where(jnp.abs(spacing) <= FILTER_HALF, jnp.pi * gap * spacing, 0.0)
        for part, taps in enumerate((window * jnp.cos(angle), window * jnp.sin(angle))):
            spread = jnp.broadcast_to(taps, (LANES, 2 * LANES))
            spread = pltpu.roll(spread, 0, 1, stride=1, stride_axis=0)
            high, low = halves(spread)
            weight_ref[0, part * LANES : (part + 1) * LANES, :] = high
            weight_ref[1, part * LANES : (part + 1) * LANES, :] = low
        both = jnp.concatenate([resampled_ref[own], resampled_ref[other]], axis=0)
        for begin in range(0, up(chunk, LANES), LANES):
            end = min(begin + span, held)
            taken = end - begin
            total = dot_nt(both[:, begin:end], weight_ref[0, :, :taken])
            total += dot_nt(both[:, begin:end], weight_ref[1, :, :taken])
            cos, sin = total[:, :LANES], total[:, LANES:]
            re, im = slice(0, lines), slice(lines, 2 * lines)
            master_re = cos[re] + sin[im]
            master_im = cos[im] - sin[re]
            re, im = slice(2 * lines, 3 * lines), slice(3 * lines, 4 * lines)
            partner_re = cos[re] - sin[im]
            partner_im = cos[im] + sin[re]
            for part, product in enumerate(
                (
                    master_re * partner_re + master_im * partner_im,
                    master_im * partner_re - master_re * partner_im,
                )
            ):
                summed = sum(product[k * groups : (k + 1) * groups] for k in range(LOOK_AZ))
                product_ref[place, part, :, begin : begin + LANES] = summed

    if isinstance(pairs, int):
        count = pairs

        def step(place, carry):
            one_pair(place, table_of_pairs[place, 0], table_of_pairs[place, 1])
            return carry

        lax.fori_loop(0, count, step, 0)
    else:
        count = len(pairs)
        for place, (own, other) in enumerate(pairs):
            one_pair(place, own, other)

    out_width = out_ref.shape[2]
    column = lax.broadcasted_iota(jnp.int32, (product_ref.shape[3], out_width), 0)
    lane = lax.broadcasted_iota(jnp.int32, (product_ref.shape[3], out_width), 1)
    collect = jnp.where(column // LOOK_RG == lane % looks, 1.0, 0.0).astype(jnp.bfloat16)
    high, low = halves(product_ref[...].reshape(count * 2 * groups, product_ref.shape[3]))
    total = (dot(high, collect) + dot(low, collect)) * (1.0 / (LOOK_AZ * LOOK_RG))
    total = total.reshape(count, 2, groups, out_width)
    own_lane = lax.broadcasted_iota(jnp.int32, (groups, out_width), 1) // looks
    place = 0
    for own in range(dates):
        value = jnp.zeros((groups, out_width), jnp.float32)
        for lag in range(min(LAGS, dates - 1 - own)):
            for part in range(2):
                value = jnp.where(own_lane == lag * 2 + part, total[place, part], value)
            place += 1
        out_ref[own * az_count : (own + 1) * az_count] = value.reshape(az_count, groups // az_count, out_width)


def unpack_kernel(used_lags, looks, recv_ref, out_ref):
    sources, groups, width = recv_ref.shape
    columns = out_ref.shape[-1]
    lane = lax.broadcasted_iota(jnp.int32, (groups, columns), 1) // looks
    out_ref[...] = jnp.zeros_like(out_ref)
    for lag in range(used_lags):
        for part in range(2):
            value = jnp.zeros((groups, columns), jnp.float32)
            for source in range(sources):
                block = recv_ref[source]
                if width != columns:
                    block = block[:, :columns]
                shift = looks * (source - lag * 2 - part) % columns
                if shift:
                    block = pltpu.roll(block, shift, 1)
                value = jnp.where(lane == source, block, value)
            out_ref[part, lag] = value


def chunked_body(slc, offsets, kernel_index, range_shift):
    axes = ("date", "az")
    date_count, az_count, rng_count = (lax.axis_size(a) for a in ("date", "az", "rng"))
    peers = date_count * az_count
    lines, columns = slc.shape[2], slc.shape[3]
    dates = range_shift.shape[0]
    chunk = columns // peers
    looks = chunk // LOOK_RG
    groups = lines * az_count // LOOK_AZ
    wide = up(chunk + 2 * FILTER_HALF + TAPS - 1 + META, LANES)
    held = up(chunk + 2 * FILTER_HALF, LANES)
    used_lags = min(LAGS, dates - 1)
    out_width = up(used_lags * 2 * looks, LANES)
    vmem = pl.BlockSpec(memory_space=pltpu.VMEM)
    smem = pl.BlockSpec(memory_space=pltpu.SMEM)
    limit = pltpu.CompilerParams(vmem_limit_bytes=32 * 1024 * 1024)

    cells = slc.reshape(2 * lines, columns)
    place = lax.axis_index("rng")
    if rng_count == 2:
        edge = jnp.where(place == 0, cells[:, columns - LANES :], cells[:, :LANES])
        before = after = lax.ppermute(edge, "rng", [(0, 1), (1, 0)])
    else:
        forth = [(i, i + 1) for i in range(rng_count - 1)]
        before = lax.ppermute(cells[:, columns - LANES :], "rng", forth)
        after = lax.ppermute(cells[:, :LANES], "rng", [(b, a) for a, b in forth])

    packed = pl.pallas_call(
        functools.partial(pack_kernel, chunk),
        out_shape=jax.ShapeDtypeStruct((peers, 2 * lines, wide), jnp.bfloat16),
        in_specs=[smem] * 3 + [vmem] * 3,
        out_specs=vmem,
        scratch_shapes=[pltpu.VMEM((2 * lines, columns + 2 * LANES), jnp.bfloat16)],
        compiler_params=limit,
    )(jnp.stack([place, rng_count]).astype(jnp.int32), offsets, kernel_index, cells, before, after)
    arrived = lax.all_to_all(packed, axes, 0, 0, tiled=True)

    pairs = [(own, own + lag) for own in range(dates) for lag in range(1, LAGS + 1) if own + lag < dates]
    count = len(pairs)
    first = [jnp.asarray(np.array(pairs, np.int32))] if count > UNROLLED_PAIRS else []
    looked = pl.pallas_call(
        functools.partial(pairs_kernel, chunk, count if first else pairs),
        out_shape=jax.ShapeDtypeStruct((peers, groups // az_count, out_width), jnp.float32),
        in_specs=[smem] * len(first) + [smem] + [vmem] * 3,
        out_specs=vmem,
        scratch_shapes=[
            pltpu.VMEM((dates, 4 * (groups * LOOK_AZ) // 2, held), jnp.bfloat16),
            pltpu.VMEM((2, 2 * LANES, 2 * LANES), jnp.bfloat16),
            pltpu.VMEM((count, 2, groups, up(chunk, LANES)), jnp.float32),
        ],
        compiler_params=limit,
    )(*first, range_shift, jnp.asarray(kernel_table()), jnp.asarray(lowpass_row(2 * LANES)), arrived)
    returned = lax.all_to_all(looked, axes, 0, 0, tiled=True)

    out = pl.pallas_call(
        functools.partial(unpack_kernel, used_lags, looks),
        out_shape=jax.ShapeDtypeStruct((2, LAGS, groups // az_count, looks * peers), jnp.float32),
        in_specs=[vmem],
        out_specs=vmem,
        compiler_params=limit,
    )(returned)
    return out[:, None]


HALO_LINES = 16
FOLD = 16
TAIL = 2 * FILTER_HALF


def reach(step, dates):
    return {dates - 1: dates // 2, dates // 2: dates - 1}.get(step, step)


def sinc(value):
    angle = jnp.pi * value
    return jnp.where(angle == 0.0, 1.0, jnp.sin(angle) / jnp.where(angle == 0.0, 1.0, angle))


def tap_row(index):
    lane = lax.broadcasted_iota(jnp.int32, (1, LANES), 1)
    position = lane.astype(jnp.float32) - 3.0 - index.astype(jnp.float32) / KERNELS
    shaped = sinc(position) * (0.5 + 0.5 * jnp.cos(jnp.pi * position / 5.0))
    shaped = jnp.where(lane < TAPS, shaped, 0.0)
    return shaped / jnp.sum(shaped, axis=1, keepdims=True)


def row_line(row, az):
    quarter = HALO_LINES // LOOK_AZ
    within = row % HALO_LINES
    return HALO_LINES * ((row // HALO_LINES) ^ az) + LOOK_AZ * (within % quarter) + within // quarter


def prepare_kernel(offsets_hbm, index_hbm, slc_ref, side_ref, corner_ref, lines_ref, line_ref, column_ref, held_ref, offsets_ref, index_ref, semaphores):
    lines, columns = slc_ref.shape[1:]
    az = lax.axis_index("az")
    row = pl.multiple_of((1 - az) * (lines - HALO_LINES), HALO_LINES)
    edge = pl.multiple_of((1 - lax.axis_index("rng")) * (columns - LANES), LANES)
    nearest, outermost = pl.ds(row, HALO_LINES), pl.ds(edge, LANES)
    moves = [
        (offsets_hbm, offsets_ref),
        (index_hbm, index_ref),
        (slc_ref.at[:, :, outermost], side_ref),
        (slc_ref.at[:, nearest, outermost], corner_ref),
        (slc_ref.at[:, nearest, :], lines_ref),
        (slc_ref, held_ref.at[:, :, pl.ds(LANES, columns)]),
    ]
    copies = [pltpu.make_async_copy(a, b, semaphores.at[i]) for i, (a, b) in enumerate(moves)]
    for copy in copies:
        copy.start()
    held_ref[:, :, :LANES] = jnp.zeros((2, lines, LANES), held_ref.dtype)
    held_ref[:, :, LANES + columns :] = jnp.zeros((2, lines, 2 * LANES), held_ref.dtype)
    copies[0].wait()
    copies[1].wait()
    for half in range(2):
        shape = (HALO_LINES, lines + HALO_LINES)
        line = row_line(lax.broadcasted_iota(jnp.int32, shape, 0) + half * HALO_LINES, az)
        place = lax.broadcasted_iota(jnp.int32, shape, 1)
        source = jnp.where(place < lines, place, place + jnp.where(az == 0, 0, -lines - HALO_LINES))
        taps = banded(tap_row(index_ref[0, 0]), source - line - offsets_ref[0, 0] + 3)
        line_ref[half] = jnp.concatenate(halves(taps), axis=0)
    shape = (3 * LANES, LANES)
    distance = lax.broadcasted_iota(jnp.int32, shape, 0) - lax.broadcasted_iota(jnp.int32, shape, 1)
    distance = distance - (LANES - FILTER_HALF - 3) - offsets_ref[0, 1]
    taps = banded(tap_row(index_ref[0, 1]), distance)
    column_ref[...] = jnp.concatenate(halves(taps), axis=1)
    for copy in copies[2:]:
        copy.wait()


def along_range(moved, column_ref, tiles):
    high, low = halves(moved)
    starts = range(0, tiles * LANES, LANES)
    high = jnp.concatenate([high[:, s : s + 3 * LANES] for s in starts], axis=0)
    low = jnp.concatenate([low[:, s : s + 3 * LANES] for s in starts], axis=0)
    total = dot(high, column_ref[...])
    return total[:, :LANES] + total[:, LANES:] + dot(low, column_ref[:, :LANES])


def early_kernel(tiles, held_ref, line_ref, column_ref, out_ref):
    lines = held_ref.shape[1]
    early = out_ref.shape[0] // (2 * HALO_LINES)
    dates = lax.axis_size("date")
    chunk = lax.axis_index("date") ^ reach(dates - 1, dates)
    begin = pl.multiple_of((chunk * tiles + lax.axis_index("rng")) * LANES, LANES)
    moved = []
    for plane in range(2):
        both = dot(line_ref[0, :, :lines], held_ref[plane, :, pl.ds(begin, (early + 2) * LANES)])
        moved.append(both[:HALO_LINES] + both[HALO_LINES:])
    moved = jnp.concatenate(moved, axis=0)
    out_ref[...] = along_range(moved, column_ref, early).astype(jnp.bfloat16)


def resample_kernel(side_ref, corner_ref, lines_ref, held_ref, line_ref, column_ref, *outs):
    outs, tiles_ref, tails_ref = outs[:-2], outs[-2], outs[-1]
    lines, width = held_ref.shape[1:]
    width -= LANES
    block = lax.axis_index("rng")
    taps = jnp.concatenate([line_ref[0], line_ref[1]], axis=0)
    moved = [[], []]
    for plane in range(2):
        own = jnp.concatenate([side_ref[plane], held_ref[plane, :, LANES : width - LANES], side_ref[plane]], axis=1)
        halo = jnp.concatenate([corner_ref[plane], lines_ref[plane], corner_ref[plane]], axis=1)
        both = dot(taps, jnp.concatenate([own, halo], axis=0))
        for half in range(2):
            at = 2 * half * HALO_LINES
            moved[half].append(both[at : at + HALO_LINES] + both[at + HALO_LINES : at + 2 * HALO_LINES])
    moved = jnp.concatenate(moved[0] + moved[1], axis=0)
    left = jnp.where(block > 0, moved[:, :LANES], 0.0)
    right = jnp.where(block == 0, moved[:, width - LANES :], 0.0)
    moved = jnp.concatenate([left, moved[:, LANES : width - LANES], right, jnp.zeros_like(right)], axis=1)
    total = along_range(moved, column_ref, width // LANES - 1)
    rows = 2 * lines
    tiles_ref[...] = total.astype(jnp.bfloat16)
    chunk_rows = outs[0].shape[0] - FOLD
    lane = lax.broadcasted_iota(jnp.int32, (FOLD, LANES), 1) // TAIL
    for chunk in range(len(outs)):
        begin = (chunk + 1) * chunk_rows
        folded = total[begin : begin + FOLD]
        for part in range(1, rows // FOLD):
            value = pltpu.roll(total[begin + part * FOLD : begin + (part + 1) * FOLD], part * TAIL, 1)
            folded = jnp.where(lane == part, value, folded)
        tails_ref[chunk] = folded.astype(jnp.bfloat16)
    date = lax.axis_index("date")
    for step, out_ref in enumerate(outs[:-1]):
        chunk = date ^ reach(step, len(outs))
        out_ref[:chunk_rows] = tiles_ref[pl.ds(pl.multiple_of(chunk * chunk_rows, FOLD), chunk_rows), :]
        out_ref[chunk_rows:] = tails_ref[chunk]
    out_ref = outs[-1]
    chunk = date ^ reach(len(outs) - 1, len(outs))
    early = chunk_rows // rows - 1
    for tile in range(early):
        begin = pl.multiple_of(chunk * chunk_rows + (tile + block) * rows + lines, FOLD)
        out_ref[tile * lines : (tile + 1) * lines] = tiles_ref[pl.ds(begin, lines), :]
    begin = pl.multiple_of(chunk * chunk_rows + (1 - block) * early * rows, FOLD)
    out_ref[early * lines : early * lines + rows] = tiles_ref[pl.ds(begin, rows), :]
    out_ref[early * lines + rows :] = tails_ref[chunk]


def filter_kernel(pairs, shift_hbm, early_ref, out_ref, spread_ref, shift_ref, semaphore):
    copy = pltpu.make_async_copy(shift_hbm, shift_ref, semaphore)
    copy.start()
    lines = 2 * HALO_LINES
    spread_ref[...] = jnp.zeros_like(spread_ref)
    for tile in range(early_ref.shape[0] // lines):
        begin = pl.multiple_of((tile + lax.axis_index("rng")) * 2 * lines, FOLD)
        spread_ref[pl.ds(begin, lines), :] = early_ref[tile * lines : (tile + 1) * lines]
    date = lax.axis_index("date")
    spacing = lax.broadcasted_iota(jnp.int32, (1, 2 * LANES), 1).astype(jnp.float32) - FILTER_HALF
    window = 0.4 * sinc(0.4 * spacing) * (0.54 + 0.46 * jnp.cos(jnp.pi * spacing / (FILTER_HALF + 1)))
    window = jnp.where(jnp.abs(spacing) <= FILTER_HALF, window, 0.0)
    copy.wait()
    for place, (first, second) in enumerate(pairs):
        dates = shift_ref.shape[0]
        gap = shift_ref[date ^ reach(first, dates)] - shift_ref[date ^ reach(second, dates)]
        angle = jnp.where(jnp.abs(spacing) <= FILTER_HALF, jnp.pi * gap * spacing, 0.0)
        for part, taps in enumerate((window * jnp.cos(angle), window * jnp.sin(angle))):
            spread = jnp.broadcast_to(taps, (LANES, 2 * LANES))
            spread = pltpu.roll(spread, 0, 1, stride=1, stride_axis=0)
            high, low = halves(spread)
            out_ref[place, 0, part * LANES : (part + 1) * LANES, :] = high
            out_ref[place, 1, part * LANES : (part + 1) * LANES, :] = low


def looks_kernel(pairs, dates, weight_ref, *refs):
    early_ref, chunks, outs = refs[0], list(refs[1 : dates + 1][::-1]), refs[dates + 1 : 2 * dates + 1]
    whole_ref, window_ref, product_ref = refs[-3:]
    groups, lines = outs[0].shape[0], outs[0].shape[0] * LOOK_AZ
    rows = 2 * lines
    blocks = (chunks[0].shape[0] - FOLD) // rows
    looks = blocks * LANES // LOOK_RG
    date = lax.axis_index("date")
    block = lax.axis_index("rng")
    early = blocks - 1
    whole_ref[: blocks * rows] = early_ref[...]
    for tile in range(early):
        begin = pl.multiple_of((tile + block) * rows, FOLD)
        whole_ref[pl.ds(begin + lines, lines), :] = chunks[-1][tile * lines : (tile + 1) * lines]
    begin = pl.multiple_of((1 - block) * early * rows, FOLD)
    whole_ref[pl.ds(begin, rows), :] = chunks[-1][early * lines : early * lines + rows]
    whole_ref[blocks * rows :] = chunks[-1][early * lines + rows :]
    chunks[-1] = whole_ref
    az = lax.axis_index("az")
    upper = lax.broadcasted_iota(jnp.int32, (groups, LANES), 0) // (groups // 2) == az
    for step, chunk_ref in enumerate(chunks):
        window_ref[step, :, :LANES] = chunk_ref[: blocks * rows]
        window_ref[step, : (blocks - 1) * rows, LANES:] = chunk_ref[rows : blocks * rows]
        folded = chunk_ref[blocks * rows :].astype(jnp.float32)
        for part in range(rows // FOLD):
            value = pltpu.roll(folded, LANES - part * TAIL, 1) if part else folded
            at = pl.ds((blocks - 1) * rows + part * FOLD, FOLD)
            window_ref[step, at, LANES:] = value.astype(jnp.bfloat16)
    for place, (first, second) in enumerate(pairs):
        def filtered(step):
            total = dot_nt(window_ref[step], weight_ref[place, 0]) + dot_nt(window_ref[step], weight_ref[place, 1])
            total = total.reshape(blocks, 2, 2, HALO_LINES, 2 * LANES)
            re, im = total[:, :, 0], total[:, :, 1]
            return re[..., :LANES], im[..., :LANES], re[..., LANES:], im[..., LANES:]

        cos_re, cos_im, sin_re, sin_im = filtered(first)
        master_re, master_im = cos_re + sin_im, cos_im - sin_re
        cos_re, cos_im, sin_re, sin_im = filtered(second)
        partner_re, partner_im = cos_re - sin_im, cos_im + sin_re
        for part, product in enumerate(
            (
                master_re * partner_re + master_im * partner_im,
                master_im * partner_re - master_re * partner_im,
            )
        ):
            summed = product[:, :, :groups] + product[:, :, groups:]
            at = pl.ds((place * 2 + part) * groups, groups)
            for k in range(blocks):
                both = [summed[k, half] + pltpu.roll(summed[k, half], groups // 2, 0) for half in range(2)]
                product_ref[at, k * LANES : (k + 1) * LANES] = jnp.where(upper, both[0], both[1])

    out_width = outs[0].shape[1]
    column = lax.broadcasted_iota(jnp.int32, (product_ref.shape[1], out_width), 0)
    lane = lax.broadcasted_iota(jnp.int32, (product_ref.shape[1], out_width), 1)
    collect = jnp.where(column // LOOK_RG == lane % looks, 1.0, 0.0).astype(jnp.bfloat16)
    high, low = halves(product_ref[...])
    total = (dot(high, collect) + dot(low, collect)) * (1.0 / (LOOK_AZ * LOOK_RG))
    total = total.reshape(len(pairs), 2, groups, out_width)
    own_lane = lax.broadcasted_iota(jnp.int32, (groups, out_width), 1) // looks
    for step, out_ref in enumerate(outs):
        value = jnp.zeros((groups, out_width), jnp.float32)
        for place, pair in enumerate(pairs):
            if step in pair:
                other = pair[1] if pair[0] == step else pair[0]
                lag = (date ^ reach(other, dates)) - (date ^ reach(step, dates))
                for part in range(2):
                    signed = -total[place, part] if part == 1 and pair[1] == step else total[place, part]
                    value = jnp.where(own_lane == (lag - 1) * 2 + part, signed, value)
        out_ref[...] = value


def place_kernel(used_lags, looks, *refs):
    out_ref = refs[-1]
    groups, columns = out_ref.shape[2:]
    date = lax.axis_index("date")
    lane = lax.broadcasted_iota(jnp.int32, (groups, LANES), 1) // looks
    out_ref[...] = jnp.zeros_like(out_ref)
    each = LANES // looks
    for step, recv_ref in enumerate(refs[:-1][::-1]):
        chunk = date ^ reach(step, len(refs) - 1)
        for lag in range(used_lags):
            for part in range(2):
                tile, group = divmod(lag * 2 + part, each)
                block = recv_ref[:, tile * LANES : (tile + 1) * LANES]
                block = pltpu.roll(block, lax.bitwise_and(looks * (chunk - group), LANES - 1), 1)
                out_ref[part, lag] = jnp.where(lane == chunk, block, out_ref[part, lag])


def tiled_body(slc, offsets, kernel_index, range_shift):
    dates = lax.axis_size("date")
    lines, columns = slc.shape[2], slc.shape[3]
    chunk = columns // dates
    looks = chunk // LOOK_RG
    groups = lines // LOOK_AZ
    out_width = up(min(LAGS, dates - 1) * 2 * looks, LANES)
    vmem = pl.BlockSpec(memory_space=pltpu.VMEM)
    hbm = pl.BlockSpec(memory_space=pltpu.HBM)
    limit = pltpu.CompilerParams(vmem_limit_bytes=32 * 1024 * 1024)
    bf16 = jnp.bfloat16
    cells, offsets, kernel_index, range_shift = (
        pltpu.with_memory_space_constraint(value, pltpu.HBM)
        for value in (slc.reshape(2, lines, columns), offsets, kernel_index, range_shift)
    )
    tiles = chunk // LANES
    chunk_rows = tiles * 2 * lines

    side, corner, halo_lines, line_taps, column_taps, held = pl.pallas_call(
        prepare_kernel,
        out_shape=[
            jax.ShapeDtypeStruct((2, lines, LANES), bf16),
            jax.ShapeDtypeStruct((2, HALO_LINES, LANES), bf16),
            jax.ShapeDtypeStruct((2, HALO_LINES, columns), bf16),
            jax.ShapeDtypeStruct((2, 2 * HALO_LINES, lines + HALO_LINES), bf16),
            jax.ShapeDtypeStruct((3 * LANES, 2 * LANES), bf16),
            jax.ShapeDtypeStruct((2, lines, columns + 3 * LANES), bf16),
        ],
        in_specs=[hbm] * 3,
        out_specs=[vmem] * 6,
        scratch_shapes=[
            pltpu.SMEM(offsets.shape, jnp.int32),
            pltpu.SMEM(kernel_index.shape, jnp.int32),
            pltpu.SemaphoreType.DMA((6,)),
        ],
        compiler_params=limit,
    )(offsets, kernel_index, cells)
    swap = [(0, 1), (1, 0)]
    side = lax.ppermute(side, "rng", swap)
    corner = lax.ppermute(corner, ("rng", "az"), [(0, 3), (1, 2), (2, 1), (3, 0)])
    halo_lines = lax.ppermute(halo_lines, "az", swap)

    early_rows = (tiles - 1) * lines
    early = pl.pallas_call(
        functools.partial(early_kernel, tiles),
        out_shape=jax.ShapeDtypeStruct((early_rows, LANES), bf16),
        in_specs=[vmem] * 3,
        out_specs=vmem,
        compiler_params=limit,
    )(held, line_taps, column_taps)
    early = lax.ppermute(early, "date", [(i, i ^ reach(dates - 1, dates)) for i in range(dates)])
    out_rows = [chunk_rows + FOLD] * (dates - 1) + [chunk_rows + FOLD - early_rows]
    sent = pl.pallas_call(
        resample_kernel,
        out_shape=[jax.ShapeDtypeStruct((rows, LANES), bf16) for rows in out_rows],
        in_specs=[vmem] * 6,
        out_specs=[vmem] * dates,
        scratch_shapes=[
            pltpu.VMEM(((columns // LANES + 1) * 2 * lines, LANES), bf16),
            pltpu.VMEM((dates, FOLD, LANES), bf16),
        ],
        compiler_params=limit,
    )(side, corner, halo_lines, held, line_taps, column_taps)

    def exchanged(values, order):
        arrived = {0: values[0]}
        for step in order:
            arrived[step] = lax.ppermute(values[step], "date", [(i, i ^ reach(step, dates)) for i in range(dates)])
        return [arrived[step] for step in reversed(range(dates))]

    steps = range(dates - 1, 0, -1)

    chunks = exchanged(sent, steps)
    pairs = [(first, second) for first in range(dates) for second in range(first + 1, dates)]
    weights, early = pl.pallas_call(
        functools.partial(filter_kernel, pairs),
        out_shape=[
            jax.ShapeDtypeStruct((len(pairs), 2, 2 * LANES, 2 * LANES), bf16),
            jax.ShapeDtypeStruct((chunk_rows, LANES), bf16),
        ],
        in_specs=[hbm, vmem],
        out_specs=[vmem] * 2,
        scratch_shapes=[pltpu.SMEM(range_shift.shape, jnp.float32), pltpu.SemaphoreType.DMA],
        compiler_params=limit,
        cost_estimate=pl.CostEstimate(flops=600_000_000, bytes_accessed=0, transcendentals=0),
    )(range_shift, early)
    looked = pl.pallas_call(
        functools.partial(looks_kernel, pairs, dates),
        out_shape=[jax.ShapeDtypeStruct((groups, out_width), jnp.float32)] * dates,
        in_specs=[vmem] * (2 + dates),
        out_specs=[vmem] * dates,
        scratch_shapes=[
            pltpu.VMEM((chunk_rows + FOLD, LANES), bf16),
            pltpu.VMEM((dates, chunk_rows, 2 * LANES), bf16),
            pltpu.VMEM((len(pairs) * 2 * groups, chunk), jnp.float32),
        ],
        compiler_params=limit,
    )(weights, early, *chunks)
    out = pl.pallas_call(
        functools.partial(place_kernel, min(LAGS, dates - 1), looks),
        out_shape=jax.ShapeDtypeStruct((2, LAGS, groups, looks * dates), jnp.float32),
        in_specs=[vmem] * dates,
        out_specs=vmem,
        compiler_params=limit,
    )(*exchanged(looked, steps))
    return out[:, None]


def body(slc, offsets, kernel_index, range_shift):
    dates, az_count = (lax.axis_size(a) for a in ("date", "az"))
    lines, columns = slc.shape[2], slc.shape[3]
    whole_tiles = columns % (dates * LANES) == 0 and columns % (dates * LOOK_RG) == 0
    one_row = columns // LOOK_RG == LANES and range_shift.shape[0] == dates
    few = dates & (dates - 1) == 0 and dates - 1 <= LAGS
    folds = lines == 2 * HALO_LINES and lax.axis_size("rng") == 2 and dates >= 4 and 2 * lines // FOLD * TAIL <= LANES
    if az_count == 2 and whole_tiles and one_row and few and folds:
        return tiled_body(slc, offsets, kernel_index, range_shift)
    return chunked_body(slc, offsets, kernel_index, range_shift)


def solution(mesh):
    return jax.shard_map(
        body,
        mesh=mesh,
        in_specs=(
            P(None, ("groups", "date"), "az", "rng"),
            P(("groups", "date"), None),
            P(("groups", "date"), None),
            P("groups"),
        ),
        out_specs=P(None, ("groups", "date"), None, "az", "rng"),
        check_vma=False,
    )
```

```python
import functools

import jax
import jax.numpy as jnp
import numpy as np
from jax import lax
from jax.experimental import pallas as pl
from jax.experimental.pallas import tpu as pltpu
from jax.sharding import PartitionSpec as P

LAGS = 8
KERNELS = 16
TAPS = 8
FILTER_HALF = 8
FILTER_TAPS = 2 * FILTER_HALF + 1
LOOK_AZ = 4
LOOK_RG = 20
LANES = 128
META = 3
UNROLLED_PAIRS = 12


def up(value, unit):
    return -(-value // unit) * unit


def kernel_table():
    position = np.arange(TAPS) - 3.0 - np.arange(KERNELS)[:, None] / KERNELS
    shaped = np.sinc(position) * (0.5 + 0.5 * np.cos(np.pi * position / 5.0))
    table = np.zeros((KERNELS, LANES), np.float32)
    table[:, :TAPS] = shaped / shaped.sum(1, keepdims=True)
    return table


def lowpass_row(width):
    t = np.arange(FILTER_TAPS) - FILTER_HALF
    row = np.zeros((1, width), np.float32)
    row[0, :FILTER_TAPS] = 0.4 * np.sinc(0.4 * t) * (0.54 + 0.46 * np.cos(np.pi * t / (FILTER_HALF + 1)))
    return row


def halves(value):
    high = value.astype(jnp.bfloat16)
    return high, (value - high.astype(jnp.float32)).astype(jnp.bfloat16)


def dot(a, b):
    return jnp.dot(a, b, preferred_element_type=jnp.float32)


def dot_nt(a, b):
    return lax.dot_general(a, b, (((1,), (1,)), ((), ())), preferred_element_type=jnp.float32)


def pack_kernel(chunk, place_ref, offsets_ref, index_ref, slc_ref, before_ref, after_ref, out_ref, wide_ref):
    columns = slc_ref.shape[1]
    wide = out_ref.shape[2]
    first = place_ref[0] == 0
    last = place_ref[0] == place_ref[1] - 1
    zero = jnp.zeros_like(before_ref[...])
    wide_ref[:, :LANES] = jnp.where(first, zero, before_ref[...])
    wide_ref[:, LANES : LANES + columns] = slc_ref[...]
    wide_ref[:, LANES + columns :] = jnp.where(last, zero, after_ref[...])
    lane = lax.broadcasted_iota(jnp.int32, (slc_ref.shape[0], wide), 1)
    numbers = [offsets_ref[0, 0], index_ref[0, 0], index_ref[0, 1]]
    for j in range(out_ref.shape[0]):
        start = LANES + chunk * j - FILTER_HALF - 3 + offsets_ref[0, 1]
        tile = lax.shift_right_logical(start, 7)
        within = lax.bitwise_and(start, LANES - 1)
        window = wide_ref[:, pl.ds(pl.multiple_of(tile * LANES, LANES), wide + LANES)].astype(jnp.float32)
        moved = pltpu.roll(window, wide + LANES - within, 1)[:, :wide]
        for slot, number in enumerate(numbers):
            moved = jnp.where(lane == wide - META + slot, number.astype(jnp.float32), moved)
        out_ref[j] = moved.astype(jnp.bfloat16)


def picked_taps(table, index):
    row = lax.broadcasted_iota(jnp.int32, table.shape, 0).astype(jnp.float32)
    return jnp.sum(jnp.where(row == index, table, 0.0), axis=0, keepdims=True)


def banded(taps, distance):
    out = jnp.zeros(distance.shape, jnp.float32)
    for q in range(TAPS):
        out = jnp.where(distance == q, taps[:, q : q + 1], out)
    return out


def pairs_kernel(chunk, pairs, *refs):
    if isinstance(pairs, int):
        table_of_pairs, refs = refs[0], refs[1:]
    shift_ref, table_ref, lowpass_ref, recv_ref, out_ref, resampled_ref, weight_ref, product_ref = refs
    sources, rows, wide = recv_ref.shape
    dates = shift_ref.shape[0]
    az_count = sources // dates
    own_lines = rows // 2
    lines = own_lines * az_count
    groups = lines // LOOK_AZ
    looks = chunk // LOOK_RG
    table = table_ref[...]
    held = resampled_ref.shape[2]

    out_row = lax.broadcasted_iota(jnp.int32, (lines, lines), 0)
    in_row = lax.broadcasted_iota(jnp.int32, (lines, lines), 1)
    line = LOOK_AZ * (out_row % groups) + out_row // groups
    line_distance = (in_row - line + 3).astype(jnp.float32)
    span = min(2 * LANES, wide)
    column_distance = (
        lax.broadcasted_iota(jnp.int32, (span, LANES), 0) - lax.broadcasted_iota(jnp.int32, (span, LANES), 1)
    ).astype(jnp.float32)
    for date in range(dates):
        numbers = recv_ref[date * az_count, 0:16, wide - LANES :].astype(jnp.float32)[0:1, LANES - META :]
        line_offset, line_index, column_index = (numbers[:, s : s + 1] for s in range(META))
        line_taps = banded(picked_taps(table, line_index), line_distance - line_offset)
        line_taps = jnp.concatenate(halves(line_taps), axis=0)
        column_high, column_low = halves(banded(picked_taps(table, column_index), column_distance))
        moved = []
        for plane in range(2):
            rows_of = slice(plane * own_lines, (plane + 1) * own_lines)
            source = jnp.concatenate([recv_ref[date * az_count + a, rows_of, :] for a in range(az_count)], axis=0)
            both = dot(line_taps, source)
            moved.append(both[:lines] + both[lines:])
        moved_high, moved_low = halves(jnp.concatenate(moved, axis=0))
        for begin in range(0, held, LANES):
            end = min(begin + span, wide)
            taken = end - begin
            total = dot(moved_high[:, begin:end], column_high[:taken])
            total += dot(moved_low[:, begin:end], column_high[:taken])
            total += dot(moved_high[:, begin:end], column_low[:taken])
            resampled_ref[date, :, begin : begin + LANES] = total.astype(jnp.bfloat16)

    window = lowpass_ref[...]
    spacing = lax.broadcasted_iota(jnp.int32, window.shape, 1).astype(jnp.float32) - FILTER_HALF
    span = min(2 * LANES, held)

    def one_pair(place, own, other):
        gap = shift_ref[own] - shift_ref[other]
        angle = jnp.where(jnp.abs(spacing) <= FILTER_HALF, jnp.pi * gap * spacing, 0.0)
        for part, taps in enumerate((window * jnp.cos(angle), window * jnp.sin(angle))):
            spread = jnp.broadcast_to(taps, (LANES, 2 * LANES))
            spread = pltpu.roll(spread, 0, 1, stride=1, stride_axis=0)
            high, low = halves(spread)
            weight_ref[0, part * LANES : (part + 1) * LANES, :] = high
            weight_ref[1, part * LANES : (part + 1) * LANES, :] = low
        both = jnp.concatenate([resampled_ref[own], resampled_ref[other]], axis=0)
        for begin in range(0, up(chunk, LANES), LANES):
            end = min(begin + span, held)
            taken = end - begin
            total = dot_nt(both[:, begin:end], weight_ref[0, :, :taken])
            total += dot_nt(both[:, begin:end], weight_ref[1, :, :taken])
            cos, sin = total[:, :LANES], total[:, LANES:]
            re, im = slice(0, lines), slice(lines, 2 * lines)
            master_re = cos[re] + sin[im]
            master_im = cos[im] - sin[re]
            re, im = slice(2 * lines, 3 * lines), slice(3 * lines, 4 * lines)
            partner_re = cos[re] - sin[im]
            partner_im = cos[im] + sin[re]
            for part, product in enumerate(
                (
                    master_re * partner_re + master_im * partner_im,
                    master_im * partner_re - master_re * partner_im,
                )
            ):
                summed = sum(product[k * groups : (k + 1) * groups] for k in range(LOOK_AZ))
                product_ref[place, part, :, begin : begin + LANES] = summed

    if isinstance(pairs, int):
        count = pairs

        def step(place, carry):
            one_pair(place, table_of_pairs[place, 0], table_of_pairs[place, 1])
            return carry

        lax.fori_loop(0, count, step, 0)
    else:
        count = len(pairs)
        for place, (own, other) in enumerate(pairs):
            one_pair(place, own, other)

    out_width = out_ref.shape[2]
    column = lax.broadcasted_iota(jnp.int32, (product_ref.shape[3], out_width), 0)
    lane = lax.broadcasted_iota(jnp.int32, (product_ref.shape[3], out_width), 1)
    collect = jnp.where(column // LOOK_RG == lane % looks, 1.0, 0.0).astype(jnp.bfloat16)
    high, low = halves(product_ref[...].reshape(count * 2 * groups, product_ref.shape[3]))
    total = (dot(high, collect) + dot(low, collect)) * (1.0 / (LOOK_AZ * LOOK_RG))
    total = total.reshape(count, 2, groups, out_width)
    own_lane = lax.broadcasted_iota(jnp.int32, (groups, out_width), 1) // looks
    place = 0
    for own in range(dates):
        value = jnp.zeros((groups, out_width), jnp.float32)
        for lag in range(min(LAGS, dates - 1 - own)):
            for part in range(2):
                value = jnp.where(own_lane == lag * 2 + part, total[place, part], value)
            place += 1
        out_ref[own * az_count : (own + 1) * az_count] = value.reshape(az_count, groups // az_count, out_width)


def unpack_kernel(used_lags, looks, recv_ref, out_ref):
    sources, groups, width = recv_ref.shape
    columns = out_ref.shape[-1]
    lane = lax.broadcasted_iota(jnp.int32, (groups, columns), 1) // looks
    out_ref[...] = jnp.zeros_like(out_ref)
    for lag in range(used_lags):
        for part in range(2):
            value = jnp.zeros((groups, columns), jnp.float32)
            for source in range(sources):
                block = recv_ref[source]
                if width != columns:
                    block = block[:, :columns]
                shift = looks * (source - lag * 2 - part) % columns
                if shift:
                    block = pltpu.roll(block, shift, 1)
                value = jnp.where(lane == source, block, value)
            out_ref[part, lag] = value


def chunked_body(slc, offsets, kernel_index, range_shift):
    axes = ("date", "az")
    date_count, az_count, rng_count = (lax.axis_size(a) for a in ("date", "az", "rng"))
    peers = date_count * az_count
    lines, columns = slc.shape[2], slc.shape[3]
    dates = range_shift.shape[0]
    chunk = columns // peers
    looks = chunk // LOOK_RG
    groups = lines * az_count // LOOK_AZ
    wide = up(chunk + 2 * FILTER_HALF + TAPS - 1 + META, LANES)
    held = up(chunk + 2 * FILTER_HALF, LANES)
    used_lags = min(LAGS, dates - 1)
    out_width = up(used_lags * 2 * looks, LANES)
    vmem = pl.BlockSpec(memory_space=pltpu.VMEM)
    smem = pl.BlockSpec(memory_space=pltpu.SMEM)
    limit = pltpu.CompilerParams(vmem_limit_bytes=32 * 1024 * 1024)

    cells = slc.reshape(2 * lines, columns)
    place = lax.axis_index("rng")
    if rng_count == 2:
        edge = jnp.where(place == 0, cells[:, columns - LANES :], cells[:, :LANES])
        before = after = lax.ppermute(edge, "rng", [(0, 1), (1, 0)])
    else:
        forth = [(i, i + 1) for i in range(rng_count - 1)]
        before = lax.ppermute(cells[:, columns - LANES :], "rng", forth)
        after = lax.ppermute(cells[:, :LANES], "rng", [(b, a) for a, b in forth])

    packed = pl.pallas_call(
        functools.partial(pack_kernel, chunk),
        out_shape=jax.ShapeDtypeStruct((peers, 2 * lines, wide), jnp.bfloat16),
        in_specs=[smem] * 3 + [vmem] * 3,
        out_specs=vmem,
        scratch_shapes=[pltpu.VMEM((2 * lines, columns + 2 * LANES), jnp.bfloat16)],
        compiler_params=limit,
    )(jnp.stack([place, rng_count]).astype(jnp.int32), offsets, kernel_index, cells, before, after)
    arrived = lax.all_to_all(packed, axes, 0, 0, tiled=True)

    pairs = [(own, own + lag) for own in range(dates) for lag in range(1, LAGS + 1) if own + lag < dates]
    count = len(pairs)
    first = [jnp.asarray(np.array(pairs, np.int32))] if count > UNROLLED_PAIRS else []
    looked = pl.pallas_call(
        functools.partial(pairs_kernel, chunk, count if first else pairs),
        out_shape=jax.ShapeDtypeStruct((peers, groups // az_count, out_width), jnp.float32),
        in_specs=[smem] * len(first) + [smem] + [vmem] * 3,
        out_specs=vmem,
        scratch_shapes=[
            pltpu.VMEM((dates, 4 * (groups * LOOK_AZ) // 2, held), jnp.bfloat16),
            pltpu.VMEM((2, 2 * LANES, 2 * LANES), jnp.bfloat16),
            pltpu.VMEM((count, 2, groups, up(chunk, LANES)), jnp.float32),
        ],
        compiler_params=limit,
    )(*first, range_shift, jnp.asarray(kernel_table()), jnp.asarray(lowpass_row(2 * LANES)), arrived)
    returned = lax.all_to_all(looked, axes, 0, 0, tiled=True)

    out = pl.pallas_call(
        functools.partial(unpack_kernel, used_lags, looks),
        out_shape=jax.ShapeDtypeStruct((2, LAGS, groups // az_count, looks * peers), jnp.float32),
        in_specs=[vmem],
        out_specs=vmem,
        compiler_params=limit,
    )(returned)
    return out[:, None]


HALO_LINES = 16
FOLD = 16
TAIL = 2 * FILTER_HALF


def reach(step, dates):
    return {dates - 1: dates // 2, dates // 2: dates - 1}.get(step, step)


def sinc(value):
    angle = jnp.pi * value
    return jnp.where(angle == 0.0, 1.0, jnp.sin(angle) / jnp.where(angle == 0.0, 1.0, angle))


def tap_row(index):
    lane = lax.broadcasted_iota(jnp.int32, (1, LANES), 1)
    position = lane.astype(jnp.float32) - 3.0 - index.astype(jnp.float32) / KERNELS
    shaped = sinc(position) * (0.5 + 0.5 * jnp.cos(jnp.pi * position / 5.0))
    shaped = jnp.where(lane < TAPS, shaped, 0.0)
    return shaped / jnp.sum(shaped, axis=1, keepdims=True)


def row_line(row, az):
    quarter = HALO_LINES // LOOK_AZ
    within = row % HALO_LINES
    return HALO_LINES * ((row // HALO_LINES) ^ az) + LOOK_AZ * (within % quarter) + within // quarter


def prepare_kernel(offsets_hbm, index_hbm, slc_ref, side_ref, corner_ref, lines_ref, line_ref, column_ref, held_ref, offsets_ref, index_ref, semaphores):
    lines, columns = slc_ref.shape[1:]
    az = lax.axis_index("az")
    row = pl.multiple_of((1 - az) * (lines - HALO_LINES), HALO_LINES)
    edge = pl.multiple_of((1 - lax.axis_index("rng")) * (columns - LANES), LANES)
    nearest, outermost = pl.ds(row, HALO_LINES), pl.ds(edge, LANES)
    moves = [
        (offsets_hbm, offsets_ref),
        (index_hbm, index_ref),
        (slc_ref.at[:, :, outermost], side_ref),
        (slc_ref.at[:, nearest, outermost], corner_ref),
        (slc_ref.at[:, nearest, :], lines_ref),
        (slc_ref, held_ref.at[:, :, pl.ds(LANES, columns)]),
    ]
    copies = [pltpu.make_async_copy(a, b, semaphores.at[i]) for i, (a, b) in enumerate(moves)]
    for copy in copies:
        copy.start()
    held_ref[:, :, :LANES] = jnp.zeros((2, lines, LANES), held_ref.dtype)
    held_ref[:, :, LANES + columns :] = jnp.zeros((2, lines, 2 * LANES), held_ref.dtype)
    copies[0].wait()
    copies[1].wait()
    for half in range(2):
        shape = (HALO_LINES, lines + HALO_LINES)
        line = row_line(lax.broadcasted_iota(jnp.int32, shape, 0) + half * HALO_LINES, az)
        place = lax.broadcasted_iota(jnp.int32, shape, 1)
        source = jnp.where(place < lines, place, place + jnp.where(az == 0, 0, -lines - HALO_LINES))
        taps = banded(tap_row(index_ref[0, 0]), source - line - offsets_ref[0, 0] + 3)
        line_ref[half] = jnp.concatenate(halves(taps), axis=0)
    shape = (3 * LANES, LANES)
    distance = lax.broadcasted_iota(jnp.int32, shape, 0) - lax.broadcasted_iota(jnp.int32, shape, 1)
    distance = distance - (LANES - FILTER_HALF - 3) - offsets_ref[0, 1]
    taps = banded(tap_row(index_ref[0, 1]), distance)
    column_ref[...] = jnp.concatenate(halves(taps), axis=1)
    for copy in copies[2:]:
        copy.wait()


def along_range(moved, column_ref, tiles):
    high, low = halves(moved)
    starts = range(0, tiles * LANES, LANES)
    high = jnp.concatenate([high[:, s : s + 3 * LANES] for s in starts], axis=0)
    low = jnp.concatenate([low[:, s : s + 3 * LANES] for s in starts], axis=0)
    total = dot(high, column_ref[...])
    return total[:, :LANES] + total[:, LANES:] + dot(low, column_ref[:, :LANES])


def early_kernel(tiles, held_ref, line_ref, column_ref, out_ref):
    lines = held_ref.shape[1]
    early = out_ref.shape[0] // (2 * HALO_LINES)
    dates = lax.axis_size("date")
    chunk = lax.axis_index("date") ^ reach(dates - 1, dates)
    begin = pl.multiple_of((chunk * tiles + lax.axis_index("rng")) * LANES, LANES)
    moved = []
    for plane in range(2):
        both = dot(line_ref[0, :, :lines], held_ref[plane, :, pl.ds(begin, (early + 2) * LANES)])
        moved.append(both[:HALO_LINES] + both[HALO_LINES:])
    moved = jnp.concatenate(moved, axis=0)
    out_ref[...] = along_range(moved, column_ref, early).astype(jnp.bfloat16)


def resample_kernel(side_ref, corner_ref, lines_ref, held_ref, line_ref, column_ref, *outs):
    outs, tiles_ref, tails_ref = outs[:-2], outs[-2], outs[-1]
    lines, width = held_ref.shape[1:]
    width -= LANES
    block = lax.axis_index("rng")
    taps = jnp.concatenate([line_ref[0], line_ref[1]], axis=0)
    moved = [[], []]
    for plane in range(2):
        own = jnp.concatenate([side_ref[plane], held_ref[plane, :, LANES : width - LANES], side_ref[plane]], axis=1)
        halo = jnp.concatenate([corner_ref[plane], lines_ref[plane], corner_ref[plane]], axis=1)
        both = dot(taps, jnp.concatenate([own, halo], axis=0))
        for half in range(2):
            at = 2 * half * HALO_LINES
            moved[half].append(both[at : at + HALO_LINES] + both[at + HALO_LINES : at + 2 * HALO_LINES])
    moved = jnp.concatenate(moved[0] + moved[1], axis=0)
    left = jnp.where(block > 0, moved[:, :LANES], 0.0)
    right = jnp.where(block == 0, moved[:, width - LANES :], 0.0)
    moved = jnp.concatenate([left, moved[:, LANES : width - LANES], right, jnp.zeros_like(right)], axis=1)
    total = along_range(moved, column_ref, width // LANES - 1)
    rows = 2 * lines
    tiles_ref[...] = total.astype(jnp.bfloat16)
    chunk_rows = outs[0].shape[0] - FOLD
    lane = lax.broadcasted_iota(jnp.int32, (FOLD, LANES), 1) // TAIL
    for chunk in range(len(outs)):
        begin = (chunk + 1) * chunk_rows
        folded = total[begin : begin + FOLD]
        for part in range(1, rows // FOLD):
            value = pltpu.roll(total[begin + part * FOLD : begin + (part + 1) * FOLD], part * TAIL, 1)
            folded = jnp.where(lane == part, value, folded)
        tails_ref[chunk] = folded.astype(jnp.bfloat16)
    date = lax.axis_index("date")
    for step, out_ref in enumerate(outs[:-1]):
        chunk = date ^ reach(step, len(outs))
        out_ref[:chunk_rows] = tiles_ref[pl.ds(pl.multiple_of(chunk * chunk_rows, FOLD), chunk_rows), :]
        out_ref[chunk_rows:] = tails_ref[chunk]
    out_ref = outs[-1]
    chunk = date ^ reach(len(outs) - 1, len(outs))
    early = chunk_rows // rows - 1
    for tile in range(early):
        begin = pl.multiple_of(chunk * chunk_rows + (tile + block) * rows + lines, FOLD)
        out_ref[tile * lines : (tile + 1) * lines] = tiles_ref[pl.ds(begin, lines), :]
    begin = pl.multiple_of(chunk * chunk_rows + (1 - block) * early * rows, FOLD)
    out_ref[early * lines : early * lines + rows] = tiles_ref[pl.ds(begin, rows), :]
    out_ref[early * lines + rows :] = tails_ref[chunk]


def filter_kernel(pairs, shift_hbm, early_ref, out_ref, spread_ref, shift_ref, semaphore):
    copy = pltpu.make_async_copy(shift_hbm, shift_ref, semaphore)
    copy.start()
    lines = 2 * HALO_LINES
    spread_ref[...] = jnp.zeros_like(spread_ref)
    for tile in range(early_ref.shape[0] // lines):
        begin = pl.multiple_of((tile + lax.axis_index("rng")) * 2 * lines, FOLD)
        spread_ref[pl.ds(begin, lines), :] = early_ref[tile * lines : (tile + 1) * lines]
    date = lax.axis_index("date")
    spacing = lax.broadcasted_iota(jnp.int32, (1, 2 * LANES), 1).astype(jnp.float32) - FILTER_HALF
    window = 0.4 * sinc(0.4 * spacing) * (0.54 + 0.46 * jnp.cos(jnp.pi * spacing / (FILTER_HALF + 1)))
    window = jnp.where(jnp.abs(spacing) <= FILTER_HALF, window, 0.0)
    copy.wait()
    for place, (first, second) in enumerate(pairs):
        dates = shift_ref.shape[0]
        gap = shift_ref[date ^ reach(first, dates)] - shift_ref[date ^ reach(second, dates)]
        angle = jnp.where(jnp.abs(spacing) <= FILTER_HALF, jnp.pi * gap * spacing, 0.0)
        for part, taps in enumerate((window * jnp.cos(angle), window * jnp.sin(angle))):
            spread = jnp.broadcast_to(taps, (LANES, 2 * LANES))
            spread = pltpu.roll(spread, 0, 1, stride=1, stride_axis=0)
            high, low = halves(spread)
            out_ref[place, 0, part * LANES : (part + 1) * LANES, :] = high
            out_ref[place, 1, part * LANES : (part + 1) * LANES, :] = low


def looks_kernel(pairs, dates, weight_ref, *refs):
    early_ref, chunks, outs = refs[0], list(refs[1 : dates + 1][::-1]), refs[dates + 1 : 2 * dates + 1]
    whole_ref, window_ref, product_ref = refs[-3:]
    groups, lines = outs[0].shape[0], outs[0].shape[0] * LOOK_AZ
    rows = 2 * lines
    blocks = (chunks[0].shape[0] - FOLD) // rows
    looks = blocks * LANES // LOOK_RG
    date = lax.axis_index("date")
    block = lax.axis_index("rng")
    early = blocks - 1
    whole_ref[: blocks * rows] = early_ref[...]
    for tile in range(early):
        begin = pl.multiple_of((tile + block) * rows, FOLD)
        whole_ref[pl.ds(begin + lines, lines), :] = chunks[-1][tile * lines : (tile + 1) * lines]
    begin = pl.multiple_of((1 - block) * early * rows, FOLD)
    whole_ref[pl.ds(begin, rows), :] = chunks[-1][early * lines : early * lines + rows]
    whole_ref[blocks * rows :] = chunks[-1][early * lines + rows :]
    chunks[-1] = whole_ref
    az = lax.axis_index("az")
    upper = lax.broadcasted_iota(jnp.int32, (groups, LANES), 0) // (groups // 2) == az
    for step, chunk_ref in enumerate(chunks):
        window_ref[step, :, :LANES] = chunk_ref[: blocks * rows]
        window_ref[step, : (blocks - 1) * rows, LANES:] = chunk_ref[rows : blocks * rows]
        folded = chunk_ref[blocks * rows :].astype(jnp.float32)
        for part in range(rows // FOLD):
            value = pltpu.roll(folded, LANES - part * TAIL, 1) if part else folded
            at = pl.ds((blocks - 1) * rows + part * FOLD, FOLD)
            window_ref[step, at, LANES:] = value.astype(jnp.bfloat16)
    for place, (first, second) in enumerate(pairs):
        def filtered(step):
            total = dot_nt(window_ref[step], weight_ref[place, 0]) + dot_nt(window_ref[step], weight_ref[place, 1])
            total = total.reshape(blocks, 2, 2, HALO_LINES, 2 * LANES)
            re, im = total[:, :, 0], total[:, :, 1]
            return re[..., :LANES], im[..., :LANES], re[..., LANES:], im[..., LANES:]

        cos_re, cos_im, sin_re, sin_im = filtered(first)
        master_re, master_im = cos_re + sin_im, cos_im - sin_re
        cos_re, cos_im, sin_re, sin_im = filtered(second)
        partner_re, partner_im = cos_re - sin_im, cos_im + sin_re
        for part, product in enumerate(
            (
                master_re * partner_re + master_im * partner_im,
                master_im * partner_re - master_re * partner_im,
            )
        ):
            summed = product[:, :, :groups] + product[:, :, groups:]
            at = pl.ds((place * 2 + part) * groups, groups)
            for k in range(blocks):
                both = [summed[k, half] + pltpu.roll(summed[k, half], groups // 2, 0) for half in range(2)]
                product_ref[at, k * LANES : (k + 1) * LANES] = jnp.where(upper, both[0], both[1])

    out_width = outs[0].shape[1]
    column = lax.broadcasted_iota(jnp.int32, (product_ref.shape[1], out_width), 0)
    lane = lax.broadcasted_iota(jnp.int32, (product_ref.shape[1], out_width), 1)
    collect = jnp.where(column // LOOK_RG == lane % looks, 1.0, 0.0).astype(jnp.bfloat16)
    high, low = halves(product_ref[...])
    total = (dot(high, collect) + dot(low, collect)) * (1.0 / (LOOK_AZ * LOOK_RG))
    total = total.reshape(len(pairs), 2, groups, out_width)
    own_lane = lax.broadcasted_iota(jnp.int32, (groups, out_width), 1) // looks
    for step, out_ref in enumerate(outs):
        value = jnp.zeros((groups, out_width), jnp.float32)
        for place, pair in enumerate(pairs):
            if step in pair:
                other = pair[1] if pair[0] == step else pair[0]
                lag = (date ^ reach(other, dates)) - (date ^ reach(step, dates))
                for part in range(2):
                    signed = -total[place, part] if part == 1 and pair[1] == step else total[place, part]
                    value = jnp.where(own_lane == (lag - 1) * 2 + part, signed, value)
        out_ref[...] = value


def place_kernel(used_lags, looks, *refs):
    out_ref = refs[-1]
    groups, columns = out_ref.shape[2:]
    date = lax.axis_index("date")
    lane = lax.broadcasted_iota(jnp.int32, (groups, LANES), 1) // looks
    out_ref[...] = jnp.zeros_like(out_ref)
    each = LANES // looks
    for step, recv_ref in enumerate(refs[:-1][::-1]):
        chunk = date ^ step
        for lag in range(used_lags):
            for part in range(2):
                tile, group = divmod(lag * 2 + part, each)
                block = recv_ref[:, tile * LANES : (tile + 1) * LANES]
                block = pltpu.roll(block, lax.bitwise_and(looks * (chunk - group), LANES - 1), 1)
                out_ref[part, lag] = jnp.where(lane == chunk, block, out_ref[part, lag])


def tiled_body(slc, offsets, kernel_index, range_shift):
    dates = lax.axis_size("date")
    lines, columns = slc.shape[2], slc.shape[3]
    chunk = columns // dates
    looks = chunk // LOOK_RG
    groups = lines // LOOK_AZ
    out_width = up(min(LAGS, dates - 1) * 2 * looks, LANES)
    vmem = pl.BlockSpec(memory_space=pltpu.VMEM)
    hbm = pl.BlockSpec(memory_space=pltpu.HBM)
    limit = pltpu.CompilerParams(vmem_limit_bytes=32 * 1024 * 1024)
    bf16 = jnp.bfloat16
    cells, offsets, kernel_index, range_shift = (
        pltpu.with_memory_space_constraint(value, pltpu.HBM)
        for value in (slc.reshape(2, lines, columns), offsets, kernel_index, range_shift)
    )
    tiles = chunk // LANES
    chunk_rows = tiles * 2 * lines

    side, corner, halo_lines, line_taps, column_taps, held = pl.pallas_call(
        prepare_kernel,
        out_shape=[
            jax.ShapeDtypeStruct((2, lines, LANES), bf16),
            jax.ShapeDtypeStruct((2, HALO_LINES, LANES), bf16),
            jax.ShapeDtypeStruct((2, HALO_LINES, columns), bf16),
            jax.ShapeDtypeStruct((2, 2 * HALO_LINES, lines + HALO_LINES), bf16),
            jax.ShapeDtypeStruct((3 * LANES, 2 * LANES), bf16),
            jax.ShapeDtypeStruct((2, lines, columns + 3 * LANES), bf16),
        ],
        in_specs=[hbm] * 3,
        out_specs=[vmem] * 6,
        scratch_shapes=[
            pltpu.SMEM(offsets.shape, jnp.int32),
            pltpu.SMEM(kernel_index.shape, jnp.int32),
            pltpu.SemaphoreType.DMA((6,)),
        ],
        compiler_params=limit,
    )(offsets, kernel_index, cells)
    swap = [(0, 1), (1, 0)]
    side = lax.ppermute(side, "rng", swap)
    corner = lax.ppermute(corner, ("rng", "az"), [(0, 3), (1, 2), (2, 1), (3, 0)])
    halo_lines = lax.ppermute(halo_lines, "az", swap)

    early_rows = (tiles - 1) * lines
    early = pl.pallas_call(
        functools.partial(early_kernel, tiles),
        out_shape=jax.ShapeDtypeStruct((early_rows, LANES), bf16),
        in_specs=[vmem] * 3,
        out_specs=vmem,
        compiler_params=limit,
    )(held, line_taps, column_taps)
    early = lax.ppermute(early, "date", [(i, i ^ reach(dates - 1, dates)) for i in range(dates)])
    out_rows = [chunk_rows + FOLD] * (dates - 1) + [chunk_rows + FOLD - early_rows]
    sent = pl.pallas_call(
        resample_kernel,
        out_shape=[jax.ShapeDtypeStruct((rows, LANES), bf16) for rows in out_rows],
        in_specs=[vmem] * 6,
        out_specs=[vmem] * dates,
        scratch_shapes=[
            pltpu.VMEM(((columns // LANES + 1) * 2 * lines, LANES), bf16),
            pltpu.VMEM((dates, FOLD, LANES), bf16),
        ],
        compiler_params=limit,
    )(side, corner, halo_lines, held, line_taps, column_taps)

    def exchanged(values, order):
        arrived = {0: values[0]}
        for step in order:
            arrived[step] = lax.ppermute(values[step], "date", [(i, i ^ reach(step, dates)) for i in range(dates)])
        return [arrived[step] for step in reversed(range(dates))]

    steps = range(dates - 1, 0, -1)

    chunks = exchanged(sent, steps)
    pairs = [(first, second) for first in range(dates) for second in range(first + 1, dates)]
    weights, early = pl.pallas_call(
        functools.partial(filter_kernel, pairs),
        out_shape=[
            jax.ShapeDtypeStruct((len(pairs), 2, 2 * LANES, 2 * LANES), bf16),
            jax.ShapeDtypeStruct((chunk_rows, LANES), bf16),
        ],
        in_specs=[hbm, vmem],
        out_specs=[vmem] * 2,
        scratch_shapes=[pltpu.SMEM(range_shift.shape, jnp.float32), pltpu.SemaphoreType.DMA],
        compiler_params=limit,
        cost_estimate=pl.CostEstimate(flops=600_000_000, bytes_accessed=0, transcendentals=0),
    )(range_shift, early)
    looked = pl.pallas_call(
        functools.partial(looks_kernel, pairs, dates),
        out_shape=[jax.ShapeDtypeStruct((groups, out_width), jnp.float32)] * dates,
        in_specs=[vmem] * (2 + dates),
        out_specs=[vmem] * dates,
        scratch_shapes=[
            pltpu.VMEM((chunk_rows + FOLD, LANES), bf16),
            pltpu.VMEM((dates, chunk_rows, 2 * LANES), bf16),
            pltpu.VMEM((len(pairs) * 2 * groups, chunk), jnp.float32),
        ],
        compiler_params=limit,
    )(weights, early, *chunks)
    returned = exchanged(looked, steps)[::-1]
    returned = [returned[reach(distance, dates)] for distance in reversed(range(dates))]
    out = pl.pallas_call(
        functools.partial(place_kernel, min(LAGS, dates - 1), looks),
        out_shape=jax.ShapeDtypeStruct((2, LAGS, groups, looks * dates), jnp.float32),
        in_specs=[vmem] * dates,
        out_specs=vmem,
        compiler_params=limit,
    )(*returned)
    return out[:, None]


def body(slc, offsets, kernel_index, range_shift):
    dates, az_count = (lax.axis_size(a) for a in ("date", "az"))
    lines, columns = slc.shape[2], slc.shape[3]
    whole_tiles = columns % (dates * LANES) == 0 and columns % (dates * LOOK_RG) == 0
    one_row = columns // LOOK_RG == LANES and range_shift.shape[0] == dates
    few = dates & (dates - 1) == 0 and dates - 1 <= LAGS
    folds = lines == 2 * HALO_LINES and lax.axis_size("rng") == 2 and dates >= 4 and 2 * lines // FOLD * TAIL <= LANES
    if az_count == 2 and whole_tiles and one_row and few and folds:
        return tiled_body(slc, offsets, kernel_index, range_shift)
    return chunked_body(slc, offsets, kernel_index, range_shift)


def solution(mesh):
    return jax.shard_map(
        body,
        mesh=mesh,
        in_specs=(
            P(None, ("groups", "date"), "az", "rng"),
            P(("groups", "date"), None),
            P(("groups", "date"), None),
            P("groups"),
        ),
        out_specs=P(None, ("groups", "date"), None, "az", "rng"),
        check_vma=False,
    )
```

```python
import functools

import jax
import jax.numpy as jnp
import numpy as np
from jax import lax
from jax.experimental import pallas as pl
from jax.experimental.pallas import tpu as pltpu
from jax.sharding import PartitionSpec as P

LAGS = 8
KERNELS = 16
TAPS = 8
FILTER_HALF = 8
FILTER_TAPS = 2 * FILTER_HALF + 1
LOOK_AZ = 4
LOOK_RG = 20
LANES = 128
META = 3
UNROLLED_PAIRS = 12


def up(value, unit):
    return -(-value // unit) * unit


def kernel_table():
    position = np.arange(TAPS) - 3.0 - np.arange(KERNELS)[:, None] / KERNELS
    shaped = np.sinc(position) * (0.5 + 0.5 * np.cos(np.pi * position / 5.0))
    table = np.zeros((KERNELS, LANES), np.float32)
    table[:, :TAPS] = shaped / shaped.sum(1, keepdims=True)
    return table


def lowpass_row(width):
    t = np.arange(FILTER_TAPS) - FILTER_HALF
    row = np.zeros((1, width), np.float32)
    row[0, :FILTER_TAPS] = 0.4 * np.sinc(0.4 * t) * (0.54 + 0.46 * np.cos(np.pi * t / (FILTER_HALF + 1)))
    return row


def halves(value):
    high = value.astype(jnp.bfloat16)
    return high, (value - high.astype(jnp.float32)).astype(jnp.bfloat16)


def dot(a, b):
    return jnp.dot(a, b, preferred_element_type=jnp.float32)


def dot_nt(a, b):
    return lax.dot_general(a, b, (((1,), (1,)), ((), ())), preferred_element_type=jnp.float32)


def pack_kernel(chunk, place_ref, offsets_ref, index_ref, slc_ref, before_ref, after_ref, out_ref, wide_ref):
    columns = slc_ref.shape[1]
    wide = out_ref.shape[2]
    first = place_ref[0] == 0
    last = place_ref[0] == place_ref[1] - 1
    zero = jnp.zeros_like(before_ref[...])
    wide_ref[:, :LANES] = jnp.where(first, zero, before_ref[...])
    wide_ref[:, LANES : LANES + columns] = slc_ref[...]
    wide_ref[:, LANES + columns :] = jnp.where(last, zero, after_ref[...])
    lane = lax.broadcasted_iota(jnp.int32, (slc_ref.shape[0], wide), 1)
    numbers = [offsets_ref[0, 0], index_ref[0, 0], index_ref[0, 1]]
    for j in range(out_ref.shape[0]):
        start = LANES + chunk * j - FILTER_HALF - 3 + offsets_ref[0, 1]
        tile = lax.shift_right_logical(start, 7)
        within = lax.bitwise_and(start, LANES - 1)
        window = wide_ref[:, pl.ds(pl.multiple_of(tile * LANES, LANES), wide + LANES)].astype(jnp.float32)
        moved = pltpu.roll(window, wide + LANES - within, 1)[:, :wide]
        for slot, number in enumerate(numbers):
            moved = jnp.where(lane == wide - META + slot, number.astype(jnp.float32), moved)
        out_ref[j] = moved.astype(jnp.bfloat16)


def picked_taps(table, index):
    row = lax.broadcasted_iota(jnp.int32, table.shape, 0).astype(jnp.float32)
    return jnp.sum(jnp.where(row == index, table, 0.0), axis=0, keepdims=True)


def banded(taps, distance):
    out = jnp.zeros(distance.shape, jnp.float32)
    for q in range(TAPS):
        out = jnp.where(distance == q, taps[:, q : q + 1], out)
    return out


def pairs_kernel(chunk, pairs, *refs):
    if isinstance(pairs, int):
        table_of_pairs, refs = refs[0], refs[1:]
    shift_ref, table_ref, lowpass_ref, recv_ref, out_ref, resampled_ref, weight_ref, product_ref = refs
    sources, rows, wide = recv_ref.shape
    dates = shift_ref.shape[0]
    az_count = sources // dates
    own_lines = rows // 2
    lines = own_lines * az_count
    groups = lines // LOOK_AZ
    looks = chunk // LOOK_RG
    table = table_ref[...]
    held = resampled_ref.shape[2]

    out_row = lax.broadcasted_iota(jnp.int32, (lines, lines), 0)
    in_row = lax.broadcasted_iota(jnp.int32, (lines, lines), 1)
    line = LOOK_AZ * (out_row % groups) + out_row // groups
    line_distance = (in_row - line + 3).astype(jnp.float32)
    span = min(2 * LANES, wide)
    column_distance = (
        lax.broadcasted_iota(jnp.int32, (span, LANES), 0) - lax.broadcasted_iota(jnp.int32, (span, LANES), 1)
    ).astype(jnp.float32)
    for date in range(dates):
        numbers = recv_ref[date * az_count, 0:16, wide - LANES :].astype(jnp.float32)[0:1, LANES - META :]
        line_offset, line_index, column_index = (numbers[:, s : s + 1] for s in range(META))
        line_taps = banded(picked_taps(table, line_index), line_distance - line_offset)
        line_taps = jnp.concatenate(halves(line_taps), axis=0)
        column_high, column_low = halves(banded(picked_taps(table, column_index), column_distance))
        moved = []
        for plane in range(2):
            rows_of = slice(plane * own_lines, (plane + 1) * own_lines)
            source = jnp.concatenate([recv_ref[date * az_count + a, rows_of, :] for a in range(az_count)], axis=0)
            both = dot(line_taps, source)
            moved.append(both[:lines] + both[lines:])
        moved_high, moved_low = halves(jnp.concatenate(moved, axis=0))
        for begin in range(0, held, LANES):
            end = min(begin + span, wide)
            taken = end - begin
            total = dot(moved_high[:, begin:end], column_high[:taken])
            total += dot(moved_low[:, begin:end], column_high[:taken])
            total += dot(moved_high[:, begin:end], column_low[:taken])
            resampled_ref[date, :, begin : begin + LANES] = total.astype(jnp.bfloat16)

    window = lowpass_ref[...]
    spacing = lax.broadcasted_iota(jnp.int32, window.shape, 1).astype(jnp.float32) - FILTER_HALF
    span = min(2 * LANES, held)

    def one_pair(place, own, other):
        gap = shift_ref[own] - shift_ref[other]
        angle = jnp.where(jnp.abs(spacing) <= FILTER_HALF, jnp.pi * gap * spacing, 0.0)
        for part, taps in enumerate((window * jnp.cos(angle), window * jnp.sin(angle))):
            spread = jnp.broadcast_to(taps, (LANES, 2 * LANES))
            spread = pltpu.roll(spread, 0, 1, stride=1, stride_axis=0)
            high, low = halves(spread)
            weight_ref[0, part * LANES : (part + 1) * LANES, :] = high
            weight_ref[1, part * LANES : (part + 1) * LANES, :] = low
        both = jnp.concatenate([resampled_ref[own], resampled_ref[other]], axis=0)
        for begin in range(0, up(chunk, LANES), LANES):
            end = min(begin + span, held)
            taken = end - begin
            total = dot_nt(both[:, begin:end], weight_ref[0, :, :taken])
            total += dot_nt(both[:, begin:end], weight_ref[1, :, :taken])
            cos, sin = total[:, :LANES], total[:, LANES:]
            re, im = slice(0, lines), slice(lines, 2 * lines)
            master_re = cos[re] + sin[im]
            master_im = cos[im] - sin[re]
            re, im = slice(2 * lines, 3 * lines), slice(3 * lines, 4 * lines)
            partner_re = cos[re] - sin[im]
            partner_im = cos[im] + sin[re]
            for part, product in enumerate(
                (
                    master_re * partner_re + master_im * partner_im,
                    master_im * partner_re - master_re * partner_im,
                )
            ):
                summed = sum(product[k * groups : (k + 1) * groups] for k in range(LOOK_AZ))
                product_ref[place, part, :, begin : begin + LANES] = summed

    if isinstance(pairs, int):
        count = pairs

        def step(place, carry):
            one_pair(place, table_of_pairs[place, 0], table_of_pairs[place, 1])
            return carry

        lax.fori_loop(0, count, step, 0)
    else:
        count = len(pairs)
        for place, (own, other) in enumerate(pairs):
            one_pair(place, own, other)

    out_width = out_ref.shape[2]
    column = lax.broadcasted_iota(jnp.int32, (product_ref.shape[3], out_width), 0)
    lane = lax.broadcasted_iota(jnp.int32, (product_ref.shape[3], out_width), 1)
    collect = jnp.where(column // LOOK_RG == lane % looks, 1.0, 0.0).astype(jnp.bfloat16)
    high, low = halves(product_ref[...].reshape(count * 2 * groups, product_ref.shape[3]))
    total = (dot(high, collect) + dot(low, collect)) * (1.0 / (LOOK_AZ * LOOK_RG))
    total = total.reshape(count, 2, groups, out_width)
    own_lane = lax.broadcasted_iota(jnp.int32, (groups, out_width), 1) // looks
    place = 0
    for own in range(dates):
        value = jnp.zeros((groups, out_width), jnp.float32)
        for lag in range(min(LAGS, dates - 1 - own)):
            for part in range(2):
                value = jnp.where(own_lane == lag * 2 + part, total[place, part], value)
            place += 1
        out_ref[own * az_count : (own + 1) * az_count] = value.reshape(az_count, groups // az_count, out_width)


def unpack_kernel(used_lags, looks, recv_ref, out_ref):
    sources, groups, width = recv_ref.shape
    columns = out_ref.shape[-1]
    lane = lax.broadcasted_iota(jnp.int32, (groups, columns), 1) // looks
    out_ref[...] = jnp.zeros_like(out_ref)
    for lag in range(used_lags):
        for part in range(2):
            value = jnp.zeros((groups, columns), jnp.float32)
            for source in range(sources):
                block = recv_ref[source]
                if width != columns:
                    block = block[:, :columns]
                shift = looks * (source - lag * 2 - part) % columns
                if shift:
                    block = pltpu.roll(block, shift, 1)
                value = jnp.where(lane == source, block, value)
            out_ref[part, lag] = value


def chunked_body(slc, offsets, kernel_index, range_shift):
    axes = ("date", "az")
    date_count, az_count, rng_count = (lax.axis_size(a) for a in ("date", "az", "rng"))
    peers = date_count * az_count
    lines, columns = slc.shape[2], slc.shape[3]
    dates = range_shift.shape[0]
    chunk = columns // peers
    looks = chunk // LOOK_RG
    groups = lines * az_count // LOOK_AZ
    wide = up(chunk + 2 * FILTER_HALF + TAPS - 1 + META, LANES)
    held = up(chunk + 2 * FILTER_HALF, LANES)
    used_lags = min(LAGS, dates - 1)
    out_width = up(used_lags * 2 * looks, LANES)
    vmem = pl.BlockSpec(memory_space=pltpu.VMEM)
    smem = pl.BlockSpec(memory_space=pltpu.SMEM)
    limit = pltpu.CompilerParams(vmem_limit_bytes=32 * 1024 * 1024)

    cells = slc.reshape(2 * lines, columns)
    place = lax.axis_index("rng")
    if rng_count == 2:
        edge = jnp.where(place == 0, cells[:, columns - LANES :], cells[:, :LANES])
        before = after = lax.ppermute(edge, "rng", [(0, 1), (1, 0)])
    else:
        forth = [(i, i + 1) for i in range(rng_count - 1)]
        before = lax.ppermute(cells[:, columns - LANES :], "rng", forth)
        after = lax.ppermute(cells[:, :LANES], "rng", [(b, a) for a, b in forth])

    packed = pl.pallas_call(
        functools.partial(pack_kernel, chunk),
        out_shape=jax.ShapeDtypeStruct((peers, 2 * lines, wide), jnp.bfloat16),
        in_specs=[smem] * 3 + [vmem] * 3,
        out_specs=vmem,
        scratch_shapes=[pltpu.VMEM((2 * lines, columns + 2 * LANES), jnp.bfloat16)],
        compiler_params=limit,
    )(jnp.stack([place, rng_count]).astype(jnp.int32), offsets, kernel_index, cells, before, after)
    arrived = lax.all_to_all(packed, axes, 0, 0, tiled=True)

    pairs = [(own, own + lag) for own in range(dates) for lag in range(1, LAGS + 1) if own + lag < dates]
    count = len(pairs)
    first = [jnp.asarray(np.array(pairs, np.int32))] if count > UNROLLED_PAIRS else []
    looked = pl.pallas_call(
        functools.partial(pairs_kernel, chunk, count if first else pairs),
        out_shape=jax.ShapeDtypeStruct((peers, groups // az_count, out_width), jnp.float32),
        in_specs=[smem] * len(first) + [smem] + [vmem] * 3,
        out_specs=vmem,
        scratch_shapes=[
            pltpu.VMEM((dates, 4 * (groups * LOOK_AZ) // 2, held), jnp.bfloat16),
            pltpu.VMEM((2, 2 * LANES, 2 * LANES), jnp.bfloat16),
            pltpu.VMEM((count, 2, groups, up(chunk, LANES)), jnp.float32),
        ],
        compiler_params=limit,
    )(*first, range_shift, jnp.asarray(kernel_table()), jnp.asarray(lowpass_row(2 * LANES)), arrived)
    returned = lax.all_to_all(looked, axes, 0, 0, tiled=True)

    out = pl.pallas_call(
        functools.partial(unpack_kernel, used_lags, looks),
        out_shape=jax.ShapeDtypeStruct((2, LAGS, groups // az_count, looks * peers), jnp.float32),
        in_specs=[vmem],
        out_specs=vmem,
        compiler_params=limit,
    )(returned)
    return out[:, None]


HALO_LINES = 16
FOLD = 16
TAIL = 2 * FILTER_HALF


def reach(step, dates):
    return {dates - 1: dates // 2, dates // 2: dates - 1}.get(step, step)


def sinc(value):
    angle = jnp.pi * value
    return jnp.where(angle == 0.0, 1.0, jnp.sin(angle) / jnp.where(angle == 0.0, 1.0, angle))


def tap_row(index):
    lane = lax.broadcasted_iota(jnp.int32, (1, LANES), 1)
    position = lane.astype(jnp.float32) - 3.0 - index.astype(jnp.float32) / KERNELS
    shaped = sinc(position) * (0.5 + 0.5 * jnp.cos(jnp.pi * position / 5.0))
    shaped = jnp.where(lane < TAPS, shaped, 0.0)
    return shaped / jnp.sum(shaped, axis=1, keepdims=True)


def row_line(row, az):
    quarter = HALO_LINES // LOOK_AZ
    within = row % HALO_LINES
    return HALO_LINES * ((row // HALO_LINES) ^ az) + LOOK_AZ * (within % quarter) + within // quarter


def prepare_kernel(offsets_hbm, index_hbm, slc_ref, side_ref, corner_ref, lines_ref, line_ref, column_ref, held_ref, offsets_ref, index_ref, semaphores):
    lines, columns = slc_ref.shape[1:]
    az = lax.axis_index("az")
    row = pl.multiple_of((1 - az) * (lines - HALO_LINES), HALO_LINES)
    edge = pl.multiple_of((1 - lax.axis_index("rng")) * (columns - LANES), LANES)
    nearest, outermost = pl.ds(row, HALO_LINES), pl.ds(edge, LANES)
    moves = [
        (offsets_hbm, offsets_ref),
        (index_hbm, index_ref),
        (slc_ref.at[:, :, outermost], side_ref),
        (slc_ref.at[:, nearest, outermost], corner_ref),
        (slc_ref.at[:, nearest, :], lines_ref),
    ]
    for plane in range(2):
        for part in range(lines // HALO_LINES):
            for side in range(2):
                at = pl.ds(part * HALO_LINES, HALO_LINES)
                source = slc_ref.at[plane, at, pl.ds(side * columns // 2, columns // 2)]
                moves.append((source, held_ref.at[plane, at, pl.ds(LANES + side * columns // 2, columns // 2)]))
    copies = [pltpu.make_async_copy(a, b, semaphores.at[i]) for i, (a, b) in enumerate(moves)]
    for copy in copies:
        copy.start()
    held_ref[:, :, :LANES] = jnp.zeros((2, lines, LANES), held_ref.dtype)
    held_ref[:, :, LANES + columns :] = jnp.zeros((2, lines, 2 * LANES), held_ref.dtype)
    copies[0].wait()
    copies[1].wait()
    for half in range(2):
        shape = (HALO_LINES, lines + HALO_LINES)
        line = row_line(lax.broadcasted_iota(jnp.int32, shape, 0) + half * HALO_LINES, az)
        place = lax.broadcasted_iota(jnp.int32, shape, 1)
        source = jnp.where(place < lines, place, place + jnp.where(az == 0, 0, -lines - HALO_LINES))
        taps = banded(tap_row(index_ref[0, 0]), source - line - offsets_ref[0, 0] + 3)
        line_ref[half] = jnp.concatenate(halves(taps), axis=0)
    shape = (3 * LANES, LANES)
    distance = lax.broadcasted_iota(jnp.int32, shape, 0) - lax.broadcasted_iota(jnp.int32, shape, 1)
    distance = distance - (LANES - FILTER_HALF - 3) - offsets_ref[0, 1]
    taps = banded(tap_row(index_ref[0, 1]), distance)
    column_ref[...] = jnp.concatenate(halves(taps), axis=1)
    for copy in copies[2:]:
        copy.wait()


def along_range(moved, column_ref, tiles):
    high, low = halves(moved)
    starts = range(0, tiles * LANES, LANES)
    high = jnp.concatenate([high[:, s : s + 3 * LANES] for s in starts], axis=0)
    low = jnp.concatenate([low[:, s : s + 3 * LANES] for s in starts], axis=0)
    total = dot(high, column_ref[...])
    return total[:, :LANES] + total[:, LANES:] + dot(low, column_ref[:, :LANES])


def early_kernel(tiles, held_ref, line_ref, column_ref, out_ref):
    lines = held_ref.shape[1]
    early = out_ref.shape[0] // (2 * HALO_LINES)
    dates = lax.axis_size("date")
    chunk = lax.axis_index("date") ^ reach(dates - 1, dates)
    begin = pl.multiple_of((chunk * tiles + lax.axis_index("rng")) * LANES, LANES)
    moved = []
    for plane in range(2):
        both = dot(line_ref[0, :, :lines], held_ref[plane, :, pl.ds(begin, (early + 2) * LANES)])
        moved.append(both[:HALO_LINES] + both[HALO_LINES:])
    moved = jnp.concatenate(moved, axis=0)
    out_ref[...] = along_range(moved, column_ref, early).astype(jnp.bfloat16)


def resample_kernel(side_ref, corner_ref, lines_ref, held_ref, line_ref, column_ref, *outs):
    outs, tiles_ref, tails_ref = outs[:-2], outs[-2], outs[-1]
    lines, width = held_ref.shape[1:]
    width -= LANES
    block = lax.axis_index("rng")
    taps = jnp.concatenate([line_ref[0], line_ref[1]], axis=0)
    moved = [[], []]
    for plane in range(2):
        own = jnp.concatenate([side_ref[plane], held_ref[plane, :, LANES : width - LANES], side_ref[plane]], axis=1)
        halo = jnp.concatenate([corner_ref[plane], lines_ref[plane], corner_ref[plane]], axis=1)
        both = dot(taps, jnp.concatenate([own, halo], axis=0))
        for half in range(2):
            at = 2 * half * HALO_LINES
            moved[half].append(both[at : at + HALO_LINES] + both[at + HALO_LINES : at + 2 * HALO_LINES])
    moved = jnp.concatenate(moved[0] + moved[1], axis=0)
    left = jnp.where(block > 0, moved[:, :LANES], 0.0)
    right = jnp.where(block == 0, moved[:, width - LANES :], 0.0)
    moved = jnp.concatenate([left, moved[:, LANES : width - LANES], right, jnp.zeros_like(right)], axis=1)
    total = along_range(moved, column_ref, width // LANES - 1)
    rows = 2 * lines
    tiles_ref[...] = total.astype(jnp.bfloat16)
    chunk_rows = outs[0].shape[0] - FOLD
    lane = lax.broadcasted_iota(jnp.int32, (FOLD, LANES), 1) // TAIL
    for chunk in range(len(outs)):
        begin = (chunk + 1) * chunk_rows
        folded = total[begin : begin + FOLD]
        for part in range(1, rows // FOLD):
            value = pltpu.roll(total[begin + part * FOLD : begin + (part + 1) * FOLD], part * TAIL, 1)
            folded = jnp.where(lane == part, value, folded)
        tails_ref[chunk] = folded.astype(jnp.bfloat16)
    date = lax.axis_index("date")
    for step, out_ref in enumerate(outs[:-1]):
        chunk = date ^ reach(step, len(outs))
        out_ref[:chunk_rows] = tiles_ref[pl.ds(pl.multiple_of(chunk * chunk_rows, FOLD), chunk_rows), :]
        out_ref[chunk_rows:] = tails_ref[chunk]
    out_ref = outs[-1]
    chunk = date ^ reach(len(outs) - 1, len(outs))
    early = chunk_rows // rows - 1
    for tile in range(early):
        begin = pl.multiple_of(chunk * chunk_rows + (tile + block) * rows + lines, FOLD)
        out_ref[tile * lines : (tile + 1) * lines] = tiles_ref[pl.ds(begin, lines), :]
    begin = pl.multiple_of(chunk * chunk_rows + (1 - block) * early * rows, FOLD)
    out_ref[early * lines : early * lines + rows] = tiles_ref[pl.ds(begin, rows), :]
    out_ref[early * lines + rows :] = tails_ref[chunk]


def filter_kernel(pairs, shift_hbm, early_ref, out_ref, spread_ref, shift_ref, semaphore):
    copy = pltpu.make_async_copy(shift_hbm, shift_ref, semaphore)
    copy.start()
    lines = 2 * HALO_LINES
    spread_ref[...] = jnp.zeros_like(spread_ref)
    for tile in range(early_ref.shape[0] // lines):
        begin = pl.multiple_of((tile + lax.axis_index("rng")) * 2 * lines, FOLD)
        spread_ref[pl.ds(begin, lines), :] = early_ref[tile * lines : (tile + 1) * lines]
    date = lax.axis_index("date")
    spacing = lax.broadcasted_iota(jnp.int32, (1, 2 * LANES), 1).astype(jnp.float32) - FILTER_HALF
    window = 0.4 * sinc(0.4 * spacing) * (0.54 + 0.46 * jnp.cos(jnp.pi * spacing / (FILTER_HALF + 1)))
    window = jnp.where(jnp.abs(spacing) <= FILTER_HALF, window, 0.0)
    copy.wait()
    for place, (first, second) in enumerate(pairs):
        dates = shift_ref.shape[0]
        gap = shift_ref[date ^ reach(first, dates)] - shift_ref[date ^ reach(second, dates)]
        angle = jnp.where(jnp.abs(spacing) <= FILTER_HALF, jnp.pi * gap * spacing, 0.0)
        for part, taps in enumerate((window * jnp.cos(angle), window * jnp.sin(angle))):
            spread = jnp.broadcast_to(taps, (LANES, 2 * LANES))
            spread = pltpu.roll(spread, 0, 1, stride=1, stride_axis=0)
            high, low = halves(spread)
            out_ref[place, part * LANES : (part + 1) * LANES, : 2 * LANES] = high
            out_ref[place, part * LANES : (part + 1) * LANES, 2 * LANES :] = low


def looks_kernel(pairs, dates, weight_ref, *refs):
    early_ref, chunks, outs = refs[0], list(refs[1 : dates + 1][::-1]), refs[dates + 1 : 2 * dates + 1]
    whole_ref, window_ref, product_ref = refs[-3:]
    groups, lines = outs[0].shape[0], outs[0].shape[0] * LOOK_AZ
    rows = 2 * lines
    blocks = (chunks[0].shape[0] - FOLD) // rows
    looks = blocks * LANES // LOOK_RG
    date = lax.axis_index("date")
    block = lax.axis_index("rng")
    early = blocks - 1
    whole_ref[: blocks * rows] = early_ref[...]
    for tile in range(early):
        begin = pl.multiple_of((tile + block) * rows, FOLD)
        whole_ref[pl.ds(begin + lines, lines), :] = chunks[-1][tile * lines : (tile + 1) * lines]
    begin = pl.multiple_of((1 - block) * early * rows, FOLD)
    whole_ref[pl.ds(begin, rows), :] = chunks[-1][early * lines : early * lines + rows]
    whole_ref[blocks * rows :] = chunks[-1][early * lines + rows :]
    chunks[-1] = whole_ref
    az = lax.axis_index("az")
    upper = lax.broadcasted_iota(jnp.int32, (groups, LANES), 0) // (groups // 2) == az
    for step, chunk_ref in enumerate(chunks):
        window_ref[step, :, :LANES] = chunk_ref[: blocks * rows]
        window_ref[step, : (blocks - 1) * rows, LANES:] = chunk_ref[rows : blocks * rows]
        folded = chunk_ref[blocks * rows :].astype(jnp.float32)
        for part in range(rows // FOLD):
            value = pltpu.roll(folded, LANES - part * TAIL, 1) if part else folded
            at = pl.ds((blocks - 1) * rows + part * FOLD, FOLD)
            window_ref[step, at, LANES:] = value.astype(jnp.bfloat16)
    for place, (first, second) in enumerate(pairs):
        def filtered(step):
            window = window_ref[step]
            total = dot_nt(jnp.concatenate([window, window], axis=1), weight_ref[place])
            total = total.reshape(blocks, 2, 2, HALO_LINES, 2 * LANES)
            re, im = total[:, :, 0], total[:, :, 1]
            return re[..., :LANES], im[..., :LANES], re[..., LANES:], im[..., LANES:]

        cos_re, cos_im, sin_re, sin_im = filtered(first)
        master_re, master_im = cos_re + sin_im, cos_im - sin_re
        cos_re, cos_im, sin_re, sin_im = filtered(second)
        partner_re, partner_im = cos_re - sin_im, cos_im + sin_re
        for part, product in enumerate(
            (
                master_re * partner_re + master_im * partner_im,
                master_im * partner_re - master_re * partner_im,
            )
        ):
            summed = product[:, :, :groups] + product[:, :, groups:]
            at = pl.ds((place * 2 + part) * groups, groups)
            for k in range(blocks):
                both = [summed[k, half] + pltpu.roll(summed[k, half], groups // 2, 0) for half in range(2)]
                product_ref[at, k * LANES : (k + 1) * LANES] = jnp.where(upper, both[0], both[1])

    out_width = outs[0].shape[1]
    column = lax.broadcasted_iota(jnp.int32, (product_ref.shape[1], out_width), 0)
    lane = lax.broadcasted_iota(jnp.int32, (product_ref.shape[1], out_width), 1)
    collect = jnp.where(column // LOOK_RG == lane % looks, 1.0, 0.0).astype(jnp.bfloat16)
    high, low = halves(product_ref[...])
    total = (dot(high, collect) + dot(low, collect)) * (1.0 / (LOOK_AZ * LOOK_RG))
    total = total.reshape(len(pairs), 2, groups, out_width)
    own_lane = lax.broadcasted_iota(jnp.int32, (groups, out_width), 1) // looks
    for step, out_ref in enumerate(outs):
        value = jnp.zeros((groups, out_width), jnp.float32)
        for place, pair in enumerate(pairs):
            if step in pair:
                other = pair[1] if pair[0] == step else pair[0]
                lag = (date ^ reach(other, dates)) - (date ^ reach(step, dates))
                for part in range(2):
                    signed = -total[place, part] if part == 1 and pair[1] == step else total[place, part]
                    value = jnp.where(own_lane == (lag - 1) * 2 + part, signed, value)
        out_ref[...] = value


def place_kernel(used_lags, looks, *refs):
    out_ref = refs[-1]
    groups, columns = out_ref.shape[2:]
    date = lax.axis_index("date")
    lane = lax.broadcasted_iota(jnp.int32, (groups, LANES), 1) // looks
    out_ref[...] = jnp.zeros_like(out_ref)
    each = LANES // looks
    for step, recv_ref in enumerate(refs[:-1][::-1]):
        chunk = date ^ step
        for lag in range(used_lags):
            for part in range(2):
                tile, group = divmod(lag * 2 + part, each)
                block = recv_ref[:, tile * LANES : (tile + 1) * LANES]
                block = pltpu.roll(block, lax.bitwise_and(looks * (chunk - group), LANES - 1), 1)
                out_ref[part, lag] = jnp.where(lane == chunk, block, out_ref[part, lag])


def tiled_body(slc, offsets, kernel_index, range_shift):
    dates = lax.axis_size("date")
    lines, columns = slc.shape[2], slc.shape[3]
    chunk = columns // dates
    looks = chunk // LOOK_RG
    groups = lines // LOOK_AZ
    out_width = up(min(LAGS, dates - 1) * 2 * looks, LANES)
    vmem = pl.BlockSpec(memory_space=pltpu.VMEM)
    hbm = pl.BlockSpec(memory_space=pltpu.HBM)
    limit = pltpu.CompilerParams(vmem_limit_bytes=32 * 1024 * 1024)
    bf16 = jnp.bfloat16
    cells, offsets, kernel_index, range_shift = (
        pltpu.with_memory_space_constraint(value, pltpu.HBM)
        for value in (slc.reshape(2, lines, columns), offsets, kernel_index, range_shift)
    )
    tiles = chunk // LANES
    chunk_rows = tiles * 2 * lines

    side, corner, halo_lines, line_taps, column_taps, held = pl.pallas_call(
        prepare_kernel,
        out_shape=[
            jax.ShapeDtypeStruct((2, lines, LANES), bf16),
            jax.ShapeDtypeStruct((2, HALO_LINES, LANES), bf16),
            jax.ShapeDtypeStruct((2, HALO_LINES, columns), bf16),
            jax.ShapeDtypeStruct((2, 2 * HALO_LINES, lines + HALO_LINES), bf16),
            jax.ShapeDtypeStruct((3 * LANES, 2 * LANES), bf16),
            jax.ShapeDtypeStruct((2, lines, columns + 3 * LANES), bf16),
        ],
        in_specs=[hbm] * 3,
        out_specs=[vmem] * 6,
        scratch_shapes=[
            pltpu.SMEM(offsets.shape, jnp.int32),
            pltpu.SMEM(kernel_index.shape, jnp.int32),
            pltpu.SemaphoreType.DMA((5 + 4 * (lines // HALO_LINES),)),
        ],
        compiler_params=limit,
    )(offsets, kernel_index, cells)
    swap = [(0, 1), (1, 0)]
    side = lax.ppermute(side, "rng", swap)
    corner = lax.ppermute(corner, ("rng", "az"), [(0, 3), (1, 2), (2, 1), (3, 0)])
    halo_lines = lax.ppermute(halo_lines, "az", swap)

    early_rows = (tiles - 1) * lines
    early = pl.pallas_call(
        functools.partial(early_kernel, tiles),
        out_shape=jax.ShapeDtypeStruct((early_rows, LANES), bf16),
        in_specs=[vmem] * 3,
        out_specs=vmem,
        compiler_params=limit,
    )(held, line_taps, column_taps)
    early = lax.ppermute(early, "date", [(i, i ^ reach(dates - 1, dates)) for i in range(dates)])
    out_rows = [chunk_rows + FOLD] * (dates - 1) + [chunk_rows + FOLD - early_rows]
    sent = pl.pallas_call(
        resample_kernel,
        out_shape=[jax.ShapeDtypeStruct((rows, LANES), bf16) for rows in out_rows],
        in_specs=[vmem] * 6,
        out_specs=[vmem] * dates,
        scratch_shapes=[
            pltpu.VMEM(((columns // LANES + 1) * 2 * lines, LANES), bf16),
            pltpu.VMEM((dates, FOLD, LANES), bf16),
        ],
        compiler_params=limit,
    )(side, corner, halo_lines, held, line_taps, column_taps)

    def exchanged(values, order):
        arrived = {0: values[0]}
        for step in order:
            arrived[step] = lax.ppermute(values[step], "date", [(i, i ^ reach(step, dates)) for i in range(dates)])
        return [arrived[step] for step in reversed(range(dates))]

    steps = range(dates - 1, 0, -1)

    chunks = exchanged(sent, steps)
    pairs = [(first, second) for first in range(dates) for second in range(first + 1, dates)]
    weights, early = pl.pallas_call(
        functools.partial(filter_kernel, pairs),
        out_shape=[
            jax.ShapeDtypeStruct((len(pairs), 2 * LANES, 4 * LANES), bf16),
            jax.ShapeDtypeStruct((chunk_rows, LANES), bf16),
        ],
        in_specs=[hbm, vmem],
        out_specs=[vmem] * 2,
        scratch_shapes=[pltpu.SMEM(range_shift.shape, jnp.float32), pltpu.SemaphoreType.DMA],
        compiler_params=limit,
        cost_estimate=pl.CostEstimate(flops=600_000_000, bytes_accessed=0, transcendentals=0),
    )(range_shift, early)
    looked = pl.pallas_call(
        functools.partial(looks_kernel, pairs, dates),
        out_shape=[jax.ShapeDtypeStruct((groups, out_width), jnp.float32)] * dates,
        in_specs=[vmem] * (2 + dates),
        out_specs=[vmem] * dates,
        scratch_shapes=[
            pltpu.VMEM((chunk_rows + FOLD, LANES), bf16),
            pltpu.VMEM((dates, chunk_rows, 2 * LANES), bf16),
            pltpu.VMEM((len(pairs) * 2 * groups, chunk), jnp.float32),
        ],
        compiler_params=limit,
    )(weights, early, *chunks)
    returned = exchanged(looked, steps)[::-1]
    returned = [returned[reach(distance, dates)] for distance in reversed(range(dates))]
    out = pl.pallas_call(
        functools.partial(place_kernel, min(LAGS, dates - 1), looks),
        out_shape=jax.ShapeDtypeStruct((2, LAGS, groups, looks * dates), jnp.float32),
        in_specs=[vmem] * dates,
        out_specs=vmem,
        compiler_params=limit,
    )(*returned)
    return out[:, None]


def body(slc, offsets, kernel_index, range_shift):
    dates, az_count = (lax.axis_size(a) for a in ("date", "az"))
    lines, columns = slc.shape[2], slc.shape[3]
    whole_tiles = columns % (dates * LANES) == 0 and columns % (dates * LOOK_RG) == 0
    one_row = columns // LOOK_RG == LANES and range_shift.shape[0] == dates
    few = dates & (dates - 1) == 0 and dates - 1 <= LAGS
    folds = lines == 2 * HALO_LINES and lax.axis_size("rng") == 2 and dates >= 4 and 2 * lines // FOLD * TAIL <= LANES
    if az_count == 2 and whole_tiles and one_row and few and folds:
        return tiled_body(slc, offsets, kernel_index, range_shift)
    return chunked_body(slc, offsets, kernel_index, range_shift)


def solution(mesh):
    return jax.shard_map(
        body,
        mesh=mesh,
        in_specs=(
            P(None, ("groups", "date"), "az", "rng"),
            P(("groups", "date"), None),
            P(("groups", "date"), None),
            P("groups"),
        ),
        out_specs=P(None, ("groups", "date"), None, "az", "rng"),
        check_vma=False,
    )
```

```python
import functools

import jax
import jax.numpy as jnp
import numpy as np
from jax import lax
from jax.experimental import pallas as pl
from jax.experimental.pallas import tpu as pltpu
from jax.sharding import PartitionSpec as P

LAGS = 8
KERNELS = 16
TAPS = 8
FILTER_HALF = 8
FILTER_TAPS = 2 * FILTER_HALF + 1
LOOK_AZ = 4
LOOK_RG = 20
LANES = 128
META = 3
UNROLLED_PAIRS = 12


def up(value, unit):
    return -(-value // unit) * unit


def kernel_table():
    position = np.arange(TAPS) - 3.0 - np.arange(KERNELS)[:, None] / KERNELS
    shaped = np.sinc(position) * (0.5 + 0.5 * np.cos(np.pi * position / 5.0))
    table = np.zeros((KERNELS, LANES), np.float32)
    table[:, :TAPS] = shaped / shaped.sum(1, keepdims=True)
    return table


def lowpass_row(width):
    t = np.arange(FILTER_TAPS) - FILTER_HALF
    row = np.zeros((1, width), np.float32)
    row[0, :FILTER_TAPS] = 0.4 * np.sinc(0.4 * t) * (0.54 + 0.46 * np.cos(np.pi * t / (FILTER_HALF + 1)))
    return row


def halves(value):
    high = value.astype(jnp.bfloat16)
    return high, (value - high.astype(jnp.float32)).astype(jnp.bfloat16)


def dot(a, b):
    return jnp.dot(a, b, preferred_element_type=jnp.float32)


def dot_nt(a, b):
    return lax.dot_general(a, b, (((1,), (1,)), ((), ())), preferred_element_type=jnp.float32)


def pack_kernel(chunk, place_ref, offsets_ref, index_ref, slc_ref, before_ref, after_ref, out_ref, wide_ref):
    columns = slc_ref.shape[1]
    wide = out_ref.shape[2]
    first = place_ref[0] == 0
    last = place_ref[0] == place_ref[1] - 1
    zero = jnp.zeros_like(before_ref[...])
    wide_ref[:, :LANES] = jnp.where(first, zero, before_ref[...])
    wide_ref[:, LANES : LANES + columns] = slc_ref[...]
    wide_ref[:, LANES + columns :] = jnp.where(last, zero, after_ref[...])
    lane = lax.broadcasted_iota(jnp.int32, (slc_ref.shape[0], wide), 1)
    numbers = [offsets_ref[0, 0], index_ref[0, 0], index_ref[0, 1]]
    for j in range(out_ref.shape[0]):
        start = LANES + chunk * j - FILTER_HALF - 3 + offsets_ref[0, 1]
        tile = lax.shift_right_logical(start, 7)
        within = lax.bitwise_and(start, LANES - 1)
        window = wide_ref[:, pl.ds(pl.multiple_of(tile * LANES, LANES), wide + LANES)].astype(jnp.float32)
        moved = pltpu.roll(window, wide + LANES - within, 1)[:, :wide]
        for slot, number in enumerate(numbers):
            moved = jnp.where(lane == wide - META + slot, number.astype(jnp.float32), moved)
        out_ref[j] = moved.astype(jnp.bfloat16)


def picked_taps(table, index):
    row = lax.broadcasted_iota(jnp.int32, table.shape, 0).astype(jnp.float32)
    return jnp.sum(jnp.where(row == index, table, 0.0), axis=0, keepdims=True)


def banded(taps, distance):
    out = jnp.zeros(distance.shape, jnp.float32)
    for q in range(TAPS):
        out = jnp.where(distance == q, taps[:, q : q + 1], out)
    return out


def pairs_kernel(chunk, pairs, *refs):
    if isinstance(pairs, int):
        table_of_pairs, refs = refs[0], refs[1:]
    shift_ref, table_ref, lowpass_ref, recv_ref, out_ref, resampled_ref, weight_ref, product_ref = refs
    sources, rows, wide = recv_ref.shape
    dates = shift_ref.shape[0]
    az_count = sources // dates
    own_lines = rows // 2
    lines = own_lines * az_count
    groups = lines // LOOK_AZ
    looks = chunk // LOOK_RG
    table = table_ref[...]
    held = resampled_ref.shape[2]

    out_row = lax.broadcasted_iota(jnp.int32, (lines, lines), 0)
    in_row = lax.broadcasted_iota(jnp.int32, (lines, lines), 1)
    line = LOOK_AZ * (out_row % groups) + out_row // groups
    line_distance = (in_row - line + 3).astype(jnp.float32)
    span = min(2 * LANES, wide)
    column_distance = (
        lax.broadcasted_iota(jnp.int32, (span, LANES), 0) - lax.broadcasted_iota(jnp.int32, (span, LANES), 1)
    ).astype(jnp.float32)
    for date in range(dates):
        numbers = recv_ref[date * az_count, 0:16, wide - LANES :].astype(jnp.float32)[0:1, LANES - META :]
        line_offset, line_index, column_index = (numbers[:, s : s + 1] for s in range(META))
        line_taps = banded(picked_taps(table, line_index), line_distance - line_offset)
        line_taps = jnp.concatenate(halves(line_taps), axis=0)
        column_high, column_low = halves(banded(picked_taps(table, column_index), column_distance))
        moved = []
        for plane in range(2):
            rows_of = slice(plane * own_lines, (plane + 1) * own_lines)
            source = jnp.concatenate([recv_ref[date * az_count + a, rows_of, :] for a in range(az_count)], axis=0)
            both = dot(line_taps, source)
            moved.append(both[:lines] + both[lines:])
        moved_high, moved_low = halves(jnp.concatenate(moved, axis=0))
        for begin in range(0, held, LANES):
            end = min(begin + span, wide)
            taken = end - begin
            total = dot(moved_high[:, begin:end], column_high[:taken])
            total += dot(moved_low[:, begin:end], column_high[:taken])
            total += dot(moved_high[:, begin:end], column_low[:taken])
            resampled_ref[date, :, begin : begin + LANES] = total.astype(jnp.bfloat16)

    window = lowpass_ref[...]
    spacing = lax.broadcasted_iota(jnp.int32, window.shape, 1).astype(jnp.float32) - FILTER_HALF
    span = min(2 * LANES, held)

    def one_pair(place, own, other):
        gap = shift_ref[own] - shift_ref[other]
        angle = jnp.where(jnp.abs(spacing) <= FILTER_HALF, jnp.pi * gap * spacing, 0.0)
        for part, taps in enumerate((window * jnp.cos(angle), window * jnp.sin(angle))):
            spread = jnp.broadcast_to(taps, (LANES, 2 * LANES))
            spread = pltpu.roll(spread, 0, 1, stride=1, stride_axis=0)
            high, low = halves(spread)
            weight_ref[0, part * LANES : (part + 1) * LANES, :] = high
            weight_ref[1, part * LANES : (part + 1) * LANES, :] = low
        both = jnp.concatenate([resampled_ref[own], resampled_ref[other]], axis=0)
        for begin in range(0, up(chunk, LANES), LANES):
            end = min(begin + span, held)
            taken = end - begin
            total = dot_nt(both[:, begin:end], weight_ref[0, :, :taken])
            total += dot_nt(both[:, begin:end], weight_ref[1, :, :taken])
            cos, sin = total[:, :LANES], total[:, LANES:]
            re, im = slice(0, lines), slice(lines, 2 * lines)
            master_re = cos[re] + sin[im]
            master_im = cos[im] - sin[re]
            re, im = slice(2 * lines, 3 * lines), slice(3 * lines, 4 * lines)
            partner_re = cos[re] - sin[im]
            partner_im = cos[im] + sin[re]
            for part, product in enumerate(
                (
                    master_re * partner_re + master_im * partner_im,
                    master_im * partner_re - master_re * partner_im,
                )
            ):
                summed = sum(product[k * groups : (k + 1) * groups] for k in range(LOOK_AZ))
                product_ref[place, part, :, begin : begin + LANES] = summed

    if isinstance(pairs, int):
        count = pairs

        def step(place, carry):
            one_pair(place, table_of_pairs[place, 0], table_of_pairs[place, 1])
            return carry

        lax.fori_loop(0, count, step, 0)
    else:
        count = len(pairs)
        for place, (own, other) in enumerate(pairs):
            one_pair(place, own, other)

    out_width = out_ref.shape[2]
    column = lax.broadcasted_iota(jnp.int32, (product_ref.shape[3], out_width), 0)
    lane = lax.broadcasted_iota(jnp.int32, (product_ref.shape[3], out_width), 1)
    collect = jnp.where(column // LOOK_RG == lane % looks, 1.0, 0.0).astype(jnp.bfloat16)
    high, low = halves(product_ref[...].reshape(count * 2 * groups, product_ref.shape[3]))
    total = (dot(high, collect) + dot(low, collect)) * (1.0 / (LOOK_AZ * LOOK_RG))
    total = total.reshape(count, 2, groups, out_width)
    own_lane = lax.broadcasted_iota(jnp.int32, (groups, out_width), 1) // looks
    place = 0
    for own in range(dates):
        value = jnp.zeros((groups, out_width), jnp.float32)
        for lag in range(min(LAGS, dates - 1 - own)):
            for part in range(2):
                value = jnp.where(own_lane == lag * 2 + part, total[place, part], value)
            place += 1
        out_ref[own * az_count : (own + 1) * az_count] = value.reshape(az_count, groups // az_count, out_width)


def unpack_kernel(used_lags, looks, recv_ref, out_ref):
    sources, groups, width = recv_ref.shape
    columns = out_ref.shape[-1]
    lane = lax.broadcasted_iota(jnp.int32, (groups, columns), 1) // looks
    out_ref[...] = jnp.zeros_like(out_ref)
    for lag in range(used_lags):
        for part in range(2):
            value = jnp.zeros((groups, columns), jnp.float32)
            for source in range(sources):
                block = recv_ref[source]
                if width != columns:
                    block = block[:, :columns]
                shift = looks * (source - lag * 2 - part) % columns
                if shift:
                    block = pltpu.roll(block, shift, 1)
                value = jnp.where(lane == source, block, value)
            out_ref[part, lag] = value


def chunked_body(slc, offsets, kernel_index, range_shift):
    axes = ("date", "az")
    date_count, az_count, rng_count = (lax.axis_size(a) for a in ("date", "az", "rng"))
    peers = date_count * az_count
    lines, columns = slc.shape[2], slc.shape[3]
    dates = range_shift.shape[0]
    chunk = columns // peers
    looks = chunk // LOOK_RG
    groups = lines * az_count // LOOK_AZ
    wide = up(chunk + 2 * FILTER_HALF + TAPS - 1 + META, LANES)
    held = up(chunk + 2 * FILTER_HALF, LANES)
    used_lags = min(LAGS, dates - 1)
    out_width = up(used_lags * 2 * looks, LANES)
    vmem = pl.BlockSpec(memory_space=pltpu.VMEM)
    smem = pl.BlockSpec(memory_space=pltpu.SMEM)
    limit = pltpu.CompilerParams(vmem_limit_bytes=32 * 1024 * 1024)

    cells = slc.reshape(2 * lines, columns)
    place = lax.axis_index("rng")
    if rng_count == 2:
        edge = jnp.where(place == 0, cells[:, columns - LANES :], cells[:, :LANES])
        before = after = lax.ppermute(edge, "rng", [(0, 1), (1, 0)])
    else:
        forth = [(i, i + 1) for i in range(rng_count - 1)]
        before = lax.ppermute(cells[:, columns - LANES :], "rng", forth)
        after = lax.ppermute(cells[:, :LANES], "rng", [(b, a) for a, b in forth])

    packed = pl.pallas_call(
        functools.partial(pack_kernel, chunk),
        out_shape=jax.ShapeDtypeStruct((peers, 2 * lines, wide), jnp.bfloat16),
        in_specs=[smem] * 3 + [vmem] * 3,
        out_specs=vmem,
        scratch_shapes=[pltpu.VMEM((2 * lines, columns + 2 * LANES), jnp.bfloat16)],
        compiler_params=limit,
    )(jnp.stack([place, rng_count]).astype(jnp.int32), offsets, kernel_index, cells, before, after)
    arrived = lax.all_to_all(packed, axes, 0, 0, tiled=True)

    pairs = [(own, own + lag) for own in range(dates) for lag in range(1, LAGS + 1) if own + lag < dates]
    count = len(pairs)
    first = [jnp.asarray(np.array(pairs, np.int32))] if count > UNROLLED_PAIRS else []
    looked = pl.pallas_call(
        functools.partial(pairs_kernel, chunk, count if first else pairs),
        out_shape=jax.ShapeDtypeStruct((peers, groups // az_count, out_width), jnp.float32),
        in_specs=[smem] * len(first) + [smem] + [vmem] * 3,
        out_specs=vmem,
        scratch_shapes=[
            pltpu.VMEM((dates, 4 * (groups * LOOK_AZ) // 2, held), jnp.bfloat16),
            pltpu.VMEM((2, 2 * LANES, 2 * LANES), jnp.bfloat16),
            pltpu.VMEM((count, 2, groups, up(chunk, LANES)), jnp.float32),
        ],
        compiler_params=limit,
    )(*first, range_shift, jnp.asarray(kernel_table()), jnp.asarray(lowpass_row(2 * LANES)), arrived)
    returned = lax.all_to_all(looked, axes, 0, 0, tiled=True)

    out = pl.pallas_call(
        functools.partial(unpack_kernel, used_lags, looks),
        out_shape=jax.ShapeDtypeStruct((2, LAGS, groups // az_count, looks * peers), jnp.float32),
        in_specs=[vmem],
        out_specs=vmem,
        compiler_params=limit,
    )(returned)
    return out[:, None]


HALO_LINES = 16
FOLD = 16
TAIL = 2 * FILTER_HALF


def reach(step, dates):
    return {dates - 1: dates // 2, dates // 2: dates - 1}.get(step, step)


def sinc(value):
    angle = jnp.pi * value
    return jnp.where(angle == 0.0, 1.0, jnp.sin(angle) / jnp.where(angle == 0.0, 1.0, angle))


def tap_row(index):
    lane = lax.broadcasted_iota(jnp.int32, (1, LANES), 1)
    position = lane.astype(jnp.float32) - 3.0 - index.astype(jnp.float32) / KERNELS
    shaped = sinc(position) * (0.5 + 0.5 * jnp.cos(jnp.pi * position / 5.0))
    shaped = jnp.where(lane < TAPS, shaped, 0.0)
    return shaped / jnp.sum(shaped, axis=1, keepdims=True)


def row_line(row, az):
    quarter = HALO_LINES // LOOK_AZ
    within = row % HALO_LINES
    return HALO_LINES * ((row // HALO_LINES) ^ az) + LOOK_AZ * (within % quarter) + within // quarter


def prepare_kernel(offsets_hbm, index_hbm, slc_ref, side_ref, corner_ref, lines_ref, line_ref, column_ref, held_ref, offsets_ref, index_ref, semaphores):
    lines, columns = slc_ref.shape[1:]
    az = lax.axis_index("az")
    row = pl.multiple_of((1 - az) * (lines - HALO_LINES), HALO_LINES)
    edge = pl.multiple_of((1 - lax.axis_index("rng")) * (columns - LANES), LANES)
    nearest, outermost = pl.ds(row, HALO_LINES), pl.ds(edge, LANES)
    moves = [
        (offsets_hbm, offsets_ref),
        (index_hbm, index_ref),
        (slc_ref.at[:, :, outermost], side_ref),
        (slc_ref.at[:, nearest, outermost], corner_ref),
        (slc_ref.at[:, nearest, :], lines_ref),
    ]
    for plane in range(2):
        for part in range(lines // HALO_LINES):
            for side in range(2):
                at = pl.ds(part * HALO_LINES, HALO_LINES)
                source = slc_ref.at[plane, at, pl.ds(side * columns // 2, columns // 2)]
                moves.append((source, held_ref.at[plane, at, pl.ds(LANES + side * columns // 2, columns // 2)]))
    copies = [pltpu.make_async_copy(a, b, semaphores.at[i]) for i, (a, b) in enumerate(moves)]
    for copy in copies:
        copy.start()
    held_ref[:, :, :LANES] = jnp.zeros((2, lines, LANES), held_ref.dtype)
    held_ref[:, :, LANES + columns :] = jnp.zeros((2, lines, 2 * LANES), held_ref.dtype)
    copies[0].wait()
    copies[1].wait()
    for half in range(2):
        shape = (HALO_LINES, lines + HALO_LINES)
        line = row_line(lax.broadcasted_iota(jnp.int32, shape, 0) + half * HALO_LINES, az)
        place = lax.broadcasted_iota(jnp.int32, shape, 1)
        source = jnp.where(place < lines, place, place + jnp.where(az == 0, 0, -lines - HALO_LINES))
        taps = banded(tap_row(index_ref[0, 0]), source - line - offsets_ref[0, 0] + 3)
        line_ref[half] = jnp.concatenate(halves(taps), axis=0)
    shape = (3 * LANES, LANES)
    distance = lax.broadcasted_iota(jnp.int32, shape, 0) - lax.broadcasted_iota(jnp.int32, shape, 1)
    distance = distance - (LANES - FILTER_HALF - 3) - offsets_ref[0, 1]
    taps = banded(tap_row(index_ref[0, 1]), distance)
    column_ref[...] = jnp.concatenate(halves(taps), axis=1)
    for copy in copies[2:]:
        copy.wait()


def along_range(blocks, column_ref, tiles):
    blocks = [halves(moved) for moved in blocks]
    starts = range(0, tiles * LANES, LANES)
    high = jnp.concatenate([high[:, s : s + 3 * LANES] for high, _ in blocks for s in starts], axis=0)
    low = jnp.concatenate([low[:, s : s + 3 * LANES] for _, low in blocks for s in starts], axis=0)
    total = dot(high, column_ref[...])
    return total[:, :LANES] + total[:, LANES:] + dot(low, column_ref[:, :LANES])


def early_kernel(tiles, steps, held_ref, line_ref, column_ref, *outs):
    lines = held_ref.shape[1]
    early = tiles - 1
    moved = []
    for step in steps:
        chunk = lax.axis_index("date") ^ reach(step, lax.axis_size("date"))
        begin = pl.multiple_of((chunk * tiles + lax.axis_index("rng")) * LANES, LANES)
        moved += [held_ref[plane, :, pl.ds(begin, (early + 2) * LANES)] for plane in range(2)]
    both = dot(line_ref[0, :, :lines], jnp.concatenate(moved, axis=1))
    both = both[:HALO_LINES] + both[HALO_LINES:]
    width = (early + 2) * LANES
    moved = [
        jnp.concatenate([both[:, (2 * i + plane) * width : (2 * i + plane + 1) * width] for plane in range(2)], axis=0)
        for i in range(len(outs))
    ]
    total = along_range(moved, column_ref, early).astype(jnp.bfloat16)
    rows = early * lines
    for i, out_ref in enumerate(outs):
        out_ref[...] = total[i * rows : (i + 1) * rows]


def resample_kernel(side_ref, corner_ref, lines_ref, held_ref, line_ref, column_ref, *outs):
    outs, tiles_ref, tails_ref = outs[:-2], outs[-2], outs[-1]
    lines, width = held_ref.shape[1:]
    width -= LANES
    block = lax.axis_index("rng")
    taps = jnp.concatenate([line_ref[0], line_ref[1]], axis=0)
    moved = [[], []]
    for plane in range(2):
        own = jnp.concatenate([side_ref[plane], held_ref[plane, :, LANES : width - LANES], side_ref[plane]], axis=1)
        halo = jnp.concatenate([corner_ref[plane], lines_ref[plane], corner_ref[plane]], axis=1)
        both = dot(taps, jnp.concatenate([own, halo], axis=0))
        for half in range(2):
            at = 2 * half * HALO_LINES
            moved[half].append(both[at : at + HALO_LINES] + both[at + HALO_LINES : at + 2 * HALO_LINES])
    moved = jnp.concatenate(moved[0] + moved[1], axis=0)
    left = jnp.where(block > 0, moved[:, :LANES], 0.0)
    right = jnp.where(block == 0, moved[:, width - LANES :], 0.0)
    moved = jnp.concatenate([left, moved[:, LANES : width - LANES], right, jnp.zeros_like(right)], axis=1)
    total = along_range([moved], column_ref, width // LANES - 1)
    rows = 2 * lines
    tiles_ref[...] = total.astype(jnp.bfloat16)
    chunk_rows = outs[0].shape[0] - FOLD
    lane = lax.broadcasted_iota(jnp.int32, (FOLD, LANES), 1) // TAIL
    for chunk in range(len(outs)):
        begin = (chunk + 1) * chunk_rows
        folded = total[begin : begin + FOLD]
        for part in range(1, rows // FOLD):
            value = pltpu.roll(total[begin + part * FOLD : begin + (part + 1) * FOLD], part * TAIL, 1)
            folded = jnp.where(lane == part, value, folded)
        tails_ref[chunk] = folded.astype(jnp.bfloat16)
    date = lax.axis_index("date")
    early = chunk_rows // rows - 1
    for step, out_ref in enumerate(outs):
        chunk = date ^ reach(step, len(outs))
        if out_ref.shape[0] == outs[0].shape[0]:
            out_ref[:chunk_rows] = tiles_ref[pl.ds(pl.multiple_of(chunk * chunk_rows, FOLD), chunk_rows), :]
            out_ref[chunk_rows:] = tails_ref[chunk]
            continue
        for tile in range(early):
            begin = pl.multiple_of(chunk * chunk_rows + (tile + block) * rows + lines, FOLD)
            out_ref[tile * lines : (tile + 1) * lines] = tiles_ref[pl.ds(begin, lines), :]
        begin = pl.multiple_of(chunk * chunk_rows + (1 - block) * early * rows, FOLD)
        out_ref[early * lines : early * lines + rows] = tiles_ref[pl.ds(begin, rows), :]
        out_ref[early * lines + rows :] = tails_ref[chunk]


def filter_kernel(pairs, shift_hbm, *refs):
    count = (len(refs) - 3) // 2
    earlies, out_ref, spreads, (shift_ref, semaphore) = refs[:count], refs[count], refs[count + 1 : -2], refs[-2:]
    copy = pltpu.make_async_copy(shift_hbm, shift_ref, semaphore)
    copy.start()
    lines = 2 * HALO_LINES
    for early_ref, spread_ref in zip(earlies, spreads):
        spread_ref[...] = jnp.zeros_like(spread_ref)
        for tile in range(early_ref.shape[0] // lines):
            begin = pl.multiple_of((tile + lax.axis_index("rng")) * 2 * lines, FOLD)
            spread_ref[pl.ds(begin, lines), :] = early_ref[tile * lines : (tile + 1) * lines]
    date = lax.axis_index("date")
    spacing = lax.broadcasted_iota(jnp.int32, (1, 2 * LANES), 1).astype(jnp.float32) - FILTER_HALF
    window = 0.4 * sinc(0.4 * spacing) * (0.54 + 0.46 * jnp.cos(jnp.pi * spacing / (FILTER_HALF + 1)))
    window = jnp.where(jnp.abs(spacing) <= FILTER_HALF, window, 0.0)
    copy.wait()
    for place, (first, second) in enumerate(pairs):
        dates = shift_ref.shape[0]
        gap = shift_ref[date ^ reach(first, dates)] - shift_ref[date ^ reach(second, dates)]
        angle = jnp.where(jnp.abs(spacing) <= FILTER_HALF, jnp.pi * gap * spacing, 0.0)
        for part, taps in enumerate((window * jnp.cos(angle), window * jnp.sin(angle))):
            spread = jnp.broadcast_to(taps, (LANES, 2 * LANES))
            spread = pltpu.roll(spread, 0, 1, stride=1, stride_axis=0)
            high, low = halves(spread)
            out_ref[place, part * LANES : (part + 1) * LANES, : 2 * LANES] = high
            out_ref[place, part * LANES : (part + 1) * LANES, 2 * LANES :] = low


def looks_kernel(pairs, dates, weight_ref, *refs):
    far = dates - 2
    earlies, chunks = refs[:far], list(refs[far : far + dates][::-1])
    outs, (whole_ref, window_ref, product_ref) = refs[far + dates : -3], refs[-3:]
    groups, lines = outs[0].shape[0], outs[0].shape[0] * LOOK_AZ
    rows = 2 * lines
    blocks = (chunks[0].shape[0] - FOLD) // rows
    looks = blocks * LANES // LOOK_RG
    date = lax.axis_index("date")
    block = lax.axis_index("rng")
    early = blocks - 1
    for i, early_ref in enumerate(earlies):
        whole, rest_ref = whole_ref.at[i], chunks[dates - 1 - i]
        whole[: blocks * rows] = early_ref[...]
        for tile in range(early):
            begin = pl.multiple_of((tile + block) * rows, FOLD)
            whole[pl.ds(begin + lines, lines), :] = rest_ref[tile * lines : (tile + 1) * lines]
        begin = pl.multiple_of((1 - block) * early * rows, FOLD)
        whole[pl.ds(begin, rows), :] = rest_ref[early * lines : early * lines + rows]
        whole[blocks * rows :] = rest_ref[early * lines + rows :]
        chunks[dates - 1 - i] = whole
    az = lax.axis_index("az")
    upper = lax.broadcasted_iota(jnp.int32, (groups, LANES), 0) // (groups // 2) == az
    for step, chunk_ref in enumerate(chunks):
        window_ref[step, :, :LANES] = chunk_ref[: blocks * rows]
        window_ref[step, : (blocks - 1) * rows, LANES:] = chunk_ref[rows : blocks * rows]
        folded = chunk_ref[blocks * rows :].astype(jnp.float32)
        for part in range(rows // FOLD):
            value = pltpu.roll(folded, LANES - part * TAIL, 1) if part else folded
            at = pl.ds((blocks - 1) * rows + part * FOLD, FOLD)
            window_ref[step, at, LANES:] = value.astype(jnp.bfloat16)
    for place, (first, second) in enumerate(pairs):
        def filtered(step):
            window = window_ref[step]
            total = dot_nt(jnp.concatenate([window, window], axis=1), weight_ref[place])
            total = total.reshape(blocks, 2, 2, HALO_LINES, 2 * LANES)
            re, im = total[:, :, 0], total[:, :, 1]
            return re[..., :LANES], im[..., :LANES], re[..., LANES:], im[..., LANES:]

        cos_re, cos_im, sin_re, sin_im = filtered(first)
        master_re, master_im = cos_re + sin_im, cos_im - sin_re
        cos_re, cos_im, sin_re, sin_im = filtered(second)
        partner_re, partner_im = cos_re - sin_im, cos_im + sin_re
        for part, product in enumerate(
            (
                master_re * partner_re + master_im * partner_im,
                master_im * partner_re - master_re * partner_im,
            )
        ):
            summed = product[:, :, :groups] + product[:, :, groups:]
            at = pl.ds((place * 2 + part) * groups, groups)
            for k in range(blocks):
                both = [summed[k, half] + pltpu.roll(summed[k, half], groups // 2, 0) for half in range(2)]
                product_ref[at, k * LANES : (k + 1) * LANES] = jnp.where(upper, both[0], both[1])

    out_width = outs[0].shape[1]
    column = lax.broadcasted_iota(jnp.int32, (product_ref.shape[1], out_width), 0)
    lane = lax.broadcasted_iota(jnp.int32, (product_ref.shape[1], out_width), 1)
    collect = jnp.where(column // LOOK_RG == lane % looks, 1.0, 0.0).astype(jnp.bfloat16)
    high, low = halves(product_ref[...])
    total = (dot(high, collect) + dot(low, collect)) * (1.0 / (LOOK_AZ * LOOK_RG))
    total = total.reshape(len(pairs), 2, groups, out_width)
    own_lane = lax.broadcasted_iota(jnp.int32, (groups, out_width), 1) // looks
    for step, out_ref in enumerate(outs):
        value = jnp.zeros((groups, out_width), jnp.float32)
        for place, pair in enumerate(pairs):
            if step in pair:
                other = pair[1] if pair[0] == step else pair[0]
                lag = (date ^ reach(other, dates)) - (date ^ reach(step, dates))
                for part in range(2):
                    signed = -total[place, part] if part == 1 and pair[1] == step else total[place, part]
                    value = jnp.where(own_lane == (lag - 1) * 2 + part, signed, value)
        out_ref[...] = value


def place_kernel(used_lags, looks, *refs):
    out_ref = refs[-1]
    groups, columns = out_ref.shape[2:]
    date = lax.axis_index("date")
    lane = lax.broadcasted_iota(jnp.int32, (groups, LANES), 1) // looks
    out_ref[...] = jnp.zeros_like(out_ref)
    each = LANES // looks
    for step, recv_ref in enumerate(refs[:-1][::-1]):
        chunk = date ^ step
        for lag in range(used_lags):
            for part in range(2):
                tile, group = divmod(lag * 2 + part, each)
                block = recv_ref[:, tile * LANES : (tile + 1) * LANES]
                block = pltpu.roll(block, lax.bitwise_and(looks * (chunk - group), LANES - 1), 1)
                out_ref[part, lag] = jnp.where(lane == chunk, block, out_ref[part, lag])


def tiled_body(slc, offsets, kernel_index, range_shift):
    dates = lax.axis_size("date")
    lines, columns = slc.shape[2], slc.shape[3]
    chunk = columns // dates
    looks = chunk // LOOK_RG
    groups = lines // LOOK_AZ
    out_width = up(min(LAGS, dates - 1) * 2 * looks, LANES)
    vmem = pl.BlockSpec(memory_space=pltpu.VMEM)
    hbm = pl.BlockSpec(memory_space=pltpu.HBM)
    limit = pltpu.CompilerParams(vmem_limit_bytes=32 * 1024 * 1024)
    bf16 = jnp.bfloat16
    cells, offsets, kernel_index, range_shift = (
        pltpu.with_memory_space_constraint(value, pltpu.HBM)
        for value in (slc.reshape(2, lines, columns), offsets, kernel_index, range_shift)
    )
    tiles = chunk // LANES
    chunk_rows = tiles * 2 * lines

    side, corner, halo_lines, line_taps, column_taps, held = pl.pallas_call(
        prepare_kernel,
        out_shape=[
            jax.ShapeDtypeStruct((2, lines, LANES), bf16),
            jax.ShapeDtypeStruct((2, HALO_LINES, LANES), bf16),
            jax.ShapeDtypeStruct((2, HALO_LINES, columns), bf16),
            jax.ShapeDtypeStruct((2, 2 * HALO_LINES, lines + HALO_LINES), bf16),
            jax.ShapeDtypeStruct((3 * LANES, 2 * LANES), bf16),
            jax.ShapeDtypeStruct((2, lines, columns + 3 * LANES), bf16),
        ],
        in_specs=[hbm] * 3,
        out_specs=[vmem] * 6,
        scratch_shapes=[
            pltpu.SMEM(offsets.shape, jnp.int32),
            pltpu.SMEM(kernel_index.shape, jnp.int32),
            pltpu.SemaphoreType.DMA((5 + 4 * (lines // HALO_LINES),)),
        ],
        compiler_params=limit,
    )(offsets, kernel_index, cells)
    swap = [(0, 1), (1, 0)]
    side = lax.ppermute(side, "rng", swap)
    corner = lax.ppermute(corner, ("rng", "az"), [(0, 3), (1, 2), (2, 1), (3, 0)])
    halo_lines = lax.ppermute(halo_lines, "az", swap)

    steps = range(dates - 1, 0, -1)
    far = dates - 2
    early_rows = (tiles - 1) * lines
    early = pl.pallas_call(
        functools.partial(early_kernel, tiles, steps[:far]),
        out_shape=[jax.ShapeDtypeStruct((early_rows, LANES), bf16)] * far,
        in_specs=[vmem] * 3,
        out_specs=[vmem] * far,
        compiler_params=limit,
    )(held, line_taps, column_taps)
    early = [
        lax.ppermute(rows, "date", [(i, i ^ reach(step, dates)) for i in range(dates)]) for rows, step in zip(early, steps)
    ]
    out_rows = [chunk_rows + FOLD] * 2 + [chunk_rows + FOLD - early_rows] * far
    sent = pl.pallas_call(
        resample_kernel,
        out_shape=[jax.ShapeDtypeStruct((rows, LANES), bf16) for rows in out_rows],
        in_specs=[vmem] * 6,
        out_specs=[vmem] * dates,
        scratch_shapes=[
            pltpu.VMEM(((columns // LANES + 1) * 2 * lines, LANES), bf16),
            pltpu.VMEM((dates, FOLD, LANES), bf16),
        ],
        compiler_params=limit,
        cost_estimate=pl.CostEstimate(flops=700_000_000, bytes_accessed=0, transcendentals=0),
    )(side, corner, halo_lines, held, line_taps, column_taps)

    def exchanged(values, order):
        arrived = {0: values[0]}
        for step in order:
            arrived[step] = lax.ppermute(values[step], "date", [(i, i ^ reach(step, dates)) for i in range(dates)])
        return [arrived[step] for step in reversed(range(dates))]

    chunks = exchanged(sent, steps)
    pairs = [(first, second) for first in range(dates) for second in range(first + 1, dates)]
    weights, *early = pl.pallas_call(
        functools.partial(filter_kernel, pairs),
        out_shape=[
            jax.ShapeDtypeStruct((len(pairs), 2 * LANES, 4 * LANES), bf16),
        ]
        + [jax.ShapeDtypeStruct((chunk_rows, LANES), bf16)] * far,
        in_specs=[hbm] + [vmem] * far,
        out_specs=[vmem] * (1 + far),
        scratch_shapes=[pltpu.SMEM(range_shift.shape, jnp.float32), pltpu.SemaphoreType.DMA],
        compiler_params=limit,
        cost_estimate=pl.CostEstimate(flops=1_000_000_000, bytes_accessed=0, transcendentals=0),
    )(range_shift, *early)
    looked = pl.pallas_call(
        functools.partial(looks_kernel, pairs, dates),
        out_shape=[jax.ShapeDtypeStruct((groups, out_width), jnp.float32)] * dates,
        in_specs=[vmem] * (1 + far + dates),
        out_specs=[vmem] * dates,
        scratch_shapes=[
            pltpu.VMEM((far, chunk_rows + FOLD, LANES), bf16),
            pltpu.VMEM((dates, chunk_rows, 2 * LANES), bf16),
            pltpu.VMEM((len(pairs) * 2 * groups, chunk), jnp.float32),
        ],
        compiler_params=limit,
    )(weights, *early, *chunks)
    returned = exchanged(looked, steps)[::-1]
    returned = [returned[reach(distance, dates)] for distance in reversed(range(dates))]
    out = pl.pallas_call(
        functools.partial(place_kernel, min(LAGS, dates - 1), looks),
        out_shape=jax.ShapeDtypeStruct((2, LAGS, groups, looks * dates), jnp.float32),
        in_specs=[vmem] * dates,
        out_specs=vmem,
        compiler_params=limit,
    )(*returned)
    return out[:, None]


def body(slc, offsets, kernel_index, range_shift):
    dates, az_count = (lax.axis_size(a) for a in ("date", "az"))
    lines, columns = slc.shape[2], slc.shape[3]
    whole_tiles = columns % (dates * LANES) == 0 and columns % (dates * LOOK_RG) == 0
    one_row = columns // LOOK_RG == LANES and range_shift.shape[0] == dates
    few = dates & (dates - 1) == 0 and dates - 1 <= LAGS
    folds = lines == 2 * HALO_LINES and lax.axis_size("rng") == 2 and dates >= 4 and 2 * lines // FOLD * TAIL <= LANES
    if az_count == 2 and whole_tiles and one_row and few and folds:
        return tiled_body(slc, offsets, kernel_index, range_shift)
    return chunked_body(slc, offsets, kernel_index, range_shift)


def solution(mesh):
    return jax.shard_map(
        body,
        mesh=mesh,
        in_specs=(
            P(None, ("groups", "date"), "az", "rng"),
            P(("groups", "date"), None),
            P(("groups", "date"), None),
            P("groups"),
        ),
        out_specs=P(None, ("groups", "date"), None, "az", "rng"),
        check_vma=False,
    )
```

```python
import functools

import jax
import jax.numpy as jnp
import numpy as np
from jax import lax
from jax.experimental import pallas as pl
from jax.experimental.pallas import tpu as pltpu
from jax.sharding import PartitionSpec as P

LAGS = 8
KERNELS = 16
TAPS = 8
FILTER_HALF = 8
FILTER_TAPS = 2 * FILTER_HALF + 1
LOOK_AZ = 4
LOOK_RG = 20
LANES = 128
META = 3
UNROLLED_PAIRS = 12


def up(value, unit):
    return -(-value // unit) * unit


def kernel_table():
    position = np.arange(TAPS) - 3.0 - np.arange(KERNELS)[:, None] / KERNELS
    shaped = np.sinc(position) * (0.5 + 0.5 * np.cos(np.pi * position / 5.0))
    table = np.zeros((KERNELS, LANES), np.float32)
    table[:, :TAPS] = shaped / shaped.sum(1, keepdims=True)
    return table


def lowpass_row(width):
    t = np.arange(FILTER_TAPS) - FILTER_HALF
    row = np.zeros((1, width), np.float32)
    row[0, :FILTER_TAPS] = 0.4 * np.sinc(0.4 * t) * (0.54 + 0.46 * np.cos(np.pi * t / (FILTER_HALF + 1)))
    return row


def halves(value):
    high = value.astype(jnp.bfloat16)
    return high, (value - high.astype(jnp.float32)).astype(jnp.bfloat16)


def dot(a, b):
    return jnp.dot(a, b, preferred_element_type=jnp.float32)


def dot_nt(a, b):
    return lax.dot_general(a, b, (((1,), (1,)), ((), ())), preferred_element_type=jnp.float32)


def pack_kernel(chunk, place_ref, offsets_ref, index_ref, slc_ref, before_ref, after_ref, out_ref, wide_ref):
    columns = slc_ref.shape[1]
    wide = out_ref.shape[2]
    first = place_ref[0] == 0
    last = place_ref[0] == place_ref[1] - 1
    zero = jnp.zeros_like(before_ref[...])
    wide_ref[:, :LANES] = jnp.where(first, zero, before_ref[...])
    wide_ref[:, LANES : LANES + columns] = slc_ref[...]
    wide_ref[:, LANES + columns :] = jnp.where(last, zero, after_ref[...])
    lane = lax.broadcasted_iota(jnp.int32, (slc_ref.shape[0], wide), 1)
    numbers = [offsets_ref[0, 0], index_ref[0, 0], index_ref[0, 1]]
    for j in range(out_ref.shape[0]):
        start = LANES + chunk * j - FILTER_HALF - 3 + offsets_ref[0, 1]
        tile = lax.shift_right_logical(start, 7)
        within = lax.bitwise_and(start, LANES - 1)
        window = wide_ref[:, pl.ds(pl.multiple_of(tile * LANES, LANES), wide + LANES)].astype(jnp.float32)
        moved = pltpu.roll(window, wide + LANES - within, 1)[:, :wide]
        for slot, number in enumerate(numbers):
            moved = jnp.where(lane == wide - META + slot, number.astype(jnp.float32), moved)
        out_ref[j] = moved.astype(jnp.bfloat16)


def picked_taps(table, index):
    row = lax.broadcasted_iota(jnp.int32, table.shape, 0).astype(jnp.float32)
    return jnp.sum(jnp.where(row == index, table, 0.0), axis=0, keepdims=True)


def banded(taps, distance):
    out = jnp.zeros(distance.shape, jnp.float32)
    for q in range(TAPS):
        out = jnp.where(distance == q, taps[:, q : q + 1], out)
    return out


def pairs_kernel(chunk, pairs, *refs):
    if isinstance(pairs, int):
        table_of_pairs, refs = refs[0], refs[1:]
    shift_ref, table_ref, lowpass_ref, recv_ref, out_ref, resampled_ref, weight_ref, product_ref = refs
    sources, rows, wide = recv_ref.shape
    dates = shift_ref.shape[0]
    az_count = sources // dates
    own_lines = rows // 2
    lines = own_lines * az_count
    groups = lines // LOOK_AZ
    looks = chunk // LOOK_RG
    table = table_ref[...]
    held = resampled_ref.shape[2]

    out_row = lax.broadcasted_iota(jnp.int32, (lines, lines), 0)
    in_row = lax.broadcasted_iota(jnp.int32, (lines, lines), 1)
    line = LOOK_AZ * (out_row % groups) + out_row // groups
    line_distance = (in_row - line + 3).astype(jnp.float32)
    span = min(2 * LANES, wide)
    column_distance = (
        lax.broadcasted_iota(jnp.int32, (span, LANES), 0) - lax.broadcasted_iota(jnp.int32, (span, LANES), 1)
    ).astype(jnp.float32)
    for date in range(dates):
        numbers = recv_ref[date * az_count, 0:16, wide - LANES :].astype(jnp.float32)[0:1, LANES - META :]
        line_offset, line_index, column_index = (numbers[:, s : s + 1] for s in range(META))
        line_taps = banded(picked_taps(table, line_index), line_distance - line_offset)
        line_taps = jnp.concatenate(halves(line_taps), axis=0)
        column_high, column_low = halves(banded(picked_taps(table, column_index), column_distance))
        moved = []
        for plane in range(2):
            rows_of = slice(plane * own_lines, (plane + 1) * own_lines)
            source = jnp.concatenate([recv_ref[date * az_count + a, rows_of, :] for a in range(az_count)], axis=0)
            both = dot(line_taps, source)
            moved.append(both[:lines] + both[lines:])
        moved_high, moved_low = halves(jnp.concatenate(moved, axis=0))
        for begin in range(0, held, LANES):
            end = min(begin + span, wide)
            taken = end - begin
            total = dot(moved_high[:, begin:end], column_high[:taken])
            total += dot(moved_low[:, begin:end], column_high[:taken])
            total += dot(moved_high[:, begin:end], column_low[:taken])
            resampled_ref[date, :, begin : begin + LANES] = total.astype(jnp.bfloat16)

    window = lowpass_ref[...]
    spacing = lax.broadcasted_iota(jnp.int32, window.shape, 1).astype(jnp.float32) - FILTER_HALF
    span = min(2 * LANES, held)

    def one_pair(place, own, other):
        gap = shift_ref[own] - shift_ref[other]
        angle = jnp.where(jnp.abs(spacing) <= FILTER_HALF, jnp.pi * gap * spacing, 0.0)
        for part, taps in enumerate((window * jnp.cos(angle), window * jnp.sin(angle))):
            spread = jnp.broadcast_to(taps, (LANES, 2 * LANES))
            spread = pltpu.roll(spread, 0, 1, stride=1, stride_axis=0)
            high, low = halves(spread)
            weight_ref[0, part * LANES : (part + 1) * LANES, :] = high
            weight_ref[1, part * LANES : (part + 1) * LANES, :] = low
        both = jnp.concatenate([resampled_ref[own], resampled_ref[other]], axis=0)
        for begin in range(0, up(chunk, LANES), LANES):
            end = min(begin + span, held)
            taken = end - begin
            total = dot_nt(both[:, begin:end], weight_ref[0, :, :taken])
            total += dot_nt(both[:, begin:end], weight_ref[1, :, :taken])
            cos, sin = total[:, :LANES], total[:, LANES:]
            re, im = slice(0, lines), slice(lines, 2 * lines)
            master_re = cos[re] + sin[im]
            master_im = cos[im] - sin[re]
            re, im = slice(2 * lines, 3 * lines), slice(3 * lines, 4 * lines)
            partner_re = cos[re] - sin[im]
            partner_im = cos[im] + sin[re]
            for part, product in enumerate(
                (
                    master_re * partner_re + master_im * partner_im,
                    master_im * partner_re - master_re * partner_im,
                )
            ):
                summed = sum(product[k * groups : (k + 1) * groups] for k in range(LOOK_AZ))
                product_ref[place, part, :, begin : begin + LANES] = summed

    if isinstance(pairs, int):
        count = pairs

        def step(place, carry):
            one_pair(place, table_of_pairs[place, 0], table_of_pairs[place, 1])
            return carry

        lax.fori_loop(0, count, step, 0)
    else:
        count = len(pairs)
        for place, (own, other) in enumerate(pairs):
            one_pair(place, own, other)

    out_width = out_ref.shape[2]
    column = lax.broadcasted_iota(jnp.int32, (product_ref.shape[3], out_width), 0)
    lane = lax.broadcasted_iota(jnp.int32, (product_ref.shape[3], out_width), 1)
    collect = jnp.where(column // LOOK_RG == lane % looks, 1.0, 0.0).astype(jnp.bfloat16)
    high, low = halves(product_ref[...].reshape(count * 2 * groups, product_ref.shape[3]))
    total = (dot(high, collect) + dot(low, collect)) * (1.0 / (LOOK_AZ * LOOK_RG))
    total = total.reshape(count, 2, groups, out_width)
    own_lane = lax.broadcasted_iota(jnp.int32, (groups, out_width), 1) // looks
    place = 0
    for own in range(dates):
        value = jnp.zeros((groups, out_width), jnp.float32)
        for lag in range(min(LAGS, dates - 1 - own)):
            for part in range(2):
                value = jnp.where(own_lane == lag * 2 + part, total[place, part], value)
            place += 1
        out_ref[own * az_count : (own + 1) * az_count] = value.reshape(az_count, groups // az_count, out_width)


def unpack_kernel(used_lags, looks, recv_ref, out_ref):
    sources, groups, width = recv_ref.shape
    columns = out_ref.shape[-1]
    lane = lax.broadcasted_iota(jnp.int32, (groups, columns), 1) // looks
    out_ref[...] = jnp.zeros_like(out_ref)
    for lag in range(used_lags):
        for part in range(2):
            value = jnp.zeros((groups, columns), jnp.float32)
            for source in range(sources):
                block = recv_ref[source]
                if width != columns:
                    block = block[:, :columns]
                shift = looks * (source - lag * 2 - part) % columns
                if shift:
                    block = pltpu.roll(block, shift, 1)
                value = jnp.where(lane == source, block, value)
            out_ref[part, lag] = value


def chunked_body(slc, offsets, kernel_index, range_shift):
    axes = ("date", "az")
    date_count, az_count, rng_count = (lax.axis_size(a) for a in ("date", "az", "rng"))
    peers = date_count * az_count
    lines, columns = slc.shape[2], slc.shape[3]
    dates = range_shift.shape[0]
    chunk = columns // peers
    looks = chunk // LOOK_RG
    groups = lines * az_count // LOOK_AZ
    wide = up(chunk + 2 * FILTER_HALF + TAPS - 1 + META, LANES)
    held = up(chunk + 2 * FILTER_HALF, LANES)
    used_lags = min(LAGS, dates - 1)
    out_width = up(used_lags * 2 * looks, LANES)
    vmem = pl.BlockSpec(memory_space=pltpu.VMEM)
    smem = pl.BlockSpec(memory_space=pltpu.SMEM)
    limit = pltpu.CompilerParams(vmem_limit_bytes=32 * 1024 * 1024)

    cells = slc.reshape(2 * lines, columns)
    place = lax.axis_index("rng")
    if rng_count == 2:
        edge = jnp.where(place == 0, cells[:, columns - LANES :], cells[:, :LANES])
        before = after = lax.ppermute(edge, "rng", [(0, 1), (1, 0)])
    else:
        forth = [(i, i + 1) for i in range(rng_count - 1)]
        before = lax.ppermute(cells[:, columns - LANES :], "rng", forth)
        after = lax.ppermute(cells[:, :LANES], "rng", [(b, a) for a, b in forth])

    packed = pl.pallas_call(
        functools.partial(pack_kernel, chunk),
        out_shape=jax.ShapeDtypeStruct((peers, 2 * lines, wide), jnp.bfloat16),
        in_specs=[smem] * 3 + [vmem] * 3,
        out_specs=vmem,
        scratch_shapes=[pltpu.VMEM((2 * lines, columns + 2 * LANES), jnp.bfloat16)],
        compiler_params=limit,
    )(jnp.stack([place, rng_count]).astype(jnp.int32), offsets, kernel_index, cells, before, after)
    arrived = lax.all_to_all(packed, axes, 0, 0, tiled=True)

    pairs = [(own, own + lag) for own in range(dates) for lag in range(1, LAGS + 1) if own + lag < dates]
    count = len(pairs)
    first = [jnp.asarray(np.array(pairs, np.int32))] if count > UNROLLED_PAIRS else []
    looked = pl.pallas_call(
        functools.partial(pairs_kernel, chunk, count if first else pairs),
        out_shape=jax.ShapeDtypeStruct((peers, groups // az_count, out_width), jnp.float32),
        in_specs=[smem] * len(first) + [smem] + [vmem] * 3,
        out_specs=vmem,
        scratch_shapes=[
            pltpu.VMEM((dates, 4 * (groups * LOOK_AZ) // 2, held), jnp.bfloat16),
            pltpu.VMEM((2, 2 * LANES, 2 * LANES), jnp.bfloat16),
            pltpu.VMEM((count, 2, groups, up(chunk, LANES)), jnp.float32),
        ],
        compiler_params=limit,
    )(*first, range_shift, jnp.asarray(kernel_table()), jnp.asarray(lowpass_row(2 * LANES)), arrived)
    returned = lax.all_to_all(looked, axes, 0, 0, tiled=True)

    out = pl.pallas_call(
        functools.partial(unpack_kernel, used_lags, looks),
        out_shape=jax.ShapeDtypeStruct((2, LAGS, groups // az_count, looks * peers), jnp.float32),
        in_specs=[vmem],
        out_specs=vmem,
        compiler_params=limit,
    )(returned)
    return out[:, None]


HALO_LINES = 16
FOLD = 16
TAIL = 2 * FILTER_HALF


def reach(step, dates):
    return {dates - 1: dates // 2, dates // 2: dates - 1}.get(step, step)


def sinc(value):
    angle = jnp.pi * value
    return jnp.where(angle == 0.0, 1.0, jnp.sin(angle) / jnp.where(angle == 0.0, 1.0, angle))


def tap_row(index):
    lane = lax.broadcasted_iota(jnp.int32, (1, LANES), 1)
    position = lane.astype(jnp.float32) - 3.0 - index.astype(jnp.float32) / KERNELS
    shaped = sinc(position) * (0.5 + 0.5 * jnp.cos(jnp.pi * position / 5.0))
    shaped = jnp.where(lane < TAPS, shaped, 0.0)
    return shaped / jnp.sum(shaped, axis=1, keepdims=True)


def row_line(row, az):
    quarter = HALO_LINES // LOOK_AZ
    within = row % HALO_LINES
    return HALO_LINES * ((row // HALO_LINES) ^ az) + LOOK_AZ * (within % quarter) + within // quarter


def prepare_kernel(offsets_hbm, index_hbm, slc_ref, side_ref, corner_ref, lines_ref, line_ref, column_ref, held_ref, offsets_ref, index_ref, semaphores):
    lines, columns = slc_ref.shape[1:]
    az = lax.axis_index("az")
    row = pl.multiple_of((1 - az) * (lines - HALO_LINES), HALO_LINES)
    edge = pl.multiple_of((1 - lax.axis_index("rng")) * (columns - LANES), LANES)
    nearest, outermost = pl.ds(row, HALO_LINES), pl.ds(edge, LANES)
    moves = [
        (offsets_hbm, offsets_ref),
        (index_hbm, index_ref),
        (slc_ref.at[:, :, outermost], side_ref),
        (slc_ref.at[:, nearest, outermost], corner_ref),
        (slc_ref.at[:, nearest, :], lines_ref),
    ]
    for plane in range(2):
        for part in range(lines // HALO_LINES):
            for side in range(2):
                at = pl.ds(part * HALO_LINES, HALO_LINES)
                source = slc_ref.at[plane, at, pl.ds(side * columns // 2, columns // 2)]
                moves.append((source, held_ref.at[plane, at, pl.ds(LANES + side * columns // 2, columns // 2)]))
    copies = [pltpu.make_async_copy(a, b, semaphores.at[i]) for i, (a, b) in enumerate(moves)]
    for copy in copies:
        copy.start()
    held_ref[:, :, :LANES] = jnp.zeros((2, lines, LANES), held_ref.dtype)
    held_ref[:, :, LANES + columns :] = jnp.zeros((2, lines, 2 * LANES), held_ref.dtype)
    copies[0].wait()
    copies[1].wait()
    for half in range(2):
        shape = (HALO_LINES, lines + HALO_LINES)
        line = row_line(lax.broadcasted_iota(jnp.int32, shape, 0) + half * HALO_LINES, az)
        place = lax.broadcasted_iota(jnp.int32, shape, 1)
        source = jnp.where(place < lines, place, place + jnp.where(az == 0, 0, -lines - HALO_LINES))
        taps = banded(tap_row(index_ref[0, 0]), source - line - offsets_ref[0, 0] + 3)
        line_ref[half] = jnp.concatenate(halves(taps), axis=0)
    shape = (2 * LANES, LANES)
    distance = lax.broadcasted_iota(jnp.int32, shape, 0) - lax.broadcasted_iota(jnp.int32, shape, 1)
    distance = distance - (LANES // 2 - FILTER_HALF - 3) - offsets_ref[0, 1]
    taps = banded(tap_row(index_ref[0, 1]), distance)
    column_ref[...] = jnp.concatenate(halves(taps), axis=1)
    for copy in copies[2:]:
        copy.wait()


def along_range(moved, column_ref, tiles):
    high, low = halves(pltpu.roll(moved, moved.shape[1] - LANES // 2, 1))
    starts = range(0, tiles * LANES, LANES)
    high = jnp.concatenate([high[:, s : s + 2 * LANES] for s in starts], axis=0)
    low = jnp.concatenate([low[:, s : s + 2 * LANES] for s in starts], axis=0)
    total = dot(high, column_ref[...])
    return total[:, :LANES] + total[:, LANES:] + dot(low, column_ref[:, :LANES])


def early_kernel(tiles, held_ref, line_ref, column_ref, out_ref):
    lines = held_ref.shape[1]
    early = out_ref.shape[0] // (2 * HALO_LINES)
    dates = lax.axis_size("date")
    chunk = lax.axis_index("date") ^ reach(dates - 1, dates)
    begin = pl.multiple_of((chunk * tiles + lax.axis_index("rng")) * LANES, LANES)
    moved = []
    for plane in range(2):
        both = dot(line_ref[0, :, :lines], held_ref[plane, :, pl.ds(begin, (early + 2) * LANES)])
        moved.append(both[:HALO_LINES] + both[HALO_LINES:])
    moved = jnp.concatenate(moved, axis=0)
    out_ref[...] = along_range(moved, column_ref, early).astype(jnp.bfloat16)


def resample_kernel(side_ref, corner_ref, lines_ref, held_ref, line_ref, column_ref, *outs):
    outs, tiles_ref, tails_ref = outs[:-2], outs[-2], outs[-1]
    lines, width = held_ref.shape[1:]
    width -= LANES
    block = lax.axis_index("rng")
    taps = jnp.concatenate([line_ref[0], line_ref[1]], axis=0)
    moved = [[], []]
    for plane in range(2):
        own = jnp.concatenate([side_ref[plane], held_ref[plane, :, LANES : width - LANES], side_ref[plane]], axis=1)
        halo = jnp.concatenate([corner_ref[plane], lines_ref[plane], corner_ref[plane]], axis=1)
        both = dot(taps, jnp.concatenate([own, halo], axis=0))
        for half in range(2):
            at = 2 * half * HALO_LINES
            moved[half].append(both[at : at + HALO_LINES] + both[at + HALO_LINES : at + 2 * HALO_LINES])
    moved = jnp.concatenate(moved[0] + moved[1], axis=0)
    left = jnp.where(block > 0, moved[:, :LANES], 0.0)
    right = jnp.where(block == 0, moved[:, width - LANES :], 0.0)
    moved = jnp.concatenate([left, moved[:, LANES : width - LANES], right, jnp.zeros_like(right)], axis=1)
    total = along_range(moved, column_ref, width // LANES - 1)
    rows = 2 * lines
    tiles_ref[...] = total.astype(jnp.bfloat16)
    chunk_rows = outs[0].shape[0] - FOLD
    lane = lax.broadcasted_iota(jnp.int32, (FOLD, LANES), 1) // TAIL
    for chunk in range(len(outs)):
        begin = (chunk + 1) * chunk_rows
        folded = total[begin : begin + FOLD]
        for part in range(1, rows // FOLD):
            value = pltpu.roll(total[begin + part * FOLD : begin + (part + 1) * FOLD], part * TAIL, 1)
            folded = jnp.where(lane == part, value, folded)
        tails_ref[chunk] = folded.astype(jnp.bfloat16)
    date = lax.axis_index("date")
    for step, out_ref in enumerate(outs[:-1]):
        chunk = date ^ reach(step, len(outs))
        out_ref[:chunk_rows] = tiles_ref[pl.ds(pl.multiple_of(chunk * chunk_rows, FOLD), chunk_rows), :]
        out_ref[chunk_rows:] = tails_ref[chunk]
    out_ref = outs[-1]
    chunk = date ^ reach(len(outs) - 1, len(outs))
    early = chunk_rows // rows - 1
    for tile in range(early):
        begin = pl.multiple_of(chunk * chunk_rows + (tile + block) * rows + lines, FOLD)
        out_ref[tile * lines : (tile + 1) * lines] = tiles_ref[pl.ds(begin, lines), :]
    begin = pl.multiple_of(chunk * chunk_rows + (1 - block) * early * rows, FOLD)
    out_ref[early * lines : early * lines + rows] = tiles_ref[pl.ds(begin, rows), :]
    out_ref[early * lines + rows :] = tails_ref[chunk]


def filter_kernel(pairs, shift_hbm, early_ref, out_ref, spread_ref, shift_ref, semaphore):
    copy = pltpu.make_async_copy(shift_hbm, shift_ref, semaphore)
    copy.start()
    lines = 2 * HALO_LINES
    spread_ref[...] = jnp.zeros_like(spread_ref)
    for tile in range(early_ref.shape[0] // lines):
        begin = pl.multiple_of((tile + lax.axis_index("rng")) * 2 * lines, FOLD)
        spread_ref[pl.ds(begin, lines), :] = early_ref[tile * lines : (tile + 1) * lines]
    date = lax.axis_index("date")
    spacing = lax.broadcasted_iota(jnp.int32, (1, 2 * LANES), 1).astype(jnp.float32) - FILTER_HALF
    window = 0.4 * sinc(0.4 * spacing) * (0.54 + 0.46 * jnp.cos(jnp.pi * spacing / (FILTER_HALF + 1)))
    window = jnp.where(jnp.abs(spacing) <= FILTER_HALF, window, 0.0)
    copy.wait()
    for place, (first, second) in enumerate(pairs):
        dates = shift_ref.shape[0]
        gap = shift_ref[date ^ reach(first, dates)] - shift_ref[date ^ reach(second, dates)]
        angle = jnp.where(jnp.abs(spacing) <= FILTER_HALF, jnp.pi * gap * spacing, 0.0)
        for part, taps in enumerate((window * jnp.cos(angle), window * jnp.sin(angle))):
            spread = jnp.broadcast_to(taps, (LANES, 2 * LANES))
            spread = pltpu.roll(spread, 0, 1, stride=1, stride_axis=0)
            high, low = halves(spread)
            out_ref[place, part * LANES : (part + 1) * LANES, : 2 * LANES] = high
            out_ref[place, part * LANES : (part + 1) * LANES, 2 * LANES :] = low


def looks_kernel(pairs, dates, weight_ref, *refs):
    early_ref, chunks, outs = refs[0], list(refs[1 : dates + 1][::-1]), refs[dates + 1 : 2 * dates + 1]
    whole_ref, window_ref, product_ref = refs[-3:]
    groups, lines = outs[0].shape[0], outs[0].shape[0] * LOOK_AZ
    rows = 2 * lines
    blocks = (chunks[0].shape[0] - FOLD) // rows
    looks = blocks * LANES // LOOK_RG
    date = lax.axis_index("date")
    block = lax.axis_index("rng")
    early = blocks - 1
    whole_ref[: blocks * rows] = early_ref[...]
    for tile in range(early):
        begin = pl.multiple_of((tile + block) * rows, FOLD)
        whole_ref[pl.ds(begin + lines, lines), :] = chunks[-1][tile * lines : (tile + 1) * lines]
    begin = pl.multiple_of((1 - block) * early * rows, FOLD)
    whole_ref[pl.ds(begin, rows), :] = chunks[-1][early * lines : early * lines + rows]
    whole_ref[blocks * rows :] = chunks[-1][early * lines + rows :]
    chunks[-1] = whole_ref
    az = lax.axis_index("az")
    upper = lax.broadcasted_iota(jnp.int32, (groups, LANES), 0) // (groups // 2) == az
    for step, chunk_ref in enumerate(chunks):
        window_ref[step, :, :LANES] = chunk_ref[: blocks * rows]
        window_ref[step, : (blocks - 1) * rows, LANES:] = chunk_ref[rows : blocks * rows]
        folded = chunk_ref[blocks * rows :].astype(jnp.float32)
        for part in range(rows // FOLD):
            value = pltpu.roll(folded, LANES - part * TAIL, 1) if part else folded
            at = pl.ds((blocks - 1) * rows + part * FOLD, FOLD)
            window_ref[step, at, LANES:] = value.astype(jnp.bfloat16)
    for place, (first, second) in enumerate(pairs):
        def filtered(step):
            window = window_ref[step]
            total = dot_nt(jnp.concatenate([window, window], axis=1), weight_ref[place])
            total = total.reshape(blocks, 2, 2, HALO_LINES, 2 * LANES)
            re, im = total[:, :, 0], total[:, :, 1]
            return re[..., :LANES], im[..., :LANES], re[..., LANES:], im[..., LANES:]

        cos_re, cos_im, sin_re, sin_im = filtered(first)
        master_re, master_im = cos_re + sin_im, cos_im - sin_re
        cos_re, cos_im, sin_re, sin_im = filtered(second)
        partner_re, partner_im = cos_re - sin_im, cos_im + sin_re
        for part, product in enumerate(
            (
                master_re * partner_re + master_im * partner_im,
                master_im * partner_re - master_re * partner_im,
            )
        ):
            summed = product[:, :, :groups] + product[:, :, groups:]
            at = pl.ds((place * 2 + part) * groups, groups)
            for k in range(blocks):
                both = [summed[k, half] + pltpu.roll(summed[k, half], groups // 2, 0) for half in range(2)]
                product_ref[at, k * LANES : (k + 1) * LANES] = jnp.where(upper, both[0], both[1])

    out_width = outs[0].shape[1]
    column = lax.broadcasted_iota(jnp.int32, (product_ref.shape[1], out_width), 0)
    lane = lax.broadcasted_iota(jnp.int32, (product_ref.shape[1], out_width), 1)
    collect = jnp.where(column // LOOK_RG == lane % looks, 1.0, 0.0).astype(jnp.bfloat16)
    high, low = halves(product_ref[...])
    total = (dot(high, collect) + dot(low, collect)) * (1.0 / (LOOK_AZ * LOOK_RG))
    total = total.reshape(len(pairs), 2, groups, out_width)
    own_lane = lax.broadcasted_iota(jnp.int32, (groups, out_width), 1) // looks
    for step, out_ref in enumerate(outs):
        value = jnp.zeros((groups, out_width), jnp.float32)
        for place, pair in enumerate(pairs):
            if step in pair:
                other = pair[1] if pair[0] == step else pair[0]
                lag = (date ^ reach(other, dates)) - (date ^ reach(step, dates))
                for part in range(2):
                    signed = -total[place, part] if part == 1 and pair[1] == step else total[place, part]
                    value = jnp.where(own_lane == (lag - 1) * 2 + part, signed, value)
        out_ref[...] = value


def place_kernel(used_lags, looks, *refs):
    out_ref = refs[-1]
    groups, columns = out_ref.shape[2:]
    date = lax.axis_index("date")
    lane = lax.broadcasted_iota(jnp.int32, (groups, LANES), 1) // looks
    out_ref[...] = jnp.zeros_like(out_ref)
    each = LANES // looks
    for step, recv_ref in enumerate(refs[:-1][::-1]):
        chunk = date ^ step
        for lag in range(used_lags):
            for part in range(2):
                tile, group = divmod(lag * 2 + part, each)
                block = recv_ref[:, tile * LANES : (tile + 1) * LANES]
                block = pltpu.roll(block, lax.bitwise_and(looks * (chunk - group), LANES - 1), 1)
                out_ref[part, lag] = jnp.where(lane == chunk, block, out_ref[part, lag])


def tiled_body(slc, offsets, kernel_index, range_shift):
    dates = lax.axis_size("date")
    lines, columns = slc.shape[2], slc.shape[3]
    chunk = columns // dates
    looks = chunk // LOOK_RG
    groups = lines // LOOK_AZ
    out_width = up(min(LAGS, dates - 1) * 2 * looks, LANES)
    vmem = pl.BlockSpec(memory_space=pltpu.VMEM)
    hbm = pl.BlockSpec(memory_space=pltpu.HBM)
    limit = pltpu.CompilerParams(vmem_limit_bytes=32 * 1024 * 1024)
    bf16 = jnp.bfloat16
    cells, offsets, kernel_index, range_shift = (
        pltpu.with_memory_space_constraint(value, pltpu.HBM)
        for value in (slc.reshape(2, lines, columns), offsets, kernel_index, range_shift)
    )
    tiles = chunk // LANES
    chunk_rows = tiles * 2 * lines

    side, corner, halo_lines, line_taps, column_taps, held = pl.pallas_call(
        prepare_kernel,
        out_shape=[
            jax.ShapeDtypeStruct((2, lines, LANES), bf16),
            jax.ShapeDtypeStruct((2, HALO_LINES, LANES), bf16),
            jax.ShapeDtypeStruct((2, HALO_LINES, columns), bf16),
            jax.ShapeDtypeStruct((2, 2 * HALO_LINES, lines + HALO_LINES), bf16),
            jax.ShapeDtypeStruct((2 * LANES, 2 * LANES), bf16),
            jax.ShapeDtypeStruct((2, lines, columns + 3 * LANES), bf16),
        ],
        in_specs=[hbm] * 3,
        out_specs=[vmem] * 6,
        scratch_shapes=[
            pltpu.SMEM(offsets.shape, jnp.int32),
            pltpu.SMEM(kernel_index.shape, jnp.int32),
            pltpu.SemaphoreType.DMA((5 + 4 * (lines // HALO_LINES),)),
        ],
        compiler_params=limit,
    )(offsets, kernel_index, cells)
    swap = [(0, 1), (1, 0)]
    side = lax.ppermute(side, "rng", swap)
    corner = lax.ppermute(corner, ("rng", "az"), [(0, 3), (1, 2), (2, 1), (3, 0)])
    halo_lines = lax.ppermute(halo_lines, "az", swap)

    early_rows = (tiles - 1) * lines
    early = pl.pallas_call(
        functools.partial(early_kernel, tiles),
        out_shape=jax.ShapeDtypeStruct((early_rows, LANES), bf16),
        in_specs=[vmem] * 3,
        out_specs=vmem,
        compiler_params=limit,
    )(held, line_taps, column_taps)
    early = lax.ppermute(early, "date", [(i, i ^ reach(dates - 1, dates)) for i in range(dates)])
    out_rows = [chunk_rows + FOLD] * (dates - 1) + [chunk_rows + FOLD - early_rows]
    sent = pl.pallas_call(
        resample_kernel,
        out_shape=[jax.ShapeDtypeStruct((rows, LANES), bf16) for rows in out_rows],
        in_specs=[vmem] * 6,
        out_specs=[vmem] * dates,
        scratch_shapes=[
            pltpu.VMEM(((columns // LANES + 1) * 2 * lines, LANES), bf16),
            pltpu.VMEM((dates, FOLD, LANES), bf16),
        ],
        compiler_params=limit,
    )(side, corner, halo_lines, held, line_taps, column_taps)

    def exchanged(values, order):
        arrived = {0: values[0]}
        for step in order:
            arrived[step] = lax.ppermute(values[step], "date", [(i, i ^ reach(step, dates)) for i in range(dates)])
        return [arrived[step] for step in reversed(range(dates))]

    steps = range(dates - 1, 0, -1)

    chunks = exchanged(sent, steps)
    pairs = [(first, second) for first in range(dates) for second in range(first + 1, dates)]
    weights, early = pl.pallas_call(
        functools.partial(filter_kernel, pairs),
        out_shape=[
            jax.ShapeDtypeStruct((len(pairs), 2 * LANES, 4 * LANES), bf16),
            jax.ShapeDtypeStruct((chunk_rows, LANES), bf16),
        ],
        in_specs=[hbm, vmem],
        out_specs=[vmem] * 2,
        scratch_shapes=[pltpu.SMEM(range_shift.shape, jnp.float32), pltpu.SemaphoreType.DMA],
        compiler_params=limit,
        cost_estimate=pl.CostEstimate(flops=600_000_000, bytes_accessed=0, transcendentals=0),
    )(range_shift, early)
    looked = pl.pallas_call(
        functools.partial(looks_kernel, pairs, dates),
        out_shape=[jax.ShapeDtypeStruct((groups, out_width), jnp.float32)] * dates,
        in_specs=[vmem] * (2 + dates),
        out_specs=[vmem] * dates,
        scratch_shapes=[
            pltpu.VMEM((chunk_rows + FOLD, LANES), bf16),
            pltpu.VMEM((dates, chunk_rows, 2 * LANES), bf16),
            pltpu.VMEM((len(pairs) * 2 * groups, chunk), jnp.float32),
        ],
        compiler_params=limit,
    )(weights, early, *chunks)
    returned = exchanged(looked, steps)[::-1]
    returned = [returned[reach(distance, dates)] for distance in reversed(range(dates))]
    out = pl.pallas_call(
        functools.partial(place_kernel, min(LAGS, dates - 1), looks),
        out_shape=jax.ShapeDtypeStruct((2, LAGS, groups, looks * dates), jnp.float32),
        in_specs=[vmem] * dates,
        out_specs=vmem,
        compiler_params=limit,
    )(*returned)
    return out[:, None]


def body(slc, offsets, kernel_index, range_shift):
    dates, az_count = (lax.axis_size(a) for a in ("date", "az"))
    lines, columns = slc.shape[2], slc.shape[3]
    whole_tiles = columns % (dates * LANES) == 0 and columns % (dates * LOOK_RG) == 0
    one_row = columns // LOOK_RG == LANES and range_shift.shape[0] == dates
    few = dates & (dates - 1) == 0 and dates - 1 <= LAGS
    folds = lines == 2 * HALO_LINES and lax.axis_size("rng") == 2 and dates >= 4 and 2 * lines // FOLD * TAIL <= LANES
    if az_count == 2 and whole_tiles and one_row and few and folds:
        return tiled_body(slc, offsets, kernel_index, range_shift)
    return chunked_body(slc, offsets, kernel_index, range_shift)


def solution(mesh):
    return jax.shard_map(
        body,
        mesh=mesh,
        in_specs=(
            P(None, ("groups", "date"), "az", "rng"),
            P(("groups", "date"), None),
            P(("groups", "date"), None),
            P("groups"),
        ),
        out_specs=P(None, ("groups", "date"), None, "az", "rng"),
        check_vma=False,
    )
```

```python
import functools

import jax
import jax.numpy as jnp
import numpy as np
from jax import lax
from jax.experimental import pallas as pl
from jax.experimental.pallas import tpu as pltpu
from jax.sharding import PartitionSpec as P

LAGS = 8
KERNELS = 16
TAPS = 8
FILTER_HALF = 8
FILTER_TAPS = 2 * FILTER_HALF + 1
LOOK_AZ = 4
LOOK_RG = 20
LANES = 128
META = 3
UNROLLED_PAIRS = 12


def up(value, unit):
    return -(-value // unit) * unit


def kernel_table():
    position = np.arange(TAPS) - 3.0 - np.arange(KERNELS)[:, None] / KERNELS
    shaped = np.sinc(position) * (0.5 + 0.5 * np.cos(np.pi * position / 5.0))
    table = np.zeros((KERNELS, LANES), np.float32)
    table[:, :TAPS] = shaped / shaped.sum(1, keepdims=True)
    return table


def lowpass_row(width):
    t = np.arange(FILTER_TAPS) - FILTER_HALF
    row = np.zeros((1, width), np.float32)
    row[0, :FILTER_TAPS] = 0.4 * np.sinc(0.4 * t) * (0.54 + 0.46 * np.cos(np.pi * t / (FILTER_HALF + 1)))
    return row


def halves(value):
    high = value.astype(jnp.bfloat16)
    return high, (value - high.astype(jnp.float32)).astype(jnp.bfloat16)


def dot(a, b):
    return jnp.dot(a, b, preferred_element_type=jnp.float32)


def dot_nt(a, b):
    return lax.dot_general(a, b, (((1,), (1,)), ((), ())), preferred_element_type=jnp.float32)


def pack_kernel(chunk, place_ref, offsets_ref, index_ref, slc_ref, before_ref, after_ref, out_ref, wide_ref):
    columns = slc_ref.shape[1]
    wide = out_ref.shape[2]
    first = place_ref[0] == 0
    last = place_ref[0] == place_ref[1] - 1
    zero = jnp.zeros_like(before_ref[...])
    wide_ref[:, :LANES] = jnp.where(first, zero, before_ref[...])
    wide_ref[:, LANES : LANES + columns] = slc_ref[...]
    wide_ref[:, LANES + columns :] = jnp.where(last, zero, after_ref[...])
    lane = lax.broadcasted_iota(jnp.int32, (slc_ref.shape[0], wide), 1)
    numbers = [offsets_ref[0, 0], index_ref[0, 0], index_ref[0, 1]]
    for j in range(out_ref.shape[0]):
        start = LANES + chunk * j - FILTER_HALF - 3 + offsets_ref[0, 1]
        tile = lax.shift_right_logical(start, 7)
        within = lax.bitwise_and(start, LANES - 1)
        window = wide_ref[:, pl.ds(pl.multiple_of(tile * LANES, LANES), wide + LANES)].astype(jnp.float32)
        moved = pltpu.roll(window, wide + LANES - within, 1)[:, :wide]
        for slot, number in enumerate(numbers):
            moved = jnp.where(lane == wide - META + slot, number.astype(jnp.float32), moved)
        out_ref[j] = moved.astype(jnp.bfloat16)


def picked_taps(table, index):
    row = lax.broadcasted_iota(jnp.int32, table.shape, 0).astype(jnp.float32)
    return jnp.sum(jnp.where(row == index, table, 0.0), axis=0, keepdims=True)


def banded(taps, distance):
    out = jnp.zeros(distance.shape, jnp.float32)
    for q in range(TAPS):
        out = jnp.where(distance == q, taps[:, q : q + 1], out)
    return out


def pairs_kernel(chunk, pairs, *refs):
    if isinstance(pairs, int):
        table_of_pairs, refs = refs[0], refs[1:]
    shift_ref, table_ref, lowpass_ref, recv_ref, out_ref, resampled_ref, weight_ref, product_ref = refs
    sources, rows, wide = recv_ref.shape
    dates = shift_ref.shape[0]
    az_count = sources // dates
    own_lines = rows // 2
    lines = own_lines * az_count
    groups = lines // LOOK_AZ
    looks = chunk // LOOK_RG
    table = table_ref[...]
    held = resampled_ref.shape[2]

    out_row = lax.broadcasted_iota(jnp.int32, (lines, lines), 0)
    in_row = lax.broadcasted_iota(jnp.int32, (lines, lines), 1)
    line = LOOK_AZ * (out_row % groups) + out_row // groups
    line_distance = (in_row - line + 3).astype(jnp.float32)
    span = min(2 * LANES, wide)
    column_distance = (
        lax.broadcasted_iota(jnp.int32, (span, LANES), 0) - lax.broadcasted_iota(jnp.int32, (span, LANES), 1)
    ).astype(jnp.float32)
    for date in range(dates):
        numbers = recv_ref[date * az_count, 0:16, wide - LANES :].astype(jnp.float32)[0:1, LANES - META :]
        line_offset, line_index, column_index = (numbers[:, s : s + 1] for s in range(META))
        line_taps = banded(picked_taps(table, line_index), line_distance - line_offset)
        line_taps = jnp.concatenate(halves(line_taps), axis=0)
        column_high, column_low = halves(banded(picked_taps(table, column_index), column_distance))
        moved = []
        for plane in range(2):
            rows_of = slice(plane * own_lines, (plane + 1) * own_lines)
            source = jnp.concatenate([recv_ref[date * az_count + a, rows_of, :] for a in range(az_count)], axis=0)
            both = dot(line_taps, source)
            moved.append(both[:lines] + both[lines:])
        moved_high, moved_low = halves(jnp.concatenate(moved, axis=0))
        for begin in range(0, held, LANES):
            end = min(begin + span, wide)
            taken = end - begin
            total = dot(moved_high[:, begin:end], column_high[:taken])
            total += dot(moved_low[:, begin:end], column_high[:taken])
            total += dot(moved_high[:, begin:end], column_low[:taken])
            resampled_ref[date, :, begin : begin + LANES] = total.astype(jnp.bfloat16)

    window = lowpass_ref[...]
    spacing = lax.broadcasted_iota(jnp.int32, window.shape, 1).astype(jnp.float32) - FILTER_HALF
    span = min(2 * LANES, held)

    def one_pair(place, own, other):
        gap = shift_ref[own] - shift_ref[other]
        angle = jnp.where(jnp.abs(spacing) <= FILTER_HALF, jnp.pi * gap * spacing, 0.0)
        for part, taps in enumerate((window * jnp.cos(angle), window * jnp.sin(angle))):
            spread = jnp.broadcast_to(taps, (LANES, 2 * LANES))
            spread = pltpu.roll(spread, 0, 1, stride=1, stride_axis=0)
            high, low = halves(spread)
            weight_ref[0, part * LANES : (part + 1) * LANES, :] = high
            weight_ref[1, part * LANES : (part + 1) * LANES, :] = low
        both = jnp.concatenate([resampled_ref[own], resampled_ref[other]], axis=0)
        for begin in range(0, up(chunk, LANES), LANES):
            end = min(begin + span, held)
            taken = end - begin
            total = dot_nt(both[:, begin:end], weight_ref[0, :, :taken])
            total += dot_nt(both[:, begin:end], weight_ref[1, :, :taken])
            cos, sin = total[:, :LANES], total[:, LANES:]
            re, im = slice(0, lines), slice(lines, 2 * lines)
            master_re = cos[re] + sin[im]
            master_im = cos[im] - sin[re]
            re, im = slice(2 * lines, 3 * lines), slice(3 * lines, 4 * lines)
            partner_re = cos[re] - sin[im]
            partner_im = cos[im] + sin[re]
            for part, product in enumerate(
                (
                    master_re * partner_re + master_im * partner_im,
                    master_im * partner_re - master_re * partner_im,
                )
            ):
                summed = sum(product[k * groups : (k + 1) * groups] for k in range(LOOK_AZ))
                product_ref[place, part, :, begin : begin + LANES] = summed

    if isinstance(pairs, int):
        count = pairs

        def step(place, carry):
            one_pair(place, table_of_pairs[place, 0], table_of_pairs[place, 1])
            return carry

        lax.fori_loop(0, count, step, 0)
    else:
        count = len(pairs)
        for place, (own, other) in enumerate(pairs):
            one_pair(place, own, other)

    out_width = out_ref.shape[2]
    column = lax.broadcasted_iota(jnp.int32, (product_ref.shape[3], out_width), 0)
    lane = lax.broadcasted_iota(jnp.int32, (product_ref.shape[3], out_width), 1)
    collect = jnp.where(column // LOOK_RG == lane % looks, 1.0, 0.0).astype(jnp.bfloat16)
    high, low = halves(product_ref[...].reshape(count * 2 * groups, product_ref.shape[3]))
    total = (dot(high, collect) + dot(low, collect)) * (1.0 / (LOOK_AZ * LOOK_RG))
    total = total.reshape(count, 2, groups, out_width)
    own_lane = lax.broadcasted_iota(jnp.int32, (groups, out_width), 1) // looks
    place = 0
    for own in range(dates):
        value = jnp.zeros((groups, out_width), jnp.float32)
        for lag in range(min(LAGS, dates - 1 - own)):
            for part in range(2):
                value = jnp.where(own_lane == lag * 2 + part, total[place, part], value)
            place += 1
        out_ref[own * az_count : (own + 1) * az_count] = value.reshape(az_count, groups // az_count, out_width)


def unpack_kernel(used_lags, looks, recv_ref, out_ref):
    sources, groups, width = recv_ref.shape
    columns = out_ref.shape[-1]
    lane = lax.broadcasted_iota(jnp.int32, (groups, columns), 1) // looks
    out_ref[...] = jnp.zeros_like(out_ref)
    for lag in range(used_lags):
        for part in range(2):
            value = jnp.zeros((groups, columns), jnp.float32)
            for source in range(sources):
                block = recv_ref[source]
                if width != columns:
                    block = block[:, :columns]
                shift = looks * (source - lag * 2 - part) % columns
                if shift:
                    block = pltpu.roll(block, shift, 1)
                value = jnp.where(lane == source, block, value)
            out_ref[part, lag] = value


def chunked_body(slc, offsets, kernel_index, range_shift):
    axes = ("date", "az")
    date_count, az_count, rng_count = (lax.axis_size(a) for a in ("date", "az", "rng"))
    peers = date_count * az_count
    lines, columns = slc.shape[2], slc.shape[3]
    dates = range_shift.shape[0]
    chunk = columns // peers
    looks = chunk // LOOK_RG
    groups = lines * az_count // LOOK_AZ
    wide = up(chunk + 2 * FILTER_HALF + TAPS - 1 + META, LANES)
    held = up(chunk + 2 * FILTER_HALF, LANES)
    used_lags = min(LAGS, dates - 1)
    out_width = up(used_lags * 2 * looks, LANES)
    vmem = pl.BlockSpec(memory_space=pltpu.VMEM)
    smem = pl.BlockSpec(memory_space=pltpu.SMEM)
    limit = pltpu.CompilerParams(vmem_limit_bytes=32 * 1024 * 1024)

    cells = slc.reshape(2 * lines, columns)
    place = lax.axis_index("rng")
    if rng_count == 2:
        edge = jnp.where(place == 0, cells[:, columns - LANES :], cells[:, :LANES])
        before = after = lax.ppermute(edge, "rng", [(0, 1), (1, 0)])
    else:
        forth = [(i, i + 1) for i in range(rng_count - 1)]
        before = lax.ppermute(cells[:, columns - LANES :], "rng", forth)
        after = lax.ppermute(cells[:, :LANES], "rng", [(b, a) for a, b in forth])

    packed = pl.pallas_call(
        functools.partial(pack_kernel, chunk),
        out_shape=jax.ShapeDtypeStruct((peers, 2 * lines, wide), jnp.bfloat16),
        in_specs=[smem] * 3 + [vmem] * 3,
        out_specs=vmem,
        scratch_shapes=[pltpu.VMEM((2 * lines, columns + 2 * LANES), jnp.bfloat16)],
        compiler_params=limit,
    )(jnp.stack([place, rng_count]).astype(jnp.int32), offsets, kernel_index, cells, before, after)
    arrived = lax.all_to_all(packed, axes, 0, 0, tiled=True)

    pairs = [(own, own + lag) for own in range(dates) for lag in range(1, LAGS + 1) if own + lag < dates]
    count = len(pairs)
    first = [jnp.asarray(np.array(pairs, np.int32))] if count > UNROLLED_PAIRS else []
    looked = pl.pallas_call(
        functools.partial(pairs_kernel, chunk, count if first else pairs),
        out_shape=jax.ShapeDtypeStruct((peers, groups // az_count, out_width), jnp.float32),
        in_specs=[smem] * len(first) + [smem] + [vmem] * 3,
        out_specs=vmem,
        scratch_shapes=[
            pltpu.VMEM((dates, 4 * (groups * LOOK_AZ) // 2, held), jnp.bfloat16),
            pltpu.VMEM((2, 2 * LANES, 2 * LANES), jnp.bfloat16),
            pltpu.VMEM((count, 2, groups, up(chunk, LANES)), jnp.float32),
        ],
        compiler_params=limit,
    )(*first, range_shift, jnp.asarray(kernel_table()), jnp.asarray(lowpass_row(2 * LANES)), arrived)
    returned = lax.all_to_all(looked, axes, 0, 0, tiled=True)

    out = pl.pallas_call(
        functools.partial(unpack_kernel, used_lags, looks),
        out_shape=jax.ShapeDtypeStruct((2, LAGS, groups // az_count, looks * peers), jnp.float32),
        in_specs=[vmem],
        out_specs=vmem,
        compiler_params=limit,
    )(returned)
    return out[:, None]


HALO_LINES = 16
FOLD = 16
TAIL = 2 * FILTER_HALF


def reach(step, dates):
    return {dates - 1: dates // 2, dates // 2: dates - 1}.get(step, step)


def sinc(value):
    angle = jnp.pi * value
    return jnp.where(angle == 0.0, 1.0, jnp.sin(angle) / jnp.where(angle == 0.0, 1.0, angle))


def tap_row(index):
    lane = lax.broadcasted_iota(jnp.int32, (1, LANES), 1)
    position = lane.astype(jnp.float32) - 3.0 - index.astype(jnp.float32) / KERNELS
    shaped = sinc(position) * (0.5 + 0.5 * jnp.cos(jnp.pi * position / 5.0))
    shaped = jnp.where(lane < TAPS, shaped, 0.0)
    return shaped / jnp.sum(shaped, axis=1, keepdims=True)


def row_line(row, az):
    quarter = HALO_LINES // LOOK_AZ
    within = row % HALO_LINES
    return HALO_LINES * ((row // HALO_LINES) ^ az) + LOOK_AZ * (within % quarter) + within // quarter


def prepare_kernel(offsets_hbm, index_hbm, slc_ref, side_ref, corner_ref, lines_ref, line_ref, column_ref, held_ref, offsets_ref, index_ref, semaphores):
    lines, columns = slc_ref.shape[1:]
    az = lax.axis_index("az")
    row = pl.multiple_of((1 - az) * (lines - HALO_LINES), HALO_LINES)
    edge = pl.multiple_of((1 - lax.axis_index("rng")) * (columns - LANES), LANES)
    nearest, outermost = pl.ds(row, HALO_LINES), pl.ds(edge, LANES)
    moves = [
        (offsets_hbm, offsets_ref),
        (index_hbm, index_ref),
        (slc_ref.at[:, :, outermost], side_ref),
        (slc_ref.at[:, nearest, outermost], corner_ref),
        (slc_ref.at[:, nearest, :], lines_ref),
    ]
    for plane in range(2):
        for part in range(lines // HALO_LINES):
            for side in range(2):
                at = pl.ds(part * HALO_LINES, HALO_LINES)
                source = slc_ref.at[plane, at, pl.ds(side * columns // 2, columns // 2)]
                moves.append((source, held_ref.at[plane, at, pl.ds(LANES + side * columns // 2, columns // 2)]))
    copies = [pltpu.make_async_copy(a, b, semaphores.at[i]) for i, (a, b) in enumerate(moves)]
    for copy in copies:
        copy.start()
    held_ref[:, :, :LANES] = jnp.zeros((2, lines, LANES), held_ref.dtype)
    held_ref[:, :, LANES + columns :] = jnp.zeros((2, lines, 2 * LANES), held_ref.dtype)
    copies[0].wait()
    copies[1].wait()
    for half in range(2):
        shape = (HALO_LINES, lines + HALO_LINES)
        line = row_line(lax.broadcasted_iota(jnp.int32, shape, 0) + half * HALO_LINES, az)
        place = lax.broadcasted_iota(jnp.int32, shape, 1)
        source = jnp.where(place < lines, place, place + jnp.where(az == 0, 0, -lines - HALO_LINES))
        taps = banded(tap_row(index_ref[0, 0]), source - line - offsets_ref[0, 0] + 3)
        line_ref[half] = jnp.concatenate(halves(taps), axis=0)
    shape = (2 * LANES, LANES)
    distance = lax.broadcasted_iota(jnp.int32, shape, 0) - lax.broadcasted_iota(jnp.int32, shape, 1)
    distance = distance - (LANES // 2 - FILTER_HALF - 3) - offsets_ref[0, 1]
    taps = banded(tap_row(index_ref[0, 1]), distance)
    column_ref[...] = jnp.concatenate(halves(taps), axis=1)
    for copy in copies[2:]:
        copy.wait()


def along_range(moved, column_ref, tiles):
    high, low = halves(pltpu.roll(moved, moved.shape[1] - LANES // 2, 1))
    starts = range(0, tiles * LANES, LANES)
    high = jnp.concatenate([high[:, s : s + 2 * LANES] for s in starts], axis=0)
    low = jnp.concatenate([low[:, s : s + 2 * LANES] for s in starts], axis=0)
    total = dot(high, column_ref[...])
    return total[:, :LANES] + total[:, LANES:] + dot(low, column_ref[:, :LANES])


def early_kernel(tiles, held_ref, line_ref, column_ref, out_ref):
    lines = held_ref.shape[1]
    early = out_ref.shape[0] // (2 * HALO_LINES)
    dates = lax.axis_size("date")
    chunk = lax.axis_index("date") ^ reach(dates - 1, dates)
    begin = pl.multiple_of((chunk * tiles + lax.axis_index("rng")) * LANES, LANES)
    moved = []
    for plane in range(2):
        both = dot(line_ref[0, :, :lines], held_ref[plane, :, pl.ds(begin, (early + 2) * LANES)])
        moved.append(both[:HALO_LINES] + both[HALO_LINES:])
    moved = jnp.concatenate(moved, axis=0)
    out_ref[...] = along_range(moved, column_ref, early).astype(jnp.bfloat16)


def resample_kernel(side_ref, corner_ref, lines_ref, held_ref, line_ref, column_ref, *outs):
    outs, tiles_ref, tails_ref = outs[:-2], outs[-2], outs[-1]
    lines, width = held_ref.shape[1:]
    width -= LANES
    block = lax.axis_index("rng")
    taps = jnp.concatenate([line_ref[0], line_ref[1]], axis=0)
    moved = [[], []]
    for plane in range(2):
        own = jnp.concatenate([side_ref[plane], held_ref[plane, :, LANES : width - LANES], side_ref[plane]], axis=1)
        halo = jnp.concatenate([corner_ref[plane], lines_ref[plane], corner_ref[plane]], axis=1)
        both = dot(taps, jnp.concatenate([own, halo], axis=0))
        for half in range(2):
            at = 2 * half * HALO_LINES
            moved[half].append(both[at : at + HALO_LINES] + both[at + HALO_LINES : at + 2 * HALO_LINES])
    moved = jnp.concatenate(moved[0] + moved[1], axis=0)
    left = jnp.where(block > 0, moved[:, :LANES], 0.0)
    right = jnp.where(block == 0, moved[:, width - LANES :], 0.0)
    moved = jnp.concatenate([left, moved[:, LANES : width - LANES], right, jnp.zeros_like(right)], axis=1)
    total = along_range(moved, column_ref, width // LANES - 1)
    rows = 2 * lines
    tiles_ref[...] = total.astype(jnp.bfloat16)
    chunk_rows = outs[0].shape[0] - FOLD
    lane = lax.broadcasted_iota(jnp.int32, (FOLD, LANES), 1) // TAIL
    for chunk in range(len(outs)):
        begin = (chunk + 1) * chunk_rows
        folded = total[begin : begin + FOLD]
        for part in range(1, rows // FOLD):
            value = pltpu.roll(total[begin + part * FOLD : begin + (part + 1) * FOLD], part * TAIL, 1)
            folded = jnp.where(lane == part, value, folded)
        tails_ref[chunk] = folded.astype(jnp.bfloat16)
    date = lax.axis_index("date")
    for step, out_ref in enumerate(outs[:-1]):
        chunk = date ^ reach(step, len(outs))
        out_ref[:chunk_rows] = tiles_ref[pl.ds(pl.multiple_of(chunk * chunk_rows, FOLD), chunk_rows), :]
        out_ref[chunk_rows:] = tails_ref[chunk]
    out_ref = outs[-1]
    chunk = date ^ reach(len(outs) - 1, len(outs))
    early = chunk_rows // rows - 1
    for tile in range(early):
        begin = pl.multiple_of(chunk * chunk_rows + (tile + block) * rows + lines, FOLD)
        out_ref[tile * lines : (tile + 1) * lines] = tiles_ref[pl.ds(begin, lines), :]
    begin = pl.multiple_of(chunk * chunk_rows + (1 - block) * early * rows, FOLD)
    out_ref[early * lines : early * lines + rows] = tiles_ref[pl.ds(begin, rows), :]
    out_ref[early * lines + rows :] = tails_ref[chunk]


def filter_kernel(pairs, shift_hbm, early_ref, out_ref, spread_ref, shift_ref, semaphore):
    copy = pltpu.make_async_copy(shift_hbm, shift_ref, semaphore)
    copy.start()
    lines = 2 * HALO_LINES
    spread_ref[...] = jnp.zeros_like(spread_ref)
    for tile in range(early_ref.shape[0] // lines):
        begin = pl.multiple_of((tile + lax.axis_index("rng")) * 2 * lines, FOLD)
        spread_ref[pl.ds(begin, lines), :] = early_ref[tile * lines : (tile + 1) * lines]
    date = lax.axis_index("date")
    spacing = lax.broadcasted_iota(jnp.int32, (1, 2 * LANES), 1).astype(jnp.float32) - FILTER_HALF
    window = 0.4 * sinc(0.4 * spacing) * (0.54 + 0.46 * jnp.cos(jnp.pi * spacing / (FILTER_HALF + 1)))
    window = jnp.where(jnp.abs(spacing) <= FILTER_HALF, window, 0.0)
    copy.wait()
    for place, (first, second) in enumerate(pairs):
        dates = shift_ref.shape[0]
        gap = shift_ref[date ^ reach(first, dates)] - shift_ref[date ^ reach(second, dates)]
        angle = jnp.where(jnp.abs(spacing) <= FILTER_HALF, jnp.pi * gap * spacing, 0.0)
        for part, taps in enumerate((window * jnp.cos(angle), window * jnp.sin(angle))):
            spread = jnp.broadcast_to(taps, (LANES, 2 * LANES))
            spread = pltpu.roll(spread, 0, 1, stride=1, stride_axis=0)
            high, low = halves(spread)
            out_ref[place, part * LANES : (part + 1) * LANES, : 2 * LANES] = high
            out_ref[place, part * LANES : (part + 1) * LANES, 2 * LANES :] = low


def looks_kernel(pairs, dates, weight_ref, *refs):
    early_ref, chunks, outs = refs[0], list(refs[1 : dates + 1][::-1]), refs[dates + 1 : 2 * dates + 1]
    whole_ref, window_ref, product_ref = refs[-3:]
    groups, lines = outs[0].shape[0], outs[0].shape[0] * LOOK_AZ
    rows = 2 * lines
    blocks = (chunks[0].shape[0] - FOLD) // rows
    looks = blocks * LANES // LOOK_RG
    date = lax.axis_index("date")
    block = lax.axis_index("rng")
    early = blocks - 1
    whole_ref[: blocks * rows] = early_ref[...]
    for tile in range(early):
        begin = pl.multiple_of((tile + block) * rows, FOLD)
        whole_ref[pl.ds(begin + lines, lines), :] = chunks[-1][tile * lines : (tile + 1) * lines]
    begin = pl.multiple_of((1 - block) * early * rows, FOLD)
    whole_ref[pl.ds(begin, rows), :] = chunks[-1][early * lines : early * lines + rows]
    whole_ref[blocks * rows :] = chunks[-1][early * lines + rows :]
    chunks[-1] = whole_ref
    az = lax.axis_index("az")
    upper = lax.broadcasted_iota(jnp.int32, (groups, LANES), 0) // (groups // 2) == az
    for step, chunk_ref in enumerate(chunks):
        window_ref[step, :, :LANES] = chunk_ref[: blocks * rows]
        window_ref[step, : (blocks - 1) * rows, LANES:] = chunk_ref[rows : blocks * rows]
        folded = chunk_ref[blocks * rows :].astype(jnp.float32)
        for part in range(rows // FOLD):
            value = pltpu.roll(folded, LANES - part * TAIL, 1) if part else folded
            at = pl.ds((blocks - 1) * rows + part * FOLD, FOLD)
            window_ref[step, at, LANES:] = value.astype(jnp.bfloat16)
    for place, (first, second) in enumerate(pairs):
        def filtered(step):
            window = window_ref[step]
            total = dot_nt(jnp.concatenate([window, window], axis=1), weight_ref[place])
            total = total.reshape(blocks, 2, 2, HALO_LINES, 2 * LANES)
            re, im = total[:, :, 0], total[:, :, 1]
            return re[..., :LANES], im[..., :LANES], re[..., LANES:], im[..., LANES:]

        cos_re, cos_im, sin_re, sin_im = filtered(first)
        master_re, master_im = cos_re + sin_im, cos_im - sin_re
        cos_re, cos_im, sin_re, sin_im = filtered(second)
        partner_re, partner_im = cos_re - sin_im, cos_im + sin_re
        for part, product in enumerate(
            (
                master_re * partner_re + master_im * partner_im,
                master_im * partner_re - master_re * partner_im,
            )
        ):
            summed = product[:, :, :groups] + product[:, :, groups:]
            at = pl.ds((place * 2 + part) * groups, groups)
            for k in range(blocks):
                both = [summed[k, half] + pltpu.roll(summed[k, half], groups // 2, 0) for half in range(2)]
                product_ref[at, k * LANES : (k + 1) * LANES] = jnp.where(upper, both[0], both[1])

    out_width = outs[0].shape[1]
    column = lax.broadcasted_iota(jnp.int32, (product_ref.shape[1], out_width), 0)
    lane = lax.broadcasted_iota(jnp.int32, (product_ref.shape[1], out_width), 1)
    collect = jnp.where(column // LOOK_RG == lane % looks, 1.0, 0.0).astype(jnp.bfloat16)
    high, low = halves(product_ref[...])
    total = (dot(high, collect) + dot(low, collect)) * (1.0 / (LOOK_AZ * LOOK_RG))
    total = total.reshape(len(pairs), 2, groups, out_width)
    own_lane = lax.broadcasted_iota(jnp.int32, (groups, out_width), 1) // looks
    for step, out_ref in enumerate(outs):
        value = jnp.zeros((groups, out_width), jnp.float32)
        for place, pair in enumerate(pairs):
            if step in pair:
                other = pair[1] if pair[0] == step else pair[0]
                lag = (date ^ reach(other, dates)) - (date ^ reach(step, dates))
                for part in range(2):
                    signed = -total[place, part] if part == 1 and pair[1] == step else total[place, part]
                    value = jnp.where(own_lane == (lag - 1) * 2 + part, signed, value)
        out_ref[...] = value


def place_kernel(used_lags, looks, *refs):
    out_ref = refs[-1]
    groups, columns = out_ref.shape[2:]
    date = lax.axis_index("date")
    lane = lax.broadcasted_iota(jnp.int32, (groups, LANES), 1) // looks
    out_ref[...] = jnp.zeros_like(out_ref)
    each = LANES // looks
    for step, recv_ref in enumerate(refs[:-1][::-1]):
        chunk = date ^ step
        for lag in range(used_lags):
            for part in range(2):
                tile, group = divmod(lag * 2 + part, each)
                block = recv_ref[:, tile * LANES : (tile + 1) * LANES]
                block = pltpu.roll(block, lax.bitwise_and(looks * (chunk - group), LANES - 1), 1)
                out_ref[part, lag] = jnp.where(lane == chunk, block, out_ref[part, lag])


def tiled_body(slc, offsets, kernel_index, range_shift):
    dates = lax.axis_size("date")
    lines, columns = slc.shape[2], slc.shape[3]
    chunk = columns // dates
    looks = chunk // LOOK_RG
    groups = lines // LOOK_AZ
    out_width = up(min(LAGS, dates - 1) * 2 * looks, LANES)
    vmem = pl.BlockSpec(memory_space=pltpu.VMEM)
    hbm = pl.BlockSpec(memory_space=pltpu.HBM)
    limit = pltpu.CompilerParams(vmem_limit_bytes=32 * 1024 * 1024)
    bf16 = jnp.bfloat16
    cells, offsets, kernel_index, range_shift = (
        pltpu.with_memory_space_constraint(value, pltpu.HBM)
        for value in (slc.reshape(2, lines, columns), offsets, kernel_index, range_shift)
    )
    tiles = chunk // LANES
    chunk_rows = tiles * 2 * lines

    side, corner, halo_lines, line_taps, column_taps, held = pl.pallas_call(
        prepare_kernel,
        out_shape=[
            jax.ShapeDtypeStruct((2, lines, LANES), bf16),
            jax.ShapeDtypeStruct((2, HALO_LINES, LANES), bf16),
            jax.ShapeDtypeStruct((2, HALO_LINES, columns), bf16),
            jax.ShapeDtypeStruct((2, 2 * HALO_LINES, lines + HALO_LINES), bf16),
            jax.ShapeDtypeStruct((2 * LANES, 2 * LANES), bf16),
            jax.ShapeDtypeStruct((2, lines, columns + 3 * LANES), bf16),
        ],
        in_specs=[hbm] * 3,
        out_specs=[vmem] * 6,
        scratch_shapes=[
            pltpu.SMEM(offsets.shape, jnp.int32),
            pltpu.SMEM(kernel_index.shape, jnp.int32),
            pltpu.SemaphoreType.DMA((5 + 4 * (lines // HALO_LINES),)),
        ],
        compiler_params=limit,
    )(offsets, kernel_index, cells)
    swap = [(0, 1), (1, 0)]
    side = lax.ppermute(side, "rng", swap)
    corner = lax.ppermute(corner, ("rng", "az"), [(0, 3), (1, 2), (2, 1), (3, 0)])
    halo_lines = lax.ppermute(halo_lines, "az", swap)

    early_rows = (tiles - 1) * lines
    early = pl.pallas_call(
        functools.partial(early_kernel, tiles),
        out_shape=jax.ShapeDtypeStruct((early_rows, LANES), bf16),
        in_specs=[vmem] * 3,
        out_specs=vmem,
        compiler_params=limit,
        cost_estimate=pl.CostEstimate(flops=2_500_000_000, bytes_accessed=0, transcendentals=0),
    )(held, line_taps, column_taps)
    early = lax.ppermute(early, "date", [(i, i ^ reach(dates - 1, dates)) for i in range(dates)])
    out_rows = [chunk_rows + FOLD] * (dates - 1) + [chunk_rows + FOLD - early_rows]
    sent = pl.pallas_call(
        resample_kernel,
        out_shape=[jax.ShapeDtypeStruct((rows, LANES), bf16) for rows in out_rows],
        in_specs=[vmem] * 6,
        out_specs=[vmem] * dates,
        scratch_shapes=[
            pltpu.VMEM(((columns // LANES + 1) * 2 * lines, LANES), bf16),
            pltpu.VMEM((dates, FOLD, LANES), bf16),
        ],
        compiler_params=limit,
    )(side, corner, halo_lines, held, line_taps, column_taps)

    def exchanged(values, order):
        arrived = {0: values[0]}
        for step in order:
            arrived[step] = lax.ppermute(values[step], "date", [(i, i ^ reach(step, dates)) for i in range(dates)])
        return [arrived[step] for step in reversed(range(dates))]

    steps = range(dates - 1, 0, -1)

    chunks = exchanged(sent, steps)
    pairs = [(first, second) for first in range(dates) for second in range(first + 1, dates)]
    weights, early = pl.pallas_call(
        functools.partial(filter_kernel, pairs),
        out_shape=[
            jax.ShapeDtypeStruct((len(pairs), 2 * LANES, 4 * LANES), bf16),
            jax.ShapeDtypeStruct((chunk_rows, LANES), bf16),
        ],
        in_specs=[hbm, vmem],
        out_specs=[vmem] * 2,
        scratch_shapes=[pltpu.SMEM(range_shift.shape, jnp.float32), pltpu.SemaphoreType.DMA],
        compiler_params=limit,
        cost_estimate=pl.CostEstimate(flops=600_000_000, bytes_accessed=0, transcendentals=0),
    )(range_shift, early)
    looked = pl.pallas_call(
        functools.partial(looks_kernel, pairs, dates),
        out_shape=[jax.ShapeDtypeStruct((groups, out_width), jnp.float32)] * dates,
        in_specs=[vmem] * (2 + dates),
        out_specs=[vmem] * dates,
        scratch_shapes=[
            pltpu.VMEM((chunk_rows + FOLD, LANES), bf16),
            pltpu.VMEM((dates, chunk_rows, 2 * LANES), bf16),
            pltpu.VMEM((len(pairs) * 2 * groups, chunk), jnp.float32),
        ],
        compiler_params=limit,
    )(weights, early, *chunks)
    returned = exchanged(looked, steps)[::-1]
    returned = [returned[reach(distance, dates)] for distance in reversed(range(dates))]
    out = pl.pallas_call(
        functools.partial(place_kernel, min(LAGS, dates - 1), looks),
        out_shape=jax.ShapeDtypeStruct((2, LAGS, groups, looks * dates), jnp.float32),
        in_specs=[vmem] * dates,
        out_specs=vmem,
        compiler_params=limit,
    )(*returned)
    return out[:, None]


def body(slc, offsets, kernel_index, range_shift):
    dates, az_count = (lax.axis_size(a) for a in ("date", "az"))
    lines, columns = slc.shape[2], slc.shape[3]
    whole_tiles = columns % (dates * LANES) == 0 and columns % (dates * LOOK_RG) == 0
    one_row = columns // LOOK_RG == LANES and range_shift.shape[0] == dates
    few = dates & (dates - 1) == 0 and dates - 1 <= LAGS
    folds = lines == 2 * HALO_LINES and lax.axis_size("rng") == 2 and dates >= 4 and 2 * lines // FOLD * TAIL <= LANES
    if az_count == 2 and whole_tiles and one_row and few and folds:
        return tiled_body(slc, offsets, kernel_index, range_shift)
    return chunked_body(slc, offsets, kernel_index, range_shift)


def solution(mesh):
    return jax.shard_map(
        body,
        mesh=mesh,
        in_specs=(
            P(None, ("groups", "date"), "az", "rng"),
            P(("groups", "date"), None),
            P(("groups", "date"), None),
            P("groups"),
        ),
        out_specs=P(None, ("groups", "date"), None, "az", "rng"),
        check_vma=False,
    )
```

```python
import functools

import jax
import jax.numpy as jnp
import numpy as np
from jax import lax
from jax.experimental import pallas as pl
from jax.experimental.pallas import tpu as pltpu
from jax.sharding import PartitionSpec as P

LAGS = 8
KERNELS = 16
TAPS = 8
FILTER_HALF = 8
FILTER_TAPS = 2 * FILTER_HALF + 1
LOOK_AZ = 4
LOOK_RG = 20
LANES = 128
META = 3
UNROLLED_PAIRS = 12


def up(value, unit):
    return -(-value // unit) * unit


def kernel_table():
    position = np.arange(TAPS) - 3.0 - np.arange(KERNELS)[:, None] / KERNELS
    shaped = np.sinc(position) * (0.5 + 0.5 * np.cos(np.pi * position / 5.0))
    table = np.zeros((KERNELS, LANES), np.float32)
    table[:, :TAPS] = shaped / shaped.sum(1, keepdims=True)
    return table


def lowpass_row(width):
    t = np.arange(FILTER_TAPS) - FILTER_HALF
    row = np.zeros((1, width), np.float32)
    row[0, :FILTER_TAPS] = 0.4 * np.sinc(0.4 * t) * (0.54 + 0.46 * np.cos(np.pi * t / (FILTER_HALF + 1)))
    return row


def halves(value):
    high = value.astype(jnp.bfloat16)
    return high, (value - high.astype(jnp.float32)).astype(jnp.bfloat16)


def dot(a, b):
    return jnp.dot(a, b, preferred_element_type=jnp.float32)


def dot_nt(a, b):
    return lax.dot_general(a, b, (((1,), (1,)), ((), ())), preferred_element_type=jnp.float32)


def pack_kernel(chunk, place_ref, offsets_ref, index_ref, slc_ref, before_ref, after_ref, out_ref, wide_ref):
    columns = slc_ref.shape[1]
    wide = out_ref.shape[2]
    first = place_ref[0] == 0
    last = place_ref[0] == place_ref[1] - 1
    zero = jnp.zeros_like(before_ref[...])
    wide_ref[:, :LANES] = jnp.where(first, zero, before_ref[...])
    wide_ref[:, LANES : LANES + columns] = slc_ref[...]
    wide_ref[:, LANES + columns :] = jnp.where(last, zero, after_ref[...])
    lane = lax.broadcasted_iota(jnp.int32, (slc_ref.shape[0], wide), 1)
    numbers = [offsets_ref[0, 0], index_ref[0, 0], index_ref[0, 1]]
    for j in range(out_ref.shape[0]):
        start = LANES + chunk * j - FILTER_HALF - 3 + offsets_ref[0, 1]
        tile = lax.shift_right_logical(start, 7)
        within = lax.bitwise_and(start, LANES - 1)
        window = wide_ref[:, pl.ds(pl.multiple_of(tile * LANES, LANES), wide + LANES)].astype(jnp.float32)
        moved = pltpu.roll(window, wide + LANES - within, 1)[:, :wide]
        for slot, number in enumerate(numbers):
            moved = jnp.where(lane == wide - META + slot, number.astype(jnp.float32), moved)
        out_ref[j] = moved.astype(jnp.bfloat16)


def picked_taps(table, index):
    row = lax.broadcasted_iota(jnp.int32, table.shape, 0).astype(jnp.float32)
    return jnp.sum(jnp.where(row == index, table, 0.0), axis=0, keepdims=True)


def banded(taps, distance):
    out = jnp.zeros(distance.shape, jnp.float32)
    for q in range(TAPS):
        out = jnp.where(distance == q, taps[:, q : q + 1], out)
    return out


def pairs_kernel(chunk, pairs, *refs):
    if isinstance(pairs, int):
        table_of_pairs, refs = refs[0], refs[1:]
    shift_ref, table_ref, lowpass_ref, recv_ref, out_ref, resampled_ref, weight_ref, product_ref = refs
    sources, rows, wide = recv_ref.shape
    dates = shift_ref.shape[0]
    az_count = sources // dates
    own_lines = rows // 2
    lines = own_lines * az_count
    groups = lines // LOOK_AZ
    looks = chunk // LOOK_RG
    table = table_ref[...]
    held = resampled_ref.shape[2]

    out_row = lax.broadcasted_iota(jnp.int32, (lines, lines), 0)
    in_row = lax.broadcasted_iota(jnp.int32, (lines, lines), 1)
    line = LOOK_AZ * (out_row % groups) + out_row // groups
    line_distance = (in_row - line + 3).astype(jnp.float32)
    span = min(2 * LANES, wide)
    column_distance = (
        lax.broadcasted_iota(jnp.int32, (span, LANES), 0) - lax.broadcasted_iota(jnp.int32, (span, LANES), 1)
    ).astype(jnp.float32)
    for date in range(dates):
        numbers = recv_ref[date * az_count, 0:16, wide - LANES :].astype(jnp.float32)[0:1, LANES - META :]
        line_offset, line_index, column_index = (numbers[:, s : s + 1] for s in range(META))
        line_taps = banded(picked_taps(table, line_index), line_distance - line_offset)
        line_taps = jnp.concatenate(halves(line_taps), axis=0)
        column_high, column_low = halves(banded(picked_taps(table, column_index), column_distance))
        moved = []
        for plane in range(2):
            rows_of = slice(plane * own_lines, (plane + 1) * own_lines)
            source = jnp.concatenate([recv_ref[date * az_count + a, rows_of, :] for a in range(az_count)], axis=0)
            both = dot(line_taps, source)
            moved.append(both[:lines] + both[lines:])
        moved_high, moved_low = halves(jnp.concatenate(moved, axis=0))
        for begin in range(0, held, LANES):
            end = min(begin + span, wide)
            taken = end - begin
            total = dot(moved_high[:, begin:end], column_high[:taken])
            total += dot(moved_low[:, begin:end], column_high[:taken])
            total += dot(moved_high[:, begin:end], column_low[:taken])
            resampled_ref[date, :, begin : begin + LANES] = total.astype(jnp.bfloat16)

    window = lowpass_ref[...]
    spacing = lax.broadcasted_iota(jnp.int32, window.shape, 1).astype(jnp.float32) - FILTER_HALF
    span = min(2 * LANES, held)

    def one_pair(place, own, other):
        gap = shift_ref[own] - shift_ref[other]
        angle = jnp.where(jnp.abs(spacing) <= FILTER_HALF, jnp.pi * gap * spacing, 0.0)
        for part, taps in enumerate((window * jnp.cos(angle), window * jnp.sin(angle))):
            spread = jnp.broadcast_to(taps, (LANES, 2 * LANES))
            spread = pltpu.roll(spread, 0, 1, stride=1, stride_axis=0)
            high, low = halves(spread)
            weight_ref[0, part * LANES : (part + 1) * LANES, :] = high
            weight_ref[1, part * LANES : (part + 1) * LANES, :] = low
        both = jnp.concatenate([resampled_ref[own], resampled_ref[other]], axis=0)
        for begin in range(0, up(chunk, LANES), LANES):
            end = min(begin + span, held)
            taken = end - begin
            total = dot_nt(both[:, begin:end], weight_ref[0, :, :taken])
            total += dot_nt(both[:, begin:end], weight_ref[1, :, :taken])
            cos, sin = total[:, :LANES], total[:, LANES:]
            re, im = slice(0, lines), slice(lines, 2 * lines)
            master_re = cos[re] + sin[im]
            master_im = cos[im] - sin[re]
            re, im = slice(2 * lines, 3 * lines), slice(3 * lines, 4 * lines)
            partner_re = cos[re] - sin[im]
            partner_im = cos[im] + sin[re]
            for part, product in enumerate(
                (
                    master_re * partner_re + master_im * partner_im,
                    master_im * partner_re - master_re * partner_im,
                )
            ):
                summed = sum(product[k * groups : (k + 1) * groups] for k in range(LOOK_AZ))
                product_ref[place, part, :, begin : begin + LANES] = summed

    if isinstance(pairs, int):
        count = pairs

        def step(place, carry):
            one_pair(place, table_of_pairs[place, 0], table_of_pairs[place, 1])
            return carry

        lax.fori_loop(0, count, step, 0)
    else:
        count = len(pairs)
        for place, (own, other) in enumerate(pairs):
            one_pair(place, own, other)

    out_width = out_ref.shape[2]
    column = lax.broadcasted_iota(jnp.int32, (product_ref.shape[3], out_width), 0)
    lane = lax.broadcasted_iota(jnp.int32, (product_ref.shape[3], out_width), 1)
    collect = jnp.where(column // LOOK_RG == lane % looks, 1.0, 0.0).astype(jnp.bfloat16)
    high, low = halves(product_ref[...].reshape(count * 2 * groups, product_ref.shape[3]))
    total = (dot(high, collect) + dot(low, collect)) * (1.0 / (LOOK_AZ * LOOK_RG))
    total = total.reshape(count, 2, groups, out_width)
    own_lane = lax.broadcasted_iota(jnp.int32, (groups, out_width), 1) // looks
    place = 0
    for own in range(dates):
        value = jnp.zeros((groups, out_width), jnp.float32)
        for lag in range(min(LAGS, dates - 1 - own)):
            for part in range(2):
                value = jnp.where(own_lane == lag * 2 + part, total[place, part], value)
            place += 1
        out_ref[own * az_count : (own + 1) * az_count] = value.reshape(az_count, groups // az_count, out_width)


def unpack_kernel(used_lags, looks, recv_ref, out_ref):
    sources, groups, width = recv_ref.shape
    columns = out_ref.shape[-1]
    lane = lax.broadcasted_iota(jnp.int32, (groups, columns), 1) // looks
    out_ref[...] = jnp.zeros_like(out_ref)
    for lag in range(used_lags):
        for part in range(2):
            value = jnp.zeros((groups, columns), jnp.float32)
            for source in range(sources):
                block = recv_ref[source]
                if width != columns:
                    block = block[:, :columns]
                shift = looks * (source - lag * 2 - part) % columns
                if shift:
                    block = pltpu.roll(block, shift, 1)
                value = jnp.where(lane == source, block, value)
            out_ref[part, lag] = value


def chunked_body(slc, offsets, kernel_index, range_shift):
    axes = ("date", "az")
    date_count, az_count, rng_count = (lax.axis_size(a) for a in ("date", "az", "rng"))
    peers = date_count * az_count
    lines, columns = slc.shape[2], slc.shape[3]
    dates = range_shift.shape[0]
    chunk = columns // peers
    looks = chunk // LOOK_RG
    groups = lines * az_count // LOOK_AZ
    wide = up(chunk + 2 * FILTER_HALF + TAPS - 1 + META, LANES)
    held = up(chunk + 2 * FILTER_HALF, LANES)
    used_lags = min(LAGS, dates - 1)
    out_width = up(used_lags * 2 * looks, LANES)
    vmem = pl.BlockSpec(memory_space=pltpu.VMEM)
    smem = pl.BlockSpec(memory_space=pltpu.SMEM)
    limit = pltpu.CompilerParams(vmem_limit_bytes=32 * 1024 * 1024)

    cells = slc.reshape(2 * lines, columns)
    place = lax.axis_index("rng")
    if rng_count == 2:
        edge = jnp.where(place == 0, cells[:, columns - LANES :], cells[:, :LANES])
        before = after = lax.ppermute(edge, "rng", [(0, 1), (1, 0)])
    else:
        forth = [(i, i + 1) for i in range(rng_count - 1)]
        before = lax.ppermute(cells[:, columns - LANES :], "rng", forth)
        after = lax.ppermute(cells[:, :LANES], "rng", [(b, a) for a, b in forth])

    packed = pl.pallas_call(
        functools.partial(pack_kernel, chunk),
        out_shape=jax.ShapeDtypeStruct((peers, 2 * lines, wide), jnp.bfloat16),
        in_specs=[smem] * 3 + [vmem] * 3,
        out_specs=vmem,
        scratch_shapes=[pltpu.VMEM((2 * lines, columns + 2 * LANES), jnp.bfloat16)],
        compiler_params=limit,
    )(jnp.stack([place, rng_count]).astype(jnp.int32), offsets, kernel_index, cells, before, after)
    arrived = lax.all_to_all(packed, axes, 0, 0, tiled=True)

    pairs = [(own, own + lag) for own in range(dates) for lag in range(1, LAGS + 1) if own + lag < dates]
    count = len(pairs)
    first = [jnp.asarray(np.array(pairs, np.int32))] if count > UNROLLED_PAIRS else []
    looked = pl.pallas_call(
        functools.partial(pairs_kernel, chunk, count if first else pairs),
        out_shape=jax.ShapeDtypeStruct((peers, groups // az_count, out_width), jnp.float32),
        in_specs=[smem] * len(first) + [smem] + [vmem] * 3,
        out_specs=vmem,
        scratch_shapes=[
            pltpu.VMEM((dates, 4 * (groups * LOOK_AZ) // 2, held), jnp.bfloat16),
            pltpu.VMEM((2, 2 * LANES, 2 * LANES), jnp.bfloat16),
            pltpu.VMEM((count, 2, groups, up(chunk, LANES)), jnp.float32),
        ],
        compiler_params=limit,
    )(*first, range_shift, jnp.asarray(kernel_table()), jnp.asarray(lowpass_row(2 * LANES)), arrived)
    returned = lax.all_to_all(looked, axes, 0, 0, tiled=True)

    out = pl.pallas_call(
        functools.partial(unpack_kernel, used_lags, looks),
        out_shape=jax.ShapeDtypeStruct((2, LAGS, groups // az_count, looks * peers), jnp.float32),
        in_specs=[vmem],
        out_specs=vmem,
        compiler_params=limit,
    )(returned)
    return out[:, None]


HALO_LINES = 16
FOLD = 16
TAIL = 2 * FILTER_HALF


def reach(step, dates):
    return {dates - 1: dates // 2, dates // 2: dates - 1}.get(step, step)


def sinc(value):
    angle = jnp.pi * value
    return jnp.where(angle == 0.0, 1.0, jnp.sin(angle) / jnp.where(angle == 0.0, 1.0, angle))


def tap_row(index):
    lane = lax.broadcasted_iota(jnp.int32, (1, LANES), 1)
    position = lane.astype(jnp.float32) - 3.0 - index.astype(jnp.float32) / KERNELS
    shaped = sinc(position) * (0.5 + 0.5 * jnp.cos(jnp.pi * position / 5.0))
    shaped = jnp.where(lane < TAPS, shaped, 0.0)
    return shaped / jnp.sum(shaped, axis=1, keepdims=True)


def row_line(row, az):
    quarter = HALO_LINES // LOOK_AZ
    within = row % HALO_LINES
    return HALO_LINES * ((row // HALO_LINES) ^ az) + LOOK_AZ * (within % quarter) + within // quarter


def prepare_kernel(offsets_hbm, index_hbm, slc_ref, side_ref, corner_ref, lines_ref, line_ref, column_ref, held_ref, offsets_ref, index_ref, semaphores):
    lines, columns = slc_ref.shape[1:]
    az = lax.axis_index("az")
    row = pl.multiple_of((1 - az) * (lines - HALO_LINES), HALO_LINES)
    edge = pl.multiple_of((1 - lax.axis_index("rng")) * (columns - LANES), LANES)
    nearest, outermost = pl.ds(row, HALO_LINES), pl.ds(edge, LANES)
    moves = [
        (offsets_hbm, offsets_ref),
        (index_hbm, index_ref),
        (slc_ref.at[:, :, outermost], side_ref),
        (slc_ref.at[:, nearest, outermost], corner_ref),
        (slc_ref.at[:, nearest, :], lines_ref),
    ]
    for plane in range(2):
        for part in range(lines // HALO_LINES):
            for side in range(2):
                at = pl.ds(part * HALO_LINES, HALO_LINES)
                source = slc_ref.at[plane, at, pl.ds(side * columns // 2, columns // 2)]
                moves.append((source, held_ref.at[plane, at, pl.ds(LANES + side * columns // 2, columns // 2)]))
    copies = [pltpu.make_async_copy(a, b, semaphores.at[i]) for i, (a, b) in enumerate(moves)]
    for copy in copies:
        copy.start()
    held_ref[:, :, :LANES] = jnp.zeros((2, lines, LANES), held_ref.dtype)
    held_ref[:, :, LANES + columns :] = jnp.zeros((2, lines, 2 * LANES), held_ref.dtype)
    copies[0].wait()
    copies[1].wait()
    for half in range(2):
        shape = (HALO_LINES, lines + HALO_LINES)
        line = row_line(lax.broadcasted_iota(jnp.int32, shape, 0) + half * HALO_LINES, az)
        place = lax.broadcasted_iota(jnp.int32, shape, 1)
        source = jnp.where(place < lines, place, place + jnp.where(az == 0, 0, -lines - HALO_LINES))
        taps = banded(tap_row(index_ref[0, 0]), source - line - offsets_ref[0, 0] + 3)
        line_ref[half] = jnp.concatenate(halves(taps), axis=0)
    shape = (2 * LANES, LANES)
    distance = lax.broadcasted_iota(jnp.int32, shape, 0) - lax.broadcasted_iota(jnp.int32, shape, 1)
    distance = distance - (LANES // 2 - FILTER_HALF - 3) - offsets_ref[0, 1]
    taps = banded(tap_row(index_ref[0, 1]), distance)
    column_ref[...] = jnp.concatenate(halves(taps), axis=1)
    for copy in copies[2:]:
        copy.wait()


def along_range(moved, column_ref, tiles):
    high, low = halves(pltpu.roll(moved, moved.shape[1] - LANES // 2, 1))
    starts = range(0, tiles * LANES, LANES)
    high = jnp.concatenate([high[:, s : s + 2 * LANES] for s in starts], axis=0)
    low = jnp.concatenate([low[:, s : s + 2 * LANES] for s in starts], axis=0)
    total = dot(high, column_ref[...])
    return total[:, :LANES] + total[:, LANES:] + dot(low, column_ref[:, :LANES])


def early_kernel(tiles, held_ref, line_ref, column_ref, out_ref):
    lines = held_ref.shape[1]
    early = out_ref.shape[0] // (2 * HALO_LINES)
    dates = lax.axis_size("date")
    chunk = lax.axis_index("date") ^ reach(dates - 1, dates)
    begin = pl.multiple_of((chunk * tiles + lax.axis_index("rng")) * LANES, LANES)
    moved = []
    for plane in range(2):
        both = dot(line_ref[0, :, :lines], held_ref[plane, :, pl.ds(begin, (early + 2) * LANES)])
        moved.append(both[:HALO_LINES] + both[HALO_LINES:])
    moved = jnp.concatenate(moved, axis=0)
    out_ref[...] = along_range(moved, column_ref, early).astype(jnp.bfloat16)


def whole_lines(taps, sources):
    moved = [[], []]
    for source in sources:
        both = dot(taps, source)
        for half in range(2):
            at = 2 * half * HALO_LINES
            moved[half].append(both[at : at + HALO_LINES] + both[at + HALO_LINES : at + 2 * HALO_LINES])
    return jnp.concatenate(moved[0] + moved[1], axis=0)


def folded_tail(tile):
    lane = lax.broadcasted_iota(jnp.int32, (FOLD, LANES), 1) // TAIL
    folded = tile[:FOLD]
    for part in range(1, tile.shape[0] // FOLD):
        folded = jnp.where(lane == part, pltpu.roll(tile[part * FOLD : (part + 1) * FOLD], part * TAIL, 1), folded)
    return folded.astype(jnp.bfloat16)


def first_kernel(tiles, step, side_ref, corner_ref, lines_ref, held_ref, line_ref, column_ref, out_ref, wide_ref):
    lines, width = held_ref.shape[1:]
    block = lax.axis_index("rng")
    zero = jnp.zeros((lines, LANES), wide_ref.dtype)
    for plane in range(2):
        side, corner = side_ref[plane], corner_ref[plane]
        right = width - 2 * LANES
        wide_ref[plane, :lines, :LANES] = jnp.where(block > 0, side, zero)
        wide_ref[plane, :lines, LANES:right] = held_ref[plane, :, LANES:right]
        wide_ref[plane, :lines, right : right + LANES] = jnp.where(block == 0, side, zero)
        wide_ref[plane, :lines, right + LANES :] = zero
        wide_ref[plane, lines:, :LANES] = jnp.where(block > 0, corner, zero[:HALO_LINES])
        wide_ref[plane, lines:, LANES:right] = lines_ref[plane]
        wide_ref[plane, lines:, right : right + LANES] = jnp.where(block == 0, corner, zero[:HALO_LINES])
        wide_ref[plane, lines:, right + LANES :] = zero[:HALO_LINES]
    taps = jnp.concatenate([line_ref[0], line_ref[1]], axis=0)
    chunk = lax.axis_index("date") ^ reach(step, lax.axis_size("date"))
    read = pl.ds(pl.multiple_of(chunk * tiles * LANES, LANES), (tiles + 3) * LANES)
    moved = whole_lines(taps, [wide_ref[plane, :, read] for plane in range(2)])
    total = along_range(moved, column_ref, tiles + 1)
    rows = tiles * 2 * lines
    out_ref[:rows] = total[:rows].astype(jnp.bfloat16)
    out_ref[rows : rows + FOLD] = folded_tail(total[rows:])
    out_ref[rows + FOLD :] = jnp.zeros((out_ref.shape[0] - rows - FOLD, LANES), out_ref.dtype)


def rest_kernel(tiles, steps, wide_ref, line_ref, column_ref, *outs):
    lines = wide_ref.shape[1] - HALO_LINES
    block = lax.axis_index("rng")
    date = lax.axis_index("date")
    taps = jnp.concatenate([line_ref[0], line_ref[1]], axis=0)
    rows = 2 * lines
    for step, out_ref in zip(steps, outs):
        chunk = date ^ reach(step, lax.axis_size("date"))
        read = pl.ds(pl.multiple_of(chunk * tiles * LANES, LANES), (tiles + 3) * LANES)
        moved = whole_lines(taps, [wide_ref[plane, :, read] for plane in range(2)])
        total = along_range(moved, column_ref, tiles + 1)
        tail = folded_tail(total[tiles * rows :])
        total = total.astype(jnp.bfloat16)
        if out_ref.shape[0] == tiles * rows + FOLD:
            out_ref[: tiles * rows] = total[: tiles * rows]
            out_ref[tiles * rows :] = tail
            continue
        for tile in range(tiles - 1):
            near, far = (total[at * rows + lines : (at + 1) * rows] for at in (tile, tile + 1))
            out_ref[tile * lines : (tile + 1) * lines] = jnp.where(block == 0, near, far)
        begin = (tiles - 1) * rows
        out_ref[begin // 2 : begin // 2 + rows] = jnp.where(block == 0, total[begin : begin + rows], total[:rows])
        out_ref[begin // 2 + rows :] = tail


def filter_kernel(pairs, shift_hbm, early_ref, out_ref, spread_ref, shift_ref, semaphore):
    copy = pltpu.make_async_copy(shift_hbm, shift_ref, semaphore)
    copy.start()
    lines = 2 * HALO_LINES
    spread_ref[...] = jnp.zeros_like(spread_ref)
    for tile in range(early_ref.shape[0] // lines):
        begin = pl.multiple_of((tile + lax.axis_index("rng")) * 2 * lines, FOLD)
        spread_ref[pl.ds(begin, lines), :] = early_ref[tile * lines : (tile + 1) * lines]
    date = lax.axis_index("date")
    spacing = lax.broadcasted_iota(jnp.int32, (1, 2 * LANES), 1).astype(jnp.float32) - FILTER_HALF
    window = 0.4 * sinc(0.4 * spacing) * (0.54 + 0.46 * jnp.cos(jnp.pi * spacing / (FILTER_HALF + 1)))
    window = jnp.where(jnp.abs(spacing) <= FILTER_HALF, window, 0.0)
    copy.wait()
    for place, (first, second) in enumerate(pairs):
        dates = shift_ref.shape[0]
        gap = shift_ref[date ^ reach(first, dates)] - shift_ref[date ^ reach(second, dates)]
        angle = jnp.where(jnp.abs(spacing) <= FILTER_HALF, jnp.pi * gap * spacing, 0.0)
        for part, taps in enumerate((window * jnp.cos(angle), window * jnp.sin(angle))):
            spread = jnp.broadcast_to(taps, (LANES, 2 * LANES))
            spread = pltpu.roll(spread, 0, 1, stride=1, stride_axis=0)
            high, low = halves(spread)
            out_ref[place, part * LANES : (part + 1) * LANES, : 2 * LANES] = high
            out_ref[place, part * LANES : (part + 1) * LANES, 2 * LANES :] = low


def looks_kernel(pairs, dates, weight_ref, *refs):
    early_ref, chunks, outs = refs[0], list(refs[1 : dates + 1][::-1]), refs[dates + 1 : 2 * dates + 1]
    whole_ref, window_ref, product_ref = refs[-3:]
    groups, lines = outs[0].shape[0], outs[0].shape[0] * LOOK_AZ
    rows = 2 * lines
    blocks = (chunks[0].shape[0] - FOLD) // rows
    looks = blocks * LANES // LOOK_RG
    date = lax.axis_index("date")
    block = lax.axis_index("rng")
    early = blocks - 1
    whole_ref[: blocks * rows] = early_ref[...]
    for tile in range(early):
        begin = pl.multiple_of((tile + block) * rows, FOLD)
        whole_ref[pl.ds(begin + lines, lines), :] = chunks[-1][tile * lines : (tile + 1) * lines]
    begin = pl.multiple_of((1 - block) * early * rows, FOLD)
    whole_ref[pl.ds(begin, rows), :] = chunks[-1][early * lines : early * lines + rows]
    whole_ref[blocks * rows :] = chunks[-1][early * lines + rows :]
    chunks[-1] = whole_ref
    az = lax.axis_index("az")
    upper = lax.broadcasted_iota(jnp.int32, (groups, LANES), 0) // (groups // 2) == az
    for step, chunk_ref in enumerate(chunks):
        window_ref[step, :, :LANES] = chunk_ref[: blocks * rows]
        window_ref[step, : (blocks - 1) * rows, LANES:] = chunk_ref[rows : blocks * rows]
        folded = chunk_ref[blocks * rows : blocks * rows + FOLD].astype(jnp.float32)
        for part in range(rows // FOLD):
            value = pltpu.roll(folded, LANES - part * TAIL, 1) if part else folded
            at = pl.ds((blocks - 1) * rows + part * FOLD, FOLD)
            window_ref[step, at, LANES:] = value.astype(jnp.bfloat16)
    for place, (first, second) in enumerate(pairs):
        def filtered(step):
            window = window_ref[step]
            total = dot_nt(jnp.concatenate([window, window], axis=1), weight_ref[place])
            total = total.reshape(blocks, 2, 2, HALO_LINES, 2 * LANES)
            re, im = total[:, :, 0], total[:, :, 1]
            return re[..., :LANES], im[..., :LANES], re[..., LANES:], im[..., LANES:]

        cos_re, cos_im, sin_re, sin_im = filtered(first)
        master_re, master_im = cos_re + sin_im, cos_im - sin_re
        cos_re, cos_im, sin_re, sin_im = filtered(second)
        partner_re, partner_im = cos_re - sin_im, cos_im + sin_re
        for part, product in enumerate(
            (
                master_re * partner_re + master_im * partner_im,
                master_im * partner_re - master_re * partner_im,
            )
        ):
            summed = product[:, :, :groups] + product[:, :, groups:]
            at = pl.ds((place * 2 + part) * groups, groups)
            for k in range(blocks):
                both = [summed[k, half] + pltpu.roll(summed[k, half], groups // 2, 0) for half in range(2)]
                product_ref[at, k * LANES : (k + 1) * LANES] = jnp.where(upper, both[0], both[1])

    out_width = outs[0].shape[1]
    column = lax.broadcasted_iota(jnp.int32, (product_ref.shape[1], out_width), 0)
    lane = lax.broadcasted_iota(jnp.int32, (product_ref.shape[1], out_width), 1)
    collect = jnp.where(column // LOOK_RG == lane % looks, 1.0, 0.0).astype(jnp.bfloat16)
    high, low = halves(product_ref[...])
    total = (dot(high, collect) + dot(low, collect)) * (1.0 / (LOOK_AZ * LOOK_RG))
    total = total.reshape(len(pairs), 2, groups, out_width)
    own_lane = lax.broadcasted_iota(jnp.int32, (groups, out_width), 1) // looks
    for step, out_ref in enumerate(outs):
        value = jnp.zeros((groups, out_width), jnp.float32)
        for place, pair in enumerate(pairs):
            if step in pair:
                other = pair[1] if pair[0] == step else pair[0]
                lag = (date ^ reach(other, dates)) - (date ^ reach(step, dates))
                for part in range(2):
                    signed = -total[place, part] if part == 1 and pair[1] == step else total[place, part]
                    value = jnp.where(own_lane == (lag - 1) * 2 + part, signed, value)
        out_ref[...] = value


def place_kernel(used_lags, looks, *refs):
    out_ref = refs[-1]
    groups, columns = out_ref.shape[2:]
    date = lax.axis_index("date")
    lane = lax.broadcasted_iota(jnp.int32, (groups, LANES), 1) // looks
    out_ref[...] = jnp.zeros_like(out_ref)
    each = LANES // looks
    for step, recv_ref in enumerate(refs[:-1][::-1]):
        chunk = date ^ step
        for lag in range(used_lags):
            for part in range(2):
                tile, group = divmod(lag * 2 + part, each)
                block = recv_ref[:, tile * LANES : (tile + 1) * LANES]
                block = pltpu.roll(block, lax.bitwise_and(looks * (chunk - group), LANES - 1), 1)
                out_ref[part, lag] = jnp.where(lane == chunk, block, out_ref[part, lag])


def tiled_body(slc, offsets, kernel_index, range_shift):
    dates = lax.axis_size("date")
    lines, columns = slc.shape[2], slc.shape[3]
    chunk = columns // dates
    looks = chunk // LOOK_RG
    groups = lines // LOOK_AZ
    out_width = up(min(LAGS, dates - 1) * 2 * looks, LANES)
    vmem = pl.BlockSpec(memory_space=pltpu.VMEM)
    hbm = pl.BlockSpec(memory_space=pltpu.HBM)
    limit = pltpu.CompilerParams(vmem_limit_bytes=32 * 1024 * 1024)
    bf16 = jnp.bfloat16
    cells, offsets, kernel_index, range_shift = (
        pltpu.with_memory_space_constraint(value, pltpu.HBM)
        for value in (slc.reshape(2, lines, columns), offsets, kernel_index, range_shift)
    )
    tiles = chunk // LANES
    chunk_rows = tiles * 2 * lines

    side, corner, halo_lines, line_taps, column_taps, held = pl.pallas_call(
        prepare_kernel,
        out_shape=[
            jax.ShapeDtypeStruct((2, lines, LANES), bf16),
            jax.ShapeDtypeStruct((2, HALO_LINES, LANES), bf16),
            jax.ShapeDtypeStruct((2, HALO_LINES, columns), bf16),
            jax.ShapeDtypeStruct((2, 2 * HALO_LINES, lines + HALO_LINES), bf16),
            jax.ShapeDtypeStruct((2 * LANES, 2 * LANES), bf16),
            jax.ShapeDtypeStruct((2, lines, columns + 3 * LANES), bf16),
        ],
        in_specs=[hbm] * 3,
        out_specs=[vmem] * 6,
        scratch_shapes=[
            pltpu.SMEM(offsets.shape, jnp.int32),
            pltpu.SMEM(kernel_index.shape, jnp.int32),
            pltpu.SemaphoreType.DMA((5 + 4 * (lines // HALO_LINES),)),
        ],
        compiler_params=limit,
    )(offsets, kernel_index, cells)
    swap = [(0, 1), (1, 0)]
    side = lax.ppermute(side, "rng", swap)
    corner = lax.ppermute(corner, ("rng", "az"), [(0, 3), (1, 2), (2, 1), (3, 0)])
    halo_lines = lax.ppermute(halo_lines, "az", swap)

    early_rows = (tiles - 1) * lines
    early = pl.pallas_call(
        functools.partial(early_kernel, tiles),
        out_shape=jax.ShapeDtypeStruct((early_rows, LANES), bf16),
        in_specs=[vmem] * 3,
        out_specs=vmem,
        compiler_params=limit,
        cost_estimate=pl.CostEstimate(flops=2_500_000_000, bytes_accessed=0, transcendentals=0),
    )(held, line_taps, column_taps)
    early = lax.ppermute(early, "date", [(i, i ^ reach(dates - 1, dates)) for i in range(dates)])
    def swapped(value, step):
        return lax.ppermute(value, "date", [(i, i ^ reach(step, dates)) for i in range(dates)])

    steps = range(dates - 1, 0, -1)
    first, wide = pl.pallas_call(
        functools.partial(first_kernel, tiles, steps[1]),
        out_shape=[
            jax.ShapeDtypeStruct((chunk_rows + 2 * FOLD, LANES), bf16),
            jax.ShapeDtypeStruct((2, lines + HALO_LINES, columns + 3 * LANES), bf16),
        ],
        in_specs=[vmem] * 6,
        out_specs=[vmem] * 2,
        compiler_params=limit,
    )(side, corner, halo_lines, held, line_taps, column_taps)
    first = swapped(first, steps[1])
    others = [steps[0], *steps[2:], 0]
    rest = pl.pallas_call(
        functools.partial(rest_kernel, tiles, others),
        out_shape=[
            jax.ShapeDtypeStruct((chunk_rows + FOLD - (early_rows if step == steps[0] else 0), LANES), bf16)
            for step in others
        ],
        in_specs=[vmem] * 3,
        out_specs=[vmem] * (dates - 1),
        compiler_params=limit,
        cost_estimate=pl.CostEstimate(flops=250_000_000, bytes_accessed=0, transcendentals=0),
    )(wide, line_taps, column_taps)
    rest = [swapped(rows, step) if step else rows for rows, step in zip(rest, others)]
    chunks = [rest[0], first, *rest[1:]]

    pairs = [(first, second) for first in range(dates) for second in range(first + 1, dates)]
    weights, early = pl.pallas_call(
        functools.partial(filter_kernel, pairs),
        out_shape=[
            jax.ShapeDtypeStruct((len(pairs), 2 * LANES, 4 * LANES), bf16),
            jax.ShapeDtypeStruct((chunk_rows, LANES), bf16),
        ],
        in_specs=[hbm, vmem],
        out_specs=[vmem] * 2,
        scratch_shapes=[pltpu.SMEM(range_shift.shape, jnp.float32), pltpu.SemaphoreType.DMA],
        compiler_params=limit,
        cost_estimate=pl.CostEstimate(flops=800_000_000, bytes_accessed=0, transcendentals=0),
    )(range_shift, early)
    looked = pl.pallas_call(
        functools.partial(looks_kernel, pairs, dates),
        out_shape=[jax.ShapeDtypeStruct((groups, out_width), jnp.float32)] * dates,
        in_specs=[vmem] * (2 + dates),
        out_specs=[vmem] * dates,
        scratch_shapes=[
            pltpu.VMEM((chunk_rows + FOLD, LANES), bf16),
            pltpu.VMEM((dates, chunk_rows, 2 * LANES), bf16),
            pltpu.VMEM((len(pairs) * 2 * groups, chunk), jnp.float32),
        ],
        compiler_params=limit,
    )(weights, early, *chunks)
    returned = [looked[0]] + [swapped(looked[step], step) for step in range(1, dates)]
    returned = [returned[reach(distance, dates)] for distance in reversed(range(dates))]
    out = pl.pallas_call(
        functools.partial(place_kernel, min(LAGS, dates - 1), looks),
        out_shape=jax.ShapeDtypeStruct((2, LAGS, groups, looks * dates), jnp.float32),
        in_specs=[vmem] * dates,
        out_specs=vmem,
        compiler_params=limit,
    )(*returned)
    return out[:, None]


def body(slc, offsets, kernel_index, range_shift):
    dates, az_count = (lax.axis_size(a) for a in ("date", "az"))
    lines, columns = slc.shape[2], slc.shape[3]
    whole_tiles = columns % (dates * LANES) == 0 and columns % (dates * LOOK_RG) == 0
    one_row = columns // LOOK_RG == LANES and range_shift.shape[0] == dates
    few = dates & (dates - 1) == 0 and dates - 1 <= LAGS
    folds = lines == 2 * HALO_LINES and lax.axis_size("rng") == 2 and dates >= 4 and 2 * lines // FOLD * TAIL <= LANES
    if az_count == 2 and whole_tiles and one_row and few and folds:
        return tiled_body(slc, offsets, kernel_index, range_shift)
    return chunked_body(slc, offsets, kernel_index, range_shift)


def solution(mesh):
    return jax.shard_map(
        body,
        mesh=mesh,
        in_specs=(
            P(None, ("groups", "date"), "az", "rng"),
            P(("groups", "date"), None),
            P(("groups", "date"), None),
            P("groups"),
        ),
        out_specs=P(None, ("groups", "date"), None, "az", "rng"),
        check_vma=False,
    )
```

```python
import functools

import jax
import jax.numpy as jnp
import numpy as np
from jax import lax
from jax.experimental import pallas as pl
from jax.experimental.pallas import tpu as pltpu
from jax.sharding import PartitionSpec as P

LAGS = 8
KERNELS = 16
TAPS = 8
FILTER_HALF = 8
FILTER_TAPS = 2 * FILTER_HALF + 1
LOOK_AZ = 4
LOOK_RG = 20
LANES = 128
META = 3
UNROLLED_PAIRS = 12


def up(value, unit):
    return -(-value // unit) * unit


def kernel_table():
    position = np.arange(TAPS) - 3.0 - np.arange(KERNELS)[:, None] / KERNELS
    shaped = np.sinc(position) * (0.5 + 0.5 * np.cos(np.pi * position / 5.0))
    table = np.zeros((KERNELS, LANES), np.float32)
    table[:, :TAPS] = shaped / shaped.sum(1, keepdims=True)
    return table


def lowpass_row(width):
    t = np.arange(FILTER_TAPS) - FILTER_HALF
    row = np.zeros((1, width), np.float32)
    row[0, :FILTER_TAPS] = 0.4 * np.sinc(0.4 * t) * (0.54 + 0.46 * np.cos(np.pi * t / (FILTER_HALF + 1)))
    return row


def halves(value):
    high = value.astype(jnp.bfloat16)
    return high, (value - high.astype(jnp.float32)).astype(jnp.bfloat16)


def dot(a, b):
    return jnp.dot(a, b, preferred_element_type=jnp.float32)


def dot_nt(a, b):
    return lax.dot_general(a, b, (((1,), (1,)), ((), ())), preferred_element_type=jnp.float32)


def pack_kernel(chunk, place_ref, offsets_ref, index_ref, slc_ref, before_ref, after_ref, out_ref, wide_ref):
    columns = slc_ref.shape[1]
    wide = out_ref.shape[2]
    first = place_ref[0] == 0
    last = place_ref[0] == place_ref[1] - 1
    zero = jnp.zeros_like(before_ref[...])
    wide_ref[:, :LANES] = jnp.where(first, zero, before_ref[...])
    wide_ref[:, LANES : LANES + columns] = slc_ref[...]
    wide_ref[:, LANES + columns :] = jnp.where(last, zero, after_ref[...])
    lane = lax.broadcasted_iota(jnp.int32, (slc_ref.shape[0], wide), 1)
    numbers = [offsets_ref[0, 0], index_ref[0, 0], index_ref[0, 1]]
    for j in range(out_ref.shape[0]):
        start = LANES + chunk * j - FILTER_HALF - 3 + offsets_ref[0, 1]
        tile = lax.shift_right_logical(start, 7)
        within = lax.bitwise_and(start, LANES - 1)
        window = wide_ref[:, pl.ds(pl.multiple_of(tile * LANES, LANES), wide + LANES)].astype(jnp.float32)
        moved = pltpu.roll(window, wide + LANES - within, 1)[:, :wide]
        for slot, number in enumerate(numbers):
            moved = jnp.where(lane == wide - META + slot, number.astype(jnp.float32), moved)
        out_ref[j] = moved.astype(jnp.bfloat16)


def picked_taps(table, index):
    row = lax.broadcasted_iota(jnp.int32, table.shape, 0).astype(jnp.float32)
    return jnp.sum(jnp.where(row == index, table, 0.0), axis=0, keepdims=True)


def banded(taps, distance):
    out = jnp.zeros(distance.shape, jnp.float32)
    for q in range(TAPS):
        out = jnp.where(distance == q, taps[:, q : q + 1], out)
    return out


def pairs_kernel(chunk, pairs, *refs):
    if isinstance(pairs, int):
        table_of_pairs, refs = refs[0], refs[1:]
    shift_ref, table_ref, lowpass_ref, recv_ref, out_ref, resampled_ref, weight_ref, product_ref = refs
    sources, rows, wide = recv_ref.shape
    dates = shift_ref.shape[0]
    az_count = sources // dates
    own_lines = rows // 2
    lines = own_lines * az_count
    groups = lines // LOOK_AZ
    looks = chunk // LOOK_RG
    table = table_ref[...]
    held = resampled_ref.shape[2]

    out_row = lax.broadcasted_iota(jnp.int32, (lines, lines), 0)
    in_row = lax.broadcasted_iota(jnp.int32, (lines, lines), 1)
    line = LOOK_AZ * (out_row % groups) + out_row // groups
    line_distance = (in_row - line + 3).astype(jnp.float32)
    span = min(2 * LANES, wide)
    column_distance = (
        lax.broadcasted_iota(jnp.int32, (span, LANES), 0) - lax.broadcasted_iota(jnp.int32, (span, LANES), 1)
    ).astype(jnp.float32)
    for date in range(dates):
        numbers = recv_ref[date * az_count, 0:16, wide - LANES :].astype(jnp.float32)[0:1, LANES - META :]
        line_offset, line_index, column_index = (numbers[:, s : s + 1] for s in range(META))
        line_taps = banded(picked_taps(table, line_index), line_distance - line_offset)
        line_taps = jnp.concatenate(halves(line_taps), axis=0)
        column_high, column_low = halves(banded(picked_taps(table, column_index), column_distance))
        moved = []
        for plane in range(2):
            rows_of = slice(plane * own_lines, (plane + 1) * own_lines)
            source = jnp.concatenate([recv_ref[date * az_count + a, rows_of, :] for a in range(az_count)], axis=0)
            both = dot(line_taps, source)
            moved.append(both[:lines] + both[lines:])
        moved_high, moved_low = halves(jnp.concatenate(moved, axis=0))
        for begin in range(0, held, LANES):
            end = min(begin + span, wide)
            taken = end - begin
            total = dot(moved_high[:, begin:end], column_high[:taken])
            total += dot(moved_low[:, begin:end], column_high[:taken])
            total += dot(moved_high[:, begin:end], column_low[:taken])
            resampled_ref[date, :, begin : begin + LANES] = total.astype(jnp.bfloat16)

    window = lowpass_ref[...]
    spacing = lax.broadcasted_iota(jnp.int32, window.shape, 1).astype(jnp.float32) - FILTER_HALF
    span = min(2 * LANES, held)

    def one_pair(place, own, other):
        gap = shift_ref[own] - shift_ref[other]
        angle = jnp.where(jnp.abs(spacing) <= FILTER_HALF, jnp.pi * gap * spacing, 0.0)
        for part, taps in enumerate((window * jnp.cos(angle), window * jnp.sin(angle))):
            spread = jnp.broadcast_to(taps, (LANES, 2 * LANES))
            spread = pltpu.roll(spread, 0, 1, stride=1, stride_axis=0)
            high, low = halves(spread)
            weight_ref[0, part * LANES : (part + 1) * LANES, :] = high
            weight_ref[1, part * LANES : (part + 1) * LANES, :] = low
        both = jnp.concatenate([resampled_ref[own], resampled_ref[other]], axis=0)
        for begin in range(0, up(chunk, LANES), LANES):
            end = min(begin + span, held)
            taken = end - begin
            total = dot_nt(both[:, begin:end], weight_ref[0, :, :taken])
            total += dot_nt(both[:, begin:end], weight_ref[1, :, :taken])
            cos, sin = total[:, :LANES], total[:, LANES:]
            re, im = slice(0, lines), slice(lines, 2 * lines)
            master_re = cos[re] + sin[im]
            master_im = cos[im] - sin[re]
            re, im = slice(2 * lines, 3 * lines), slice(3 * lines, 4 * lines)
            partner_re = cos[re] - sin[im]
            partner_im = cos[im] + sin[re]
            for part, product in enumerate(
                (
                    master_re * partner_re + master_im * partner_im,
                    master_im * partner_re - master_re * partner_im,
                )
            ):
                summed = sum(product[k * groups : (k + 1) * groups] for k in range(LOOK_AZ))
                product_ref[place, part, :, begin : begin + LANES] = summed

    if isinstance(pairs, int):
        count = pairs

        def step(place, carry):
            one_pair(place, table_of_pairs[place, 0], table_of_pairs[place, 1])
            return carry

        lax.fori_loop(0, count, step, 0)
    else:
        count = len(pairs)
        for place, (own, other) in enumerate(pairs):
            one_pair(place, own, other)

    out_width = out_ref.shape[2]
    column = lax.broadcasted_iota(jnp.int32, (product_ref.shape[3], out_width), 0)
    lane = lax.broadcasted_iota(jnp.int32, (product_ref.shape[3], out_width), 1)
    collect = jnp.where(column // LOOK_RG == lane % looks, 1.0, 0.0).astype(jnp.bfloat16)
    high, low = halves(product_ref[...].reshape(count * 2 * groups, product_ref.shape[3]))
    total = (dot(high, collect) + dot(low, collect)) * (1.0 / (LOOK_AZ * LOOK_RG))
    total = total.reshape(count, 2, groups, out_width)
    own_lane = lax.broadcasted_iota(jnp.int32, (groups, out_width), 1) // looks
    place = 0
    for own in range(dates):
        value = jnp.zeros((groups, out_width), jnp.float32)
        for lag in range(min(LAGS, dates - 1 - own)):
            for part in range(2):
                value = jnp.where(own_lane == lag * 2 + part, total[place, part], value)
            place += 1
        out_ref[own * az_count : (own + 1) * az_count] = value.reshape(az_count, groups // az_count, out_width)


def unpack_kernel(used_lags, looks, recv_ref, out_ref):
    sources, groups, width = recv_ref.shape
    columns = out_ref.shape[-1]
    lane = lax.broadcasted_iota(jnp.int32, (groups, columns), 1) // looks
    out_ref[...] = jnp.zeros_like(out_ref)
    for lag in range(used_lags):
        for part in range(2):
            value = jnp.zeros((groups, columns), jnp.float32)
            for source in range(sources):
                block = recv_ref[source]
                if width != columns:
                    block = block[:, :columns]
                shift = looks * (source - lag * 2 - part) % columns
                if shift:
                    block = pltpu.roll(block, shift, 1)
                value = jnp.where(lane == source, block, value)
            out_ref[part, lag] = value


def chunked_body(slc, offsets, kernel_index, range_shift):
    axes = ("date", "az")
    date_count, az_count, rng_count = (lax.axis_size(a) for a in ("date", "az", "rng"))
    peers = date_count * az_count
    lines, columns = slc.shape[2], slc.shape[3]
    dates = range_shift.shape[0]
    chunk = columns // peers
    looks = chunk // LOOK_RG
    groups = lines * az_count // LOOK_AZ
    wide = up(chunk + 2 * FILTER_HALF + TAPS - 1 + META, LANES)
    held = up(chunk + 2 * FILTER_HALF, LANES)
    used_lags = min(LAGS, dates - 1)
    out_width = up(used_lags * 2 * looks, LANES)
    vmem = pl.BlockSpec(memory_space=pltpu.VMEM)
    smem = pl.BlockSpec(memory_space=pltpu.SMEM)
    limit = pltpu.CompilerParams(vmem_limit_bytes=32 * 1024 * 1024)

    cells = slc.reshape(2 * lines, columns)
    place = lax.axis_index("rng")
    if rng_count == 2:
        edge = jnp.where(place == 0, cells[:, columns - LANES :], cells[:, :LANES])
        before = after = lax.ppermute(edge, "rng", [(0, 1), (1, 0)])
    else:
        forth = [(i, i + 1) for i in range(rng_count - 1)]
        before = lax.ppermute(cells[:, columns - LANES :], "rng", forth)
        after = lax.ppermute(cells[:, :LANES], "rng", [(b, a) for a, b in forth])

    packed = pl.pallas_call(
        functools.partial(pack_kernel, chunk),
        out_shape=jax.ShapeDtypeStruct((peers, 2 * lines, wide), jnp.bfloat16),
        in_specs=[smem] * 3 + [vmem] * 3,
        out_specs=vmem,
        scratch_shapes=[pltpu.VMEM((2 * lines, columns + 2 * LANES), jnp.bfloat16)],
        compiler_params=limit,
    )(jnp.stack([place, rng_count]).astype(jnp.int32), offsets, kernel_index, cells, before, after)
    arrived = lax.all_to_all(packed, axes, 0, 0, tiled=True)

    pairs = [(own, own + lag) for own in range(dates) for lag in range(1, LAGS + 1) if own + lag < dates]
    count = len(pairs)
    first = [jnp.asarray(np.array(pairs, np.int32))] if count > UNROLLED_PAIRS else []
    looked = pl.pallas_call(
        functools.partial(pairs_kernel, chunk, count if first else pairs),
        out_shape=jax.ShapeDtypeStruct((peers, groups // az_count, out_width), jnp.float32),
        in_specs=[smem] * len(first) + [smem] + [vmem] * 3,
        out_specs=vmem,
        scratch_shapes=[
            pltpu.VMEM((dates, 4 * (groups * LOOK_AZ) // 2, held), jnp.bfloat16),
            pltpu.VMEM((2, 2 * LANES, 2 * LANES), jnp.bfloat16),
            pltpu.VMEM((count, 2, groups, up(chunk, LANES)), jnp.float32),
        ],
        compiler_params=limit,
    )(*first, range_shift, jnp.asarray(kernel_table()), jnp.asarray(lowpass_row(2 * LANES)), arrived)
    returned = lax.all_to_all(looked, axes, 0, 0, tiled=True)

    out = pl.pallas_call(
        functools.partial(unpack_kernel, used_lags, looks),
        out_shape=jax.ShapeDtypeStruct((2, LAGS, groups // az_count, looks * peers), jnp.float32),
        in_specs=[vmem],
        out_specs=vmem,
        compiler_params=limit,
    )(returned)
    return out[:, None]


HALO_LINES = 16
FOLD = 16
TAIL = 2 * FILTER_HALF


def reach(step, dates):
    return {dates - 1: dates // 2, dates // 2: dates - 1}.get(step, step)


def sinc(value):
    angle = jnp.pi * value
    return jnp.where(angle == 0.0, 1.0, jnp.sin(angle) / jnp.where(angle == 0.0, 1.0, angle))


def tap_row(index):
    lane = lax.broadcasted_iota(jnp.int32, (1, LANES), 1)
    position = lane.astype(jnp.float32) - 3.0 - index.astype(jnp.float32) / KERNELS
    shaped = sinc(position) * (0.5 + 0.5 * jnp.cos(jnp.pi * position / 5.0))
    shaped = jnp.where(lane < TAPS, shaped, 0.0)
    return shaped / jnp.sum(shaped, axis=1, keepdims=True)


def row_line(row, az):
    quarter = HALO_LINES // LOOK_AZ
    within = row % HALO_LINES
    return HALO_LINES * ((row // HALO_LINES) ^ az) + LOOK_AZ * (within % quarter) + within // quarter


def prepare_kernel(offsets_hbm, index_hbm, slc_ref, side_ref, lines_ref, line_ref, column_ref, held_ref, offsets_ref, index_ref, semaphores):
    lines, columns = slc_ref.shape[1:]
    az = lax.axis_index("az")
    row = pl.multiple_of((1 - az) * (lines - HALO_LINES), HALO_LINES)
    edge = pl.multiple_of((1 - lax.axis_index("rng")) * (columns - LANES), LANES)
    nearest, outermost = pl.ds(row, HALO_LINES), pl.ds(edge, LANES)
    moves = [
        (offsets_hbm, offsets_ref),
        (index_hbm, index_ref),
        (slc_ref.at[:, :, outermost], side_ref),
        (slc_ref.at[:, nearest, :], lines_ref),
    ]
    for plane in range(2):
        for part in range(lines // HALO_LINES):
            for side in range(2):
                at = pl.ds(part * HALO_LINES, HALO_LINES)
                source = slc_ref.at[plane, at, pl.ds(side * columns // 2, columns // 2)]
                moves.append((source, held_ref.at[plane, at, pl.ds(LANES + side * columns // 2, columns // 2)]))
    copies = [pltpu.make_async_copy(a, b, semaphores.at[i]) for i, (a, b) in enumerate(moves)]
    for copy in copies:
        copy.start()
    held_ref[:, :, :LANES] = jnp.zeros((2, lines, LANES), held_ref.dtype)
    held_ref[:, :, LANES + columns :] = jnp.zeros((2, lines, 2 * LANES), held_ref.dtype)
    copies[0].wait()
    copies[1].wait()
    for half in range(2):
        shape = (HALO_LINES, lines + HALO_LINES)
        line = row_line(lax.broadcasted_iota(jnp.int32, shape, 0) + half * HALO_LINES, az)
        place = lax.broadcasted_iota(jnp.int32, shape, 1)
        source = jnp.where(place < lines, place, place + jnp.where(az == 0, 0, -lines - HALO_LINES))
        taps = banded(tap_row(index_ref[0, 0]), source - line - offsets_ref[0, 0] + 3)
        line_ref[half] = jnp.concatenate(halves(taps), axis=0)
    shape = (2 * LANES, LANES)
    distance = lax.broadcasted_iota(jnp.int32, shape, 0) - lax.broadcasted_iota(jnp.int32, shape, 1)
    distance = distance - (LANES // 2 - FILTER_HALF - 3) - offsets_ref[0, 1]
    taps = banded(tap_row(index_ref[0, 1]), distance)
    column_ref[...] = jnp.concatenate(halves(taps), axis=1)
    for copy in copies[2:]:
        copy.wait()


def along_range(moved, column_ref, tiles):
    high, low = halves(pltpu.roll(moved, moved.shape[1] - LANES // 2, 1))
    starts = range(0, tiles * LANES, LANES)
    high = jnp.concatenate([high[:, s : s + 2 * LANES] for s in starts], axis=0)
    low = jnp.concatenate([low[:, s : s + 2 * LANES] for s in starts], axis=0)
    total = dot(high, column_ref[...])
    return total[:, :LANES] + total[:, LANES:] + dot(low, column_ref[:, :LANES])


def early_kernel(tiles, held_ref, line_ref, column_ref, out_ref):
    lines = held_ref.shape[1]
    early = out_ref.shape[0] // (2 * HALO_LINES)
    dates = lax.axis_size("date")
    chunk = lax.axis_index("date") ^ reach(dates - 1, dates)
    begin = pl.multiple_of((chunk * tiles + lax.axis_index("rng")) * LANES, LANES)
    moved = []
    for plane in range(2):
        both = dot(line_ref[0, :, :lines], held_ref[plane, :, pl.ds(begin, (early + 2) * LANES)])
        moved.append(both[:HALO_LINES] + both[HALO_LINES:])
    moved = jnp.concatenate(moved, axis=0)
    out_ref[...] = along_range(moved, column_ref, early).astype(jnp.bfloat16)


def resample_kernel(corner_ref, side_ref, lines_ref, held_ref, line_ref, column_ref, *outs):
    outs, tiles_ref, tails_ref = outs[:-2], outs[-2], outs[-1]
    lines, width = held_ref.shape[1:]
    width -= LANES
    block = lax.axis_index("rng")
    nearest = pl.multiple_of(lax.axis_index("az") * (lines - HALO_LINES), HALO_LINES)
    taps = jnp.concatenate([line_ref[0], line_ref[1]], axis=0)
    moved = [[], []]
    for plane in range(2):
        own = jnp.concatenate([side_ref[plane], held_ref[plane, :, LANES : width - LANES], side_ref[plane]], axis=1)
        corner = corner_ref[plane, pl.ds(nearest, HALO_LINES), :]
        halo = jnp.concatenate([corner, lines_ref[plane], corner], axis=1)
        both = dot(taps, jnp.concatenate([own, halo], axis=0))
        for half in range(2):
            at = 2 * half * HALO_LINES
            moved[half].append(both[at : at + HALO_LINES] + both[at + HALO_LINES : at + 2 * HALO_LINES])
    moved = jnp.concatenate(moved[0] + moved[1], axis=0)
    left = jnp.where(block > 0, moved[:, :LANES], 0.0)
    right = jnp.where(block == 0, moved[:, width - LANES :], 0.0)
    moved = jnp.concatenate([left, moved[:, LANES : width - LANES], right, jnp.zeros_like(right)], axis=1)
    total = along_range(moved, column_ref, width // LANES - 1)
    rows = 2 * lines
    tiles_ref[...] = total.astype(jnp.bfloat16)
    chunk_rows = outs[0].shape[0] - FOLD
    lane = lax.broadcasted_iota(jnp.int32, (FOLD, LANES), 1) // TAIL
    for chunk in range(len(outs)):
        begin = (chunk + 1) * chunk_rows
        folded = total[begin : begin + FOLD]
        for part in range(1, rows // FOLD):
            value = pltpu.roll(total[begin + part * FOLD : begin + (part + 1) * FOLD], part * TAIL, 1)
            folded = jnp.where(lane == part, value, folded)
        tails_ref[chunk] = folded.astype(jnp.bfloat16)
    date = lax.axis_index("date")
    for step, out_ref in enumerate(outs[:-1]):
        chunk = date ^ reach(step, len(outs))
        out_ref[:chunk_rows] = tiles_ref[pl.ds(pl.multiple_of(chunk * chunk_rows, FOLD), chunk_rows), :]
        out_ref[chunk_rows:] = tails_ref[chunk]
    out_ref = outs[-1]
    chunk = date ^ reach(len(outs) - 1, len(outs))
    early = chunk_rows // rows - 1
    for tile in range(early):
        begin = pl.multiple_of(chunk * chunk_rows + (tile + block) * rows + lines, FOLD)
        out_ref[tile * lines : (tile + 1) * lines] = tiles_ref[pl.ds(begin, lines), :]
    begin = pl.multiple_of(chunk * chunk_rows + (1 - block) * early * rows, FOLD)
    out_ref[early * lines : early * lines + rows] = tiles_ref[pl.ds(begin, rows), :]
    out_ref[early * lines + rows :] = tails_ref[chunk]


def filter_kernel(pairs, shift_hbm, early_ref, out_ref, spread_ref, shift_ref, semaphore):
    copy = pltpu.make_async_copy(shift_hbm, shift_ref, semaphore)
    copy.start()
    lines = 2 * HALO_LINES
    spread_ref[...] = jnp.zeros_like(spread_ref)
    for tile in range(early_ref.shape[0] // lines):
        begin = pl.multiple_of((tile + lax.axis_index("rng")) * 2 * lines, FOLD)
        spread_ref[pl.ds(begin, lines), :] = early_ref[tile * lines : (tile + 1) * lines]
    date = lax.axis_index("date")
    spacing = lax.broadcasted_iota(jnp.int32, (1, 2 * LANES), 1).astype(jnp.float32) - FILTER_HALF
    window = 0.4 * sinc(0.4 * spacing) * (0.54 + 0.46 * jnp.cos(jnp.pi * spacing / (FILTER_HALF + 1)))
    window = jnp.where(jnp.abs(spacing) <= FILTER_HALF, window, 0.0)
    copy.wait()
    for place, (first, second) in enumerate(pairs):
        dates = shift_ref.shape[0]
        gap = shift_ref[date ^ reach(first, dates)] - shift_ref[date ^ reach(second, dates)]
        angle = jnp.where(jnp.abs(spacing) <= FILTER_HALF, jnp.pi * gap * spacing, 0.0)
        for part, taps in enumerate((window * jnp.cos(angle), window * jnp.sin(angle))):
            spread = jnp.broadcast_to(taps, (LANES, 2 * LANES))
            spread = pltpu.roll(spread, 0, 1, stride=1, stride_axis=0)
            high, low = halves(spread)
            out_ref[place, part * LANES : (part + 1) * LANES, : 2 * LANES] = high
            out_ref[place, part * LANES : (part + 1) * LANES, 2 * LANES :] = low


def looks_kernel(pairs, dates, weight_ref, *refs):
    early_ref, chunks, outs = refs[0], list(refs[1 : dates + 1][::-1]), refs[dates + 1 : 2 * dates + 1]
    whole_ref, window_ref, product_ref = refs[-3:]
    groups, lines = outs[0].shape[0], outs[0].shape[0] * LOOK_AZ
    rows = 2 * lines
    blocks = (chunks[0].shape[0] - FOLD) // rows
    looks = blocks * LANES // LOOK_RG
    date = lax.axis_index("date")
    block = lax.axis_index("rng")
    early = blocks - 1
    whole_ref[: blocks * rows] = early_ref[...]
    for tile in range(early):
        begin = pl.multiple_of((tile + block) * rows, FOLD)
        whole_ref[pl.ds(begin + lines, lines), :] = chunks[-1][tile * lines : (tile + 1) * lines]
    begin = pl.multiple_of((1 - block) * early * rows, FOLD)
    whole_ref[pl.ds(begin, rows), :] = chunks[-1][early * lines : early * lines + rows]
    whole_ref[blocks * rows :] = chunks[-1][early * lines + rows :]
    chunks[-1] = whole_ref
    az = lax.axis_index("az")
    upper = lax.broadcasted_iota(jnp.int32, (groups, LANES), 0) // (groups // 2) == az
    for step, chunk_ref in enumerate(chunks):
        window_ref[step, :, :LANES] = chunk_ref[: blocks * rows]
        window_ref[step, : (blocks - 1) * rows, LANES:] = chunk_ref[rows : blocks * rows]
        folded = chunk_ref[blocks * rows :].astype(jnp.float32)
        for part in range(rows // FOLD):
            value = pltpu.roll(folded, LANES - part * TAIL, 1) if part else folded
            at = pl.ds((blocks - 1) * rows + part * FOLD, FOLD)
            window_ref[step, at, LANES:] = value.astype(jnp.bfloat16)
    for place, (first, second) in enumerate(pairs):
        def filtered(step):
            window = window_ref[step]
            total = dot_nt(jnp.concatenate([window, window], axis=1), weight_ref[place])
            total = total.reshape(blocks, 2, 2, HALO_LINES, 2 * LANES)
            re, im = total[:, :, 0], total[:, :, 1]
            return re[..., :LANES], im[..., :LANES], re[..., LANES:], im[..., LANES:]

        cos_re, cos_im, sin_re, sin_im = filtered(first)
        master_re, master_im = cos_re + sin_im, cos_im - sin_re
        cos_re, cos_im, sin_re, sin_im = filtered(second)
        partner_re, partner_im = cos_re - sin_im, cos_im + sin_re
        for part, product in enumerate(
            (
                master_re * partner_re + master_im * partner_im,
                master_im * partner_re - master_re * partner_im,
            )
        ):
            summed = product[:, :, :groups] + product[:, :, groups:]
            at = pl.ds((place * 2 + part) * groups, groups)
            for k in range(blocks):
                both = [summed[k, half] + pltpu.roll(summed[k, half], groups // 2, 0) for half in range(2)]
                product_ref[at, k * LANES : (k + 1) * LANES] = jnp.where(upper, both[0], both[1])

    out_width = outs[0].shape[1]
    column = lax.broadcasted_iota(jnp.int32, (product_ref.shape[1], out_width), 0)
    lane = lax.broadcasted_iota(jnp.int32, (product_ref.shape[1], out_width), 1)
    collect = jnp.where(column // LOOK_RG == lane % looks, 1.0, 0.0).astype(jnp.bfloat16)
    high, low = halves(product_ref[...])
    total = (dot(high, collect) + dot(low, collect)) * (1.0 / (LOOK_AZ * LOOK_RG))
    total = total.reshape(len(pairs), 2, groups, out_width)
    own_lane = lax.broadcasted_iota(jnp.int32, (groups, out_width), 1) // looks
    for step, out_ref in enumerate(outs):
        value = jnp.zeros((groups, out_width), jnp.float32)
        for place, pair in enumerate(pairs):
            if step in pair:
                other = pair[1] if pair[0] == step else pair[0]
                lag = (date ^ reach(other, dates)) - (date ^ reach(step, dates))
                for part in range(2):
                    signed = -total[place, part] if part == 1 and pair[1] == step else total[place, part]
                    value = jnp.where(own_lane == (lag - 1) * 2 + part, signed, value)
        out_ref[...] = value


def place_kernel(used_lags, looks, *refs):
    out_ref = refs[-1]
    groups, columns = out_ref.shape[2:]
    date = lax.axis_index("date")
    lane = lax.broadcasted_iota(jnp.int32, (groups, LANES), 1) // looks
    out_ref[...] = jnp.zeros_like(out_ref)
    each = LANES // looks
    for step, recv_ref in enumerate(refs[:-1][::-1]):
        chunk = date ^ step
        for lag in range(used_lags):
            for part in range(2):
                tile, group = divmod(lag * 2 + part, each)
                block = recv_ref[:, tile * LANES : (tile + 1) * LANES]
                block = pltpu.roll(block, lax.bitwise_and(looks * (chunk - group), LANES - 1), 1)
                out_ref[part, lag] = jnp.where(lane == chunk, block, out_ref[part, lag])


def tiled_body(slc, offsets, kernel_index, range_shift):
    dates = lax.axis_size("date")
    lines, columns = slc.shape[2], slc.shape[3]
    chunk = columns // dates
    looks = chunk // LOOK_RG
    groups = lines // LOOK_AZ
    out_width = up(min(LAGS, dates - 1) * 2 * looks, LANES)
    vmem = pl.BlockSpec(memory_space=pltpu.VMEM)
    hbm = pl.BlockSpec(memory_space=pltpu.HBM)
    limit = pltpu.CompilerParams(vmem_limit_bytes=32 * 1024 * 1024)
    bf16 = jnp.bfloat16
    cells, offsets, kernel_index, range_shift = (
        pltpu.with_memory_space_constraint(value, pltpu.HBM)
        for value in (slc.reshape(2, lines, columns), offsets, kernel_index, range_shift)
    )
    tiles = chunk // LANES
    chunk_rows = tiles * 2 * lines

    side, halo_lines, line_taps, column_taps, held = pl.pallas_call(
        prepare_kernel,
        out_shape=[
            jax.ShapeDtypeStruct((2, lines, LANES), bf16),
            jax.ShapeDtypeStruct((2, HALO_LINES, columns), bf16),
            jax.ShapeDtypeStruct((2, 2 * HALO_LINES, lines + HALO_LINES), bf16),
            jax.ShapeDtypeStruct((2 * LANES, 2 * LANES), bf16),
            jax.ShapeDtypeStruct((2, lines, columns + 3 * LANES), bf16),
        ],
        in_specs=[hbm] * 3,
        out_specs=[vmem] * 5,
        scratch_shapes=[
            pltpu.SMEM(offsets.shape, jnp.int32),
            pltpu.SMEM(kernel_index.shape, jnp.int32),
            pltpu.SemaphoreType.DMA((4 + 4 * (lines // HALO_LINES),)),
        ],
        compiler_params=limit,
    )(offsets, kernel_index, cells)
    swap = [(0, 1), (1, 0)]
    corner = lax.ppermute(side, ("rng", "az"), [(0, 3), (1, 2), (2, 1), (3, 0)])
    side = lax.ppermute(side, "rng", swap)
    halo_lines = lax.ppermute(halo_lines, "az", swap)

    early_rows = (tiles - 1) * lines
    early = pl.pallas_call(
        functools.partial(early_kernel, tiles),
        out_shape=jax.ShapeDtypeStruct((early_rows, LANES), bf16),
        in_specs=[vmem] * 3,
        out_specs=vmem,
        compiler_params=limit,
        cost_estimate=pl.CostEstimate(flops=2_500_000_000, bytes_accessed=0, transcendentals=0),
    )(held, line_taps, column_taps)
    early = lax.ppermute(early, "date", [(i, i ^ reach(dates - 1, dates)) for i in range(dates)])
    out_rows = [chunk_rows + FOLD] * (dates - 1) + [chunk_rows + FOLD - early_rows]
    sent = pl.pallas_call(
        resample_kernel,
        out_shape=[jax.ShapeDtypeStruct((rows, LANES), bf16) for rows in out_rows],
        in_specs=[vmem] * 6,
        out_specs=[vmem] * dates,
        scratch_shapes=[
            pltpu.VMEM(((columns // LANES + 1) * 2 * lines, LANES), bf16),
            pltpu.VMEM((dates, FOLD, LANES), bf16),
        ],
        compiler_params=limit,
    )(corner, side, halo_lines, held, line_taps, column_taps)

    def exchanged(values, order):
        arrived = {0: values[0]}
        for step in order:
            arrived[step] = lax.ppermute(values[step], "date", [(i, i ^ reach(step, dates)) for i in range(dates)])
        return [arrived[step] for step in reversed(range(dates))]

    steps = range(dates - 1, 0, -1)

    chunks = exchanged(sent, steps)
    pairs = [(first, second) for first in range(dates) for second in range(first + 1, dates)]
    weights, early = pl.pallas_call(
        functools.partial(filter_kernel, pairs),
        out_shape=[
            jax.ShapeDtypeStruct((len(pairs), 2 * LANES, 4 * LANES), bf16),
            jax.ShapeDtypeStruct((chunk_rows, LANES), bf16),
        ],
        in_specs=[hbm, vmem],
        out_specs=[vmem] * 2,
        scratch_shapes=[pltpu.SMEM(range_shift.shape, jnp.float32), pltpu.SemaphoreType.DMA],
        compiler_params=limit,
        cost_estimate=pl.CostEstimate(flops=600_000_000, bytes_accessed=0, transcendentals=0),
    )(range_shift, early)
    looked = pl.pallas_call(
        functools.partial(looks_kernel, pairs, dates),
        out_shape=[jax.ShapeDtypeStruct((groups, out_width), jnp.float32)] * dates,
        in_specs=[vmem] * (2 + dates),
        out_specs=[vmem] * dates,
        scratch_shapes=[
            pltpu.VMEM((chunk_rows + FOLD, LANES), bf16),
            pltpu.VMEM((dates, chunk_rows, 2 * LANES), bf16),
            pltpu.VMEM((len(pairs) * 2 * groups, chunk), jnp.float32),
        ],
        compiler_params=limit,
    )(weights, early, *chunks)
    returned = exchanged(looked, steps)[::-1]
    returned = [returned[reach(distance, dates)] for distance in reversed(range(dates))]
    out = pl.pallas_call(
        functools.partial(place_kernel, min(LAGS, dates - 1), looks),
        out_shape=jax.ShapeDtypeStruct((2, LAGS, groups, looks * dates), jnp.float32),
        in_specs=[vmem] * dates,
        out_specs=vmem,
        compiler_params=limit,
    )(*returned)
    return out[:, None]


def body(slc, offsets, kernel_index, range_shift):
    dates, az_count = (lax.axis_size(a) for a in ("date", "az"))
    lines, columns = slc.shape[2], slc.shape[3]
    whole_tiles = columns % (dates * LANES) == 0 and columns % (dates * LOOK_RG) == 0
    one_row = columns // LOOK_RG == LANES and range_shift.shape[0] == dates
    few = dates & (dates - 1) == 0 and dates - 1 <= LAGS
    folds = lines == 2 * HALO_LINES and lax.axis_size("rng") == 2 and dates >= 4 and 2 * lines // FOLD * TAIL <= LANES
    if az_count == 2 and whole_tiles and one_row and few and folds:
        return tiled_body(slc, offsets, kernel_index, range_shift)
    return chunked_body(slc, offsets, kernel_index, range_shift)


def solution(mesh):
    return jax.shard_map(
        body,
        mesh=mesh,
        in_specs=(
            P(None, ("groups", "date"), "az", "rng"),
            P(("groups", "date"), None),
            P(("groups", "date"), None),
            P("groups"),
        ),
        out_specs=P(None, ("groups", "date"), None, "az", "rng"),
        check_vma=False,
    )
```

```python
import functools

import jax
import jax.numpy as jnp
import numpy as np
from jax import lax
from jax.experimental import pallas as pl
from jax.experimental.pallas import tpu as pltpu
from jax.sharding import PartitionSpec as P

LAGS = 8
KERNELS = 16
TAPS = 8
FILTER_HALF = 8
FILTER_TAPS = 2 * FILTER_HALF + 1
LOOK_AZ = 4
LOOK_RG = 20
LANES = 128
META = 3
UNROLLED_PAIRS = 12


def up(value, unit):
    return -(-value // unit) * unit


def kernel_table():
    position = np.arange(TAPS) - 3.0 - np.arange(KERNELS)[:, None] / KERNELS
    shaped = np.sinc(position) * (0.5 + 0.5 * np.cos(np.pi * position / 5.0))
    table = np.zeros((KERNELS, LANES), np.float32)
    table[:, :TAPS] = shaped / shaped.sum(1, keepdims=True)
    return table


def lowpass_row(width):
    t = np.arange(FILTER_TAPS) - FILTER_HALF
    row = np.zeros((1, width), np.float32)
    row[0, :FILTER_TAPS] = 0.4 * np.sinc(0.4 * t) * (0.54 + 0.46 * np.cos(np.pi * t / (FILTER_HALF + 1)))
    return row


def halves(value):
    high = value.astype(jnp.bfloat16)
    return high, (value - high.astype(jnp.float32)).astype(jnp.bfloat16)


def dot(a, b):
    return jnp.dot(a, b, preferred_element_type=jnp.float32)


def dot_nt(a, b):
    return lax.dot_general(a, b, (((1,), (1,)), ((), ())), preferred_element_type=jnp.float32)


def pack_kernel(chunk, place_ref, offsets_ref, index_ref, slc_ref, before_ref, after_ref, out_ref, wide_ref):
    columns = slc_ref.shape[1]
    wide = out_ref.shape[2]
    first = place_ref[0] == 0
    last = place_ref[0] == place_ref[1] - 1
    zero = jnp.zeros_like(before_ref[...])
    wide_ref[:, :LANES] = jnp.where(first, zero, before_ref[...])
    wide_ref[:, LANES : LANES + columns] = slc_ref[...]
    wide_ref[:, LANES + columns :] = jnp.where(last, zero, after_ref[...])
    lane = lax.broadcasted_iota(jnp.int32, (slc_ref.shape[0], wide), 1)
    numbers = [offsets_ref[0, 0], index_ref[0, 0], index_ref[0, 1]]
    for j in range(out_ref.shape[0]):
        start = LANES + chunk * j - FILTER_HALF - 3 + offsets_ref[0, 1]
        tile = lax.shift_right_logical(start, 7)
        within = lax.bitwise_and(start, LANES - 1)
        window = wide_ref[:, pl.ds(pl.multiple_of(tile * LANES, LANES), wide + LANES)].astype(jnp.float32)
        moved = pltpu.roll(window, wide + LANES - within, 1)[:, :wide]
        for slot, number in enumerate(numbers):
            moved = jnp.where(lane == wide - META + slot, number.astype(jnp.float32), moved)
        out_ref[j] = moved.astype(jnp.bfloat16)


def picked_taps(table, index):
    row = lax.broadcasted_iota(jnp.int32, table.shape, 0).astype(jnp.float32)
    return jnp.sum(jnp.where(row == index, table, 0.0), axis=0, keepdims=True)


def banded(taps, distance):
    out = jnp.zeros(distance.shape, jnp.float32)
    for q in range(TAPS):
        out = jnp.where(distance == q, taps[:, q : q + 1], out)
    return out


def pairs_kernel(chunk, pairs, *refs):
    if isinstance(pairs, int):
        table_of_pairs, refs = refs[0], refs[1:]
    shift_ref, table_ref, lowpass_ref, recv_ref, out_ref, resampled_ref, weight_ref, product_ref = refs
    sources, rows, wide = recv_ref.shape
    dates = shift_ref.shape[0]
    az_count = sources // dates
    own_lines = rows // 2
    lines = own_lines * az_count
    groups = lines // LOOK_AZ
    looks = chunk // LOOK_RG
    table = table_ref[...]
    held = resampled_ref.shape[2]

    out_row = lax.broadcasted_iota(jnp.int32, (lines, lines), 0)
    in_row = lax.broadcasted_iota(jnp.int32, (lines, lines), 1)
    line = LOOK_AZ * (out_row % groups) + out_row // groups
    line_distance = (in_row - line + 3).astype(jnp.float32)
    span = min(2 * LANES, wide)
    column_distance = (
        lax.broadcasted_iota(jnp.int32, (span, LANES), 0) - lax.broadcasted_iota(jnp.int32, (span, LANES), 1)
    ).astype(jnp.float32)
    for date in range(dates):
        numbers = recv_ref[date * az_count, 0:16, wide - LANES :].astype(jnp.float32)[0:1, LANES - META :]
        line_offset, line_index, column_index = (numbers[:, s : s + 1] for s in range(META))
        line_taps = banded(picked_taps(table, line_index), line_distance - line_offset)
        line_taps = jnp.concatenate(halves(line_taps), axis=0)
        column_high, column_low = halves(banded(picked_taps(table, column_index), column_distance))
        moved = []
        for plane in range(2):
            rows_of = slice(plane * own_lines, (plane + 1) * own_lines)
            source = jnp.concatenate([recv_ref[date * az_count + a, rows_of, :] for a in range(az_count)], axis=0)
            both = dot(line_taps, source)
            moved.append(both[:lines] + both[lines:])
        moved_high, moved_low = halves(jnp.concatenate(moved, axis=0))
        for begin in range(0, held, LANES):
            end = min(begin + span, wide)
            taken = end - begin
            total = dot(moved_high[:, begin:end], column_high[:taken])
            total += dot(moved_low[:, begin:end], column_high[:taken])
            total += dot(moved_high[:, begin:end], column_low[:taken])
            resampled_ref[date, :, begin : begin + LANES] = total.astype(jnp.bfloat16)

    window = lowpass_ref[...]
    spacing = lax.broadcasted_iota(jnp.int32, window.shape, 1).astype(jnp.float32) - FILTER_HALF
    span = min(2 * LANES, held)

    def one_pair(place, own, other):
        gap = shift_ref[own] - shift_ref[other]
        angle = jnp.where(jnp.abs(spacing) <= FILTER_HALF, jnp.pi * gap * spacing, 0.0)
        for part, taps in enumerate((window * jnp.cos(angle), window * jnp.sin(angle))):
            spread = jnp.broadcast_to(taps, (LANES, 2 * LANES))
            spread = pltpu.roll(spread, 0, 1, stride=1, stride_axis=0)
            high, low = halves(spread)
            weight_ref[0, part * LANES : (part + 1) * LANES, :] = high
            weight_ref[1, part * LANES : (part + 1) * LANES, :] = low
        both = jnp.concatenate([resampled_ref[own], resampled_ref[other]], axis=0)
        for begin in range(0, up(chunk, LANES), LANES):
            end = min(begin + span, held)
            taken = end - begin
            total = dot_nt(both[:, begin:end], weight_ref[0, :, :taken])
            total += dot_nt(both[:, begin:end], weight_ref[1, :, :taken])
            cos, sin = total[:, :LANES], total[:, LANES:]
            re, im = slice(0, lines), slice(lines, 2 * lines)
            master_re = cos[re] + sin[im]
            master_im = cos[im] - sin[re]
            re, im = slice(2 * lines, 3 * lines), slice(3 * lines, 4 * lines)
            partner_re = cos[re] - sin[im]
            partner_im = cos[im] + sin[re]
            for part, product in enumerate(
                (
                    master_re * partner_re + master_im * partner_im,
                    master_im * partner_re - master_re * partner_im,
                )
            ):
                summed = sum(product[k * groups : (k + 1) * groups] for k in range(LOOK_AZ))
                product_ref[place, part, :, begin : begin + LANES] = summed

    if isinstance(pairs, int):
        count = pairs

        def step(place, carry):
            one_pair(place, table_of_pairs[place, 0], table_of_pairs[place, 1])
            return carry

        lax.fori_loop(0, count, step, 0)
    else:
        count = len(pairs)
        for place, (own, other) in enumerate(pairs):
            one_pair(place, own, other)

    out_width = out_ref.shape[2]
    column = lax.broadcasted_iota(jnp.int32, (product_ref.shape[3], out_width), 0)
    lane = lax.broadcasted_iota(jnp.int32, (product_ref.shape[3], out_width), 1)
    collect = jnp.where(column // LOOK_RG == lane % looks, 1.0, 0.0).astype(jnp.bfloat16)
    high, low = halves(product_ref[...].reshape(count * 2 * groups, product_ref.shape[3]))
    total = (dot(high, collect) + dot(low, collect)) * (1.0 / (LOOK_AZ * LOOK_RG))
    total = total.reshape(count, 2, groups, out_width)
    own_lane = lax.broadcasted_iota(jnp.int32, (groups, out_width), 1) // looks
    place = 0
    for own in range(dates):
        value = jnp.zeros((groups, out_width), jnp.float32)
        for lag in range(min(LAGS, dates - 1 - own)):
            for part in range(2):
                value = jnp.where(own_lane == lag * 2 + part, total[place, part], value)
            place += 1
        out_ref[own * az_count : (own + 1) * az_count] = value.reshape(az_count, groups // az_count, out_width)


def unpack_kernel(used_lags, looks, recv_ref, out_ref):
    sources, groups, width = recv_ref.shape
    columns = out_ref.shape[-1]
    lane = lax.broadcasted_iota(jnp.int32, (groups, columns), 1) // looks
    out_ref[...] = jnp.zeros_like(out_ref)
    for lag in range(used_lags):
        for part in range(2):
            value = jnp.zeros((groups, columns), jnp.float32)
            for source in range(sources):
                block = recv_ref[source]
                if width != columns:
                    block = block[:, :columns]
                shift = looks * (source - lag * 2 - part) % columns
                if shift:
                    block = pltpu.roll(block, shift, 1)
                value = jnp.where(lane == source, block, value)
            out_ref[part, lag] = value


def chunked_body(slc, offsets, kernel_index, range_shift):
    axes = ("date", "az")
    date_count, az_count, rng_count = (lax.axis_size(a) for a in ("date", "az", "rng"))
    peers = date_count * az_count
    lines, columns = slc.shape[2], slc.shape[3]
    dates = range_shift.shape[0]
    chunk = columns // peers
    looks = chunk // LOOK_RG
    groups = lines * az_count // LOOK_AZ
    wide = up(chunk + 2 * FILTER_HALF + TAPS - 1 + META, LANES)
    held = up(chunk + 2 * FILTER_HALF, LANES)
    used_lags = min(LAGS, dates - 1)
    out_width = up(used_lags * 2 * looks, LANES)
    vmem = pl.BlockSpec(memory_space=pltpu.VMEM)
    smem = pl.BlockSpec(memory_space=pltpu.SMEM)
    limit = pltpu.CompilerParams(vmem_limit_bytes=32 * 1024 * 1024)

    cells = slc.reshape(2 * lines, columns)
    place = lax.axis_index("rng")
    if rng_count == 2:
        edge = jnp.where(place == 0, cells[:, columns - LANES :], cells[:, :LANES])
        before = after = lax.ppermute(edge, "rng", [(0, 1), (1, 0)])
    else:
        forth = [(i, i + 1) for i in range(rng_count - 1)]
        before = lax.ppermute(cells[:, columns - LANES :], "rng", forth)
        after = lax.ppermute(cells[:, :LANES], "rng", [(b, a) for a, b in forth])

    packed = pl.pallas_call(
        functools.partial(pack_kernel, chunk),
        out_shape=jax.ShapeDtypeStruct((peers, 2 * lines, wide), jnp.bfloat16),
        in_specs=[smem] * 3 + [vmem] * 3,
        out_specs=vmem,
        scratch_shapes=[pltpu.VMEM((2 * lines, columns + 2 * LANES), jnp.bfloat16)],
        compiler_params=limit,
    )(jnp.stack([place, rng_count]).astype(jnp.int32), offsets, kernel_index, cells, before, after)
    arrived = lax.all_to_all(packed, axes, 0, 0, tiled=True)

    pairs = [(own, own + lag) for own in range(dates) for lag in range(1, LAGS + 1) if own + lag < dates]
    count = len(pairs)
    first = [jnp.asarray(np.array(pairs, np.int32))] if count > UNROLLED_PAIRS else []
    looked = pl.pallas_call(
        functools.partial(pairs_kernel, chunk, count if first else pairs),
        out_shape=jax.ShapeDtypeStruct((peers, groups // az_count, out_width), jnp.float32),
        in_specs=[smem] * len(first) + [smem] + [vmem] * 3,
        out_specs=vmem,
        scratch_shapes=[
            pltpu.VMEM((dates, 4 * (groups * LOOK_AZ) // 2, held), jnp.bfloat16),
            pltpu.VMEM((2, 2 * LANES, 2 * LANES), jnp.bfloat16),
            pltpu.VMEM((count, 2, groups, up(chunk, LANES)), jnp.float32),
        ],
        compiler_params=limit,
    )(*first, range_shift, jnp.asarray(kernel_table()), jnp.asarray(lowpass_row(2 * LANES)), arrived)
    returned = lax.all_to_all(looked, axes, 0, 0, tiled=True)

    out = pl.pallas_call(
        functools.partial(unpack_kernel, used_lags, looks),
        out_shape=jax.ShapeDtypeStruct((2, LAGS, groups // az_count, looks * peers), jnp.float32),
        in_specs=[vmem],
        out_specs=vmem,
        compiler_params=limit,
    )(returned)
    return out[:, None]


HALO_LINES = 16
FOLD = 16
TAIL = 2 * FILTER_HALF


def reach(step, dates):
    return {dates - 1: dates // 2, dates // 2: dates - 1}.get(step, step)


def sinc(value):
    angle = jnp.pi * value
    return jnp.where(angle == 0.0, 1.0, jnp.sin(angle) / jnp.where(angle == 0.0, 1.0, angle))


def tap_row(index):
    lane = lax.broadcasted_iota(jnp.int32, (1, LANES), 1)
    position = lane.astype(jnp.float32) - 3.0 - index.astype(jnp.float32) / KERNELS
    shaped = sinc(position) * (0.5 + 0.5 * jnp.cos(jnp.pi * position / 5.0))
    shaped = jnp.where(lane < TAPS, shaped, 0.0)
    return shaped / jnp.sum(shaped, axis=1, keepdims=True)


def row_line(row, az):
    quarter = HALO_LINES // LOOK_AZ
    within = row % HALO_LINES
    return HALO_LINES * ((row // HALO_LINES) ^ az) + LOOK_AZ * (within % quarter) + within // quarter


def prepare_kernel(offsets_hbm, index_hbm, slc_ref, side_ref, lines_ref, line_ref, column_ref, held_ref, offsets_ref, index_ref, semaphores):
    lines, columns = slc_ref.shape[1:]
    az = lax.axis_index("az")
    row = pl.multiple_of((1 - az) * (lines - HALO_LINES), HALO_LINES)
    edge = pl.multiple_of((1 - lax.axis_index("rng")) * (columns - LANES), LANES)
    nearest, outermost = pl.ds(row, HALO_LINES), pl.ds(edge, LANES)
    moves = [
        (offsets_hbm, offsets_ref),
        (index_hbm, index_ref),
        (slc_ref.at[:, :, outermost], side_ref),
        (slc_ref.at[:, nearest, :], lines_ref),
    ]
    for plane in range(2):
        for part in range(lines // HALO_LINES):
            for side in range(2):
                at = pl.ds(part * HALO_LINES, HALO_LINES)
                source = slc_ref.at[plane, at, pl.ds(side * columns // 2, columns // 2)]
                moves.append((source, held_ref.at[plane, at, pl.ds(LANES + side * columns // 2, columns // 2)]))
    copies = [pltpu.make_async_copy(a, b, semaphores.at[i]) for i, (a, b) in enumerate(moves)]
    for copy in copies:
        copy.start()
    held_ref[:, :, :LANES] = jnp.zeros((2, lines, LANES), held_ref.dtype)
    held_ref[:, :, LANES + columns :] = jnp.zeros((2, lines, 2 * LANES), held_ref.dtype)
    copies[0].wait()
    copies[1].wait()
    for half in range(2):
        shape = (HALO_LINES, lines + HALO_LINES)
        line = row_line(lax.broadcasted_iota(jnp.int32, shape, 0) + half * HALO_LINES, az)
        place = lax.broadcasted_iota(jnp.int32, shape, 1)
        source = jnp.where(place < lines, place, place + jnp.where(az == 0, 0, -lines - HALO_LINES))
        taps = banded(tap_row(index_ref[0, 0]), source - line - offsets_ref[0, 0] + 3)
        line_ref[half] = jnp.concatenate(halves(taps), axis=0)
    shape = (2 * LANES, LANES)
    distance = lax.broadcasted_iota(jnp.int32, shape, 0) - lax.broadcasted_iota(jnp.int32, shape, 1)
    distance = distance - (LANES // 2 - FILTER_HALF - 3) - offsets_ref[0, 1]
    taps = banded(tap_row(index_ref[0, 1]), distance)
    column_ref[...] = jnp.concatenate(halves(taps), axis=1)
    for copy in copies[2:]:
        copy.wait()


def along_range(moved, column_ref, tiles):
    high, low = halves(pltpu.roll(moved, moved.shape[1] - LANES // 2, 1))
    starts = range(0, tiles * LANES, LANES)
    high = jnp.concatenate([high[:, s : s + 2 * LANES] for s in starts], axis=0)
    low = jnp.concatenate([low[:, s : s + 2 * LANES] for s in starts], axis=0)
    total = dot(high, column_ref[...])
    return total[:, :LANES] + total[:, LANES:] + dot(low, column_ref[:, :LANES])


def early_kernel(tiles, held_ref, line_ref, column_ref, out_ref):
    lines = held_ref.shape[1]
    early = out_ref.shape[0] // (2 * HALO_LINES)
    dates = lax.axis_size("date")
    chunk = lax.axis_index("date") ^ reach(dates - 1, dates)
    begin = pl.multiple_of((chunk * tiles + lax.axis_index("rng")) * LANES, LANES)
    moved = []
    for plane in range(2):
        both = dot(line_ref[0, :, :lines], held_ref[plane, :, pl.ds(begin, (early + 2) * LANES)])
        moved.append(both[:HALO_LINES] + both[HALO_LINES:])
    moved = jnp.concatenate(moved, axis=0)
    out_ref[...] = along_range(moved, column_ref, early).astype(jnp.bfloat16)


def resample_kernel(corner_ref, side_ref, lines_ref, held_ref, line_ref, column_ref, *outs):
    outs, tiles_ref, tails_ref = outs[:-2], outs[-2], outs[-1]
    lines, width = held_ref.shape[1:]
    width -= LANES
    block = lax.axis_index("rng")
    nearest = pl.multiple_of(lax.axis_index("az") * (lines - HALO_LINES), HALO_LINES)
    taps = jnp.concatenate([line_ref[0], line_ref[1]], axis=0)
    moved = [[], []]
    for plane in range(2):
        own = jnp.concatenate([side_ref[plane], held_ref[plane, :, LANES : width - LANES], side_ref[plane]], axis=1)
        corner = corner_ref[plane, pl.ds(nearest, HALO_LINES), :]
        halo = jnp.concatenate([corner, lines_ref[plane], corner], axis=1)
        both = dot(taps, jnp.concatenate([own, halo], axis=0))
        for half in range(2):
            at = 2 * half * HALO_LINES
            moved[half].append(both[at : at + HALO_LINES] + both[at + HALO_LINES : at + 2 * HALO_LINES])
    moved = jnp.concatenate(moved[0] + moved[1], axis=0)
    left = jnp.where(block > 0, moved[:, :LANES], 0.0)
    right = jnp.where(block == 0, moved[:, width - LANES :], 0.0)
    moved = jnp.concatenate([left, moved[:, LANES : width - LANES], right, jnp.zeros_like(right)], axis=1)
    total = along_range(moved, column_ref, width // LANES - 1)
    rows = 2 * lines
    tiles_ref[...] = total.astype(jnp.bfloat16)
    chunk_rows = outs[0].shape[0] - FOLD
    lane = lax.broadcasted_iota(jnp.int32, (FOLD, LANES), 1) // TAIL
    for chunk in range(len(outs)):
        begin = (chunk + 1) * chunk_rows
        folded = total[begin : begin + FOLD]
        for part in range(1, rows // FOLD):
            value = pltpu.roll(total[begin + part * FOLD : begin + (part + 1) * FOLD], part * TAIL, 1)
            folded = jnp.where(lane == part, value, folded)
        tails_ref[chunk] = folded.astype(jnp.bfloat16)
    date = lax.axis_index("date")
    for step, out_ref in enumerate(outs[:-1]):
        chunk = date ^ reach(step, len(outs))
        out_ref[:chunk_rows] = tiles_ref[pl.ds(pl.multiple_of(chunk * chunk_rows, FOLD), chunk_rows), :]
        out_ref[chunk_rows:] = tails_ref[chunk]
    out_ref = outs[-1]
    chunk = date ^ reach(len(outs) - 1, len(outs))
    early = chunk_rows // rows - 1
    for tile in range(early):
        begin = pl.multiple_of(chunk * chunk_rows + (tile + block) * rows + lines, FOLD)
        out_ref[tile * lines : (tile + 1) * lines] = tiles_ref[pl.ds(begin, lines), :]
    begin = pl.multiple_of(chunk * chunk_rows + (1 - block) * early * rows, FOLD)
    out_ref[early * lines : early * lines + rows] = tiles_ref[pl.ds(begin, rows), :]
    out_ref[early * lines + rows :] = tails_ref[chunk]


def filter_kernel(pairs, shift_hbm, early_ref, out_ref, spread_ref, shift_ref, semaphore):
    copy = pltpu.make_async_copy(shift_hbm, shift_ref, semaphore)
    copy.start()
    lines = 2 * HALO_LINES
    spread_ref[...] = jnp.zeros_like(spread_ref)
    for tile in range(early_ref.shape[0] // lines):
        begin = pl.multiple_of((tile + lax.axis_index("rng")) * 2 * lines, FOLD)
        spread_ref[pl.ds(begin, lines), :] = early_ref[tile * lines : (tile + 1) * lines]
    date = lax.axis_index("date")
    spacing = lax.broadcasted_iota(jnp.int32, (1, 2 * LANES), 1).astype(jnp.float32) - FILTER_HALF
    window = 0.4 * sinc(0.4 * spacing) * (0.54 + 0.46 * jnp.cos(jnp.pi * spacing / (FILTER_HALF + 1)))
    window = jnp.where(jnp.abs(spacing) <= FILTER_HALF, window, 0.0)
    copy.wait()
    for place, (first, second) in enumerate(pairs):
        dates = shift_ref.shape[0]
        gap = shift_ref[date ^ reach(first, dates)] - shift_ref[date ^ reach(second, dates)]
        angle = jnp.where(jnp.abs(spacing) <= FILTER_HALF, jnp.pi * gap * spacing, 0.0)
        for part, taps in enumerate((window * jnp.cos(angle), window * jnp.sin(angle))):
            spread = jnp.broadcast_to(taps, (LANES, 2 * LANES))
            spread = pltpu.roll(spread, 0, 1, stride=1, stride_axis=0)
            high, low = halves(spread)
            out_ref[place, part * LANES : (part + 1) * LANES, : 2 * LANES] = high
            out_ref[place, part * LANES : (part + 1) * LANES, 2 * LANES :] = low


def looks_kernel(pairs, dates, weight_ref, *refs):
    early_ref, chunks, outs = refs[0], list(refs[1 : dates + 1][::-1]), refs[dates + 1 : 2 * dates + 1]
    whole_ref, window_ref, product_ref = refs[-3:]
    groups, lines = outs[0].shape[0], outs[0].shape[0] * LOOK_AZ
    rows = 2 * lines
    blocks = (chunks[0].shape[0] - FOLD) // rows
    looks = blocks * LANES // LOOK_RG
    date = lax.axis_index("date")
    block = lax.axis_index("rng")
    early = blocks - 1
    whole_ref[: blocks * rows] = early_ref[...]
    for tile in range(early):
        begin = pl.multiple_of((tile + block) * rows, FOLD)
        whole_ref[pl.ds(begin + lines, lines), :] = chunks[-1][tile * lines : (tile + 1) * lines]
    begin = pl.multiple_of((1 - block) * early * rows, FOLD)
    whole_ref[pl.ds(begin, rows), :] = chunks[-1][early * lines : early * lines + rows]
    whole_ref[blocks * rows :] = chunks[-1][early * lines + rows :]
    chunks[-1] = whole_ref
    az = lax.axis_index("az")
    upper = lax.broadcasted_iota(jnp.int32, (groups, LANES), 0) // (groups // 2) == az
    for step, chunk_ref in enumerate(chunks):
        window_ref[step, :, :LANES] = chunk_ref[: blocks * rows]
        window_ref[step, : (blocks - 1) * rows, LANES:] = chunk_ref[rows : blocks * rows]
        folded = chunk_ref[blocks * rows :].astype(jnp.float32)
        for part in range(rows // FOLD):
            value = pltpu.roll(folded, LANES - part * TAIL, 1) if part else folded
            at = pl.ds((blocks - 1) * rows + part * FOLD, FOLD)
            window_ref[step, at, LANES:] = value.astype(jnp.bfloat16)
    for place, (first, second) in enumerate(pairs):
        def filtered(step):
            window = window_ref[step]
            total = dot_nt(jnp.concatenate([window, window], axis=1), weight_ref[place])
            total = total.reshape(blocks, 2, 2, HALO_LINES, 2 * LANES)
            re, im = total[:, :, 0], total[:, :, 1]
            return re[..., :LANES], im[..., :LANES], re[..., LANES:], im[..., LANES:]

        cos_re, cos_im, sin_re, sin_im = filtered(first)
        master_re, master_im = cos_re + sin_im, cos_im - sin_re
        cos_re, cos_im, sin_re, sin_im = filtered(second)
        partner_re, partner_im = cos_re - sin_im, cos_im + sin_re
        for part, product in enumerate(
            (
                master_re * partner_re + master_im * partner_im,
                master_im * partner_re - master_re * partner_im,
            )
        ):
            summed = product[:, :, :groups] + product[:, :, groups:]
            at = pl.ds((place * 2 + part) * groups, groups)
            for k in range(blocks):
                both = [summed[k, half] + pltpu.roll(summed[k, half], groups // 2, 0) for half in range(2)]
                product_ref[at, k * LANES : (k + 1) * LANES] = jnp.where(upper, both[0], both[1])

    out_width = outs[0].shape[1]
    column = lax.broadcasted_iota(jnp.int32, (product_ref.shape[1], out_width), 0)
    lane = lax.broadcasted_iota(jnp.int32, (product_ref.shape[1], out_width), 1)
    collect = jnp.where(column // LOOK_RG == lane % looks, 1.0, 0.0).astype(jnp.bfloat16)
    high, low = halves(product_ref[...])
    total = (dot(high, collect) + dot(low, collect)) * (1.0 / (LOOK_AZ * LOOK_RG))
    total = total.reshape(len(pairs), 2, groups, out_width)
    own_lane = lax.broadcasted_iota(jnp.int32, (groups, out_width), 1) // looks
    for step, out_ref in enumerate(outs):
        value = jnp.zeros((groups, out_width), jnp.float32)
        for place, pair in enumerate(pairs):
            if step in pair:
                other = pair[1] if pair[0] == step else pair[0]
                lag = (date ^ reach(other, dates)) - (date ^ reach(step, dates))
                for part in range(2):
                    signed = -total[place, part] if part == 1 and pair[1] == step else total[place, part]
                    value = jnp.where(own_lane == (lag - 1) * 2 + part, signed, value)
        out_ref[...] = value


def place_kernel(used_lags, looks, *refs):
    received, out_ref = refs[:-1][::-1], refs[-1]
    groups, columns = out_ref.shape[2:]
    date = lax.axis_index("date")
    lane = lax.broadcasted_iota(jnp.int32, (groups, columns), 1) // looks
    here = [lane == (date ^ step) for step in range(len(received))]
    each = columns // looks
    for part in range(2):
        for lag in range(used_lags):
            tile, group = divmod(lag * 2 + part, each)
            value = jnp.zeros((groups, columns), jnp.float32)
            for step, recv_ref in enumerate(received):
                shift = lax.bitwise_and(looks * ((date ^ step) - group), columns - 1)
                block = pltpu.roll(recv_ref[:, tile * columns : (tile + 1) * columns], shift, 1)
                value = jnp.where(here[step], block, value)
            out_ref[part, lag] = value
        for lag in range(used_lags, out_ref.shape[1]):
            out_ref[part, lag] = jnp.zeros((groups, columns), jnp.float32)


def tiled_body(slc, offsets, kernel_index, range_shift):
    dates = lax.axis_size("date")
    lines, columns = slc.shape[2], slc.shape[3]
    chunk = columns // dates
    looks = chunk // LOOK_RG
    groups = lines // LOOK_AZ
    out_width = up(min(LAGS, dates - 1) * 2 * looks, LANES)
    vmem = pl.BlockSpec(memory_space=pltpu.VMEM)
    hbm = pl.BlockSpec(memory_space=pltpu.HBM)
    limit = pltpu.CompilerParams(vmem_limit_bytes=32 * 1024 * 1024)
    bf16 = jnp.bfloat16
    cells, offsets, kernel_index, range_shift = (
        pltpu.with_memory_space_constraint(value, pltpu.HBM)
        for value in (slc.reshape(2, lines, columns), offsets, kernel_index, range_shift)
    )
    tiles = chunk // LANES
    chunk_rows = tiles * 2 * lines

    side, halo_lines, line_taps, column_taps, held = pl.pallas_call(
        prepare_kernel,
        out_shape=[
            jax.ShapeDtypeStruct((2, lines, LANES), bf16),
            jax.ShapeDtypeStruct((2, HALO_LINES, columns), bf16),
            jax.ShapeDtypeStruct((2, 2 * HALO_LINES, lines + HALO_LINES), bf16),
            jax.ShapeDtypeStruct((2 * LANES, 2 * LANES), bf16),
            jax.ShapeDtypeStruct((2, lines, columns + 3 * LANES), bf16),
        ],
        in_specs=[hbm] * 3,
        out_specs=[vmem] * 5,
        scratch_shapes=[
            pltpu.SMEM(offsets.shape, jnp.int32),
            pltpu.SMEM(kernel_index.shape, jnp.int32),
            pltpu.SemaphoreType.DMA((4 + 4 * (lines // HALO_LINES),)),
        ],
        compiler_params=limit,
    )(offsets, kernel_index, cells)
    swap = [(0, 1), (1, 0)]
    corner = lax.ppermute(side, ("rng", "az"), [(0, 3), (1, 2), (2, 1), (3, 0)])
    side = lax.ppermute(side, "rng", swap)
    halo_lines = lax.ppermute(halo_lines, "az", swap)

    early_rows = (tiles - 1) * lines
    early = pl.pallas_call(
        functools.partial(early_kernel, tiles),
        out_shape=jax.ShapeDtypeStruct((early_rows, LANES), bf16),
        in_specs=[vmem] * 3,
        out_specs=vmem,
        compiler_params=limit,
        cost_estimate=pl.CostEstimate(flops=2_500_000_000, bytes_accessed=0, transcendentals=0),
    )(held, line_taps, column_taps)
    early = lax.ppermute(early, "date", [(i, i ^ reach(dates - 1, dates)) for i in range(dates)])
    out_rows = [chunk_rows + FOLD] * (dates - 1) + [chunk_rows + FOLD - early_rows]
    sent = pl.pallas_call(
        resample_kernel,
        out_shape=[jax.ShapeDtypeStruct((rows, LANES), bf16) for rows in out_rows],
        in_specs=[vmem] * 6,
        out_specs=[vmem] * dates,
        scratch_shapes=[
            pltpu.VMEM(((columns // LANES + 1) * 2 * lines, LANES), bf16),
            pltpu.VMEM((dates, FOLD, LANES), bf16),
        ],
        compiler_params=limit,
    )(corner, side, halo_lines, held, line_taps, column_taps)

    def exchanged(values, order):
        arrived = {0: values[0]}
        for step in order:
            arrived[step] = lax.ppermute(values[step], "date", [(i, i ^ reach(step, dates)) for i in range(dates)])
        return [arrived[step] for step in reversed(range(dates))]

    steps = range(dates - 1, 0, -1)

    chunks = exchanged(sent, steps)
    pairs = [(first, second) for first in range(dates) for second in range(first + 1, dates)]
    weights, early = pl.pallas_call(
        functools.partial(filter_kernel, pairs),
        out_shape=[
            jax.ShapeDtypeStruct((len(pairs), 2 * LANES, 4 * LANES), bf16),
            jax.ShapeDtypeStruct((chunk_rows, LANES), bf16),
        ],
        in_specs=[hbm, vmem],
        out_specs=[vmem] * 2,
        scratch_shapes=[pltpu.SMEM(range_shift.shape, jnp.float32), pltpu.SemaphoreType.DMA],
        compiler_params=limit,
        cost_estimate=pl.CostEstimate(flops=600_000_000, bytes_accessed=0, transcendentals=0),
    )(range_shift, early)
    looked = pl.pallas_call(
        functools.partial(looks_kernel, pairs, dates),
        out_shape=[jax.ShapeDtypeStruct((groups, out_width), jnp.float32)] * dates,
        in_specs=[vmem] * (2 + dates),
        out_specs=[vmem] * dates,
        scratch_shapes=[
            pltpu.VMEM((chunk_rows + FOLD, LANES), bf16),
            pltpu.VMEM((dates, chunk_rows, 2 * LANES), bf16),
            pltpu.VMEM((len(pairs) * 2 * groups, chunk), jnp.float32),
        ],
        compiler_params=limit,
    )(weights, early, *chunks)
    returned = exchanged(looked, steps)[::-1]
    returned = [returned[reach(distance, dates)] for distance in reversed(range(dates))]
    out = pl.pallas_call(
        functools.partial(place_kernel, min(LAGS, dates - 1), looks),
        out_shape=jax.ShapeDtypeStruct((2, LAGS, groups, looks * dates), jnp.float32),
        in_specs=[vmem] * dates,
        out_specs=vmem,
        compiler_params=limit,
    )(*returned)
    return out[:, None]


def body(slc, offsets, kernel_index, range_shift):
    dates, az_count = (lax.axis_size(a) for a in ("date", "az"))
    lines, columns = slc.shape[2], slc.shape[3]
    whole_tiles = columns % (dates * LANES) == 0 and columns % (dates * LOOK_RG) == 0
    one_row = columns // LOOK_RG == LANES and range_shift.shape[0] == dates
    few = dates & (dates - 1) == 0 and dates - 1 <= LAGS
    folds = lines == 2 * HALO_LINES and lax.axis_size("rng") == 2 and dates >= 4 and 2 * lines // FOLD * TAIL <= LANES
    if az_count == 2 and whole_tiles and one_row and few and folds:
        return tiled_body(slc, offsets, kernel_index, range_shift)
    return chunked_body(slc, offsets, kernel_index, range_shift)


def solution(mesh):
    return jax.shard_map(
        body,
        mesh=mesh,
        in_specs=(
            P(None, ("groups", "date"), "az", "rng"),
            P(("groups", "date"), None),
            P(("groups", "date"), None),
            P("groups"),
        ),
        out_specs=P(None, ("groups", "date"), None, "az", "rng"),
        check_vma=False,
    )
```

```python
import functools

import jax
import jax.numpy as jnp
import numpy as np
from jax import lax
from jax.experimental import pallas as pl
from jax.experimental.pallas import tpu as pltpu
from jax.sharding import PartitionSpec as P

LAGS = 8
KERNELS = 16
TAPS = 8
FILTER_HALF = 8
FILTER_TAPS = 2 * FILTER_HALF + 1
LOOK_AZ = 4
LOOK_RG = 20
LANES = 128
META = 3
UNROLLED_PAIRS = 12


def up(value, unit):
    return -(-value // unit) * unit


def kernel_table():
    position = np.arange(TAPS) - 3.0 - np.arange(KERNELS)[:, None] / KERNELS
    shaped = np.sinc(position) * (0.5 + 0.5 * np.cos(np.pi * position / 5.0))
    table = np.zeros((KERNELS, LANES), np.float32)
    table[:, :TAPS] = shaped / shaped.sum(1, keepdims=True)
    return table


def lowpass_row(width):
    t = np.arange(FILTER_TAPS) - FILTER_HALF
    row = np.zeros((1, width), np.float32)
    row[0, :FILTER_TAPS] = 0.4 * np.sinc(0.4 * t) * (0.54 + 0.46 * np.cos(np.pi * t / (FILTER_HALF + 1)))
    return row


def halves(value):
    high = value.astype(jnp.bfloat16)
    return high, (value - high.astype(jnp.float32)).astype(jnp.bfloat16)


def dot(a, b):
    return jnp.dot(a, b, preferred_element_type=jnp.float32)


def dot_nt(a, b):
    return lax.dot_general(a, b, (((1,), (1,)), ((), ())), preferred_element_type=jnp.float32)


def pack_kernel(chunk, place_ref, offsets_ref, index_ref, slc_ref, before_ref, after_ref, out_ref, wide_ref):
    columns = slc_ref.shape[1]
    wide = out_ref.shape[2]
    first = place_ref[0] == 0
    last = place_ref[0] == place_ref[1] - 1
    zero = jnp.zeros_like(before_ref[...])
    wide_ref[:, :LANES] = jnp.where(first, zero, before_ref[...])
    wide_ref[:, LANES : LANES + columns] = slc_ref[...]
    wide_ref[:, LANES + columns :] = jnp.where(last, zero, after_ref[...])
    lane = lax.broadcasted_iota(jnp.int32, (slc_ref.shape[0], wide), 1)
    numbers = [offsets_ref[0, 0], index_ref[0, 0], index_ref[0, 1]]
    for j in range(out_ref.shape[0]):
        start = LANES + chunk * j - FILTER_HALF - 3 + offsets_ref[0, 1]
        tile = lax.shift_right_logical(start, 7)
        within = lax.bitwise_and(start, LANES - 1)
        window = wide_ref[:, pl.ds(pl.multiple_of(tile * LANES, LANES), wide + LANES)].astype(jnp.float32)
        moved = pltpu.roll(window, wide + LANES - within, 1)[:, :wide]
        for slot, number in enumerate(numbers):
            moved = jnp.where(lane == wide - META + slot, number.astype(jnp.float32), moved)
        out_ref[j] = moved.astype(jnp.bfloat16)


def picked_taps(table, index):
    row = lax.broadcasted_iota(jnp.int32, table.shape, 0).astype(jnp.float32)
    return jnp.sum(jnp.where(row == index, table, 0.0), axis=0, keepdims=True)


def banded(taps, distance):
    out = jnp.zeros(distance.shape, jnp.float32)
    for q in range(TAPS):
        out = jnp.where(distance == q, taps[:, q : q + 1], out)
    return out


def pairs_kernel(chunk, pairs, *refs):
    if isinstance(pairs, int):
        table_of_pairs, refs = refs[0], refs[1:]
    shift_ref, table_ref, lowpass_ref, recv_ref, out_ref, resampled_ref, weight_ref, product_ref = refs
    sources, rows, wide = recv_ref.shape
    dates = shift_ref.shape[0]
    az_count = sources // dates
    own_lines = rows // 2
    lines = own_lines * az_count
    groups = lines // LOOK_AZ
    looks = chunk // LOOK_RG
    table = table_ref[...]
    held = resampled_ref.shape[2]

    out_row = lax.broadcasted_iota(jnp.int32, (lines, lines), 0)
    in_row = lax.broadcasted_iota(jnp.int32, (lines, lines), 1)
    line = LOOK_AZ * (out_row % groups) + out_row // groups
    line_distance = (in_row - line + 3).astype(jnp.float32)
    span = min(2 * LANES, wide)
    column_distance = (
        lax.broadcasted_iota(jnp.int32, (span, LANES), 0) - lax.broadcasted_iota(jnp.int32, (span, LANES), 1)
    ).astype(jnp.float32)
    for date in range(dates):
        numbers = recv_ref[date * az_count, 0:16, wide - LANES :].astype(jnp.float32)[0:1, LANES - META :]
        line_offset, line_index, column_index = (numbers[:, s : s + 1] for s in range(META))
        line_taps = banded(picked_taps(table, line_index), line_distance - line_offset)
        line_taps = jnp.concatenate(halves(line_taps), axis=0)
        column_high, column_low = halves(banded(picked_taps(table, column_index), column_distance))
        moved = []
        for plane in range(2):
            rows_of = slice(plane * own_lines, (plane + 1) * own_lines)
            source = jnp.concatenate([recv_ref[date * az_count + a, rows_of, :] for a in range(az_count)], axis=0)
            both = dot(line_taps, source)
            moved.append(both[:lines] + both[lines:])
        moved_high, moved_low = halves(jnp.concatenate(moved, axis=0))
        for begin in range(0, held, LANES):
            end = min(begin + span, wide)
            taken = end - begin
            total = dot(moved_high[:, begin:end], column_high[:taken])
            total += dot(moved_low[:, begin:end], column_high[:taken])
            total += dot(moved_high[:, begin:end], column_low[:taken])
            resampled_ref[date, :, begin : begin + LANES] = total.astype(jnp.bfloat16)

    window = lowpass_ref[...]
    spacing = lax.broadcasted_iota(jnp.int32, window.shape, 1).astype(jnp.float32) - FILTER_HALF
    span = min(2 * LANES, held)

    def one_pair(place, own, other):
        gap = shift_ref[own] - shift_ref[other]
        angle = jnp.where(jnp.abs(spacing) <= FILTER_HALF, jnp.pi * gap * spacing, 0.0)
        for part, taps in enumerate((window * jnp.cos(angle), window * jnp.sin(angle))):
            spread = jnp.broadcast_to(taps, (LANES, 2 * LANES))
            spread = pltpu.roll(spread, 0, 1, stride=1, stride_axis=0)
            high, low = halves(spread)
            weight_ref[0, part * LANES : (part + 1) * LANES, :] = high
            weight_ref[1, part * LANES : (part + 1) * LANES, :] = low
        both = jnp.concatenate([resampled_ref[own], resampled_ref[other]], axis=0)
        for begin in range(0, up(chunk, LANES), LANES):
            end = min(begin + span, held)
            taken = end - begin
            total = dot_nt(both[:, begin:end], weight_ref[0, :, :taken])
            total += dot_nt(both[:, begin:end], weight_ref[1, :, :taken])
            cos, sin = total[:, :LANES], total[:, LANES:]
            re, im = slice(0, lines), slice(lines, 2 * lines)
            master_re = cos[re] + sin[im]
            master_im = cos[im] - sin[re]
            re, im = slice(2 * lines, 3 * lines), slice(3 * lines, 4 * lines)
            partner_re = cos[re] - sin[im]
            partner_im = cos[im] + sin[re]
            for part, product in enumerate(
                (
                    master_re * partner_re + master_im * partner_im,
                    master_im * partner_re - master_re * partner_im,
                )
            ):
                summed = sum(product[k * groups : (k + 1) * groups] for k in range(LOOK_AZ))
                product_ref[place, part, :, begin : begin + LANES] = summed

    if isinstance(pairs, int):
        count = pairs

        def step(place, carry):
            one_pair(place, table_of_pairs[place, 0], table_of_pairs[place, 1])
            return carry

        lax.fori_loop(0, count, step, 0)
    else:
        count = len(pairs)
        for place, (own, other) in enumerate(pairs):
            one_pair(place, own, other)

    out_width = out_ref.shape[2]
    column = lax.broadcasted_iota(jnp.int32, (product_ref.shape[3], out_width), 0)
    lane = lax.broadcasted_iota(jnp.int32, (product_ref.shape[3], out_width), 1)
    collect = jnp.where(column // LOOK_RG == lane % looks, 1.0, 0.0).astype(jnp.bfloat16)
    high, low = halves(product_ref[...].reshape(count * 2 * groups, product_ref.shape[3]))
    total = (dot(high, collect) + dot(low, collect)) * (1.0 / (LOOK_AZ * LOOK_RG))
    total = total.reshape(count, 2, groups, out_width)
    own_lane = lax.broadcasted_iota(jnp.int32, (groups, out_width), 1) // looks
    place = 0
    for own in range(dates):
        value = jnp.zeros((groups, out_width), jnp.float32)
        for lag in range(min(LAGS, dates - 1 - own)):
            for part in range(2):
                value = jnp.where(own_lane == lag * 2 + part, total[place, part], value)
            place += 1
        out_ref[own * az_count : (own + 1) * az_count] = value.reshape(az_count, groups // az_count, out_width)


def unpack_kernel(used_lags, looks, recv_ref, out_ref):
    sources, groups, width = recv_ref.shape
    columns = out_ref.shape[-1]
    lane = lax.broadcasted_iota(jnp.int32, (groups, columns), 1) // looks
    out_ref[...] = jnp.zeros_like(out_ref)
    for lag in range(used_lags):
        for part in range(2):
            value = jnp.zeros((groups, columns), jnp.float32)
            for source in range(sources):
                block = recv_ref[source]
                if width != columns:
                    block = block[:, :columns]
                shift = looks * (source - lag * 2 - part) % columns
                if shift:
                    block = pltpu.roll(block, shift, 1)
                value = jnp.where(lane == source, block, value)
            out_ref[part, lag] = value


def chunked_body(slc, offsets, kernel_index, range_shift):
    axes = ("date", "az")
    date_count, az_count, rng_count = (lax.axis_size(a) for a in ("date", "az", "rng"))
    peers = date_count * az_count
    lines, columns = slc.shape[2], slc.shape[3]
    dates = range_shift.shape[0]
    chunk = columns // peers
    looks = chunk // LOOK_RG
    groups = lines * az_count // LOOK_AZ
    wide = up(chunk + 2 * FILTER_HALF + TAPS - 1 + META, LANES)
    held = up(chunk + 2 * FILTER_HALF, LANES)
    used_lags = min(LAGS, dates - 1)
    out_width = up(used_lags * 2 * looks, LANES)
    vmem = pl.BlockSpec(memory_space=pltpu.VMEM)
    smem = pl.BlockSpec(memory_space=pltpu.SMEM)
    limit = pltpu.CompilerParams(vmem_limit_bytes=32 * 1024 * 1024)

    cells = slc.reshape(2 * lines, columns)
    place = lax.axis_index("rng")
    if rng_count == 2:
        edge = jnp.where(place == 0, cells[:, columns - LANES :], cells[:, :LANES])
        before = after = lax.ppermute(edge, "rng", [(0, 1), (1, 0)])
    else:
        forth = [(i, i + 1) for i in range(rng_count - 1)]
        before = lax.ppermute(cells[:, columns - LANES :], "rng", forth)
        after = lax.ppermute(cells[:, :LANES], "rng", [(b, a) for a, b in forth])

    packed = pl.pallas_call(
        functools.partial(pack_kernel, chunk),
        out_shape=jax.ShapeDtypeStruct((peers, 2 * lines, wide), jnp.bfloat16),
        in_specs=[smem] * 3 + [vmem] * 3,
        out_specs=vmem,
        scratch_shapes=[pltpu.VMEM((2 * lines, columns + 2 * LANES), jnp.bfloat16)],
        compiler_params=limit,
    )(jnp.stack([place, rng_count]).astype(jnp.int32), offsets, kernel_index, cells, before, after)
    arrived = lax.all_to_all(packed, axes, 0, 0, tiled=True)

    pairs = [(own, own + lag) for own in range(dates) for lag in range(1, LAGS + 1) if own + lag < dates]
    count = len(pairs)
    first = [jnp.asarray(np.array(pairs, np.int32))] if count > UNROLLED_PAIRS else []
    looked = pl.pallas_call(
        functools.partial(pairs_kernel, chunk, count if first else pairs),
        out_shape=jax.ShapeDtypeStruct((peers, groups // az_count, out_width), jnp.float32),
        in_specs=[smem] * len(first) + [smem] + [vmem] * 3,
        out_specs=vmem,
        scratch_shapes=[
            pltpu.VMEM((dates, 4 * (groups * LOOK_AZ) // 2, held), jnp.bfloat16),
            pltpu.VMEM((2, 2 * LANES, 2 * LANES), jnp.bfloat16),
            pltpu.VMEM((count, 2, groups, up(chunk, LANES)), jnp.float32),
        ],
        compiler_params=limit,
    )(*first, range_shift, jnp.asarray(kernel_table()), jnp.asarray(lowpass_row(2 * LANES)), arrived)
    returned = lax.all_to_all(looked, axes, 0, 0, tiled=True)

    out = pl.pallas_call(
        functools.partial(unpack_kernel, used_lags, looks),
        out_shape=jax.ShapeDtypeStruct((2, LAGS, groups // az_count, looks * peers), jnp.float32),
        in_specs=[vmem],
        out_specs=vmem,
        compiler_params=limit,
    )(returned)
    return out[:, None]


HALO_LINES = 16
FOLD = 16
TAIL = 2 * FILTER_HALF


def reach(step, dates):
    return {dates - 1: dates // 2, dates // 2: dates - 1}.get(step, step)


def sinc(value):
    angle = jnp.pi * value
    return jnp.where(angle == 0.0, 1.0, jnp.sin(angle) / jnp.where(angle == 0.0, 1.0, angle))


def tap_row(index):
    lane = lax.broadcasted_iota(jnp.int32, (1, LANES), 1)
    position = lane.astype(jnp.float32) - 3.0 - index.astype(jnp.float32) / KERNELS
    shaped = sinc(position) * (0.5 + 0.5 * jnp.cos(jnp.pi * position / 5.0))
    shaped = jnp.where(lane < TAPS, shaped, 0.0)
    return shaped / jnp.sum(shaped, axis=1, keepdims=True)


def row_line(row, az):
    quarter = HALO_LINES // LOOK_AZ
    within = row % HALO_LINES
    return HALO_LINES * ((row // HALO_LINES) ^ az) + LOOK_AZ * (within % quarter) + within // quarter


def prepare_kernel(offsets_hbm, index_hbm, slc_ref, side_ref, lines_ref, line_ref, column_ref, held_ref, offsets_ref, index_ref, semaphores):
    lines, columns = slc_ref.shape[1:]
    az = lax.axis_index("az")
    row = pl.multiple_of((1 - az) * (lines - HALO_LINES), HALO_LINES)
    edge = pl.multiple_of((1 - lax.axis_index("rng")) * (columns - LANES), LANES)
    nearest, outermost = pl.ds(row, HALO_LINES), pl.ds(edge, LANES)
    moves = [
        (offsets_hbm, offsets_ref),
        (index_hbm, index_ref),
        (slc_ref.at[:, :, outermost], side_ref),
        (slc_ref.at[:, nearest, :], lines_ref),
    ]
    for plane in range(2):
        for part in range(lines // HALO_LINES):
            for side in range(2):
                at = pl.ds(part * HALO_LINES, HALO_LINES)
                source = slc_ref.at[plane, at, pl.ds(side * columns // 2, columns // 2)]
                moves.append((source, held_ref.at[plane, at, pl.ds(LANES + side * columns // 2, columns // 2)]))
    copies = [pltpu.make_async_copy(a, b, semaphores.at[i]) for i, (a, b) in enumerate(moves)]
    for copy in copies:
        copy.start()
    held_ref[:, :, :LANES] = jnp.zeros((2, lines, LANES), held_ref.dtype)
    held_ref[:, :, LANES + columns :] = jnp.zeros((2, lines, 2 * LANES), held_ref.dtype)
    copies[0].wait()
    copies[1].wait()
    for half in range(2):
        shape = (HALO_LINES, lines + HALO_LINES)
        line = row_line(lax.broadcasted_iota(jnp.int32, shape, 0) + half * HALO_LINES, az)
        place = lax.broadcasted_iota(jnp.int32, shape, 1)
        source = jnp.where(place < lines, place, place + jnp.where(az == 0, 0, -lines - HALO_LINES))
        taps = banded(tap_row(index_ref[0, 0]), source - line - offsets_ref[0, 0] + 3)
        line_ref[half] = jnp.concatenate(halves(taps), axis=0)
    shape = (2 * LANES, LANES)
    distance = lax.broadcasted_iota(jnp.int32, shape, 0) - lax.broadcasted_iota(jnp.int32, shape, 1)
    distance = distance - (LANES // 2 - FILTER_HALF - 3) - offsets_ref[0, 1]
    taps = banded(tap_row(index_ref[0, 1]), distance)
    column_ref[...] = jnp.concatenate(halves(taps), axis=1)
    for copy in copies[2:]:
        copy.wait()


def along_range(moved, column_ref, tiles):
    high, low = halves(pltpu.roll(moved, moved.shape[1] - LANES // 2, 1))
    starts = range(0, tiles * LANES, LANES)
    high = jnp.concatenate([high[:, s : s + 2 * LANES] for s in starts], axis=0)
    low = jnp.concatenate([low[:, s : s + 2 * LANES] for s in starts], axis=0)
    total = dot(high, column_ref[...])
    return total[:, :LANES] + total[:, LANES:] + dot(low, column_ref[:, :LANES])


def early_kernel(tiles, held_ref, line_ref, column_ref, out_ref):
    lines = held_ref.shape[1]
    early = out_ref.shape[0] // (2 * HALO_LINES)
    dates = lax.axis_size("date")
    chunk = lax.axis_index("date") ^ reach(dates - 1, dates)
    begin = pl.multiple_of((chunk * tiles + lax.axis_index("rng")) * LANES, LANES)
    moved = []
    for plane in range(2):
        both = dot(line_ref[0, :, :lines], held_ref[plane, :, pl.ds(begin, (early + 2) * LANES)])
        moved.append(both[:HALO_LINES] + both[HALO_LINES:])
    moved = jnp.concatenate(moved, axis=0)
    out_ref[...] = along_range(moved, column_ref, early).astype(jnp.bfloat16)


def resample_kernel(corner_ref, side_ref, lines_ref, held_ref, line_ref, column_ref, *outs):
    outs, tiles_ref, tails_ref = outs[:-2], outs[-2], outs[-1]
    lines, width = held_ref.shape[1:]
    width -= LANES
    block = lax.axis_index("rng")
    nearest = pl.multiple_of(lax.axis_index("az") * (lines - HALO_LINES), HALO_LINES)
    taps = jnp.concatenate([line_ref[0], line_ref[1]], axis=0)
    moved = [[], []]
    for plane in range(2):
        own = jnp.concatenate([side_ref[plane], held_ref[plane, :, LANES : width - LANES], side_ref[plane]], axis=1)
        corner = corner_ref[plane, pl.ds(nearest, HALO_LINES), :]
        halo = jnp.concatenate([corner, lines_ref[plane], corner], axis=1)
        both = dot(taps, jnp.concatenate([own, halo], axis=0))
        for half in range(2):
            at = 2 * half * HALO_LINES
            moved[half].append(both[at : at + HALO_LINES] + both[at + HALO_LINES : at + 2 * HALO_LINES])
    moved = jnp.concatenate(moved[0] + moved[1], axis=0)
    left = jnp.where(block > 0, moved[:, :LANES], 0.0)
    right = jnp.where(block == 0, moved[:, width - LANES :], 0.0)
    moved = jnp.concatenate([left, moved[:, LANES : width - LANES], right, jnp.zeros_like(right)], axis=1)
    total = along_range(moved, column_ref, width // LANES - 1)
    rows = 2 * lines
    tiles_ref[...] = total.astype(jnp.bfloat16)
    chunk_rows = outs[0].shape[0] - FOLD
    lane = lax.broadcasted_iota(jnp.int32, (FOLD, LANES), 1) // TAIL
    for chunk in range(len(outs)):
        begin = (chunk + 1) * chunk_rows
        folded = total[begin : begin + FOLD]
        for part in range(1, rows // FOLD):
            value = pltpu.roll(total[begin + part * FOLD : begin + (part + 1) * FOLD], part * TAIL, 1)
            folded = jnp.where(lane == part, value, folded)
        tails_ref[chunk] = folded.astype(jnp.bfloat16)
    date = lax.axis_index("date")
    for step, out_ref in enumerate(outs[:-1]):
        chunk = date ^ reach(step, len(outs))
        out_ref[:chunk_rows] = tiles_ref[pl.ds(pl.multiple_of(chunk * chunk_rows, FOLD), chunk_rows), :]
        out_ref[chunk_rows:] = tails_ref[chunk]
    out_ref = outs[-1]
    chunk = date ^ reach(len(outs) - 1, len(outs))
    early = chunk_rows // rows - 1
    for tile in range(early):
        begin = pl.multiple_of(chunk * chunk_rows + (tile + block) * rows + lines, FOLD)
        out_ref[tile * lines : (tile + 1) * lines] = tiles_ref[pl.ds(begin, lines), :]
    begin = pl.multiple_of(chunk * chunk_rows + (1 - block) * early * rows, FOLD)
    out_ref[early * lines : early * lines + rows] = tiles_ref[pl.ds(begin, rows), :]
    out_ref[early * lines + rows :] = tails_ref[chunk]


def filter_kernel(pairs, shift_hbm, early_ref, out_ref, spread_ref, shift_ref, semaphore):
    copy = pltpu.make_async_copy(shift_hbm, shift_ref, semaphore)
    copy.start()
    lines = 2 * HALO_LINES
    spread_ref[...] = jnp.zeros_like(spread_ref)
    for tile in range(early_ref.shape[0] // lines):
        begin = pl.multiple_of((tile + lax.axis_index("rng")) * 2 * lines, FOLD)
        spread_ref[pl.ds(begin, lines), :] = early_ref[tile * lines : (tile + 1) * lines]
    date = lax.axis_index("date")
    spacing = lax.broadcasted_iota(jnp.int32, (1, 2 * LANES), 1).astype(jnp.float32) - FILTER_HALF
    window = 0.4 * sinc(0.4 * spacing) * (0.54 + 0.46 * jnp.cos(jnp.pi * spacing / (FILTER_HALF + 1)))
    window = jnp.where(jnp.abs(spacing) <= FILTER_HALF, window, 0.0)
    copy.wait()
    for place, (first, second) in enumerate(pairs):
        dates = shift_ref.shape[0]
        gap = shift_ref[date ^ reach(first, dates)] - shift_ref[date ^ reach(second, dates)]
        angle = jnp.where(jnp.abs(spacing) <= FILTER_HALF, jnp.pi * gap * spacing, 0.0)
        for part, taps in enumerate((window * jnp.cos(angle), window * jnp.sin(angle))):
            spread = jnp.broadcast_to(taps, (LANES, 2 * LANES))
            spread = pltpu.roll(spread, 0, 1, stride=1, stride_axis=0)
            high, low = halves(spread)
            out_ref[place, part * LANES : (part + 1) * LANES, : 2 * LANES] = high
            out_ref[place, part * LANES : (part + 1) * LANES, 2 * LANES :] = low


def looks_kernel(pairs, dates, weight_ref, *refs):
    early_ref, chunks, outs = refs[0], list(refs[1 : dates + 1][::-1]), refs[dates + 1 : 2 * dates + 1]
    whole_ref, window_ref, product_ref = refs[-3:]
    groups, lines = outs[0].shape[0], outs[0].shape[0] * LOOK_AZ
    rows = 2 * lines
    blocks = (chunks[0].shape[0] - FOLD) // rows
    looks = blocks * LANES // LOOK_RG
    date = lax.axis_index("date")
    block = lax.axis_index("rng")
    early = blocks - 1
    whole_ref[: blocks * rows] = early_ref[...]
    for tile in range(early):
        begin = pl.multiple_of((tile + block) * rows, FOLD)
        whole_ref[pl.ds(begin + lines, lines), :] = chunks[-1][tile * lines : (tile + 1) * lines]
    begin = pl.multiple_of((1 - block) * early * rows, FOLD)
    whole_ref[pl.ds(begin, rows), :] = chunks[-1][early * lines : early * lines + rows]
    whole_ref[blocks * rows :] = chunks[-1][early * lines + rows :]
    chunks[-1] = whole_ref
    az = lax.axis_index("az")
    upper = lax.broadcasted_iota(jnp.int32, (groups, LANES), 0) // (groups // 2) == az
    for step, chunk_ref in enumerate(chunks):
        window_ref[step, :, :LANES] = chunk_ref[: blocks * rows]
        window_ref[step, : (blocks - 1) * rows, LANES:] = chunk_ref[rows : blocks * rows]
        folded = chunk_ref[blocks * rows :].astype(jnp.float32)
        for part in range(rows // FOLD):
            value = pltpu.roll(folded, LANES - part * TAIL, 1) if part else folded
            at = pl.ds((blocks - 1) * rows + part * FOLD, FOLD)
            window_ref[step, at, LANES:] = value.astype(jnp.bfloat16)
    for place, (first, second) in enumerate(pairs):
        def filtered(step):
            window = window_ref[step]
            total = dot_nt(jnp.concatenate([window, window], axis=1), weight_ref[place])
            total = total.reshape(blocks, 2, 2, HALO_LINES, 2 * LANES)
            re, im = total[:, :, 0], total[:, :, 1]
            return re[..., :LANES], im[..., :LANES], re[..., LANES:], im[..., LANES:]

        cos_re, cos_im, sin_re, sin_im = filtered(first)
        master_re, master_im = cos_re + sin_im, cos_im - sin_re
        cos_re, cos_im, sin_re, sin_im = filtered(second)
        partner_re, partner_im = cos_re - sin_im, cos_im + sin_re
        for part, product in enumerate(
            (
                master_re * partner_re + master_im * partner_im,
                master_im * partner_re - master_re * partner_im,
            )
        ):
            summed = product[:, :, :groups] + product[:, :, groups:]
            at = pl.ds((place * 2 + part) * groups, groups)
            for k in range(blocks):
                both = [summed[k, half] + pltpu.roll(summed[k, half], groups // 2, 0) for half in range(2)]
                product_ref[at, k * LANES : (k + 1) * LANES] = jnp.where(upper, both[0], both[1])

    out_width = outs[0].shape[1]
    column = lax.broadcasted_iota(jnp.int32, (product_ref.shape[1], out_width), 0)
    lane = lax.broadcasted_iota(jnp.int32, (product_ref.shape[1], out_width), 1)
    collect = jnp.where(column // LOOK_RG == lane % looks, 1.0, 0.0).astype(jnp.bfloat16)
    high, low = halves(product_ref[...])
    total = (dot(high, collect) + dot(low, collect)) * (1.0 / (LOOK_AZ * LOOK_RG))
    total = total.reshape(len(pairs), 2, groups, out_width)
    own_lane = lax.broadcasted_iota(jnp.int32, (groups, out_width), 1) // looks
    for step, out_ref in enumerate(outs):
        value = jnp.zeros((groups, out_width), jnp.float32)
        for place, pair in enumerate(pairs):
            if step in pair:
                other = pair[1] if pair[0] == step else pair[0]
                lag = (date ^ reach(other, dates)) - (date ^ reach(step, dates))
                for part in range(2):
                    signed = -total[place, part] if part == 1 and pair[1] == step else total[place, part]
                    value = jnp.where(own_lane == (lag - 1) * 2 + part, signed, value)
        out_ref[...] = value


def place_kernel(used_lags, looks, *refs):
    received, out_ref = refs[:-1][::-1], refs[-1]
    groups, columns = out_ref.shape[2:]
    date = lax.axis_index("date")
    lane = lax.broadcasted_iota(jnp.int32, (groups, columns), 1) // looks
    here = [lane == (date ^ step) for step in range(len(received))]
    each = columns // looks
    for part in range(2):
        for lag in range(used_lags):
            tile, group = divmod(lag * 2 + part, each)
            value = jnp.zeros((groups, columns), jnp.float32)
            for step, recv_ref in enumerate(received):
                shift = lax.bitwise_and(looks * ((date ^ step) - group), columns - 1)
                block = pltpu.roll(recv_ref[:, tile * columns : (tile + 1) * columns], shift, 1)
                value = jnp.where(here[step], block, value)
            out_ref[part, lag] = value
        for lag in range(used_lags, out_ref.shape[1]):
            out_ref[part, lag] = jnp.zeros((groups, columns), jnp.float32)


def tiled_body(slc, offsets, kernel_index, range_shift):
    dates = lax.axis_size("date")
    lines, columns = slc.shape[2], slc.shape[3]
    chunk = columns // dates
    looks = chunk // LOOK_RG
    groups = lines // LOOK_AZ
    out_width = up(min(LAGS, dates - 1) * 2 * looks, LANES)
    vmem = pl.BlockSpec(memory_space=pltpu.VMEM)
    hbm = pl.BlockSpec(memory_space=pltpu.HBM)
    limit = pltpu.CompilerParams(vmem_limit_bytes=32 * 1024 * 1024)
    bf16 = jnp.bfloat16
    cells, offsets, kernel_index, range_shift = (
        pltpu.with_memory_space_constraint(value, pltpu.HBM)
        for value in (slc.reshape(2, lines, columns), offsets, kernel_index, range_shift)
    )
    tiles = chunk // LANES
    chunk_rows = tiles * 2 * lines

    side, halo_lines, line_taps, column_taps, held = pl.pallas_call(
        prepare_kernel,
        out_shape=[
            jax.ShapeDtypeStruct((2, lines, LANES), bf16),
            jax.ShapeDtypeStruct((2, HALO_LINES, columns), bf16),
            jax.ShapeDtypeStruct((2, 2 * HALO_LINES, lines + HALO_LINES), bf16),
            jax.ShapeDtypeStruct((2 * LANES, 2 * LANES), bf16),
            jax.ShapeDtypeStruct((2, lines, columns + 3 * LANES), bf16),
        ],
        in_specs=[hbm] * 3,
        out_specs=[vmem] * 5,
        scratch_shapes=[
            pltpu.SMEM(offsets.shape, jnp.int32),
            pltpu.SMEM(kernel_index.shape, jnp.int32),
            pltpu.SemaphoreType.DMA((4 + 4 * (lines // HALO_LINES),)),
        ],
        compiler_params=limit,
    )(offsets, kernel_index, cells)
    swap = [(0, 1), (1, 0)]
    corner = lax.ppermute(side, ("rng", "az"), [(0, 3), (1, 2), (2, 1), (3, 0)])
    side = lax.ppermute(side, "rng", swap)
    halo_lines = lax.ppermute(halo_lines, "az", swap)

    early_rows = (tiles - 1) * lines
    early = pl.pallas_call(
        functools.partial(early_kernel, tiles),
        out_shape=jax.ShapeDtypeStruct((early_rows, LANES), bf16),
        in_specs=[vmem] * 3,
        out_specs=vmem,
        compiler_params=limit,
        cost_estimate=pl.CostEstimate(flops=2_500_000_000, bytes_accessed=0, transcendentals=0),
    )(held, line_taps, column_taps)
    early = lax.ppermute(early, "date", [(i, i ^ reach(dates - 1, dates)) for i in range(dates)])
    out_rows = [chunk_rows + FOLD] * (dates - 1) + [chunk_rows + FOLD - early_rows]
    sent = pl.pallas_call(
        resample_kernel,
        out_shape=[jax.ShapeDtypeStruct((rows, LANES), bf16) for rows in out_rows],
        in_specs=[vmem] * 6,
        out_specs=[vmem] * dates,
        scratch_shapes=[
            pltpu.VMEM(((columns // LANES + 1) * 2 * lines, LANES), bf16),
            pltpu.VMEM((dates, FOLD, LANES), bf16),
        ],
        compiler_params=limit,
        cost_estimate=pl.CostEstimate(flops=800_000_000, bytes_accessed=0, transcendentals=0),
    )(corner, side, halo_lines, held, line_taps, column_taps)

    def exchanged(values, order):
        arrived = {0: values[0]}
        for step in order:
            arrived[step] = lax.ppermute(values[step], "date", [(i, i ^ reach(step, dates)) for i in range(dates)])
        return [arrived[step] for step in reversed(range(dates))]

    steps = range(dates - 1, 0, -1)

    chunks = exchanged(sent, steps)
    pairs = [(first, second) for first in range(dates) for second in range(first + 1, dates)]
    weights, early = pl.pallas_call(
        functools.partial(filter_kernel, pairs),
        out_shape=[
            jax.ShapeDtypeStruct((len(pairs), 2 * LANES, 4 * LANES), bf16),
            jax.ShapeDtypeStruct((chunk_rows, LANES), bf16),
        ],
        in_specs=[hbm, vmem],
        out_specs=[vmem] * 2,
        scratch_shapes=[pltpu.SMEM(range_shift.shape, jnp.float32), pltpu.SemaphoreType.DMA],
        compiler_params=limit,
        cost_estimate=pl.CostEstimate(flops=1_100_000_000, bytes_accessed=0, transcendentals=0),
    )(range_shift, early)
    looked = pl.pallas_call(
        functools.partial(looks_kernel, pairs, dates),
        out_shape=[jax.ShapeDtypeStruct((groups, out_width), jnp.float32)] * dates,
        in_specs=[vmem] * (2 + dates),
        out_specs=[vmem] * dates,
        scratch_shapes=[
            pltpu.VMEM((chunk_rows + FOLD, LANES), bf16),
            pltpu.VMEM((dates, chunk_rows, 2 * LANES), bf16),
            pltpu.VMEM((len(pairs) * 2 * groups, chunk), jnp.float32),
        ],
        compiler_params=limit,
    )(weights, early, *chunks)
    returned = exchanged(looked, steps)[::-1]
    returned = [returned[reach(distance, dates)] for distance in reversed(range(dates))]
    out = pl.pallas_call(
        functools.partial(place_kernel, min(LAGS, dates - 1), looks),
        out_shape=jax.ShapeDtypeStruct((2, LAGS, groups, looks * dates), jnp.float32),
        in_specs=[vmem] * dates,
        out_specs=vmem,
        compiler_params=limit,
    )(*returned)
    return out[:, None]


def body(slc, offsets, kernel_index, range_shift):
    dates, az_count = (lax.axis_size(a) for a in ("date", "az"))
    lines, columns = slc.shape[2], slc.shape[3]
    whole_tiles = columns % (dates * LANES) == 0 and columns % (dates * LOOK_RG) == 0
    one_row = columns // LOOK_RG == LANES and range_shift.shape[0] == dates
    few = dates & (dates - 1) == 0 and dates - 1 <= LAGS
    folds = lines == 2 * HALO_LINES and lax.axis_size("rng") == 2 and dates >= 4 and 2 * lines // FOLD * TAIL <= LANES
    if az_count == 2 and whole_tiles and one_row and few and folds:
        return tiled_body(slc, offsets, kernel_index, range_shift)
    return chunked_body(slc, offsets, kernel_index, range_shift)


def solution(mesh):
    return jax.shard_map(
        body,
        mesh=mesh,
        in_specs=(
            P(None, ("groups", "date"), "az", "rng"),
            P(("groups", "date"), None),
            P(("groups", "date"), None),
            P("groups"),
        ),
        out_specs=P(None, ("groups", "date"), None, "az", "rng"),
        check_vma=False,
    )
```

```python
import functools

import jax
import jax.numpy as jnp
import numpy as np
from jax import lax
from jax.experimental import pallas as pl
from jax.experimental.pallas import tpu as pltpu
from jax.sharding import PartitionSpec as P

LAGS = 8
KERNELS = 16
TAPS = 8
FILTER_HALF = 8
FILTER_TAPS = 2 * FILTER_HALF + 1
LOOK_AZ = 4
LOOK_RG = 20
LANES = 128
META = 3
UNROLLED_PAIRS = 12


def up(value, unit):
    return -(-value // unit) * unit


def kernel_table():
    position = np.arange(TAPS) - 3.0 - np.arange(KERNELS)[:, None] / KERNELS
    shaped = np.sinc(position) * (0.5 + 0.5 * np.cos(np.pi * position / 5.0))
    table = np.zeros((KERNELS, LANES), np.float32)
    table[:, :TAPS] = shaped / shaped.sum(1, keepdims=True)
    return table


def lowpass_row(width):
    t = np.arange(FILTER_TAPS) - FILTER_HALF
    row = np.zeros((1, width), np.float32)
    row[0, :FILTER_TAPS] = 0.4 * np.sinc(0.4 * t) * (0.54 + 0.46 * np.cos(np.pi * t / (FILTER_HALF + 1)))
    return row


def halves(value):
    high = value.astype(jnp.bfloat16)
    return high, (value - high.astype(jnp.float32)).astype(jnp.bfloat16)


def dot(a, b):
    return jnp.dot(a, b, preferred_element_type=jnp.float32)


def dot_nt(a, b):
    return lax.dot_general(a, b, (((1,), (1,)), ((), ())), preferred_element_type=jnp.float32)


def pack_kernel(chunk, place_ref, offsets_ref, index_ref, slc_ref, before_ref, after_ref, out_ref, wide_ref):
    columns = slc_ref.shape[1]
    wide = out_ref.shape[2]
    first = place_ref[0] == 0
    last = place_ref[0] == place_ref[1] - 1
    zero = jnp.zeros_like(before_ref[...])
    wide_ref[:, :LANES] = jnp.where(first, zero, before_ref[...])
    wide_ref[:, LANES : LANES + columns] = slc_ref[...]
    wide_ref[:, LANES + columns :] = jnp.where(last, zero, after_ref[...])
    lane = lax.broadcasted_iota(jnp.int32, (slc_ref.shape[0], wide), 1)
    numbers = [offsets_ref[0, 0], index_ref[0, 0], index_ref[0, 1]]
    for j in range(out_ref.shape[0]):
        start = LANES + chunk * j - FILTER_HALF - 3 + offsets_ref[0, 1]
        tile = lax.shift_right_logical(start, 7)
        within = lax.bitwise_and(start, LANES - 1)
        window = wide_ref[:, pl.ds(pl.multiple_of(tile * LANES, LANES), wide + LANES)].astype(jnp.float32)
        moved = pltpu.roll(window, wide + LANES - within, 1)[:, :wide]
        for slot, number in enumerate(numbers):
            moved = jnp.where(lane == wide - META + slot, number.astype(jnp.float32), moved)
        out_ref[j] = moved.astype(jnp.bfloat16)


def picked_taps(table, index):
    row = lax.broadcasted_iota(jnp.int32, table.shape, 0).astype(jnp.float32)
    return jnp.sum(jnp.where(row == index, table, 0.0), axis=0, keepdims=True)


def banded(taps, distance):
    out = jnp.zeros(distance.shape, jnp.float32)
    for q in range(TAPS):
        out = jnp.where(distance == q, taps[:, q : q + 1], out)
    return out


def pairs_kernel(chunk, pairs, *refs):
    if isinstance(pairs, int):
        table_of_pairs, refs = refs[0], refs[1:]
    shift_ref, table_ref, lowpass_ref, recv_ref, out_ref, resampled_ref, weight_ref, product_ref = refs
    sources, rows, wide = recv_ref.shape
    dates = shift_ref.shape[0]
    az_count = sources // dates
    own_lines = rows // 2
    lines = own_lines * az_count
    groups = lines // LOOK_AZ
    looks = chunk // LOOK_RG
    table = table_ref[...]
    held = resampled_ref.shape[2]

    out_row = lax.broadcasted_iota(jnp.int32, (lines, lines), 0)
    in_row = lax.broadcasted_iota(jnp.int32, (lines, lines), 1)
    line = LOOK_AZ * (out_row % groups) + out_row // groups
    line_distance = (in_row - line + 3).astype(jnp.float32)
    span = min(2 * LANES, wide)
    column_distance = (
        lax.broadcasted_iota(jnp.int32, (span, LANES), 0) - lax.broadcasted_iota(jnp.int32, (span, LANES), 1)
    ).astype(jnp.float32)
    for date in range(dates):
        numbers = recv_ref[date * az_count, 0:16, wide - LANES :].astype(jnp.float32)[0:1, LANES - META :]
        line_offset, line_index, column_index = (numbers[:, s : s + 1] for s in range(META))
        line_taps = banded(picked_taps(table, line_index), line_distance - line_offset)
        line_taps = jnp.concatenate(halves(line_taps), axis=0)
        column_high, column_low = halves(banded(picked_taps(table, column_index), column_distance))
        moved = []
        for plane in range(2):
            rows_of = slice(plane * own_lines, (plane + 1) * own_lines)
            source = jnp.concatenate([recv_ref[date * az_count + a, rows_of, :] for a in range(az_count)], axis=0)
            both = dot(line_taps, source)
            moved.append(both[:lines] + both[lines:])
        moved_high, moved_low = halves(jnp.concatenate(moved, axis=0))
        for begin in range(0, held, LANES):
            end = min(begin + span, wide)
            taken = end - begin
            total = dot(moved_high[:, begin:end], column_high[:taken])
            total += dot(moved_low[:, begin:end], column_high[:taken])
            total += dot(moved_high[:, begin:end], column_low[:taken])
            resampled_ref[date, :, begin : begin + LANES] = total.astype(jnp.bfloat16)

    window = lowpass_ref[...]
    spacing = lax.broadcasted_iota(jnp.int32, window.shape, 1).astype(jnp.float32) - FILTER_HALF
    span = min(2 * LANES, held)

    def one_pair(place, own, other):
        gap = shift_ref[own] - shift_ref[other]
        angle = jnp.where(jnp.abs(spacing) <= FILTER_HALF, jnp.pi * gap * spacing, 0.0)
        for part, taps in enumerate((window * jnp.cos(angle), window * jnp.sin(angle))):
            spread = jnp.broadcast_to(taps, (LANES, 2 * LANES))
            spread = pltpu.roll(spread, 0, 1, stride=1, stride_axis=0)
            high, low = halves(spread)
            weight_ref[0, part * LANES : (part + 1) * LANES, :] = high
            weight_ref[1, part * LANES : (part + 1) * LANES, :] = low
        both = jnp.concatenate([resampled_ref[own], resampled_ref[other]], axis=0)
        for begin in range(0, up(chunk, LANES), LANES):
            end = min(begin + span, held)
            taken = end - begin
            total = dot_nt(both[:, begin:end], weight_ref[0, :, :taken])
            total += dot_nt(both[:, begin:end], weight_ref[1, :, :taken])
            cos, sin = total[:, :LANES], total[:, LANES:]
            re, im = slice(0, lines), slice(lines, 2 * lines)
            master_re = cos[re] + sin[im]
            master_im = cos[im] - sin[re]
            re, im = slice(2 * lines, 3 * lines), slice(3 * lines, 4 * lines)
            partner_re = cos[re] - sin[im]
            partner_im = cos[im] + sin[re]
            for part, product in enumerate(
                (
                    master_re * partner_re + master_im * partner_im,
                    master_im * partner_re - master_re * partner_im,
                )
            ):
                summed = sum(product[k * groups : (k + 1) * groups] for k in range(LOOK_AZ))
                product_ref[place, part, :, begin : begin + LANES] = summed

    if isinstance(pairs, int):
        count = pairs

        def step(place, carry):
            one_pair(place, table_of_pairs[place, 0], table_of_pairs[place, 1])
            return carry

        lax.fori_loop(0, count, step, 0)
    else:
        count = len(pairs)
        for place, (own, other) in enumerate(pairs):
            one_pair(place, own, other)

    out_width = out_ref.shape[2]
    column = lax.broadcasted_iota(jnp.int32, (product_ref.shape[3], out_width), 0)
    lane = lax.broadcasted_iota(jnp.int32, (product_ref.shape[3], out_width), 1)
    collect = jnp.where(column // LOOK_RG == lane % looks, 1.0, 0.0).astype(jnp.bfloat16)
    high, low = halves(product_ref[...].reshape(count * 2 * groups, product_ref.shape[3]))
    total = (dot(high, collect) + dot(low, collect)) * (1.0 / (LOOK_AZ * LOOK_RG))
    total = total.reshape(count, 2, groups, out_width)
    own_lane = lax.broadcasted_iota(jnp.int32, (groups, out_width), 1) // looks
    place = 0
    for own in range(dates):
        value = jnp.zeros((groups, out_width), jnp.float32)
        for lag in range(min(LAGS, dates - 1 - own)):
            for part in range(2):
                value = jnp.where(own_lane == lag * 2 + part, total[place, part], value)
            place += 1
        out_ref[own * az_count : (own + 1) * az_count] = value.reshape(az_count, groups // az_count, out_width)


def unpack_kernel(used_lags, looks, recv_ref, out_ref):
    sources, groups, width = recv_ref.shape
    columns = out_ref.shape[-1]
    lane = lax.broadcasted_iota(jnp.int32, (groups, columns), 1) // looks
    out_ref[...] = jnp.zeros_like(out_ref)
    for lag in range(used_lags):
        for part in range(2):
            value = jnp.zeros((groups, columns), jnp.float32)
            for source in range(sources):
                block = recv_ref[source]
                if width != columns:
                    block = block[:, :columns]
                shift = looks * (source - lag * 2 - part) % columns
                if shift:
                    block = pltpu.roll(block, shift, 1)
                value = jnp.where(lane == source, block, value)
            out_ref[part, lag] = value


def chunked_body(slc, offsets, kernel_index, range_shift):
    axes = ("date", "az")
    date_count, az_count, rng_count = (lax.axis_size(a) for a in ("date", "az", "rng"))
    peers = date_count * az_count
    lines, columns = slc.shape[2], slc.shape[3]
    dates = range_shift.shape[0]
    chunk = columns // peers
    looks = chunk // LOOK_RG
    groups = lines * az_count // LOOK_AZ
    wide = up(chunk + 2 * FILTER_HALF + TAPS - 1 + META, LANES)
    held = up(chunk + 2 * FILTER_HALF, LANES)
    used_lags = min(LAGS, dates - 1)
    out_width = up(used_lags * 2 * looks, LANES)
    vmem = pl.BlockSpec(memory_space=pltpu.VMEM)
    smem = pl.BlockSpec(memory_space=pltpu.SMEM)
    limit = pltpu.CompilerParams(vmem_limit_bytes=32 * 1024 * 1024)

    cells = slc.reshape(2 * lines, columns)
    place = lax.axis_index("rng")
    if rng_count == 2:
        edge = jnp.where(place == 0, cells[:, columns - LANES :], cells[:, :LANES])
        before = after = lax.ppermute(edge, "rng", [(0, 1), (1, 0)])
    else:
        forth = [(i, i + 1) for i in range(rng_count - 1)]
        before = lax.ppermute(cells[:, columns - LANES :], "rng", forth)
        after = lax.ppermute(cells[:, :LANES], "rng", [(b, a) for a, b in forth])

    packed = pl.pallas_call(
        functools.partial(pack_kernel, chunk),
        out_shape=jax.ShapeDtypeStruct((peers, 2 * lines, wide), jnp.bfloat16),
        in_specs=[smem] * 3 + [vmem] * 3,
        out_specs=vmem,
        scratch_shapes=[pltpu.VMEM((2 * lines, columns + 2 * LANES), jnp.bfloat16)],
        compiler_params=limit,
    )(jnp.stack([place, rng_count]).astype(jnp.int32), offsets, kernel_index, cells, before, after)
    arrived = lax.all_to_all(packed, axes, 0, 0, tiled=True)

    pairs = [(own, own + lag) for own in range(dates) for lag in range(1, LAGS + 1) if own + lag < dates]
    count = len(pairs)
    first = [jnp.asarray(np.array(pairs, np.int32))] if count > UNROLLED_PAIRS else []
    looked = pl.pallas_call(
        functools.partial(pairs_kernel, chunk, count if first else pairs),
        out_shape=jax.ShapeDtypeStruct((peers, groups // az_count, out_width), jnp.float32),
        in_specs=[smem] * len(first) + [smem] + [vmem] * 3,
        out_specs=vmem,
        scratch_shapes=[
            pltpu.VMEM((dates, 4 * (groups * LOOK_AZ) // 2, held), jnp.bfloat16),
            pltpu.VMEM((2, 2 * LANES, 2 * LANES), jnp.bfloat16),
            pltpu.VMEM((count, 2, groups, up(chunk, LANES)), jnp.float32),
        ],
        compiler_params=limit,
    )(*first, range_shift, jnp.asarray(kernel_table()), jnp.asarray(lowpass_row(2 * LANES)), arrived)
    returned = lax.all_to_all(looked, axes, 0, 0, tiled=True)

    out = pl.pallas_call(
        functools.partial(unpack_kernel, used_lags, looks),
        out_shape=jax.ShapeDtypeStruct((2, LAGS, groups // az_count, looks * peers), jnp.float32),
        in_specs=[vmem],
        out_specs=vmem,
        compiler_params=limit,
    )(returned)
    return out[:, None]


HALO_LINES = 16
FOLD = 16
TAIL = 2 * FILTER_HALF


def reach(step, dates):
    return {dates - 1: dates // 2, dates // 2: dates - 1}.get(step, step)


def sinc(value):
    angle = jnp.pi * value
    return jnp.where(angle == 0.0, 1.0, jnp.sin(angle) / jnp.where(angle == 0.0, 1.0, angle))


def tap_row(index):
    lane = lax.broadcasted_iota(jnp.int32, (1, LANES), 1)
    position = lane.astype(jnp.float32) - 3.0 - index.astype(jnp.float32) / KERNELS
    shaped = sinc(position) * (0.5 + 0.5 * jnp.cos(jnp.pi * position / 5.0))
    shaped = jnp.where(lane < TAPS, shaped, 0.0)
    return shaped / jnp.sum(shaped, axis=1, keepdims=True)


def row_line(row, az):
    quarter = HALO_LINES // LOOK_AZ
    within = row % HALO_LINES
    return HALO_LINES * ((row // HALO_LINES) ^ az) + LOOK_AZ * (within % quarter) + within // quarter


def prepare_kernel(offsets_hbm, index_hbm, slc_ref, side_ref, lines_ref, line_ref, column_ref, held_ref, offsets_ref, index_ref, semaphores):
    lines, columns = slc_ref.shape[1:]
    az = lax.axis_index("az")
    row = pl.multiple_of((1 - az) * (lines - HALO_LINES), HALO_LINES)
    edge = pl.multiple_of((1 - lax.axis_index("rng")) * (columns - LANES), LANES)
    nearest, outermost = pl.ds(row, HALO_LINES), pl.ds(edge, LANES)
    moves = [
        (offsets_hbm, offsets_ref),
        (index_hbm, index_ref),
        (slc_ref.at[:, :, outermost], side_ref),
        (slc_ref.at[:, nearest, :], lines_ref),
    ]
    for plane in range(2):
        for part in range(lines // HALO_LINES):
            for side in range(2):
                at = pl.ds(part * HALO_LINES, HALO_LINES)
                source = slc_ref.at[plane, at, pl.ds(side * columns // 2, columns // 2)]
                moves.append((source, held_ref.at[plane, at, pl.ds(LANES + side * columns // 2, columns // 2)]))
    copies = [pltpu.make_async_copy(a, b, semaphores.at[i]) for i, (a, b) in enumerate(moves)]
    for copy in copies:
        copy.start()
    held_ref[:, :, :LANES] = jnp.zeros((2, lines, LANES), held_ref.dtype)
    held_ref[:, :, LANES + columns :] = jnp.zeros((2, lines, 2 * LANES), held_ref.dtype)
    copies[0].wait()
    copies[1].wait()
    for half in range(2):
        shape = (HALO_LINES, lines + HALO_LINES)
        line = row_line(lax.broadcasted_iota(jnp.int32, shape, 0) + half * HALO_LINES, az)
        place = lax.broadcasted_iota(jnp.int32, shape, 1)
        source = jnp.where(place < lines, place, place + jnp.where(az == 0, 0, -lines - HALO_LINES))
        taps = banded(tap_row(index_ref[0, 0]), source - line - offsets_ref[0, 0] + 3)
        line_ref[half] = jnp.concatenate(halves(taps), axis=0)
    shape = (2 * LANES, LANES)
    distance = lax.broadcasted_iota(jnp.int32, shape, 0) - lax.broadcasted_iota(jnp.int32, shape, 1)
    distance = distance - (LANES // 2 - FILTER_HALF - 3) - offsets_ref[0, 1]
    taps = banded(tap_row(index_ref[0, 1]), distance)
    column_ref[...] = jnp.concatenate(halves(taps), axis=1)
    for copy in copies[2:]:
        copy.wait()


def along_range(moved, column_ref, tiles):
    high, low = halves(pltpu.roll(moved, moved.shape[1] - LANES // 2, 1))
    starts = range(0, tiles * LANES, LANES)
    high = jnp.concatenate([high[:, s : s + 2 * LANES] for s in starts], axis=0)
    low = jnp.concatenate([low[:, s : s + 2 * LANES] for s in starts], axis=0)
    total = dot(high, column_ref[...])
    return total[:, :LANES] + total[:, LANES:] + dot(low, column_ref[:, :LANES])


def early_kernel(tiles, held_ref, line_ref, column_ref, out_ref):
    lines = held_ref.shape[1]
    early = out_ref.shape[0] // (2 * HALO_LINES)
    dates = lax.axis_size("date")
    chunk = lax.axis_index("date") ^ reach(dates - 1, dates)
    begin = pl.multiple_of((chunk * tiles + lax.axis_index("rng")) * LANES, LANES)
    moved = []
    for plane in range(2):
        both = dot(line_ref[0, :, :lines], held_ref[plane, :, pl.ds(begin, (early + 2) * LANES)])
        moved.append(both[:HALO_LINES] + both[HALO_LINES:])
    moved = jnp.concatenate(moved, axis=0)
    out_ref[...] = along_range(moved, column_ref, early).astype(jnp.bfloat16)


def resample_kernel(corner_ref, side_ref, lines_ref, held_ref, line_ref, column_ref, *outs):
    outs, tiles_ref, tails_ref = outs[:-2], outs[-2], outs[-1]
    lines, width = held_ref.shape[1:]
    width -= LANES
    block = lax.axis_index("rng")
    nearest = pl.multiple_of(lax.axis_index("az") * (lines - HALO_LINES), HALO_LINES)
    taps = jnp.concatenate([line_ref[0], line_ref[1]], axis=0)
    moved = [[], []]
    for plane in range(2):
        own = jnp.concatenate([side_ref[plane], held_ref[plane, :, LANES : width - LANES], side_ref[plane]], axis=1)
        corner = corner_ref[plane, pl.ds(nearest, HALO_LINES), :]
        halo = jnp.concatenate([corner, lines_ref[plane], corner], axis=1)
        both = dot(taps, jnp.concatenate([own, halo], axis=0))
        for half in range(2):
            at = 2 * half * HALO_LINES
            moved[half].append(both[at : at + HALO_LINES] + both[at + HALO_LINES : at + 2 * HALO_LINES])
    moved = jnp.concatenate(moved[0] + moved[1], axis=0)
    left = jnp.where(block > 0, moved[:, :LANES], 0.0)
    right = jnp.where(block == 0, moved[:, width - LANES :], 0.0)
    moved = jnp.concatenate([left, moved[:, LANES : width - LANES], right, jnp.zeros_like(right)], axis=1)
    total = along_range(moved, column_ref, width // LANES - 1)
    rows = 2 * lines
    tiles_ref[...] = total.astype(jnp.bfloat16)
    chunk_rows = outs[0].shape[0] - FOLD
    lane = lax.broadcasted_iota(jnp.int32, (FOLD, LANES), 1) // TAIL
    for chunk in range(len(outs)):
        begin = (chunk + 1) * chunk_rows
        folded = total[begin : begin + FOLD]
        for part in range(1, rows // FOLD):
            value = pltpu.roll(total[begin + part * FOLD : begin + (part + 1) * FOLD], part * TAIL, 1)
            folded = jnp.where(lane == part, value, folded)
        tails_ref[chunk] = folded.astype(jnp.bfloat16)
    date = lax.axis_index("date")
    for step, out_ref in enumerate(outs[:-1]):
        chunk = date ^ reach(step, len(outs))
        out_ref[:chunk_rows] = tiles_ref[pl.ds(pl.multiple_of(chunk * chunk_rows, FOLD), chunk_rows), :]
        out_ref[chunk_rows:] = tails_ref[chunk]
    out_ref = outs[-1]
    chunk = date ^ reach(len(outs) - 1, len(outs))
    early = chunk_rows // rows - 1
    for tile in range(early):
        begin = pl.multiple_of(chunk * chunk_rows + (tile + block) * rows + lines, FOLD)
        out_ref[tile * lines : (tile + 1) * lines] = tiles_ref[pl.ds(begin, lines), :]
    begin = pl.multiple_of(chunk * chunk_rows + (1 - block) * early * rows, FOLD)
    out_ref[early * lines : early * lines + rows] = tiles_ref[pl.ds(begin, rows), :]
    out_ref[early * lines + rows :] = tails_ref[chunk]


def filter_kernel(pairs, shift_hbm, early_ref, out_ref, spread_ref, shift_ref, semaphore):
    copy = pltpu.make_async_copy(shift_hbm, shift_ref, semaphore)
    copy.start()
    lines = 2 * HALO_LINES
    spread_ref[...] = jnp.zeros_like(spread_ref)
    for tile in range(early_ref.shape[0] // lines):
        begin = pl.multiple_of((tile + lax.axis_index("rng")) * 2 * lines, FOLD)
        spread_ref[pl.ds(begin, lines), :] = early_ref[tile * lines : (tile + 1) * lines]
    date = lax.axis_index("date")
    spacing = lax.broadcasted_iota(jnp.int32, (1, 2 * LANES), 1).astype(jnp.float32) - FILTER_HALF
    window = 0.4 * sinc(0.4 * spacing) * (0.54 + 0.46 * jnp.cos(jnp.pi * spacing / (FILTER_HALF + 1)))
    window = jnp.where(jnp.abs(spacing) <= FILTER_HALF, window, 0.0)
    copy.wait()
    for place, (first, second) in enumerate(pairs):
        dates = shift_ref.shape[0]
        gap = shift_ref[date ^ reach(first, dates)] - shift_ref[date ^ reach(second, dates)]
        angle = jnp.where(jnp.abs(spacing) <= FILTER_HALF, jnp.pi * gap * spacing, 0.0)
        for part, taps in enumerate((window * jnp.cos(angle), window * jnp.sin(angle))):
            spread = jnp.broadcast_to(taps, (LANES, 2 * LANES))
            spread = pltpu.roll(spread, 0, 1, stride=1, stride_axis=0)
            high, low = halves(spread)
            out_ref[place, part * LANES : (part + 1) * LANES, : 2 * LANES] = high
            out_ref[place, part * LANES : (part + 1) * LANES, 2 * LANES :] = low


def looks_kernel(pairs, dates, weight_ref, *refs):
    early_ref, chunks, outs = refs[0], list(refs[1 : dates + 1][::-1]), refs[dates + 1 : 2 * dates + 1]
    whole_ref, window_ref, product_ref = refs[-3:]
    groups, lines = outs[0].shape[0], outs[0].shape[0] * LOOK_AZ
    rows = 2 * lines
    blocks = (chunks[0].shape[0] - FOLD) // rows
    looks = blocks * LANES // LOOK_RG
    date = lax.axis_index("date")
    block = lax.axis_index("rng")
    early = blocks - 1
    whole_ref[: blocks * rows] = early_ref[...]
    for tile in range(early):
        begin = pl.multiple_of((tile + block) * rows, FOLD)
        whole_ref[pl.ds(begin + lines, lines), :] = chunks[-1][tile * lines : (tile + 1) * lines]
    begin = pl.multiple_of((1 - block) * early * rows, FOLD)
    whole_ref[pl.ds(begin, rows), :] = chunks[-1][early * lines : early * lines + rows]
    whole_ref[blocks * rows :] = chunks[-1][early * lines + rows :]
    chunks[-1] = whole_ref
    az = lax.axis_index("az")
    upper = lax.broadcasted_iota(jnp.int32, (groups, LANES), 0) // (groups // 2) == az
    for step, chunk_ref in enumerate(chunks):
        window_ref[step, :, :LANES] = chunk_ref[: blocks * rows]
        window_ref[step, : (blocks - 1) * rows, LANES:] = chunk_ref[rows : blocks * rows]
        folded = chunk_ref[blocks * rows :].astype(jnp.float32)
        for part in range(rows // FOLD):
            value = pltpu.roll(folded, LANES - part * TAIL, 1) if part else folded
            at = pl.ds((blocks - 1) * rows + part * FOLD, FOLD)
            window_ref[step, at, LANES:] = value.astype(jnp.bfloat16)
    for place, (first, second) in enumerate(pairs):
        def filtered(step):
            window = window_ref[step]
            total = dot_nt(jnp.concatenate([window, window], axis=1), weight_ref[place])
            total = total.reshape(blocks, 2, 2, HALO_LINES, 2 * LANES)
            re, im = total[:, :, 0], total[:, :, 1]
            return re[..., :LANES], im[..., :LANES], re[..., LANES:], im[..., LANES:]

        cos_re, cos_im, sin_re, sin_im = filtered(first)
        master_re, master_im = cos_re + sin_im, cos_im - sin_re
        cos_re, cos_im, sin_re, sin_im = filtered(second)
        partner_re, partner_im = cos_re - sin_im, cos_im + sin_re
        for part, product in enumerate(
            (
                master_re * partner_re + master_im * partner_im,
                master_im * partner_re - master_re * partner_im,
            )
        ):
            summed = product[:, :, :groups] + product[:, :, groups:]
            at = pl.ds((place * 2 + part) * groups, groups)
            for k in range(blocks):
                both = [summed[k, half] + pltpu.roll(summed[k, half], groups // 2, 0) for half in range(2)]
                product_ref[at, k * LANES : (k + 1) * LANES] = jnp.where(upper, both[0], both[1])

    out_width = outs[0].shape[1]
    column = lax.broadcasted_iota(jnp.int32, (product_ref.shape[1], out_width), 0)
    lane = lax.broadcasted_iota(jnp.int32, (product_ref.shape[1], out_width), 1)
    collect = jnp.where(column // LOOK_RG == lane % looks, 1.0, 0.0).astype(jnp.bfloat16)
    high, low = halves(product_ref[...])
    total = (dot(high, collect) + dot(low, collect)) * (1.0 / (LOOK_AZ * LOOK_RG))
    total = total.reshape(len(pairs), 2, groups, out_width)
    own_lane = lax.broadcasted_iota(jnp.int32, (groups, out_width), 1) // looks
    for step, out_ref in enumerate(outs):
        value = jnp.zeros((groups, out_width), jnp.float32)
        for place, pair in enumerate(pairs):
            if step in pair:
                other = pair[1] if pair[0] == step else pair[0]
                lag = (date ^ reach(other, dates)) - (date ^ reach(step, dates))
                for part in range(2):
                    signed = -total[place, part] if part == 1 and pair[1] == step else total[place, part]
                    value = jnp.where(own_lane == (lag - 1) * 2 + part, signed, value)
        out_ref[...] = value


def place_kernel(used_lags, looks, *refs):
    received, out_ref = refs[:-1][::-1], refs[-1]
    groups, columns = out_ref.shape[2:]
    date = lax.axis_index("date")
    lane = lax.broadcasted_iota(jnp.int32, (groups, columns), 1) // looks
    here = [lane == (date ^ step) for step in range(len(received))]
    each = columns // looks
    for part in range(2):
        for lag in range(used_lags):
            tile, group = divmod(lag * 2 + part, each)
            value = jnp.zeros((groups, columns), jnp.float32)
            for step, recv_ref in enumerate(received):
                shift = lax.bitwise_and(looks * ((date ^ step) - group), columns - 1)
                block = pltpu.roll(recv_ref[:, tile * columns : (tile + 1) * columns], shift, 1)
                value = jnp.where(here[step], block, value)
            out_ref[part, lag] = value
        for lag in range(used_lags, out_ref.shape[1]):
            out_ref[part, lag] = jnp.zeros((groups, columns), jnp.float32)


def tiled_body(slc, offsets, kernel_index, range_shift):
    dates = lax.axis_size("date")
    lines, columns = slc.shape[2], slc.shape[3]
    chunk = columns // dates
    looks = chunk // LOOK_RG
    groups = lines // LOOK_AZ
    out_width = up(min(LAGS, dates - 1) * 2 * looks, LANES)
    vmem = pl.BlockSpec(memory_space=pltpu.VMEM)
    hbm = pl.BlockSpec(memory_space=pltpu.HBM)
    limit = pltpu.CompilerParams(vmem_limit_bytes=32 * 1024 * 1024)
    bf16 = jnp.bfloat16
    cells, offsets, kernel_index, range_shift = (
        pltpu.with_memory_space_constraint(value, pltpu.HBM)
        for value in (slc.reshape(2, lines, columns), offsets, kernel_index, range_shift)
    )
    tiles = chunk // LANES
    chunk_rows = tiles * 2 * lines

    side, halo_lines, line_taps, column_taps, held = pl.pallas_call(
        prepare_kernel,
        out_shape=[
            jax.ShapeDtypeStruct((2, lines, LANES), bf16),
            jax.ShapeDtypeStruct((2, HALO_LINES, columns), bf16),
            jax.ShapeDtypeStruct((2, 2 * HALO_LINES, lines + HALO_LINES), bf16),
            jax.ShapeDtypeStruct((2 * LANES, 2 * LANES), bf16),
            jax.ShapeDtypeStruct((2, lines, columns + 3 * LANES), bf16),
        ],
        in_specs=[hbm] * 3,
        out_specs=[vmem] * 5,
        scratch_shapes=[
            pltpu.SMEM(offsets.shape, jnp.int32),
            pltpu.SMEM(kernel_index.shape, jnp.int32),
            pltpu.SemaphoreType.DMA((4 + 4 * (lines // HALO_LINES),)),
        ],
        compiler_params=limit,
    )(offsets, kernel_index, cells)
    swap = [(0, 1), (1, 0)]
    corner = lax.ppermute(side, ("rng", "az"), [(0, 3), (1, 2), (2, 1), (3, 0)])
    side = lax.ppermute(side, "rng", swap)
    halo_lines = lax.ppermute(halo_lines, "az", swap)

    early_rows = (tiles - 1) * lines
    early = pl.pallas_call(
        functools.partial(early_kernel, tiles),
        out_shape=jax.ShapeDtypeStruct((early_rows, LANES), bf16),
        in_specs=[vmem] * 3,
        out_specs=vmem,
        compiler_params=limit,
        cost_estimate=pl.CostEstimate(flops=1_000_000_000, bytes_accessed=0, transcendentals=0),
    )(held, line_taps, column_taps)
    early = lax.ppermute(early, "date", [(i, i ^ reach(dates - 1, dates)) for i in range(dates)])
    out_rows = [chunk_rows + FOLD] * (dates - 1) + [chunk_rows + FOLD - early_rows]
    sent = pl.pallas_call(
        resample_kernel,
        out_shape=[jax.ShapeDtypeStruct((rows, LANES), bf16) for rows in out_rows],
        in_specs=[vmem] * 6,
        out_specs=[vmem] * dates,
        scratch_shapes=[
            pltpu.VMEM(((columns // LANES + 1) * 2 * lines, LANES), bf16),
            pltpu.VMEM((dates, FOLD, LANES), bf16),
        ],
        compiler_params=limit,
    )(corner, side, halo_lines, held, line_taps, column_taps)

    def exchanged(values, order):
        arrived = {0: values[0]}
        for step in order:
            arrived[step] = lax.ppermute(values[step], "date", [(i, i ^ reach(step, dates)) for i in range(dates)])
        return [arrived[step] for step in reversed(range(dates))]

    steps = range(dates - 1, 0, -1)

    chunks = exchanged(sent, steps)
    pairs = [(first, second) for first in range(dates) for second in range(first + 1, dates)]
    weights, early = pl.pallas_call(
        functools.partial(filter_kernel, pairs),
        out_shape=[
            jax.ShapeDtypeStruct((len(pairs), 2 * LANES, 4 * LANES), bf16),
            jax.ShapeDtypeStruct((chunk_rows, LANES), bf16),
        ],
        in_specs=[hbm, vmem],
        out_specs=[vmem] * 2,
        scratch_shapes=[pltpu.SMEM(range_shift.shape, jnp.float32), pltpu.SemaphoreType.DMA],
        compiler_params=limit,
        cost_estimate=pl.CostEstimate(flops=600_000_000, bytes_accessed=0, transcendentals=0),
    )(range_shift, early)
    looked = pl.pallas_call(
        functools.partial(looks_kernel, pairs, dates),
        out_shape=[jax.ShapeDtypeStruct((groups, out_width), jnp.float32)] * dates,
        in_specs=[vmem] * (2 + dates),
        out_specs=[vmem] * dates,
        scratch_shapes=[
            pltpu.VMEM((chunk_rows + FOLD, LANES), bf16),
            pltpu.VMEM((dates, chunk_rows, 2 * LANES), bf16),
            pltpu.VMEM((len(pairs) * 2 * groups, chunk), jnp.float32),
        ],
        compiler_params=limit,
    )(weights, early, *chunks)
    returned = exchanged(looked, steps)[::-1]
    returned = [returned[reach(distance, dates)] for distance in reversed(range(dates))]
    out = pl.pallas_call(
        functools.partial(place_kernel, min(LAGS, dates - 1), looks),
        out_shape=jax.ShapeDtypeStruct((2, LAGS, groups, looks * dates), jnp.float32),
        in_specs=[vmem] * dates,
        out_specs=vmem,
        compiler_params=limit,
    )(*returned)
    return out[:, None]


def body(slc, offsets, kernel_index, range_shift):
    dates, az_count = (lax.axis_size(a) for a in ("date", "az"))
    lines, columns = slc.shape[2], slc.shape[3]
    whole_tiles = columns % (dates * LANES) == 0 and columns % (dates * LOOK_RG) == 0
    one_row = columns // LOOK_RG == LANES and range_shift.shape[0] == dates
    few = dates & (dates - 1) == 0 and dates - 1 <= LAGS
    folds = lines == 2 * HALO_LINES and lax.axis_size("rng") == 2 and dates >= 4 and 2 * lines // FOLD * TAIL <= LANES
    if az_count == 2 and whole_tiles and one_row and few and folds:
        return tiled_body(slc, offsets, kernel_index, range_shift)
    return chunked_body(slc, offsets, kernel_index, range_shift)


def solution(mesh):
    return jax.shard_map(
        body,
        mesh=mesh,
        in_specs=(
            P(None, ("groups", "date"), "az", "rng"),
            P(("groups", "date"), None),
            P(("groups", "date"), None),
            P("groups"),
        ),
        out_specs=P(None, ("groups", "date"), None, "az", "rng"),
        check_vma=False,
    )
```
